32 devices in a mesh: groups: 2 (over x), grid: 8 (over z, y), depth: 2 (over core).
Axes of the slice: x: 2, y: 2, z: 4, core: 2. Of those that a mesh axis runs over, the one named last changes fastest.
Arguments:
- x_band: bfloat16 [8192, 4096], P(('groups', 'grid')), parts along dimension 0, may hold values from -6 to 6
- w_band: bfloat16 [8192, 4096], P(('groups', 'grid')), parts along dimension 0, may hold values from -0.09375 to 0.09375
- a_mask: int32 [128, 64], P(('groups', 'grid')), parts along dimension 0, may hold values from 0 to 1, as said below
- keep_mask: int32 [128, 64], P(('groups', 'grid', 'depth')), parts along dimension 0, may hold values 0 or 1
Outputs:
- new_iterate: bfloat16 [8192, 4096], P(('groups', 'grid', 'depth')), parts along dimension 0
The draws below stay inside these ranges and needn't reach their ends.
There are 2 independent parts, one for each index of `groups`. The reference program is written for one: setup_inputs(seed, part) draws one part's arguments, and reference() takes and returns one part's arrays. A program takes and returns all parts, laid end to end along the dimension named above; each array names one. Nothing has to cross between parts.
Inputs may be any that keep to these rules, and one draw needn't show every extreme that they name: `a_mask`: 0 or 1 per block; the share of ones differs from block row to block row.
All inputs are finite; a program needn't handle non-finite values. No bound on the sum of `keep_mask` on one device may be relied on, other than what follows from the above.
Results may differ from the reference program's by a relative error of at most 0.0046.
Values may be sent and summed in bfloat16 or wider, within the bound.
No kernel may reach another device: no remote copies, remote signals or barrier semaphores. Data moves between devices by JAX's collectives and lax.ppermute only.
A program may use at most 128 MiB of HBM per device.

```python
import jax
import jax.numpy as jnp

BLOCK = 64
RB = 8
BAND = 8
ORDER = 4096
NBLK = 64
N_GRID = 8


def draw_a_mask(key, part):
    key = jax.random.fold_in(key, 11)
    first, second = jax.random.split(key)
    density = jax.random.randint(first, (NBLK, 1), 2, 10)
    values = jax.random.randint(second, (NBLK, BAND * RB), 0, 10)
    return (values < density).astype(jnp.int32)


def plant(result, stream_key, low, high):
    index_at = [jax.random.randint(jax.random.fold_in(stream_key, axis), (), 0, length) for axis, length in enumerate(result.shape)]
    longest = result.shape.index(max(result.shape))
    neighbour = index_at[:longest] + [(index_at[longest] + 1) % result.shape[longest]] + index_at[longest + 1:]
    return result.at[tuple(index_at)].set(low).at[tuple(neighbour)].set(high)


def steps_of(rng, extent, cuts, low, largest):
    loudness, own = 1.0, jax.random.fold_in(rng, 6)
    for dim, shards_of in cuts:
        steps = jnp.exp(jax.random.uniform(jax.random.fold_in(own, dim), (shards_of,), jnp.float32, low / len(cuts), largest / len(cuts)))
        loudness = loudness * jnp.repeat(steps, extent[dim] // shards_of).reshape([-1 if axis == dim else 1 for axis in range(len(extent))])
    return loudness


def bell_draw(stream_key, shape, scale, limit, pieces=(), dtype=jnp.bfloat16):
    array = jax.random.normal(stream_key, shape, jnp.float32) * scale
    if len(pieces) > 0:
        array = steps_of(stream_key, shape, pieces, -0.22, 0.18) * array
    return jnp.clip(array, min=-limit, max=limit).astype(dtype)


def setup_inputs(seed: int = 0, part: int = 0) -> dict:
    key_of = jax.random.split(jax.random.key(seed), 5)
    own_keys = jax.random.split(jax.random.fold_in(key_of[4], part), 5)
    return {
        "x_band": bell_draw(own_keys[0], (ORDER, BAND * RB * BLOCK), 1.0, 6.0, ((0, 8),)),
        "w_band": bell_draw(own_keys[1], (ORDER, BAND * RB * BLOCK), (BAND * RB * BLOCK) ** -0.5, 0.09375, ((0, 8),)),
        "a_mask": draw_a_mask(jax.random.fold_in(jax.random.fold_in(key_of[4], part), 71), part),
        "keep_mask": plant((jax.random.randint(own_keys[3], (NBLK, BAND * RB), 0, 4) < 3).astype(jnp.int32), jax.random.fold_in(own_keys[3], 1), 0, 1),
    }


def expand_blocks(mask, block):
    rows, cols = mask.shape
    wide = jnp.broadcast_to(mask[:, None, :, None], (rows, block, cols, block))
    return wide.reshape(rows * block, cols * block)


def reference(x_band, w_band, a_mask, keep_mask):
    panel = RB * BLOCK
    xm = x_band * expand_blocks(a_mask, BLOCK).astype(jnp.bfloat16)
    rows = jnp.arange(ORDER)[:, None] % panel
    cols = jnp.arange(BAND * panel)[None, :]
    identity = jnp.where(cols == rows + 4 * panel, 1.0, 0.0).astype(jnp.float32)
    b_band = (1.5 * identity - 0.5 * w_band.astype(jnp.float32)).astype(jnp.bfloat16)
    results = []
    for g in range(N_GRID):
        wide = jnp.zeros((panel, 2 * BAND * panel), jnp.float32)
        for delta in range(-4, 4):
            h = (g + delta) % N_GRID
            ablock = xm[g * panel:(g + 1) * panel, (delta + 4) * panel:(delta + 5) * panel]
            term = jnp.dot(ablock, b_band[h * panel:(h + 1) * panel], preferred_element_type=jnp.float32)
            wide = wide.at[:, (delta + 4) * panel:(delta + 12) * panel].add(term)
        results.append(wide[:, 4 * panel:12 * panel])
    product = jnp.concatenate(results, axis=0)
    keep = expand_blocks(keep_mask, BLOCK).astype(jnp.float32)
    return (product * keep).astype(jnp.bfloat16)
```

```python
import functools

import jax
import jax.numpy as jnp
from jax import lax
from jax.experimental import pallas as pl
from jax.experimental.pallas import tpu as pltpu
from jax.sharding import PartitionSpec as P

LANES = 128
MIB = 1 << 20


def shifted(shard, axis, by):
    count = lax.axis_size(axis)
    return lax.ppermute(shard, axis, [(i, (i + by) % count) for i in range(count)])


def expand_blocks(mask, block):
    rows, cols = mask.shape
    wide = jnp.broadcast_to(mask[:, None, :, None], (rows, block, cols, block))
    return wide.reshape(rows * block, cols * block)


def ring(x_band, w_band, a_mask, keep_mask):
    panel = x_band.shape[0]
    block = panel // a_mask.shape[0]
    band_cols = x_band.shape[1]
    xm = x_band * expand_blocks(a_mask, block).astype(jnp.bfloat16)
    rows = lax.broadcasted_iota(jnp.int32, x_band.shape, 0)
    cols = lax.broadcasted_iota(jnp.int32, x_band.shape, 1)
    identity = jnp.where(cols == rows + 4 * panel, 1.0, 0.0).astype(jnp.float32)
    b_panel = (1.5 * identity - 0.5 * w_band.astype(jnp.float32)).astype(jnp.bfloat16)
    layer = lax.axis_index("depth")
    current = shifted(b_panel, ("grid", "depth"), -5)
    wide = jnp.zeros((panel, 2 * band_cols), jnp.float32)
    for step in range(4):
        offset = 6 + layer - 2 * step
        ablock = lax.dynamic_slice_in_dim(xm, offset * panel, panel, 1)
        term = jnp.dot(ablock, current, preferred_element_type=jnp.float32)
        region = lax.dynamic_slice_in_dim(wide, offset * panel, band_cols, 1)
        wide = lax.dynamic_update_slice_in_dim(wide, region + term, offset * panel, 1)
        if step < 3:
            current = shifted(current, "grid", 2)
    partial_band = wide[:, 4 * panel : 12 * panel]
    mine = lax.psum_scatter(partial_band, "depth", scatter_dimension=0, tiled=True)
    keep = expand_blocks(keep_mask, block).astype(jnp.float32)
    return (mine * keep).astype(jnp.bfloat16)


def strips_kernel(quarter_ref, w_ref, b_ref, held, sems):
    panel = held.shape[0]
    quarter = quarter_ref[0]
    band = held.shape[1] // LANES
    copies = []
    for j in range(band):
        at = pl.multiple_of(j * panel + quarter * LANES, LANES)
        copies.append(
            pltpu.make_async_copy(
                w_ref.at[:, pl.ds(at, LANES)],
                held.at[:, j * LANES : (j + 1) * LANES],
                sems.at[j],
            )
        )
        copies[-1].start()
    for j in range(band):
        copies[j].wait()
        value = -0.5 * held[:, j * LANES : (j + 1) * LANES].astype(jnp.float32)
        if j == band // 2:
            rows = lax.broadcasted_iota(jnp.int32, value.shape, 0)
            cols = lax.broadcasted_iota(jnp.int32, value.shape, 1)
            value = value + jnp.where(rows == cols + quarter * LANES, 1.5, 0.0)
        b_ref[:, j * LANES : (j + 1) * LANES] = value.astype(jnp.bfloat16)


def b_strips(w_band, quarter):
    panel = w_band.shape[0]
    band = w_band.shape[1] // panel
    shape = (panel, band * LANES)
    return pl.pallas_call(
        strips_kernel,
        out_shape=jax.ShapeDtypeStruct(shape, jnp.bfloat16),
        in_specs=[
            pl.BlockSpec(memory_space=pltpu.SMEM),
            pl.BlockSpec(memory_space=pl.ANY),
        ],
        out_specs=pl.BlockSpec(memory_space=pltpu.VMEM),
        scratch_shapes=[pltpu.VMEM(shape, jnp.bfloat16), pltpu.SemaphoreType.DMA((band,))],
        compiler_params=pltpu.CompilerParams(vmem_limit_bytes=16 * MIB),
        cost_estimate=pl.CostEstimate(flops=1000, bytes_accessed=4 * shape[0] * shape[1], transcendentals=0),
        name="b_strips",
    )(quarter.reshape(1), w_band)


def mask_kernel(half_ref, mask_ref, x_ref, out_ref):
    out_ref[...] = (x_ref[...].astype(jnp.float32) * mask_ref[0]).astype(jnp.bfloat16)


def masked_half(x_band, mask_wide, half):
    block = x_band.shape[0] // mask_wide.shape[0]
    per_half = mask_wide.shape[0] // 2
    cols = x_band.shape[1]
    return pl.pallas_call(
        mask_kernel,
        grid_spec=pltpu.PrefetchScalarGridSpec(
            num_scalar_prefetch=1,
            grid=(per_half,),
            in_specs=[
                pl.BlockSpec((1, 1, cols), lambda i, h: (h[0] * per_half + i, 0, 0)),
                pl.BlockSpec((block, cols), lambda i, h: (h[0] * per_half + i, 0)),
            ],
            out_specs=pl.BlockSpec((block, cols), lambda i, h: (i, 0)),
        ),
        out_shape=jax.ShapeDtypeStruct((x_band.shape[0] // 2, cols), jnp.bfloat16),
        compiler_params=pltpu.CompilerParams(vmem_limit_bytes=16 * MIB),
        cost_estimate=pl.CostEstimate(flops=1000, bytes_accessed=2 * x_band.shape[0] * cols, transcendentals=0),
        name="masked_half",
    )(half.reshape(1), mask_wide, x_band)


def product_kernel(widths, has_prev, final, meta_ref, *refs):
    n_b = len(widths)
    x_refs, refs = refs[:4], refs[4:]
    middle_refs, refs = refs[:n_b], refs[n_b:]
    end_refs, refs = refs[:n_b], refs[n_b:]
    prev_ref, refs = (refs[0], refs[1:]) if has_prev else (None, refs)
    n_out = 4 if final else 1
    out_refs, refs = refs[:n_out], refs[n_out:]
    xv, bv, acc, x_sems, b_sems, prev_sem = refs
    panel = bv.shape[1]
    quarter = bv.shape[2]
    band = quarter // LANES
    low = band // 2 * LANES
    is_end = meta_ref[0]

    def window(p):
        return pl.ds(pl.multiple_of(meta_ref[1 + 3 * p] * LANES, LANES), widths[p] * LANES)

    def b_copies(p):
        return (
            pltpu.make_async_copy(middle_refs[p], bv.at[p], b_sems.at[p]),
            pltpu.make_async_copy(end_refs[p], bv.at[p, :, window(p)], b_sems.at[p]),
        )

    def x_copy(p, r):
        at = pl.multiple_of(meta_ref[1 + 3 * p + 1 + r // 2] * panel, panel)
        return pltpu.make_async_copy(
            x_refs[r].at[:, pl.ds(at, panel)], xv.at[p, r], x_sems.at[p, r]
        )

    if has_prev:
        prev_copy = pltpu.make_async_copy(prev_ref, acc.at[:, :, low : low + quarter], prev_sem)
        prev_copy.start()
    for p in range(n_b):
        middle, end = b_copies(p)

        @pl.when(is_end == 0)
        def _():
            middle.start()

        @pl.when(is_end != 0)
        def _():
            end.start()

        for r in range(4):
            x_copy(p, r).start()
    if has_prev:
        prev_copy.wait()
    else:
        acc[...] = jnp.zeros_like(acc)
    for p in range(n_b):
        middle, end = b_copies(p)

        @pl.when(is_end == 0)
        def _():
            middle.wait()

        @pl.when(is_end != 0)
        def _():
            end.wait()

        for r in range(4):
            x_copy(p, r).wait()

        def step(r, carry):
            offset = meta_ref[1 + 3 * p + 1 + r // 2]
            cols = pl.ds(pl.multiple_of(offset * LANES, LANES), quarter)
            acc[r, :, cols] += jnp.dot(xv[p, r], bv[p], preferred_element_type=jnp.float32)
            return carry

        lax.fori_loop(0, 4, step, 0)
    if final:
        for r in range(4):
            out_refs[r][...] = acc[r, :, low : low + quarter].astype(jnp.bfloat16)
    else:
        out_refs[0][...] = acc[:, :, low : low + quarter]


def products(meta, xs, middle, end, prev, final, name):
    rows = xs[0].shape[0]
    panel, quarter = middle[0].shape
    n_b = len(middle)
    widths = tuple(e.shape[1] // LANES for e in end)
    any_spec = pl.BlockSpec(memory_space=pl.ANY)
    vmem_spec = pl.BlockSpec(memory_space=pltpu.VMEM)
    operands = [meta, *xs, *middle, *end] + ([] if prev is None else [prev])
    if final:
        out_shape = [jax.ShapeDtypeStruct((rows, quarter), jnp.bfloat16)] * 4
        out_specs = [vmem_spec] * 4
    else:
        out_shape = jax.ShapeDtypeStruct((4, rows, quarter), jnp.float32)
        out_specs = vmem_spec
    return pl.pallas_call(
        functools.partial(product_kernel, widths, prev is not None, final),
        out_shape=out_shape,
        in_specs=[pl.BlockSpec(memory_space=pltpu.SMEM)] + [any_spec] * (len(operands) - 1),
        out_specs=out_specs,
        scratch_shapes=[
            pltpu.VMEM((n_b, 4, rows, panel), jnp.bfloat16),
            pltpu.VMEM((n_b, panel, quarter), jnp.bfloat16),
            pltpu.VMEM((4, rows, 2 * quarter), jnp.float32),
            pltpu.SemaphoreType.DMA((n_b, 4)),
            pltpu.SemaphoreType.DMA((n_b,)),
            pltpu.SemaphoreType.DMA,
        ],
        compiler_params=pltpu.CompilerParams(vmem_limit_bytes=40 * MIB),
        cost_estimate=pl.CostEstimate(
            flops=2 * n_b * 4 * rows * panel * quarter,
            bytes_accessed=n_b * 2 * (4 * rows * panel + panel * quarter),
            transcendentals=0,
        ),
        name=name,
    )(*operands)


def assemble_kernel(quarter_ref, mask_ref, *refs):
    *pieces, out_ref = refs
    n = len(pieces)
    band = pieces[0].shape[1] // LANES
    panel = n * LANES
    for mine in range(n):

        @pl.when(quarter_ref[0] == mine)
        def _():
            for t in range(n):
                for j in range(band):
                    cols = slice(j * panel + t * LANES, j * panel + (t + 1) * LANES)
                    value = pieces[t ^ mine][:, j * LANES : (j + 1) * LANES].astype(jnp.float32)
                    out_ref[:, cols] = (value * mask_ref[0, :, cols]).astype(jnp.bfloat16)


def assembled(quarter, keep_wide, pieces):
    rows, width = pieces[0].shape
    steps = keep_wide.shape[0]
    block = rows // steps
    cols = width * len(pieces)
    return pl.pallas_call(
        assemble_kernel,
        grid_spec=pltpu.PrefetchScalarGridSpec(
            num_scalar_prefetch=1,
            grid=(steps,),
            in_specs=[pl.BlockSpec((1, 1, cols), lambda i, q: (i, 0, 0))]
            + [pl.BlockSpec((block, width), lambda i, q: (i, 0))] * len(pieces),
            out_specs=pl.BlockSpec((block, cols), lambda i, q: (i, 0)),
        ),
        out_shape=jax.ShapeDtypeStruct((rows, cols), jnp.bfloat16),
        compiler_params=pltpu.CompilerParams(vmem_limit_bytes=16 * MIB),
        cost_estimate=pl.CostEstimate(flops=1000, bytes_accessed=4 * rows * cols, transcendentals=0),
        name="assembled",
    )(quarter.reshape(1), keep_wide, *pieces)


def widen(mask, block):
    rows, cols = mask.shape
    wide = jnp.broadcast_to(mask.astype(jnp.float32)[:, :, None], (rows, cols, block))
    return wide.reshape(rows, 1, cols * block)


def pairs_in_line(x_band, w_band, a_mask, keep_mask):
    panel = x_band.shape[0]
    block = panel // a_mask.shape[0]
    g, c = lax.axis_index("grid"), lax.axis_index("depth")
    z, y = g // 2, g % 2
    left = z < 2
    is_end = ((z == 0) | (z == 3)).astype(jnp.int32)
    toward = jnp.where(left, 1, -1)
    q = 2 * y + c

    inward = [(0, 2), (1, 3), (6, 4), (7, 5)]
    outward = [(2, 0), (3, 1), (4, 6), (5, 7)]
    cross = [(2, 4), (3, 5), (4, 2), (5, 3)]
    across = [(i, i ^ 1) for i in range(8)]
    layers = [(0, 1), (1, 0)]
    opposite = [(i, i ^ 3) for i in range(16)]
    line = lambda value, pairs: lax.ppermute(value, "grid", pairs)
    seven = 7 * LANES
    start_near = jnp.where(left, 0, 1)
    start_far = jnp.where(left, 1, 0)
    near = lambda value: lax.dynamic_slice_in_dim(value, start_near * LANES, seven, 1)
    far = lambda value: lax.dynamic_slice_in_dim(value, start_far * LANES, seven, 1)

    own_a = b_strips(w_band, q)
    cross_a = line(own_a, cross)
    in_a = line(own_a, inward)
    near_a = line(near(own_a), outward)
    own_b = line(b_strips(w_band, q ^ 2), across)
    cross_b = line(own_b, cross)
    in_b = line(own_b, inward)
    near_b = line(near(own_b), outward)

    mask_wide = widen(a_mask, block)
    x_mine = masked_half(x_band, mask_wide, c)
    x_rest = masked_half(x_band, mask_wide, 1 - c)
    x_across = line(x_mine, across)
    x_opposite = lax.ppermute(x_across, "depth", layers)
    xs = [x_mine, x_rest, x_across, x_opposite]

    mid_a = line(cross_a, outward)
    fwd_a = line(in_a, cross)
    mid_b = line(cross_b, outward)
    fwd_b = line(in_b, cross)
    far_a = line(far(fwd_a), outward)
    far_b = line(far(fwd_b), outward)

    def offsets(delta, start):
        tilt = 2 * y - 1
        a = [start, (2 * delta + 4) % 8, (2 * delta + tilt + 4) % 8]
        b = [start, (2 * delta - tilt + 4) % 8, (2 * delta + 4) % 8]
        return a + b

    zero = jnp.zeros_like(z)
    third = jnp.where(is_end == 1, 2, -toward)
    fourth = jnp.where(is_end == 1, -toward, 2)
    meta = [is_end] + offsets(zero, zero) + offsets(toward, start_near) + offsets(third, zero)
    meta = jnp.stack(meta).astype(jnp.int32)
    meta_last = jnp.stack([is_end] + offsets(fourth, start_far)).astype(jnp.int32)
    total = products(
        meta,
        xs,
        [own_a, own_b, cross_a, cross_b, in_a, in_b],
        [own_a, own_b, near_a, near_b, mid_a, mid_b],
        None,
        False,
        "first_products",
    )
    pieces = products(meta_last, xs, [fwd_a, fwd_b], [far_a, far_b], total, True, "last_products")
    pieces = [
        pieces[0],
        lax.ppermute(pieces[1], "depth", layers),
        line(pieces[2], across),
        lax.ppermute(pieces[3], ("grid", "depth"), opposite),
    ]
    return assembled(q, widen(keep_mask, block), pieces)


def solution(mesh):
    placed = (
        P(("groups", "grid"), None),
        P(("groups", "grid"), None),
        P(("groups", "grid"), None),
        P(("groups", "grid", "depth"), None),
    )

    def local(x_band, w_band, a_mask, keep_mask):
        panel, cols = x_band.shape
        pairs = mesh.shape["grid"] == 8 and mesh.shape["depth"] == 2
        pairs = pairs and cols == 8 * panel and panel == 4 * LANES
        return (pairs_in_line if pairs else ring)(x_band, w_band, a_mask, keep_mask)

    return jax.shard_map(
        local,
        mesh=mesh,
        in_specs=placed,
        out_specs=P(("groups", "grid", "depth"), None),
        check_vma=False,
    )
```

```python
import functools

import jax
import jax.numpy as jnp
from jax import lax
from jax.experimental import pallas as pl
from jax.experimental.pallas import tpu as pltpu
from jax.sharding import PartitionSpec as P

LANES = 128
MIB = 1 << 20


def shifted(shard, axis, by):
    count = lax.axis_size(axis)
    return lax.ppermute(shard, axis, [(i, (i + by) % count) for i in range(count)])


def expand_blocks(mask, block):
    rows, cols = mask.shape
    wide = jnp.broadcast_to(mask[:, None, :, None], (rows, block, cols, block))
    return wide.reshape(rows * block, cols * block)


def ring(x_band, w_band, a_mask, keep_mask):
    panel = x_band.shape[0]
    block = panel // a_mask.shape[0]
    band_cols = x_band.shape[1]
    xm = x_band * expand_blocks(a_mask, block).astype(jnp.bfloat16)
    rows = lax.broadcasted_iota(jnp.int32, x_band.shape, 0)
    cols = lax.broadcasted_iota(jnp.int32, x_band.shape, 1)
    identity = jnp.where(cols == rows + 4 * panel, 1.0, 0.0).astype(jnp.float32)
    b_panel = (1.5 * identity - 0.5 * w_band.astype(jnp.float32)).astype(jnp.bfloat16)
    layer = lax.axis_index("depth")
    current = shifted(b_panel, ("grid", "depth"), -5)
    wide = jnp.zeros((panel, 2 * band_cols), jnp.float32)
    for step in range(4):
        offset = 6 + layer - 2 * step
        ablock = lax.dynamic_slice_in_dim(xm, offset * panel, panel, 1)
        term = jnp.dot(ablock, current, preferred_element_type=jnp.float32)
        region = lax.dynamic_slice_in_dim(wide, offset * panel, band_cols, 1)
        wide = lax.dynamic_update_slice_in_dim(wide, region + term, offset * panel, 1)
        if step < 3:
            current = shifted(current, "grid", 2)
    partial_band = wide[:, 4 * panel : 12 * panel]
    mine = lax.psum_scatter(partial_band, "depth", scatter_dimension=0, tiled=True)
    keep = expand_blocks(keep_mask, block).astype(jnp.float32)
    return (mine * keep).astype(jnp.bfloat16)


def strips_kernel(quarter_ref, w_ref, b_ref, held, sems):
    panel = held.shape[0]
    quarter = quarter_ref[0]
    band = held.shape[1] // LANES
    copies = []
    for j in range(band):
        at = pl.multiple_of(j * panel + quarter * LANES, LANES)
        copies.append(
            pltpu.make_async_copy(
                w_ref.at[:, pl.ds(at, LANES)],
                held.at[:, j * LANES : (j + 1) * LANES],
                sems.at[j],
            )
        )
        copies[-1].start()
    for j in range(band):
        copies[j].wait()
        value = -0.5 * held[:, j * LANES : (j + 1) * LANES].astype(jnp.float32)
        if j == band // 2:
            rows = lax.broadcasted_iota(jnp.int32, value.shape, 0)
            cols = lax.broadcasted_iota(jnp.int32, value.shape, 1)
            value = value + jnp.where(rows == cols + quarter * LANES, 1.5, 0.0)
        b_ref[:, j * LANES : (j + 1) * LANES] = value.astype(jnp.bfloat16)


def b_strips(w_band, quarter):
    panel = w_band.shape[0]
    band = w_band.shape[1] // panel
    shape = (panel, band * LANES)
    return pl.pallas_call(
        strips_kernel,
        out_shape=jax.ShapeDtypeStruct(shape, jnp.bfloat16),
        in_specs=[
            pl.BlockSpec(memory_space=pltpu.SMEM),
            pl.BlockSpec(memory_space=pl.ANY),
        ],
        out_specs=pl.BlockSpec(memory_space=pltpu.VMEM),
        scratch_shapes=[pltpu.VMEM(shape, jnp.bfloat16), pltpu.SemaphoreType.DMA((band,))],
        compiler_params=pltpu.CompilerParams(vmem_limit_bytes=16 * MIB),
        cost_estimate=pl.CostEstimate(flops=1000, bytes_accessed=4 * shape[0] * shape[1], transcendentals=0),
        name="b_strips",
    )(quarter.reshape(1), w_band)


def mask_kernel(half_ref, mask_ref, x_ref, out_ref):
    out_ref[...] = (x_ref[...].astype(jnp.float32) * mask_ref[0]).astype(jnp.bfloat16)


def masked_half(x_band, mask_wide, half):
    block = x_band.shape[0] // mask_wide.shape[0]
    per_half = mask_wide.shape[0] // 2
    cols = x_band.shape[1]
    return pl.pallas_call(
        mask_kernel,
        grid_spec=pltpu.PrefetchScalarGridSpec(
            num_scalar_prefetch=1,
            grid=(per_half,),
            in_specs=[
                pl.BlockSpec((1, 1, cols), lambda i, h: (h[0] * per_half + i, 0, 0)),
                pl.BlockSpec((block, cols), lambda i, h: (h[0] * per_half + i, 0)),
            ],
            out_specs=pl.BlockSpec((block, cols), lambda i, h: (i, 0)),
        ),
        out_shape=jax.ShapeDtypeStruct((x_band.shape[0] // 2, cols), jnp.bfloat16),
        compiler_params=pltpu.CompilerParams(vmem_limit_bytes=16 * MIB),
        cost_estimate=pl.CostEstimate(flops=1000, bytes_accessed=2 * x_band.shape[0] * cols, transcendentals=0),
        name="masked_half",
    )(half.reshape(1), mask_wide, x_band)


def x_copies(x_refs, xv, sems, offset_of):
    n_b, _, rows, panel = xv.shape
    half = rows // 2
    copies = {}
    for p in range(n_b):
        for r in range(4):
            at = pl.multiple_of(offset_of(p, r // 2) * panel, panel)
            copies[p, r] = pltpu.make_async_copy(
                x_refs[r].at[:, pl.ds(at, panel)],
                xv.at[p, r // 2, (r % 2) * half : (r % 2 + 1) * half],
                sems.at[p, r],
            )
    return copies


def add_products(acc, xv, p, strips, offset_of, start):
    def step(g, carry):
        at = (offset_of(p, g) + start) * LANES
        cols = pl.ds(pl.multiple_of(at, LANES), strips.shape[1])
        acc[g, :, cols] += jnp.dot(xv[p, g], strips[...], preferred_element_type=jnp.float32)
        return carry

    lax.fori_loop(0, 2, step, 0)


def first_kernel(windows, meta_ref, *refs):
    n_b = len(windows)
    x_refs, middle_refs, end_refs = refs[:4], refs[4 : 4 + n_b], refs[4 + n_b : 4 + 2 * n_b]
    out_ref, xv, bv, acc, x_sems, b_sems, out_sem = refs[4 + 2 * n_b :]
    quarter = bv.shape[2]
    low = quarter // 2
    is_end = meta_ref[0]

    def offset_of(p, g):
        return meta_ref[1 + 2 * p + g]

    def b_copies(p):
        start, width = windows[p]
        target = bv.at[p, :, start * LANES : (start + width) * LANES]
        return (
            pltpu.make_async_copy(middle_refs[p], bv.at[p], b_sems.at[p]),
            pltpu.make_async_copy(end_refs[p], target, b_sems.at[p]),
        )

    copies = x_copies(x_refs, xv, x_sems, offset_of)
    for p in range(n_b):
        middle, end = b_copies(p)
        pl.when(is_end == 0)(middle.start)
        pl.when(is_end != 0)(end.start)
        for r in range(4):
            copies[p, r].start()
    acc[...] = jnp.zeros_like(acc)
    for p in range(n_b):
        middle, end = b_copies(p)
        pl.when(is_end == 0)(middle.wait)
        pl.when(is_end != 0)(end.wait)
        for r in range(4):
            copies[p, r].wait()
        add_products(acc, xv, p, bv.at[p], offset_of, 0)
    out = pltpu.make_async_copy(acc.at[:, :, low : low + quarter], out_ref, out_sem)
    out.start()
    out.wait()


def first_products(meta, xs, middle, end, windows):
    rows = xs[0].shape[0]
    panel, quarter = middle[0].shape
    n_b = len(middle)
    any_spec = pl.BlockSpec(memory_space=pl.ANY)
    operands = [meta, *xs, *middle, *end]
    return pl.pallas_call(
        functools.partial(first_kernel, windows),
        out_shape=jax.ShapeDtypeStruct((2, 2 * rows, quarter), jnp.float32),
        in_specs=[pl.BlockSpec(memory_space=pltpu.SMEM)] + [any_spec] * (len(operands) - 1),
        out_specs=any_spec,
        scratch_shapes=[
            pltpu.VMEM((n_b, 2, 2 * rows, panel), jnp.bfloat16),
            pltpu.VMEM((n_b, panel, quarter), jnp.bfloat16),
            pltpu.VMEM((2, 2 * rows, 2 * quarter), jnp.float32),
            pltpu.SemaphoreType.DMA((n_b, 4)),
            pltpu.SemaphoreType.DMA((n_b,)),
            pltpu.SemaphoreType.DMA,
        ],
        compiler_params=pltpu.CompilerParams(vmem_limit_bytes=32 * MIB),
        cost_estimate=pl.CostEstimate(
            flops=2 * n_b * 4 * rows * panel * quarter,
            bytes_accessed=n_b * 2 * (4 * rows * panel + panel * quarter),
            transcendentals=0,
        ),
        name="first_products",
    )(*operands)


def give_pieces(out_refs, acc, at):
    half, width = out_refs[0].shape
    cols = pl.ds(pl.multiple_of(at * LANES, LANES), width)
    for r in range(4):
        rows = slice((r % 2) * half, (r % 2 + 1) * half)
        out_refs[r][...] = acc[r // 2, rows, cols].astype(jnp.bfloat16)


def half_kernel(meta_ref, *refs):
    x_refs, prev_ref, middle_ref, end_ref, second_ref = refs[:4], *refs[4:8]
    out_refs, rest_ref, xv, bv, acc, x_sems, b_sems, prev_sem, rest_sem = refs[8:12], *refs[12:]
    quarter = bv.shape[2]
    half = quarter // 2
    low = quarter // 2
    band = quarter // LANES
    is_end = meta_ref[0]

    def offset_of(p, g):
        return meta_ref[5 + 2 * p + g]

    copies = x_copies(x_refs, xv, x_sems, offset_of)
    middle = pltpu.make_async_copy(middle_ref, bv.at[0], b_sems.at[0])
    end = pltpu.make_async_copy(end_ref, bv.at[0], b_sems.at[0])
    second = pltpu.make_async_copy(second_ref, bv.at[1], b_sems.at[1])
    prev = pltpu.make_async_copy(prev_ref, acc.at[:, :, low : low + quarter], prev_sem)
    prev.start()
    for copy in copies.values():
        copy.start()

    @pl.when(is_end == 0)
    def _():
        middle.start()
        second.start()

    pl.when(is_end != 0)(end.start)
    prev.wait()
    for copy in copies.values():
        copy.wait()
    pl.when(is_end == 0)(middle.wait)
    pl.when(is_end != 0)(end.wait)
    for p in range(2):
        add_products(acc, xv, p, bv.at[0, :, p * half : (p + 1) * half], offset_of, meta_ref[1])

    @pl.when(is_end == 0)
    def _():
        second.wait()
        for p in range(2):
            add_products(acc, xv, p, bv.at[1, :, p * half : (p + 1) * half], offset_of, meta_ref[2])

    at = pl.multiple_of((meta_ref[4] + band // 2) * LANES, LANES)
    rest = pltpu.make_async_copy(acc.at[:, :, pl.ds(at, rest_ref.shape[2])], rest_ref, rest_sem)
    rest.start()
    give_pieces(out_refs, acc, meta_ref[3] + band // 2)
    rest.wait()


def half_products(meta, xs, prev, middle, end, second, n_done):
    rows = xs[0].shape[0]
    panel, quarter = middle.shape
    any_spec = pl.BlockSpec(memory_space=pl.ANY)
    n_rest = quarter // LANES - n_done
    return pl.pallas_call(
        half_kernel,
        out_shape=[jax.ShapeDtypeStruct((rows, n_done * LANES), jnp.bfloat16)] * 4
        + [jax.ShapeDtypeStruct((2, 2 * rows, n_rest * LANES), jnp.float32)],
        in_specs=[pl.BlockSpec(memory_space=pltpu.SMEM)] + [any_spec] * 8,
        out_specs=[pl.BlockSpec(memory_space=pltpu.VMEM)] * 4 + [any_spec],
        scratch_shapes=[
            pltpu.VMEM((2, 2, 2 * rows, panel), jnp.bfloat16),
            pltpu.VMEM((2, panel, quarter), jnp.bfloat16),
            pltpu.VMEM((2, 2 * rows, 2 * quarter), jnp.float32),
            pltpu.SemaphoreType.DMA((2, 4)),
            pltpu.SemaphoreType.DMA((2,)),
            pltpu.SemaphoreType.DMA,
            pltpu.SemaphoreType.DMA,
        ],
        compiler_params=pltpu.CompilerParams(vmem_limit_bytes=24 * MIB),
        cost_estimate=pl.CostEstimate(
            flops=2 * 2 * 4 * rows * panel * quarter, bytes_accessed=10 * MIB, transcendentals=0
        ),
        name="half_products",
    )(meta, *xs, prev, middle, end, second)


def rest_kernel(meta_ref, *refs):
    x_refs, rest_ref, b_ref = refs[:4], *refs[4:6]
    out_refs, xv, bv, acc, x_sems, b_sem, rest_sem = refs[6:10], *refs[10:]
    band = acc.shape[2] // (2 * LANES)
    half = bv.shape[1] // 2
    is_end = meta_ref[0]

    def offset_of(p, g):
        return meta_ref[3 + 2 * p + g]

    at = pl.multiple_of((meta_ref[2] + band // 2) * LANES, LANES)
    rest = pltpu.make_async_copy(rest_ref, acc.at[:, :, pl.ds(at, rest_ref.shape[2])], rest_sem)
    rest.start()
    copies = x_copies(x_refs, xv, x_sems, offset_of)
    b_copy = pltpu.make_async_copy(b_ref, bv, b_sem)

    @pl.when(is_end != 0)
    def _():
        b_copy.start()
        for copy in copies.values():
            copy.start()

    rest.wait()

    @pl.when(is_end != 0)
    def _():
        b_copy.wait()
        for copy in copies.values():
            copy.wait()
        for p in range(2):
            add_products(acc, xv, p, bv.at[:, p * half : (p + 1) * half], offset_of, meta_ref[1])

    give_pieces(out_refs, acc, meta_ref[2] + band // 2)


def rest_products(meta, xs, rest, b, quarter):
    rows = xs[0].shape[0]
    panel = b.shape[0]
    width = rest.shape[2]
    any_spec = pl.BlockSpec(memory_space=pl.ANY)
    return pl.pallas_call(
        rest_kernel,
        out_shape=[jax.ShapeDtypeStruct((rows, width), jnp.bfloat16)] * 4,
        in_specs=[pl.BlockSpec(memory_space=pltpu.SMEM)] + [any_spec] * 6,
        out_specs=[pl.BlockSpec(memory_space=pltpu.VMEM)] * 4,
        scratch_shapes=[
            pltpu.VMEM((2, 2, 2 * rows, panel), jnp.bfloat16),
            pltpu.VMEM(b.shape, jnp.bfloat16),
            pltpu.VMEM((2, 2 * rows, 2 * quarter), jnp.float32),
            pltpu.SemaphoreType.DMA((2, 4)),
            pltpu.SemaphoreType.DMA,
            pltpu.SemaphoreType.DMA,
        ],
        compiler_params=pltpu.CompilerParams(vmem_limit_bytes=24 * MIB),
        cost_estimate=pl.CostEstimate(
            flops=2 * 4 * rows * panel * b.shape[1], bytes_accessed=5 * MIB, transcendentals=0
        ),
        name="rest_products",
    )(meta, *xs, rest, b)


def assemble_kernel(place_ref, mask_ref, *refs):
    *pieces, out_ref = refs
    n = len(pieces) // 2
    done, rest = pieces[:n], pieces[n:]
    n_done, n_rest = done[0].shape[1] // LANES, rest[0].shape[1] // LANES
    panel = n * LANES
    for left in range(2):
        for mine in range(n):

            @pl.when((place_ref[0] == mine) & (place_ref[1] == left))
            def _():
                for j in range(n_done + n_rest):
                    if left:
                        source, at = (rest, j) if j < n_rest else (done, j - n_rest)
                    else:
                        source, at = (done, j) if j < n_done else (rest, j - n_done)
                    for t in range(n):
                        cols = slice(j * panel + t * LANES, j * panel + (t + 1) * LANES)
                        value = source[t ^ mine][:, at * LANES : (at + 1) * LANES].astype(jnp.float32)
                        out_ref[:, cols] = (value * mask_ref[0, :, cols]).astype(jnp.bfloat16)


def assembled(place, keep_wide, done, rest):
    rows = done[0].shape[0]
    steps = keep_wide.shape[0]
    block = rows // steps
    cols = keep_wide.shape[2]
    return pl.pallas_call(
        assemble_kernel,
        grid_spec=pltpu.PrefetchScalarGridSpec(
            num_scalar_prefetch=1,
            grid=(steps,),
            in_specs=[pl.BlockSpec((1, 1, cols), lambda i, q: (i, 0, 0))]
            + [pl.BlockSpec((block, piece.shape[1]), lambda i, q: (i, 0)) for piece in done + rest],
            out_specs=pl.BlockSpec((block, cols), lambda i, q: (i, 0)),
        ),
        out_shape=jax.ShapeDtypeStruct((rows, cols), jnp.bfloat16),
        compiler_params=pltpu.CompilerParams(vmem_limit_bytes=16 * MIB),
        cost_estimate=pl.CostEstimate(flops=1000, bytes_accessed=4 * rows * cols, transcendentals=0),
        name="assembled",
    )(place, keep_wide, *done, *rest)


def widen(mask, block):
    rows, cols = mask.shape
    wide = jnp.broadcast_to(mask.astype(jnp.float32)[:, :, None], (rows, cols, block))
    return wide.reshape(rows, 1, cols * block)


def together(*values):
    return lax.optimization_barrier(values)


def pairs_in_line(x_band, w_band, a_mask, keep_mask):
    panel = x_band.shape[0]
    block = panel // a_mask.shape[0]
    g, c = lax.axis_index("grid"), lax.axis_index("depth")
    z, y = g // 2, g % 2
    left = z < 2
    is_end = ((z == 0) | (z == 3)).astype(jnp.int32)
    toward = jnp.where(left, 1, -1)
    q = 2 * y + c

    swap = [(0, 2), (1, 3), (2, 0), (3, 1), (4, 6), (5, 7), (6, 4), (7, 5)]
    outward = [(2, 0), (3, 1), (4, 6), (5, 7)]
    cross = [(2, 4), (3, 5), (4, 2), (5, 3)]
    across = [(i, i ^ 1) for i in range(8)]
    layers = [(0, 1), (1, 0)]
    opposite = [(i, i ^ 3) for i in range(16)]

    def line(value, pairs):
        return lax.ppermute(value, "grid", pairs)

    def strips(value, start, count):
        return lax.dynamic_slice_in_dim(value, start * LANES, count * LANES, 1)

    first_out, second_out = jnp.where(left, 0, 4), jnp.where(left, 4, 0)
    first_in, second_in = second_out, first_out
    last_in = jnp.where(left, 1, 4)

    own_a = b_strips(w_band, q)
    swap_a = line(own_a, swap)
    cross_a = line(own_a, cross)
    own_b = line(b_strips(w_band, q ^ 2), across)
    mask_wide = widen(a_mask, block)
    x_mine = masked_half(x_band, mask_wide, c)
    own_b, x_mine = together(own_b, x_mine)
    swap_b = line(own_b, swap)
    cross_b = line(own_b, cross)
    x_across = line(x_mine, across)
    x_rest = masked_half(x_band, mask_wide, 1 - c)

    swap_a, cross_a, swap_b, cross_b = together(swap_a, cross_a, swap_b, cross_b)
    even = jnp.where(y == 0, cross_a, cross_b)
    odd = jnp.where(y == 0, cross_b[:, 3 * LANES :], cross_a[:, 3 * LANES :])
    mid = line(jnp.concatenate([even, odd], 1), outward)
    fwd_first = line(jnp.concatenate([strips(v, first_out, 4) for v in (swap_a, swap_b)], 1), cross)
    fwd_second_out = jnp.concatenate([strips(v, second_out, 4) for v in (swap_a, swap_b)], 1)
    fwd_first, fwd_second_out, x_across, mid = together(fwd_first, fwd_second_out, x_across, mid)
    fwd_second = line(fwd_second_out, cross)
    x_opposite = lax.ppermute(x_across, "depth", layers)
    xs = [x_mine, x_rest, x_across, x_opposite]
    far_first = line(fwd_first, outward)

    def offsets(delta):
        tilt = 2 * y - 1
        return [(2 * delta + 4) % 8, (2 * delta + tilt + 4) % 8, (2 * delta - tilt + 4) % 8, (2 * delta + 4) % 8]

    zero = jnp.zeros_like(z)
    third = [
        jnp.where(is_end == 1, ours, theirs)
        for ours, theirs in zip([8 - y, 7 + y, 9 - y, 8 + y], offsets(-toward))
    ]
    third = [v % 8 for v in third]
    fourth = offsets(jnp.where(is_end == 1, -toward, 2))
    meta = jnp.stack([is_end, *offsets(zero), *offsets(toward), *third]).astype(jnp.int32)
    whole = (0, 8)
    total = first_products(
        meta,
        xs,
        [own_a, own_b, cross_a, cross_b, swap_a, swap_b],
        [own_a, own_b, swap_a, swap_b, mid[:, : 8 * LANES], mid[:, 8 * LANES :]],
        [whole, whole, whole, whole, whole, (3, 5)],
    )
    fwd_second, far_first, total = together(fwd_second, far_first, total)
    last = jnp.concatenate([strips(fwd_second, jnp.where(left, 1, 0), 3), strips(fwd_second, jnp.where(left, 5, 4), 3)], 1)
    far_second = line(last, outward)

    def exchanged(pieces):
        return [
            pieces[0],
            lax.ppermute(pieces[1], "depth", layers),
            line(pieces[2], across),
            lax.ppermute(pieces[3], ("grid", "depth"), opposite),
        ]

    done_at, rest_at = jnp.where(left, 3, 0), jnp.where(left, 0, 5)
    meta = jnp.stack([is_end, first_in, second_in, done_at, rest_at, *fourth]).astype(jnp.int32)
    *done, rest = half_products(meta, xs, total, fwd_first, far_first, fwd_second, 5)
    far_second, *done = together(far_second, *exchanged(done))
    meta = jnp.stack([is_end, last_in, rest_at, *fourth]).astype(jnp.int32)
    rest = exchanged(rest_products(meta, xs, rest, far_second, own_a.shape[1]))
    place = jnp.stack([q, left.astype(jnp.int32)]).astype(jnp.int32)
    return assembled(place, widen(keep_mask, block), done, rest)


def solution(mesh):
    placed = (
        P(("groups", "grid"), None),
        P(("groups", "grid"), None),
        P(("groups", "grid"), None),
        P(("groups", "grid", "depth"), None),
    )

    def local(x_band, w_band, a_mask, keep_mask):
        panel, cols = x_band.shape
        pairs = mesh.shape["grid"] == 8 and mesh.shape["depth"] == 2
        pairs = pairs and cols == 8 * panel and panel == 4 * LANES
        return (pairs_in_line if pairs else ring)(x_band, w_band, a_mask, keep_mask)

    return jax.shard_map(
        local,
        mesh=mesh,
        in_specs=placed,
        out_specs=P(("groups", "grid", "depth"), None),
        check_vma=False,
    )
```

```python
import functools

import jax
import jax.numpy as jnp
from jax import lax
from jax.experimental import pallas as pl
from jax.experimental.pallas import tpu as pltpu
from jax.sharding import PartitionSpec as P

LANES = 128
MIB = 1 << 20


def shifted(shard, axis, by):
    count = lax.axis_size(axis)
    return lax.ppermute(shard, axis, [(i, (i + by) % count) for i in range(count)])


def expand_blocks(mask, block):
    rows, cols = mask.shape
    wide = jnp.broadcast_to(mask[:, None, :, None], (rows, block, cols, block))
    return wide.reshape(rows * block, cols * block)


def ring(x_band, w_band, a_mask, keep_mask):
    panel = x_band.shape[0]
    block = panel // a_mask.shape[0]
    band_cols = x_band.shape[1]
    xm = x_band * expand_blocks(a_mask, block).astype(jnp.bfloat16)
    rows = lax.broadcasted_iota(jnp.int32, x_band.shape, 0)
    cols = lax.broadcasted_iota(jnp.int32, x_band.shape, 1)
    identity = jnp.where(cols == rows + 4 * panel, 1.0, 0.0).astype(jnp.float32)
    b_panel = (1.5 * identity - 0.5 * w_band.astype(jnp.float32)).astype(jnp.bfloat16)
    layer = lax.axis_index("depth")
    current = shifted(b_panel, ("grid", "depth"), -5)
    wide = jnp.zeros((panel, 2 * band_cols), jnp.float32)
    for step in range(4):
        offset = 6 + layer - 2 * step
        ablock = lax.dynamic_slice_in_dim(xm, offset * panel, panel, 1)
        term = jnp.dot(ablock, current, preferred_element_type=jnp.float32)
        region = lax.dynamic_slice_in_dim(wide, offset * panel, band_cols, 1)
        wide = lax.dynamic_update_slice_in_dim(wide, region + term, offset * panel, 1)
        if step < 3:
            current = shifted(current, "grid", 2)
    partial_band = wide[:, 4 * panel : 12 * panel]
    mine = lax.psum_scatter(partial_band, "depth", scatter_dimension=0, tiled=True)
    keep = expand_blocks(keep_mask, block).astype(jnp.float32)
    return (mine * keep).astype(jnp.bfloat16)


def strips_kernel(quarter_ref, w_ref, b_ref, held, sems):
    panel = held.shape[0]
    quarter = quarter_ref[0]
    band = held.shape[1] // LANES
    copies = []
    for j in range(band):
        at = pl.multiple_of(j * panel + quarter * LANES, LANES)
        copies.append(
            pltpu.make_async_copy(
                w_ref.at[:, pl.ds(at, LANES)],
                held.at[:, j * LANES : (j + 1) * LANES],
                sems.at[j],
            )
        )
        copies[-1].start()
    for j in range(band):
        copies[j].wait()
        value = -0.5 * held[:, j * LANES : (j + 1) * LANES].astype(jnp.float32)
        if j == band // 2:
            rows = lax.broadcasted_iota(jnp.int32, value.shape, 0)
            cols = lax.broadcasted_iota(jnp.int32, value.shape, 1)
            value = value + jnp.where(rows == cols + quarter * LANES, 1.5, 0.0)
        b_ref[:, j * LANES : (j + 1) * LANES] = value.astype(jnp.bfloat16)


def b_strips(w_band, quarter):
    panel = w_band.shape[0]
    band = w_band.shape[1] // panel
    shape = (panel, band * LANES)
    return pl.pallas_call(
        strips_kernel,
        out_shape=jax.ShapeDtypeStruct(shape, jnp.bfloat16),
        in_specs=[
            pl.BlockSpec(memory_space=pltpu.SMEM),
            pl.BlockSpec(memory_space=pltpu.HBM),
        ],
        out_specs=pl.BlockSpec(memory_space=pltpu.VMEM),
        scratch_shapes=[pltpu.VMEM(shape, jnp.bfloat16), pltpu.SemaphoreType.DMA((band,))],
        compiler_params=pltpu.CompilerParams(vmem_limit_bytes=60 * MIB),
        cost_estimate=pl.CostEstimate(flops=1000, bytes_accessed=4 * shape[0] * shape[1], transcendentals=0),
        name="b_strips",
    )(quarter.reshape(1), w_band)


def mask_kernel(half_ref, mask_ref, x_ref, out_ref):
    out_ref[...] = (x_ref[...].astype(jnp.float32) * mask_ref[0]).astype(jnp.bfloat16)


def masked_half(x_band, mask_wide, half):
    block = x_band.shape[0] // mask_wide.shape[0]
    per_half = mask_wide.shape[0] // 2
    cols = x_band.shape[1]
    return pl.pallas_call(
        mask_kernel,
        grid_spec=pltpu.PrefetchScalarGridSpec(
            num_scalar_prefetch=1,
            grid=(per_half,),
            in_specs=[
                pl.BlockSpec((1, 1, cols), lambda i, h: (h[0] * per_half + i, 0, 0)),
                pl.BlockSpec((block, cols), lambda i, h: (h[0] * per_half + i, 0)),
            ],
            out_specs=pl.BlockSpec((block, cols), lambda i, h: (i, 0)),
        ),
        out_shape=jax.ShapeDtypeStruct((x_band.shape[0] // 2, cols), jnp.bfloat16),
        compiler_params=pltpu.CompilerParams(vmem_limit_bytes=16 * MIB),
        cost_estimate=pl.CostEstimate(flops=1000, bytes_accessed=2 * x_band.shape[0] * cols, transcendentals=0),
        name="masked_half",
    )(half.reshape(1), mask_wide, x_band)


def x_copies(x_refs, xv, sems, offset_of):
    n_b, _, rows, panel = xv.shape
    half = rows // 2
    copies = {}
    for p in range(n_b):
        for r in range(4):
            at = pl.multiple_of(offset_of(p, r // 2) * panel, panel)
            copies[p, r] = pltpu.make_async_copy(
                x_refs[r].at[:, pl.ds(at, panel)],
                xv.at[p, r // 2, (r % 2) * half : (r % 2 + 1) * half],
                sems.at[p, r],
            )
    return copies


def add_products(acc, xv, p, strips, offset_of, start):
    def step(g, carry):
        at = (offset_of(p, g) + start) * LANES
        cols = pl.ds(pl.multiple_of(at, LANES), strips.shape[1])
        acc[g, :, cols] += jnp.dot(xv[p, g], strips[...], preferred_element_type=jnp.float32)
        return carry

    lax.fori_loop(0, 2, step, 0)


def first_kernel(meta_ref, *refs):
    x_refs, middle_refs, near_refs, (mid_a_ref, mid_b_ref), refs = refs[:4], refs[4:10], refs[10:12], refs[12:14], refs[14:]
    out_ref, xv, bv, acc, x_sems, b_sems, out_sems = refs
    n_b = len(middle_refs)
    quarter = bv.shape[2]
    low = quarter // 2
    split = quarter - mid_a_ref.shape[1]
    is_end = meta_ref[0]

    def offset_of(p, g):
        return meta_ref[2 + 2 * p + g]

    def b_middle(p):
        return [pltpu.make_async_copy(middle_refs[p], bv.at[p], b_sems.at[p])]

    def b_end(p):
        if p < 2:
            return b_middle(p)
        if p < 4:
            return [pltpu.make_async_copy(near_refs[p - 2], bv.at[p], b_sems.at[p])]
        if p == 4:
            return [
                pltpu.make_async_copy(mid_a_ref, bv.at[4, :, split:], b_sems.at[4]),
                pltpu.make_async_copy(mid_b_ref.at[:, :split], bv.at[4 + meta_ref[1], :, :split], b_sems.at[6]),
            ]
        return [pltpu.make_async_copy(mid_b_ref.at[:, split:], bv.at[5, :, split:], b_sems.at[5])]

    copies = x_copies(x_refs, xv, x_sems, offset_of)
    for p in range(n_b):

        @pl.when(is_end == 0)
        def _():
            for copy in b_middle(p):
                copy.start()

        @pl.when(is_end != 0)
        def _():
            for copy in b_end(p):
                copy.start()

        for r in range(4):
            copies[p, r].start()
    acc[...] = jnp.zeros_like(acc)
    for p in range(n_b):

        @pl.when(is_end == 0)
        def _():
            for copy in b_middle(p):
                copy.wait()

        @pl.when(is_end != 0)
        def _():
            for copy in b_end(p):
                copy.wait()

        for r in range(4):
            copies[p, r].wait()
        add_products(acc, xv, p, bv.at[p], offset_of, 0)
    outs = [
        pltpu.make_async_copy(acc.at[g, :, low : low + quarter], out_ref.at[g], out_sems.at[g]) for g in range(2)
    ]
    for out in outs:
        out.start()
    for out in outs:
        out.wait()


def first_products(meta, xs, middle, near, mid):
    rows = xs[0].shape[0]
    panel, quarter = middle[0].shape
    n_b = len(middle)
    any_spec = pl.BlockSpec(memory_space=pl.ANY)
    x_spec = pl.BlockSpec(memory_space=pltpu.HBM)
    return pl.pallas_call(
        first_kernel,
        out_shape=jax.ShapeDtypeStruct((2, 2 * rows, quarter), jnp.float32),
        in_specs=[pl.BlockSpec(memory_space=pltpu.SMEM)] + [x_spec] * 4 + [any_spec] * (n_b + 4),
        out_specs=any_spec,
        scratch_shapes=[
            pltpu.VMEM((n_b, 2, 2 * rows, panel), jnp.bfloat16),
            pltpu.VMEM((n_b, panel, quarter), jnp.bfloat16),
            pltpu.VMEM((2, 2 * rows, 2 * quarter), jnp.float32),
            pltpu.SemaphoreType.DMA((n_b, 4)),
            pltpu.SemaphoreType.DMA((n_b + 1,)),
            pltpu.SemaphoreType.DMA((2,)),
        ],
        compiler_params=pltpu.CompilerParams(vmem_limit_bytes=32 * MIB),
        cost_estimate=pl.CostEstimate(
            flops=2 * n_b * 4 * rows * panel * quarter,
            bytes_accessed=n_b * 2 * (4 * rows * panel + panel * quarter),
            transcendentals=0,
        ),
        name="first_products",
    )(meta, *xs, *middle, *near, *mid)


def give_pieces(out_refs, acc, at):
    half, width = out_refs[0].shape
    cols = pl.ds(pl.multiple_of(at * LANES, LANES), width)
    for r in range(4):
        rows = slice((r % 2) * half, (r % 2 + 1) * half)
        out_refs[r][...] = acc[r // 2, rows, cols].astype(jnp.bfloat16)


def half_kernel(meta_ref, *refs):
    x_refs, prev_ref, middle_refs, end_refs, second_ref, refs = refs[:4], refs[4], refs[5:7], refs[7:9], refs[9], refs[10:]
    out_refs, rest_ref, xv, bv, acc, x_sems, b_sems, prev_sem, rest_sem = refs[:4], *refs[4:]
    half = bv.shape[2]
    quarter = 2 * half
    low = quarter // 2
    band = quarter // LANES
    is_end = meta_ref[0]

    def offset_of(p, g):
        return meta_ref[5 + 2 * p + g]

    copies = x_copies(x_refs, xv, x_sems, offset_of)
    middle = [pltpu.make_async_copy(middle_refs[p], bv.at[p], b_sems.at[p]) for p in range(2)]
    middle += [
        pltpu.make_async_copy(second_ref.at[:, p * half : (p + 1) * half], bv.at[2 + p], b_sems.at[2 + p])
        for p in range(2)
    ]
    end = [pltpu.make_async_copy(end_refs[p], bv.at[p], b_sems.at[p]) for p in range(2)]
    prev = pltpu.make_async_copy(prev_ref, acc.at[:, :, low : low + quarter], prev_sem)
    prev.start()

    @pl.when(is_end == 0)
    def _():
        for copy in middle:
            copy.start()

    @pl.when(is_end != 0)
    def _():
        for copy in end:
            copy.start()

    for copy in copies.values():
        copy.start()

    @pl.when(is_end == 0)
    def _():
        for copy in middle:
            copy.wait()

    @pl.when(is_end != 0)
    def _():
        for copy in end:
            copy.wait()

    for copy in copies.values():
        copy.wait()
    prev.wait()
    for p in range(2):
        add_products(acc, xv, p, bv.at[p], offset_of, meta_ref[1])

    @pl.when(is_end == 0)
    def _():
        for p in range(2):
            add_products(acc, xv, p, bv.at[2 + p], offset_of, meta_ref[2])

    at = pl.multiple_of((meta_ref[4] + band // 2) * LANES, LANES)
    rest = pltpu.make_async_copy(acc.at[:, :, pl.ds(at, rest_ref.shape[2])], rest_ref, rest_sem)
    rest.start()
    give_pieces(out_refs, acc, meta_ref[3] + band // 2)
    rest.wait()


def half_products(meta, xs, prev, middle, end, second, n_done):
    rows = xs[0].shape[0]
    panel, quarter = second.shape
    any_spec = pl.BlockSpec(memory_space=pl.ANY)
    x_spec = pl.BlockSpec(memory_space=pltpu.HBM)
    n_rest = quarter // LANES - n_done
    return pl.pallas_call(
        half_kernel,
        out_shape=[jax.ShapeDtypeStruct((rows, n_done * LANES), jnp.bfloat16)] * 4
        + [jax.ShapeDtypeStruct((2, 2 * rows, n_rest * LANES), jnp.float32)],
        in_specs=[pl.BlockSpec(memory_space=pltpu.SMEM)] + [x_spec] * 4 + [any_spec] * 6,
        out_specs=[pl.BlockSpec(memory_space=pltpu.VMEM)] * 4 + [any_spec],
        scratch_shapes=[
            pltpu.VMEM((2, 2, 2 * rows, panel), jnp.bfloat16),
            pltpu.VMEM((4, panel, quarter // 2), jnp.bfloat16),
            pltpu.VMEM((2, 2 * rows, 2 * quarter), jnp.float32),
            pltpu.SemaphoreType.DMA((2, 4)),
            pltpu.SemaphoreType.DMA((4,)),
            pltpu.SemaphoreType.DMA,
            pltpu.SemaphoreType.DMA,
        ],
        compiler_params=pltpu.CompilerParams(vmem_limit_bytes=24 * MIB),
        cost_estimate=pl.CostEstimate(
            flops=2 * 2 * 4 * rows * panel * quarter, bytes_accessed=10 * MIB, transcendentals=0
        ),
        name="half_products",
    )(meta, *xs, prev, *middle, *end, second)


def rest_kernel(meta_ref, *refs):
    x_refs, rest_ref, b_ref = refs[:4], *refs[4:6]
    out_refs, xv, bv, acc, x_sems, b_sem, rest_sem = refs[6:10], *refs[10:]
    band = acc.shape[2] // (2 * LANES)
    half = bv.shape[1] // 2
    is_end = meta_ref[0]

    def offset_of(p, g):
        return meta_ref[3 + 2 * p + g]

    at = pl.multiple_of((meta_ref[2] + band // 2) * LANES, LANES)
    rest = pltpu.make_async_copy(rest_ref, acc.at[:, :, pl.ds(at, rest_ref.shape[2])], rest_sem)
    rest.start()
    copies = x_copies(x_refs, xv, x_sems, offset_of)
    b_copy = pltpu.make_async_copy(b_ref, bv, b_sem)

    @pl.when(is_end != 0)
    def _():
        b_copy.start()
        for copy in copies.values():
            copy.start()

    rest.wait()

    @pl.when(is_end != 0)
    def _():
        b_copy.wait()
        for copy in copies.values():
            copy.wait()
        for p in range(2):
            add_products(acc, xv, p, bv.at[:, p * half : (p + 1) * half], offset_of, meta_ref[1])

    give_pieces(out_refs, acc, meta_ref[2] + band // 2)


def rest_products(meta, xs, rest, b, quarter):
    rows = xs[0].shape[0]
    panel = b.shape[0]
    width = rest.shape[2]
    any_spec = pl.BlockSpec(memory_space=pl.ANY)
    x_spec = pl.BlockSpec(memory_space=pltpu.HBM)
    return pl.pallas_call(
        rest_kernel,
        out_shape=[jax.ShapeDtypeStruct((rows, width), jnp.bfloat16)] * 4,
        in_specs=[pl.BlockSpec(memory_space=pltpu.SMEM)] + [x_spec] * 4 + [any_spec] * 2,
        out_specs=[pl.BlockSpec(memory_space=pltpu.VMEM)] * 4,
        scratch_shapes=[
            pltpu.VMEM((2, 2, 2 * rows, panel), jnp.bfloat16),
            pltpu.VMEM(b.shape, jnp.bfloat16),
            pltpu.VMEM((2, 2 * rows, 2 * quarter), jnp.float32),
            pltpu.SemaphoreType.DMA((2, 4)),
            pltpu.SemaphoreType.DMA,
            pltpu.SemaphoreType.DMA,
        ],
        compiler_params=pltpu.CompilerParams(vmem_limit_bytes=24 * MIB),
        cost_estimate=pl.CostEstimate(
            flops=2 * 4 * rows * panel * b.shape[1], bytes_accessed=5 * MIB, transcendentals=0
        ),
        name="rest_products",
    )(meta, *xs, rest, b)


def assemble_kernel(place_ref, mask_ref, *refs):
    n = 4
    pieces, (out_ref, made, sem) = refs[:n], refs[-3:]
    steps = mask_ref.shape[0]
    rows = made.shape[0] // steps
    panel = n * LANES
    first = pl.multiple_of(place_ref[1] * panel, panel)
    for r in range(n):
        t = jnp.bitwise_xor(place_ref[0], r)
        for j in range(made.shape[1] // panel):
            to = pl.multiple_of(j * panel + t * LANES, LANES)
            for i in range(steps):
                keep = mask_ref[i, :, pl.ds(pl.multiple_of(first + to, LANES), LANES)]
                value = pieces[r][i * rows : (i + 1) * rows, j * LANES : (j + 1) * LANES].astype(jnp.float32)
                made[i * rows : (i + 1) * rows, pl.ds(to, LANES)] = (value * keep).astype(jnp.bfloat16)
    copy = pltpu.make_async_copy(made, out_ref.at[:, pl.ds(first, made.shape[1])], sem)
    copy.start()
    copy.wait()


def assembled(place, keep_wide, pieces, out=None):
    rows, width = pieces[0].shape
    cols = keep_wide.shape[2]
    vmem_spec = pl.BlockSpec(memory_space=pltpu.VMEM)
    any_spec = pl.BlockSpec(memory_space=pltpu.HBM)
    operands = [place, keep_wide, *pieces] + ([] if out is None else [out])
    return pl.pallas_call(
        assemble_kernel,
        out_shape=jax.ShapeDtypeStruct((rows, cols), jnp.bfloat16),
        in_specs=[pl.BlockSpec(memory_space=pltpu.SMEM)] + [vmem_spec] * 5 + [any_spec] * (len(operands) - 6),
        out_specs=any_spec,
        scratch_shapes=[pltpu.VMEM((rows, width * len(pieces)), jnp.bfloat16), pltpu.SemaphoreType.DMA],
        input_output_aliases={} if out is None else {6: 0},
        compiler_params=pltpu.CompilerParams(vmem_limit_bytes=16 * MIB),
        cost_estimate=pl.CostEstimate(flops=1000, bytes_accessed=4 * rows * width, transcendentals=0),
        name="assembled",
    )(*operands)


def widen(mask, block):
    rows, cols = mask.shape
    wide = jnp.broadcast_to(mask.astype(jnp.float32)[:, :, None], (rows, cols, block))
    return wide.reshape(rows, 1, cols * block)


def together(*values):
    return lax.optimization_barrier(values)


def pairs_in_line(x_band, w_band, a_mask, keep_mask):
    panel = x_band.shape[0]
    block = panel // a_mask.shape[0]
    g, c = lax.axis_index("grid"), lax.axis_index("depth")
    z, y = g // 2, g % 2
    left = z < 2
    is_end = ((z == 0) | (z == 3)).astype(jnp.int32)
    toward = jnp.where(left, 1, -1)
    q = 2 * y + c

    swap = [(0, 2), (1, 3), (2, 0), (3, 1), (4, 6), (5, 7), (6, 4), (7, 5)]
    outward = [(2, 0), (3, 1), (4, 6), (5, 7)]
    cross = [(2, 4), (3, 5), (4, 2), (5, 3)]
    across = [(i, i ^ 1) for i in range(8)]
    layers = [(0, 1), (1, 0)]
    opposite = [(i, i ^ 3) for i in range(16)]

    def line(value, pairs):
        return lax.ppermute(value, "grid", pairs)

    def strips(value, start, count):
        return lax.dynamic_slice_in_dim(value, start * LANES, count * LANES, 1)

    first_out, second_out = jnp.where(left, 0, 4), jnp.where(left, 4, 0)
    first_in, second_in = second_out, first_out
    last_in = jnp.where(left, 1, 4)

    own_a = b_strips(w_band, q)
    swap_a = line(own_a, swap)
    cross_a = line(own_a, cross)
    own_b = line(b_strips(w_band, q ^ 2), across)
    mask_wide = widen(a_mask, block)
    x_mine = masked_half(x_band, mask_wide, c)
    own_b, x_mine, swap_a, cross_a = together(own_b, x_mine, swap_a, cross_a)
    swap_b = line(own_b, swap)
    cross_b = line(own_b, cross)
    x_across = line(x_mine, across)
    x_rest = masked_half(x_band, mask_wide, 1 - c)

    mid_a = line(cross_a[:, 3 * LANES :], outward)
    fwd_a = line(strips(swap_a, first_out, 4), cross)
    mid_b = line(
        jnp.concatenate([jnp.where(y == 0, cross_a[:, : 3 * LANES], cross_b[:, : 3 * LANES]), cross_b[:, 3 * LANES :]], 1),
        outward,
    )
    swap_b, mid_a, fwd_a = together(swap_b, mid_a, fwd_a)
    fwd_b = line(strips(swap_b, first_out, 4), cross)
    fwd_second = line(jnp.concatenate([strips(v, second_out, 4) for v in (swap_a, swap_b)], 1), cross)
    far_a = line(fwd_a, outward)
    mid_b, fwd_b, x_across = together(mid_b, fwd_b, x_across)
    far_b = line(fwd_b, outward)
    x_opposite = lax.ppermute(x_across, "depth", layers)
    xs = [x_mine, x_rest, x_across, x_opposite]

    def offsets(delta):
        tilt = 2 * y - 1
        return [(2 * delta + 4) % 8, (2 * delta + tilt + 4) % 8, (2 * delta - tilt + 4) % 8, (2 * delta + 4) % 8]

    zero = jnp.zeros_like(z)
    third = offsets(jnp.where(is_end == 1, 2, -toward))
    fourth = offsets(jnp.where(is_end == 1, -toward, 2))
    meta = jnp.stack([is_end, y, *offsets(zero), *offsets(toward), *third]).astype(jnp.int32)
    total = first_products(
        meta, xs, [own_a, own_b, cross_a, cross_b, swap_a, swap_b], [swap_a, swap_b], [mid_a, mid_b]
    )
    fwd_second, total, far_a = together(fwd_second, total, far_a)
    last = jnp.concatenate(
        [strips(fwd_second, jnp.where(left, 1, 0), 3), strips(fwd_second, jnp.where(left, 5, 4), 3)], 1
    )
    far_second = line(last, outward)

    def exchanged(pieces):
        return [
            pieces[0],
            lax.ppermute(pieces[1], "depth", layers),
            line(pieces[2], across),
            lax.ppermute(pieces[3], ("grid", "depth"), opposite),
        ]

    done_at, rest_at = jnp.where(left, 3, 0), jnp.where(left, 0, 5)
    meta = jnp.stack([is_end, first_in, second_in, done_at, rest_at, *fourth]).astype(jnp.int32)
    *done, rest = half_products(meta, xs, total, [fwd_a, fwd_b], [far_a, far_b], fwd_second, 5)
    far_second, *done = together(far_second, *exchanged(done))
    keep_wide = widen(keep_mask, block)
    out = assembled(jnp.stack([q, done_at]).astype(jnp.int32), keep_wide, done)
    meta = jnp.stack([is_end, last_in, rest_at, *fourth]).astype(jnp.int32)
    rest = exchanged(rest_products(meta, xs, rest, far_second, own_a.shape[1]))
    return assembled(jnp.stack([q, rest_at]).astype(jnp.int32), keep_wide, rest, out)


def solution(mesh):
    placed = (
        P(("groups", "grid"), None),
        P(("groups", "grid"), None),
        P(("groups", "grid"), None),
        P(("groups", "grid", "depth"), None),
    )

    def local(x_band, w_band, a_mask, keep_mask):
        panel, cols = x_band.shape
        pairs = mesh.shape["grid"] == 8 and mesh.shape["depth"] == 2
        pairs = pairs and cols == 8 * panel and panel == 4 * LANES
        return (pairs_in_line if pairs else ring)(x_band, w_band, a_mask, keep_mask)

    return jax.shard_map(
        local,
        mesh=mesh,
        in_specs=placed,
        out_specs=P(("groups", "grid", "depth"), None),
        check_vma=False,
    )
```

```python
import functools

import jax
import jax.numpy as jnp
from jax import lax
from jax.experimental import pallas as pl
from jax.experimental.pallas import tpu as pltpu
from jax.sharding import PartitionSpec as P

LANES = 128
MIB = 1 << 20


def shifted(shard, axis, by):
    count = lax.axis_size(axis)
    return lax.ppermute(shard, axis, [(i, (i + by) % count) for i in range(count)])


def expand_blocks(mask, block):
    rows, cols = mask.shape
    wide = jnp.broadcast_to(mask[:, None, :, None], (rows, block, cols, block))
    return wide.reshape(rows * block, cols * block)


def ring(x_band, w_band, a_mask, keep_mask):
    panel = x_band.shape[0]
    block = panel // a_mask.shape[0]
    band_cols = x_band.shape[1]
    xm = x_band * expand_blocks(a_mask, block).astype(jnp.bfloat16)
    rows = lax.broadcasted_iota(jnp.int32, x_band.shape, 0)
    cols = lax.broadcasted_iota(jnp.int32, x_band.shape, 1)
    identity = jnp.where(cols == rows + 4 * panel, 1.0, 0.0).astype(jnp.float32)
    b_panel = (1.5 * identity - 0.5 * w_band.astype(jnp.float32)).astype(jnp.bfloat16)
    layer = lax.axis_index("depth")
    current = shifted(b_panel, ("grid", "depth"), -5)
    wide = jnp.zeros((panel, 2 * band_cols), jnp.float32)
    for step in range(4):
        offset = 6 + layer - 2 * step
        ablock = lax.dynamic_slice_in_dim(xm, offset * panel, panel, 1)
        term = jnp.dot(ablock, current, preferred_element_type=jnp.float32)
        region = lax.dynamic_slice_in_dim(wide, offset * panel, band_cols, 1)
        wide = lax.dynamic_update_slice_in_dim(wide, region + term, offset * panel, 1)
        if step < 3:
            current = shifted(current, "grid", 2)
    partial_band = wide[:, 4 * panel : 12 * panel]
    mine = lax.psum_scatter(partial_band, "depth", scatter_dimension=0, tiled=True)
    keep = expand_blocks(keep_mask, block).astype(jnp.float32)
    return (mine * keep).astype(jnp.bfloat16)


def strips_kernel(quarters_ref, w_ref, *refs):
    *b_refs, held, sems = refs
    _, panel, width = held.shape
    band = width // LANES

    def copy(k, j):
        at = pl.multiple_of(j * panel + quarters_ref[k] * LANES, LANES)
        to = held.at[k, :, j * LANES : (j + 1) * LANES]
        return pltpu.make_async_copy(w_ref.at[:, pl.ds(at, LANES)], to, sems.at[k, j])

    for k in range(len(b_refs)):
        for j in range(band):
            copy(k, j).start()
    for k, b_ref in enumerate(b_refs):
        for j in range(band):
            copy(k, j).wait()
            value = -0.5 * held[k, :, j * LANES : (j + 1) * LANES].astype(jnp.float32)
            if j == band // 2:
                rows = lax.broadcasted_iota(jnp.int32, value.shape, 0)
                cols = lax.broadcasted_iota(jnp.int32, value.shape, 1)
                value = value + jnp.where(rows == cols + quarters_ref[k] * LANES, 1.5, 0.0)
            b_ref[:, j * LANES : (j + 1) * LANES] = value.astype(jnp.bfloat16)


def b_strips(w_band, quarters):
    panel = w_band.shape[0]
    band = w_band.shape[1] // panel
    n = len(quarters)
    shape = (panel, band * LANES)
    return pl.pallas_call(
        strips_kernel,
        out_shape=[jax.ShapeDtypeStruct(shape, jnp.bfloat16)] * n,
        in_specs=[
            pl.BlockSpec(memory_space=pltpu.SMEM),
            pl.BlockSpec(memory_space=pltpu.HBM),
        ],
        out_specs=[pl.BlockSpec(memory_space=pltpu.VMEM)] * n,
        scratch_shapes=[pltpu.VMEM((n, *shape), jnp.bfloat16), pltpu.SemaphoreType.DMA((n, band))],
        compiler_params=pltpu.CompilerParams(vmem_limit_bytes=56 * MIB),
        cost_estimate=pl.CostEstimate(
            flops=1000, bytes_accessed=4 * n * shape[0] * shape[1], transcendentals=0
        ),
        name="b_strips",
    )(jnp.stack(quarters), w_band)


def mask_kernel(half_ref, mask_ref, x_ref, out_ref):
    out_ref[...] = (x_ref[...].astype(jnp.float32) * mask_ref[0]).astype(jnp.bfloat16)


def masked_half(x_band, mask_wide, half):
    block = x_band.shape[0] // mask_wide.shape[0]
    per_half = mask_wide.shape[0] // 2
    cols = x_band.shape[1]
    return pl.pallas_call(
        mask_kernel,
        grid_spec=pltpu.PrefetchScalarGridSpec(
            num_scalar_prefetch=1,
            grid=(per_half,),
            in_specs=[
                pl.BlockSpec((1, 1, cols), lambda i, h: (h[0] * per_half + i, 0, 0)),
                pl.BlockSpec((block, cols), lambda i, h: (h[0] * per_half + i, 0)),
            ],
            out_specs=pl.BlockSpec((block, cols), lambda i, h: (i, 0)),
        ),
        out_shape=jax.ShapeDtypeStruct((x_band.shape[0] // 2, cols), jnp.bfloat16),
        compiler_params=pltpu.CompilerParams(vmem_limit_bytes=58 * MIB),
        cost_estimate=pl.CostEstimate(flops=1000, bytes_accessed=2 * x_band.shape[0] * cols, transcendentals=0),
        name="masked_half",
    )(half.reshape(1), mask_wide, x_band)


def x_copies(x_refs, xv, sems, offset_of):
    n_b, _, rows, panel = xv.shape
    half = rows // 2
    copies = {}
    for p in range(n_b):
        for r in range(4):
            at = pl.multiple_of(offset_of(p, r // 2) * panel, panel)
            copies[p, r] = pltpu.make_async_copy(
                x_refs[r].at[:, pl.ds(at, panel)],
                xv.at[p, r // 2, (r % 2) * half : (r % 2 + 1) * half],
                sems.at[p, r],
            )
    return copies


def add_products(acc, xv, p, strips, offset_of, start):
    def step(g, carry):
        at = (offset_of(p, g) + start) * LANES
        cols = pl.ds(pl.multiple_of(at, LANES), strips.shape[1])
        acc[g, :, cols] += jnp.dot(xv[p, g], strips[...], preferred_element_type=jnp.float32)
        return carry

    lax.fori_loop(0, 2, step, 0)


def first_kernel(meta_ref, *refs):
    x_refs, middle_refs, (near_a_ref, near_b_ref, mid_b_ref), refs = refs[:4], refs[4:10], refs[10:13], refs[13:]
    out_ref, xv, bv, acc, x_sems, b_sems, out_sems = refs
    n_b = len(middle_refs)
    quarter = bv.shape[2]
    low = quarter // 2
    near = quarter - LANES
    split = quarter - (near_b_ref.shape[1] - near)
    is_end = meta_ref[0]

    def offset_of(p, g):
        return meta_ref[3 + 2 * p + g]

    def b_middle(p):
        return [pltpu.make_async_copy(middle_refs[p], bv.at[p], b_sems.at[p])]

    def b_end(p):
        if p < 2:
            return b_middle(p)
        if p == 2:
            return [pltpu.make_async_copy(near_a_ref, bv.at[2], b_sems.at[2])]
        if p == 3:
            at = pl.multiple_of(meta_ref[2] * LANES, LANES)
            return [pltpu.make_async_copy(near_b_ref.at[:, :near], bv.at[3, :, pl.ds(at, near)], b_sems.at[3])]
        if p == 4:
            return [
                pltpu.make_async_copy(near_b_ref.at[:, near:], bv.at[4, :, split:], b_sems.at[4]),
                pltpu.make_async_copy(mid_b_ref.at[:, :split], bv.at[4 + meta_ref[1], :, :split], b_sems.at[6]),
            ]
        return [pltpu.make_async_copy(mid_b_ref.at[:, split:], bv.at[5, :, split:], b_sems.at[5])]

    copies = x_copies(x_refs, xv, x_sems, offset_of)
    for p in range(n_b):

        @pl.when(is_end == 0)
        def _():
            for copy in b_middle(p):
                copy.start()

        @pl.when(is_end != 0)
        def _():
            for copy in b_end(p):
                copy.start()

        for r in range(4):
            copies[p, r].start()
    acc[...] = jnp.zeros_like(acc)
    for p in range(n_b):

        @pl.when(is_end == 0)
        def _():
            for copy in b_middle(p):
                copy.wait()

        @pl.when(is_end != 0)
        def _():
            for copy in b_end(p):
                copy.wait()

        for r in range(4):
            copies[p, r].wait()
        add_products(acc, xv, p, bv.at[p], offset_of, 0)
    outs = [
        pltpu.make_async_copy(acc.at[g, :, low : low + quarter], out_ref.at[g], out_sems.at[g]) for g in range(2)
    ]
    for out in outs:
        out.start()
    for out in outs:
        out.wait()


def first_products(meta, xs, middle, end):
    rows = xs[0].shape[0]
    panel, quarter = middle[0].shape
    n_b = len(middle)
    any_spec = pl.BlockSpec(memory_space=pl.ANY)
    x_spec = pl.BlockSpec(memory_space=pltpu.HBM)
    return pl.pallas_call(
        first_kernel,
        out_shape=jax.ShapeDtypeStruct((2, 2 * rows, quarter), jnp.float32),
        in_specs=[pl.BlockSpec(memory_space=pltpu.SMEM)] + [x_spec] * 4 + [any_spec] * (n_b + 3),
        out_specs=any_spec,
        scratch_shapes=[
            pltpu.VMEM((n_b, 2, 2 * rows, panel), jnp.bfloat16),
            pltpu.VMEM((n_b, panel, quarter), jnp.bfloat16),
            pltpu.VMEM((2, 2 * rows, 2 * quarter), jnp.float32),
            pltpu.SemaphoreType.DMA((n_b, 4)),
            pltpu.SemaphoreType.DMA((n_b + 1,)),
            pltpu.SemaphoreType.DMA((2,)),
        ],
        compiler_params=pltpu.CompilerParams(vmem_limit_bytes=59 * MIB),
        cost_estimate=pl.CostEstimate(
            flops=2 * n_b * 4 * rows * panel * quarter,
            bytes_accessed=n_b * 2 * (4 * rows * panel + panel * quarter),
            transcendentals=0,
        ),
        name="first_products",
    )(meta, *xs, *middle, *end)


def give_pieces(out_refs, acc, at):
    half, width = out_refs[0].shape
    cols = pl.ds(pl.multiple_of(at * LANES, LANES), width)
    for r in range(4):
        rows = slice((r % 2) * half, (r % 2 + 1) * half)
        out_refs[r][...] = acc[r // 2, rows, cols].astype(jnp.bfloat16)


def half_kernel(meta_ref, *refs):
    x_refs, prev_ref, middle_refs, end_refs, second_ref, refs = refs[:4], refs[4], refs[5:7], refs[7:9], refs[9], refs[10:]
    out_refs, rest_ref, xv, bv, acc, x_sems, b_sems, prev_sem, rest_sem = refs[:4], *refs[4:]
    half = bv.shape[2]
    quarter = 2 * half
    low = quarter // 2
    band = quarter // LANES
    is_end = meta_ref[0]

    def offset_of(p, g):
        return meta_ref[5 + 2 * p + g]

    copies = x_copies(x_refs, xv, x_sems, offset_of)
    middle = [pltpu.make_async_copy(middle_refs[p], bv.at[p], b_sems.at[p]) for p in range(2)]
    middle += [
        pltpu.make_async_copy(second_ref.at[:, p * half : (p + 1) * half], bv.at[2 + p], b_sems.at[2 + p])
        for p in range(2)
    ]
    end = [pltpu.make_async_copy(end_refs[p], bv.at[p], b_sems.at[p]) for p in range(2)]
    prev = pltpu.make_async_copy(prev_ref, acc.at[:, :, low : low + quarter], prev_sem)
    prev.start()

    @pl.when(is_end == 0)
    def _():
        for copy in middle:
            copy.start()

    @pl.when(is_end != 0)
    def _():
        for copy in end:
            copy.start()

    for copy in copies.values():
        copy.start()

    @pl.when(is_end == 0)
    def _():
        for copy in middle:
            copy.wait()

    @pl.when(is_end != 0)
    def _():
        for copy in end:
            copy.wait()

    for copy in copies.values():
        copy.wait()
    prev.wait()
    for p in range(2):
        add_products(acc, xv, p, bv.at[p], offset_of, meta_ref[1])

    @pl.when(is_end == 0)
    def _():
        for p in range(2):
            add_products(acc, xv, p, bv.at[2 + p], offset_of, meta_ref[2])

    at = pl.multiple_of((meta_ref[4] + band // 2) * LANES, LANES)
    rest = pltpu.make_async_copy(acc.at[:, :, pl.ds(at, rest_ref.shape[2])], rest_ref, rest_sem)
    rest.start()
    give_pieces(out_refs, acc, meta_ref[3] + band // 2)
    rest.wait()


def half_products(meta, xs, prev, middle, end, second, n_done):
    rows = xs[0].shape[0]
    panel, quarter = second.shape
    any_spec = pl.BlockSpec(memory_space=pl.ANY)
    x_spec = pl.BlockSpec(memory_space=pltpu.HBM)
    n_rest = quarter // LANES - n_done
    return pl.pallas_call(
        half_kernel,
        out_shape=[jax.ShapeDtypeStruct((rows, n_done * LANES), jnp.bfloat16)] * 4
        + [jax.ShapeDtypeStruct((2, 2 * rows, n_rest * LANES), jnp.float32)],
        in_specs=[pl.BlockSpec(memory_space=pltpu.SMEM)] + [x_spec] * 4 + [any_spec] * 6,
        out_specs=[pl.BlockSpec(memory_space=pltpu.VMEM)] * 4 + [any_spec],
        scratch_shapes=[
            pltpu.VMEM((2, 2, 2 * rows, panel), jnp.bfloat16),
            pltpu.VMEM((4, panel, quarter // 2), jnp.bfloat16),
            pltpu.VMEM((2, 2 * rows, 2 * quarter), jnp.float32),
            pltpu.SemaphoreType.DMA((2, 4)),
            pltpu.SemaphoreType.DMA((4,)),
            pltpu.SemaphoreType.DMA,
            pltpu.SemaphoreType.DMA,
        ],
        compiler_params=pltpu.CompilerParams(vmem_limit_bytes=59 * MIB),
        cost_estimate=pl.CostEstimate(
            flops=2 * 2 * 4 * rows * panel * quarter, bytes_accessed=10 * MIB, transcendentals=0
        ),
        name="half_products",
    )(meta, *xs, prev, *middle, *end, second)


def rest_kernel(meta_ref, *refs):
    x_refs, rest_ref, b_ref = refs[:4], *refs[4:6]
    out_refs, xv, bv, acc, x_sems, b_sem, rest_sem = refs[6:10], *refs[10:]
    band = acc.shape[2] // (2 * LANES)
    half = bv.shape[1] // 2
    is_end = meta_ref[0]

    def offset_of(p, g):
        return meta_ref[3 + 2 * p + g]

    at = pl.multiple_of((meta_ref[2] + band // 2) * LANES, LANES)
    rest = pltpu.make_async_copy(rest_ref, acc.at[:, :, pl.ds(at, rest_ref.shape[2])], rest_sem)
    rest.start()
    copies = x_copies(x_refs, xv, x_sems, offset_of)
    b_copy = pltpu.make_async_copy(b_ref, bv, b_sem)

    @pl.when(is_end != 0)
    def _():
        b_copy.start()
        for copy in copies.values():
            copy.start()

    rest.wait()

    @pl.when(is_end != 0)
    def _():
        b_copy.wait()
        for copy in copies.values():
            copy.wait()
        for p in range(2):
            add_products(acc, xv, p, bv.at[:, p * half : (p + 1) * half], offset_of, meta_ref[1])

    give_pieces(out_refs, acc, meta_ref[2] + band // 2)


def rest_products(meta, xs, rest, b, quarter):
    rows = xs[0].shape[0]
    panel = b.shape[0]
    width = rest.shape[2]
    any_spec = pl.BlockSpec(memory_space=pl.ANY)
    x_spec = pl.BlockSpec(memory_space=pltpu.HBM)
    return pl.pallas_call(
        rest_kernel,
        out_shape=[jax.ShapeDtypeStruct((rows, width), jnp.bfloat16)] * 4,
        in_specs=[pl.BlockSpec(memory_space=pltpu.SMEM)] + [x_spec] * 4 + [any_spec] * 2,
        out_specs=[pl.BlockSpec(memory_space=pltpu.VMEM)] * 4,
        scratch_shapes=[
            pltpu.VMEM((2, 2, 2 * rows, panel), jnp.bfloat16),
            pltpu.VMEM(b.shape, jnp.bfloat16),
            pltpu.VMEM((2, 2 * rows, 2 * quarter), jnp.float32),
            pltpu.SemaphoreType.DMA((2, 4)),
            pltpu.SemaphoreType.DMA,
            pltpu.SemaphoreType.DMA,
        ],
        compiler_params=pltpu.CompilerParams(vmem_limit_bytes=59 * MIB),
        cost_estimate=pl.CostEstimate(
            flops=2 * 4 * rows * panel * b.shape[1], bytes_accessed=5 * MIB, transcendentals=0
        ),
        name="rest_products",
    )(meta, *xs, rest, b)


def assemble_kernel(place_ref, mask_ref, *refs):
    n = 4
    pieces, (out_ref, made, sem) = refs[:n], refs[-3:]
    steps = mask_ref.shape[0]
    rows = made.shape[0] // steps
    panel = n * LANES
    first = pl.multiple_of(place_ref[1] * panel, panel)
    for r in range(n):
        t = jnp.bitwise_xor(place_ref[0], r)
        for j in range(made.shape[1] // panel):
            to = pl.multiple_of(j * panel + t * LANES, LANES)
            for i in range(steps):
                keep = mask_ref[i, :, pl.ds(pl.multiple_of(first + to, LANES), LANES)]
                value = pieces[r][i * rows : (i + 1) * rows, j * LANES : (j + 1) * LANES].astype(jnp.float32)
                made[i * rows : (i + 1) * rows, pl.ds(to, LANES)] = (value * keep).astype(jnp.bfloat16)
    copy = pltpu.make_async_copy(made, out_ref.at[:, pl.ds(first, made.shape[1])], sem)
    copy.start()
    copy.wait()


def assembled(place, keep_wide, pieces, out=None):
    rows, width = pieces[0].shape
    cols = keep_wide.shape[2]
    vmem_spec = pl.BlockSpec(memory_space=pltpu.VMEM)
    any_spec = pl.BlockSpec(memory_space=pltpu.HBM)
    operands = [place, keep_wide, *pieces] + ([] if out is None else [out])
    return pl.pallas_call(
        assemble_kernel,
        out_shape=jax.ShapeDtypeStruct((rows, cols), jnp.bfloat16),
        in_specs=[pl.BlockSpec(memory_space=pltpu.SMEM)] + [vmem_spec] * 5 + [any_spec] * (len(operands) - 6),
        out_specs=any_spec,
        scratch_shapes=[pltpu.VMEM((rows, width * len(pieces)), jnp.bfloat16), pltpu.SemaphoreType.DMA],
        input_output_aliases={} if out is None else {6: 0},
        compiler_params=pltpu.CompilerParams(vmem_limit_bytes=16 * MIB),
        cost_estimate=pl.CostEstimate(flops=1000, bytes_accessed=4 * rows * width, transcendentals=0),
        name="assembled",
    )(*operands)


def widen(mask, block):
    rows, cols = mask.shape
    wide = jnp.broadcast_to(mask.astype(jnp.float32)[:, :, None], (rows, cols, block))
    return wide.reshape(rows, 1, cols * block)


def together(*values):
    return lax.optimization_barrier(values)


def pairs_in_line(x_band, w_band, a_mask, keep_mask):
    panel = x_band.shape[0]
    block = panel // a_mask.shape[0]
    g, c = lax.axis_index("grid"), lax.axis_index("depth")
    z, y = g // 2, g % 2
    left = z < 2
    is_end = ((z == 0) | (z == 3)).astype(jnp.int32)
    toward = jnp.where(left, 1, -1)
    q = 2 * y + c

    swap = [(0, 2), (1, 3), (2, 0), (3, 1), (4, 6), (5, 7), (6, 4), (7, 5)]
    inward = [(0, 2), (1, 3), (6, 4), (7, 5)]
    outward = [(2, 0), (3, 1), (4, 6), (5, 7)]
    cross = [(2, 4), (3, 5), (4, 2), (5, 3)]
    across = [(i, i ^ 1) for i in range(8)]
    layers = [(0, 1), (1, 0)]
    opposite = [(i, i ^ 3) for i in range(16)]

    def line(value, pairs):
        return lax.ppermute(value, "grid", pairs)

    def strips(value, start, count):
        return lax.dynamic_slice_in_dim(value, start * LANES, count * LANES, 1)

    start_near = jnp.where(left, 0, 1)
    first_out, second_out = jnp.where(left, 0, 4), jnp.where(left, 4, 0)
    first_in, second_in = second_out, first_out
    last_in = jnp.where(left, 1, 4)

    sent_b, own_a = b_strips(w_band, [q ^ 2, q])
    own_b = line(sent_b, across)
    swap_a = line(own_a, swap)
    cross_a = line(own_a, cross)
    mask_wide = widen(a_mask, block)
    x_mine = masked_half(x_band, mask_wide, c)
    own_b, x_mine, swap_a, cross_a = together(own_b, x_mine, swap_a, cross_a)
    near_b = line(jnp.concatenate([strips(own_b, start_near, 7), cross_a[:, 3 * LANES :]], 1), outward)
    in_b = line(own_b, inward)
    cross_b = line(own_b, cross)
    x_across = line(x_mine, across)
    x_rest = masked_half(x_band, mask_wide, 1 - c)

    fwd_a = line(strips(swap_a, first_out, 4), cross)
    in_b, cross_b = together(in_b, cross_b)
    mid_b = line(
        jnp.concatenate([jnp.where(y == 0, cross_a[:, : 3 * LANES], cross_b[:, : 3 * LANES]), cross_b[:, 3 * LANES :]], 1),
        outward,
    )
    in_b, near_b, fwd_a = together(in_b, near_b, fwd_a)
    fwd_b = line(strips(in_b, first_out, 4), cross)
    fwd_second = line(jnp.concatenate([strips(v, second_out, 4) for v in (swap_a, in_b)], 1), cross)
    far_a = line(fwd_a, outward)
    x_across, mid_b, fwd_b = together(x_across, mid_b, fwd_b)
    far_b = line(fwd_b, outward)
    x_opposite = lax.ppermute(x_across, "depth", layers)
    xs = [x_mine, x_rest, x_across, x_opposite]

    def offsets(delta):
        tilt = 2 * y - 1
        return [(2 * delta + 4) % 8, (2 * delta + tilt + 4) % 8, (2 * delta - tilt + 4) % 8, (2 * delta + 4) % 8]

    zero = jnp.zeros_like(z)
    third = offsets(jnp.where(is_end == 1, 2, -toward))
    fourth = offsets(jnp.where(is_end == 1, -toward, 2))
    meta = jnp.stack([is_end, y, start_near, *offsets(zero), *offsets(toward), *third]).astype(jnp.int32)
    total = first_products(
        meta, xs, [own_a, own_b, cross_a, cross_b, swap_a, in_b], [swap_a, near_b, mid_b]
    )
    last = jnp.concatenate(
        [strips(fwd_second, jnp.where(left, 1, 0), 3), strips(fwd_second, jnp.where(left, 5, 4), 3)], 1
    )
    last, total, far_a = together(last, total, far_a)
    far_second = line(last, outward)

    def exchanged(pieces):
        return [
            pieces[0],
            lax.ppermute(pieces[1], "depth", layers),
            line(pieces[2], across),
            lax.ppermute(pieces[3], ("grid", "depth"), opposite),
        ]

    done_at, rest_at = jnp.where(left, 3, 0), jnp.where(left, 0, 5)
    meta = jnp.stack([is_end, first_in, second_in, done_at, rest_at, *fourth]).astype(jnp.int32)
    *done, rest = half_products(meta, xs, total, [fwd_a, fwd_b], [far_a, far_b], fwd_second, 5)
    done = exchanged(done)
    far_second, done[1] = together(far_second, done[1])
    keep_wide = widen(keep_mask, block)
    out = assembled(jnp.stack([q, done_at]).astype(jnp.int32), keep_wide, done)
    meta = jnp.stack([is_end, last_in, rest_at, *fourth]).astype(jnp.int32)
    rest = exchanged(rest_products(meta, xs, rest, far_second, own_a.shape[1]))
    return assembled(jnp.stack([q, rest_at]).astype(jnp.int32), keep_wide, rest, out)


def solution(mesh):
    placed = (
        P(("groups", "grid"), None),
        P(("groups", "grid"), None),
        P(("groups", "grid"), None),
        P(("groups", "grid", "depth"), None),
    )

    def local(x_band, w_band, a_mask, keep_mask):
        panel, cols = x_band.shape
        pairs = mesh.shape["grid"] == 8 and mesh.shape["depth"] == 2
        pairs = pairs and cols == 8 * panel and panel == 4 * LANES
        return (pairs_in_line if pairs else ring)(x_band, w_band, a_mask, keep_mask)

    return jax.shard_map(
        local,
        mesh=mesh,
        in_specs=placed,
        out_specs=P(("groups", "grid", "depth"), None),
        check_vma=False,
    )
```

```python
import functools

import jax
import jax.numpy as jnp
from jax import lax
from jax.experimental import pallas as pl
from jax.experimental.pallas import tpu as pltpu
from jax.sharding import PartitionSpec as P

LANES = 128
MIB = 1 << 20
SMALL = pl.CostEstimate(flops=1000, bytes_accessed=1000, transcendentals=0)


def shifted(shard, axis, by):
    count = lax.axis_size(axis)
    return lax.ppermute(shard, axis, [(i, (i + by) % count) for i in range(count)])


def expand_blocks(mask, block):
    rows, cols = mask.shape
    wide = jnp.broadcast_to(mask[:, None, :, None], (rows, block, cols, block))
    return wide.reshape(rows * block, cols * block)


def ring(x_band, w_band, a_mask, keep_mask):
    panel = x_band.shape[0]
    block = panel // a_mask.shape[0]
    band_cols = x_band.shape[1]
    xm = x_band * expand_blocks(a_mask, block).astype(jnp.bfloat16)
    rows = lax.broadcasted_iota(jnp.int32, x_band.shape, 0)
    cols = lax.broadcasted_iota(jnp.int32, x_band.shape, 1)
    identity = jnp.where(cols == rows + 4 * panel, 1.0, 0.0).astype(jnp.float32)
    b_panel = (1.5 * identity - 0.5 * w_band.astype(jnp.float32)).astype(jnp.bfloat16)
    layer = lax.axis_index("depth")
    current = shifted(b_panel, ("grid", "depth"), -5)
    wide = jnp.zeros((panel, 2 * band_cols), jnp.float32)
    for step in range(4):
        offset = 6 + layer - 2 * step
        ablock = lax.dynamic_slice_in_dim(xm, offset * panel, panel, 1)
        term = jnp.dot(ablock, current, preferred_element_type=jnp.float32)
        region = lax.dynamic_slice_in_dim(wide, offset * panel, band_cols, 1)
        wide = lax.dynamic_update_slice_in_dim(wide, region + term, offset * panel, 1)
        if step < 3:
            current = shifted(current, "grid", 2)
    partial_band = wide[:, 4 * panel : 12 * panel]
    mine = lax.psum_scatter(partial_band, "depth", scatter_dimension=0, tiled=True)
    keep = expand_blocks(keep_mask, block).astype(jnp.float32)
    return (mine * keep).astype(jnp.bfloat16)


def strips_kernel(quarters_ref, w_ref, *refs):
    *b_refs, held, sems = refs
    _, panel, width = held.shape
    band = width // LANES

    def copy(k, j):
        at = pl.multiple_of(j * panel + quarters_ref[k] * LANES, LANES)
        to = held.at[k, :, j * LANES : (j + 1) * LANES]
        return pltpu.make_async_copy(w_ref.at[:, pl.ds(at, LANES)], to, sems.at[k, j])

    for k in range(len(b_refs)):
        for j in range(band):
            copy(k, j).start()
    for k, b_ref in enumerate(b_refs):
        for j in range(band):
            copy(k, j).wait()
            value = -0.5 * held[k, :, j * LANES : (j + 1) * LANES].astype(jnp.float32)
            if j == band // 2:
                rows = lax.broadcasted_iota(jnp.int32, value.shape, 0)
                cols = lax.broadcasted_iota(jnp.int32, value.shape, 1)
                value = value + jnp.where(rows == cols + quarters_ref[k] * LANES, 1.5, 0.0)
            b_ref[:, j * LANES : (j + 1) * LANES] = value.astype(jnp.bfloat16)


def b_strips(w_band, quarters):
    panel = w_band.shape[0]
    band = w_band.shape[1] // panel
    n = len(quarters)
    shape = (panel, band * LANES)
    return pl.pallas_call(
        strips_kernel,
        out_shape=[jax.ShapeDtypeStruct(shape, jnp.bfloat16)] * n,
        in_specs=[
            pl.BlockSpec(memory_space=pltpu.SMEM),
            pl.BlockSpec(memory_space=pltpu.HBM),
        ],
        out_specs=[pl.BlockSpec(memory_space=pltpu.VMEM)] * n,
        scratch_shapes=[pltpu.VMEM((n, *shape), jnp.bfloat16), pltpu.SemaphoreType.DMA((n, band))],
        compiler_params=pltpu.CompilerParams(vmem_limit_bytes=56 * MIB),
        cost_estimate=SMALL,
        name="b_strips",
    )(jnp.stack(quarters), w_band)


def mask_kernel(half_ref, mask_ref, x_ref, out_ref):
    out_ref[...] = (x_ref[...].astype(jnp.float32) * mask_ref[0]).astype(jnp.bfloat16)


def masked_half(x_band, mask_wide, half):
    block = x_band.shape[0] // mask_wide.shape[0]
    per_half = mask_wide.shape[0] // 2
    cols = x_band.shape[1]
    return pl.pallas_call(
        mask_kernel,
        grid_spec=pltpu.PrefetchScalarGridSpec(
            num_scalar_prefetch=1,
            grid=(per_half,),
            in_specs=[
                pl.BlockSpec((1, 1, cols), lambda i, h: (h[0] * per_half + i, 0, 0)),
                pl.BlockSpec((block, cols), lambda i, h: (h[0] * per_half + i, 0)),
            ],
            out_specs=pl.BlockSpec((block, cols), lambda i, h: (i, 0)),
        ),
        out_shape=jax.ShapeDtypeStruct((x_band.shape[0] // 2, cols), jnp.bfloat16),
        compiler_params=pltpu.CompilerParams(vmem_limit_bytes=58 * MIB),
        cost_estimate=SMALL,
        name="masked_half",
    )(half.reshape(1), mask_wide, x_band)


def x_copies(x_refs, xv, sems, offset_of):
    n_b, _, rows, panel = xv.shape
    half = rows // 2
    copies = {}
    for p in range(n_b):
        for r in range(4):
            at = pl.multiple_of(offset_of(p, r // 2) * panel, panel)
            copies[p, r] = pltpu.make_async_copy(
                x_refs[r].at[:, pl.ds(at, panel)],
                xv.at[p, r // 2, (r % 2) * half : (r % 2 + 1) * half],
                sems.at[p, r],
            )
    return copies


def add_products(acc, xv, p, strips, offset_of, start):
    def step(g, carry):
        at = (offset_of(p, g) + start) * LANES
        cols = pl.ds(pl.multiple_of(at, LANES), strips.shape[1])
        acc[g, :, cols] += jnp.dot(xv[p, g], strips[...], preferred_element_type=jnp.float32)
        return carry

    lax.fori_loop(0, 2, step, 0)


def whole_kernel(plan, has_prev, meta_ref, *refs):
    n_b = len(plan)
    x_refs, refs = refs[:4], refs[4:]
    prev_ref, refs = (refs[0], refs[1:]) if has_prev else (None, refs)
    b_refs, (out_ref, xv, bv, acc, x_sems, b_sems, out_sems) = refs[:-7], refs[-7:]
    quarter = bv.shape[2]
    low = quarter // 2
    is_end = meta_ref[0]

    def offset_of(p, g):
        return meta_ref[3 + 2 * p + g]

    def b_middle(p):
        return [pltpu.make_async_copy(b_refs[plan[p][0]], bv.at[p], b_sems.at[p, 0])]

    def b_end(p):
        copies = []
        for k, (operand, first, count, at, to) in enumerate(plan[p][1]):
            at = pl.multiple_of(meta_ref[2] * LANES, LANES) if at is None else at * LANES
            to = meta_ref[1] if to is None else to
            source = b_refs[operand].at[:, first * LANES : (first + count) * LANES]
            copies.append(pltpu.make_async_copy(source, bv.at[to, :, pl.ds(at, count * LANES)], b_sems.at[p, k]))
        return copies

    def on_each(p, do):
        @pl.when(is_end == 0)
        def _():
            for copy in b_middle(p):
                do(copy)

        @pl.when(is_end != 0)
        def _():
            for copy in b_end(p):
                do(copy)

    prev_copies = [
        pltpu.make_async_copy(prev_ref.at[g], acc.at[g, :, low : low + quarter], out_sems.at[g])
        for g in range(2)
        if has_prev
    ]
    copies = x_copies(x_refs, xv, x_sems, offset_of)
    for p in range(n_b):
        on_each(p, lambda copy: copy.start())
        for r in range(4):
            copies[p, r].start()
        if p == 0:
            for copy in prev_copies:
                copy.start()
    if has_prev:
        for copy in prev_copies:
            copy.wait()
        for p in range(n_b):
            on_each(p, lambda copy: copy.wait())
    else:
        acc[...] = jnp.zeros_like(acc)
    for p in range(n_b):
        if not has_prev:
            on_each(p, lambda copy: copy.wait())
        for r in range(4):
            copies[p, r].wait()
        add_products(acc, xv, p, bv.at[p], offset_of, 0)
    outs = [
        pltpu.make_async_copy(acc.at[g, :, low : low + quarter], out_ref.at[g], out_sems.at[g]) for g in range(2)
    ]
    for out in outs:
        out.start()
    for out in outs:
        out.wait()


def whole_products(meta, xs, prev, operands, plan, name):
    rows = xs[0].shape[0]
    panel, quarter = operands[plan[0][0]].shape
    n_b = len(plan)
    any_spec = pl.BlockSpec(memory_space=pl.ANY)
    x_spec = pl.BlockSpec(memory_space=pltpu.HBM)
    operands = ([] if prev is None else [prev]) + operands
    return pl.pallas_call(
        functools.partial(whole_kernel, plan, prev is not None),
        out_shape=jax.ShapeDtypeStruct((2, 2 * rows, quarter), jnp.float32),
        in_specs=[pl.BlockSpec(memory_space=pltpu.SMEM)] + [x_spec] * 4 + [any_spec] * len(operands),
        out_specs=any_spec,
        scratch_shapes=[
            pltpu.VMEM((n_b, 2, 2 * rows, panel), jnp.bfloat16),
            pltpu.VMEM((n_b, panel, quarter), jnp.bfloat16),
            pltpu.VMEM((2, 2 * rows, 2 * quarter), jnp.float32),
            pltpu.SemaphoreType.DMA((n_b, 4)),
            pltpu.SemaphoreType.DMA((n_b, 2)),
            pltpu.SemaphoreType.DMA((2,)),
        ],
        compiler_params=pltpu.CompilerParams(vmem_limit_bytes=59 * MIB),
        cost_estimate=SMALL,
        name=name,
    )(meta, *xs, *operands)


def give_pieces(out_refs, acc, at):
    half, width = out_refs[0].shape
    cols = pl.ds(pl.multiple_of(at * LANES, LANES), width)
    for r in range(4):
        rows = slice((r % 2) * half, (r % 2 + 1) * half)
        out_refs[r][...] = acc[r // 2, rows, cols].astype(jnp.bfloat16)


def half_kernel(meta_ref, *refs):
    x_refs, prev_ref, middle_refs, end_refs, second_ref, refs = refs[:4], refs[4], refs[5:7], refs[7:9], refs[9], refs[10:]
    out_refs, rest_ref, xv, bv, acc, x_sems, b_sems, prev_sem, rest_sem = refs[:4], *refs[4:]
    half = bv.shape[2]
    quarter = 2 * half
    low = quarter // 2
    band = quarter // LANES
    is_end = meta_ref[0]

    def offset_of(p, g):
        return meta_ref[5 + 2 * p + g]

    copies = x_copies(x_refs, xv, x_sems, offset_of)
    middle = [pltpu.make_async_copy(middle_refs[p], bv.at[p], b_sems.at[p]) for p in range(2)]
    middle += [
        pltpu.make_async_copy(second_ref.at[:, p * half : (p + 1) * half], bv.at[2 + p], b_sems.at[2 + p])
        for p in range(2)
    ]
    end = [pltpu.make_async_copy(end_refs[p], bv.at[p], b_sems.at[p]) for p in range(2)]
    prev = pltpu.make_async_copy(prev_ref, acc.at[:, :, low : low + quarter], prev_sem)
    prev.start()

    @pl.when(is_end == 0)
    def _():
        for copy in middle:
            copy.start()

    @pl.when(is_end != 0)
    def _():
        for copy in end:
            copy.start()

    for copy in copies.values():
        copy.start()

    @pl.when(is_end == 0)
    def _():
        for copy in middle:
            copy.wait()

    @pl.when(is_end != 0)
    def _():
        for copy in end:
            copy.wait()

    for copy in copies.values():
        copy.wait()
    prev.wait()
    for p in range(2):
        add_products(acc, xv, p, bv.at[p], offset_of, meta_ref[1])

    @pl.when(is_end == 0)
    def _():
        for p in range(2):
            add_products(acc, xv, p, bv.at[2 + p], offset_of, meta_ref[2])

    at = pl.multiple_of((meta_ref[4] + band // 2) * LANES, LANES)
    rest = pltpu.make_async_copy(acc.at[:, :, pl.ds(at, rest_ref.shape[2])], rest_ref, rest_sem)
    rest.start()
    give_pieces(out_refs, acc, meta_ref[3] + band // 2)
    rest.wait()


def half_products(meta, xs, prev, middle, end, second, n_done):
    rows = xs[0].shape[0]
    panel, quarter = second.shape
    any_spec = pl.BlockSpec(memory_space=pl.ANY)
    x_spec = pl.BlockSpec(memory_space=pltpu.HBM)
    n_rest = quarter // LANES - n_done
    return pl.pallas_call(
        half_kernel,
        out_shape=[jax.ShapeDtypeStruct((rows, n_done * LANES), jnp.bfloat16)] * 4
        + [jax.ShapeDtypeStruct((2, 2 * rows, n_rest * LANES), jnp.float32)],
        in_specs=[pl.BlockSpec(memory_space=pltpu.SMEM)] + [x_spec] * 4 + [any_spec] * 6,
        out_specs=[pl.BlockSpec(memory_space=pltpu.VMEM)] * 4 + [any_spec],
        scratch_shapes=[
            pltpu.VMEM((2, 2, 2 * rows, panel), jnp.bfloat16),
            pltpu.VMEM((4, panel, quarter // 2), jnp.bfloat16),
            pltpu.VMEM((2, 2 * rows, 2 * quarter), jnp.float32),
            pltpu.SemaphoreType.DMA((2, 4)),
            pltpu.SemaphoreType.DMA((4,)),
            pltpu.SemaphoreType.DMA,
            pltpu.SemaphoreType.DMA,
        ],
        compiler_params=pltpu.CompilerParams(vmem_limit_bytes=59 * MIB),
        cost_estimate=SMALL,
        name="half_products",
    )(meta, *xs, prev, *middle, *end, second)


def rest_kernel(meta_ref, *refs):
    x_refs, rest_ref, b_ref = refs[:4], *refs[4:6]
    out_refs, xv, bv, acc, x_sems, b_sem, rest_sem = refs[6:10], *refs[10:]
    band = acc.shape[2] // (2 * LANES)
    half = bv.shape[1] // 2
    is_end = meta_ref[0]

    def offset_of(p, g):
        return meta_ref[3 + 2 * p + g]

    at = pl.multiple_of((meta_ref[2] + band // 2) * LANES, LANES)
    rest = pltpu.make_async_copy(rest_ref, acc.at[:, :, pl.ds(at, rest_ref.shape[2])], rest_sem)
    rest.start()
    copies = x_copies(x_refs, xv, x_sems, offset_of)
    b_copy = pltpu.make_async_copy(b_ref, bv, b_sem)

    @pl.when(is_end != 0)
    def _():
        b_copy.start()
        for copy in copies.values():
            copy.start()

    rest.wait()

    @pl.when(is_end != 0)
    def _():
        b_copy.wait()
        for copy in copies.values():
            copy.wait()
        for p in range(2):
            add_products(acc, xv, p, bv.at[:, p * half : (p + 1) * half], offset_of, meta_ref[1])

    give_pieces(out_refs, acc, meta_ref[2] + band // 2)


def rest_products(meta, xs, rest, b, quarter):
    rows = xs[0].shape[0]
    panel = b.shape[0]
    width = rest.shape[2]
    any_spec = pl.BlockSpec(memory_space=pl.ANY)
    x_spec = pl.BlockSpec(memory_space=pltpu.HBM)
    return pl.pallas_call(
        rest_kernel,
        out_shape=[jax.ShapeDtypeStruct((rows, width), jnp.bfloat16)] * 4,
        in_specs=[pl.BlockSpec(memory_space=pltpu.SMEM)] + [x_spec] * 4 + [any_spec] * 2,
        out_specs=[pl.BlockSpec(memory_space=pltpu.VMEM)] * 4,
        scratch_shapes=[
            pltpu.VMEM((2, 2, 2 * rows, panel), jnp.bfloat16),
            pltpu.VMEM(b.shape, jnp.bfloat16),
            pltpu.VMEM((2, 2 * rows, 2 * quarter), jnp.float32),
            pltpu.SemaphoreType.DMA((2, 4)),
            pltpu.SemaphoreType.DMA,
            pltpu.SemaphoreType.DMA,
        ],
        compiler_params=pltpu.CompilerParams(vmem_limit_bytes=59 * MIB),
        cost_estimate=SMALL,
        name="rest_products",
    )(meta, *xs, rest, b)


def assemble_kernel(place_ref, mask_ref, *refs):
    n = 4
    pieces, (out_ref, made, sem) = refs[:n], refs[-3:]
    steps = mask_ref.shape[0]
    rows = made.shape[0] // steps
    panel = n * LANES
    first = pl.multiple_of(place_ref[1] * panel, panel)
    for r in range(n):
        t = jnp.bitwise_xor(place_ref[0], r)
        for j in range(made.shape[1] // panel):
            to = pl.multiple_of(j * panel + t * LANES, LANES)
            for i in range(steps):
                keep = mask_ref[i, :, pl.ds(pl.multiple_of(first + to, LANES), LANES)]
                value = pieces[r][i * rows : (i + 1) * rows, j * LANES : (j + 1) * LANES].astype(jnp.float32)
                made[i * rows : (i + 1) * rows, pl.ds(to, LANES)] = (value * keep).astype(jnp.bfloat16)
    copy = pltpu.make_async_copy(made, out_ref.at[:, pl.ds(first, made.shape[1])], sem)
    copy.start()
    copy.wait()


def assembled(place, keep_wide, pieces, out=None):
    rows, width = pieces[0].shape
    cols = keep_wide.shape[2]
    vmem_spec = pl.BlockSpec(memory_space=pltpu.VMEM)
    any_spec = pl.BlockSpec(memory_space=pltpu.HBM)
    operands = [place, keep_wide, *pieces] + ([] if out is None else [out])
    return pl.pallas_call(
        assemble_kernel,
        out_shape=jax.ShapeDtypeStruct((rows, cols), jnp.bfloat16),
        in_specs=[pl.BlockSpec(memory_space=pltpu.SMEM)] + [vmem_spec] * 5 + [any_spec] * (len(operands) - 6),
        out_specs=any_spec,
        scratch_shapes=[pltpu.VMEM((rows, width * len(pieces)), jnp.bfloat16), pltpu.SemaphoreType.DMA],
        input_output_aliases={} if out is None else {6: 0},
        compiler_params=pltpu.CompilerParams(vmem_limit_bytes=16 * MIB),
        cost_estimate=SMALL,
        name="assembled",
    )(*operands)


def widen(mask, block):
    rows, cols = mask.shape
    wide = jnp.broadcast_to(mask.astype(jnp.float32)[:, :, None], (rows, cols, block))
    return wide.reshape(rows, 1, cols * block)


def together(*values):
    return lax.optimization_barrier(values)


def pairs_in_line(x_band, w_band, a_mask, keep_mask):
    panel = x_band.shape[0]
    block = panel // a_mask.shape[0]
    g, c = lax.axis_index("grid"), lax.axis_index("depth")
    z, y = g // 2, g % 2
    left = z < 2
    is_end = ((z == 0) | (z == 3)).astype(jnp.int32)
    toward = jnp.where(left, 1, -1)
    q = 2 * y + c

    swap = [(0, 2), (1, 3), (2, 0), (3, 1), (4, 6), (5, 7), (6, 4), (7, 5)]
    inward = [(0, 2), (1, 3), (6, 4), (7, 5)]
    outward = [(2, 0), (3, 1), (4, 6), (5, 7)]
    cross = [(2, 4), (3, 5), (4, 2), (5, 3)]
    across = [(i, i ^ 1) for i in range(8)]
    layers = [(0, 1), (1, 0)]
    opposite = [(i, i ^ 3) for i in range(16)]

    def line(value, pairs):
        return lax.ppermute(value, "grid", pairs)

    def strips(value, start, count):
        return lax.dynamic_slice_in_dim(value, start * LANES, count * LANES, 1)

    start_near = jnp.where(left, 0, 1)
    first_out, second_out = jnp.where(left, 0, 4), jnp.where(left, 4, 0)
    first_in, second_in = second_out, first_out
    last_in = jnp.where(left, 1, 4)

    sent_b, own_a = b_strips(w_band, [q ^ 2, q])
    own_b = line(sent_b, across)
    swap_a = line(own_a, swap)
    cross_a = line(own_a, cross)
    mask_wide = widen(a_mask, block)
    x_mine = masked_half(x_band, mask_wide, c)
    own_b, x_mine, swap_a, cross_a = together(own_b, x_mine, swap_a, cross_a)
    near_b = line(jnp.concatenate([strips(own_b, start_near, 7), cross_a[:, 3 * LANES :]], 1), outward)
    in_b = line(own_b, inward)
    cross_b = line(own_b, cross)
    x_across = line(x_mine, across)
    x_rest = masked_half(x_band, mask_wide, 1 - c)

    fwd_a = line(strips(swap_a, first_out, 4), cross)
    in_b, cross_b = together(in_b, cross_b)
    mid_b = jnp.concatenate(
        [jnp.where(y == 0, cross_a[:, : 3 * LANES], cross_b[:, : 3 * LANES]), cross_b[:, 3 * LANES :]], 1
    )
    fwd_b = strips(in_b, first_out, 4)
    fwd_second = jnp.concatenate([strips(v, second_out, 4) for v in (swap_a, in_b)], 1)
    near_b, fwd_a, x_across, mid_b, fwd_b, fwd_second = together(near_b, fwd_a, x_across, mid_b, fwd_b, fwd_second)
    mid_b = line(mid_b, outward)
    x_opposite = lax.ppermute(x_across, "depth", layers)
    xs = [x_mine, x_rest, x_across, x_opposite]
    fwd_b = line(fwd_b, cross)
    fwd_second = line(fwd_second, cross)
    far_a = line(fwd_a, outward)

    def offsets(delta):
        tilt = 2 * y - 1
        return [(2 * delta + 4) % 8, (2 * delta + tilt + 4) % 8, (2 * delta - tilt + 4) % 8, (2 * delta + 4) % 8]

    zero = jnp.zeros_like(z)
    third = offsets(jnp.where(is_end == 1, 2, -toward))
    fourth = offsets(jnp.where(is_end == 1, -toward, 2))
    zero = zero.astype(jnp.int32)
    meta = jnp.stack([is_end, zero, start_near, *offsets(zero), *offsets(toward)]).astype(jnp.int32)
    whole = lambda operand, p: (operand, [(operand, 0, 8, 0, p)])
    plan = [whole(0, 0), whole(1, 1), (2, [(4, 0, 8, 0, 2)]), (3, [(5, 0, 7, None, 3)])]
    total = whole_products(meta, xs, None, [own_a, own_b, cross_a, cross_b, swap_a, near_b], plan, "first_products")
    last_at = jnp.where(left, 1, 0)
    mid_b, fwd_b, total, last_at = together(mid_b, fwd_b, total, last_at)
    far_b = line(fwd_b, outward)
    meta = jnp.stack([is_end, y, zero, *third]).astype(jnp.int32)
    plan = [(0, [(2, 7, 5, 3, 0), (3, 0, 3, 0, None)]), (1, [(3, 3, 5, 3, 1)])]
    total = whole_products(meta, xs, total, [swap_a, in_b, near_b, mid_b], plan, "next_products")
    last = jnp.concatenate(
        [strips(fwd_second, last_at, 3), strips(fwd_second, last_at + 4, 3)], 1
    )
    last, far_a = together(last, far_a)
    far_second = line(last, outward)

    def exchanged(pieces):
        return [
            pieces[0],
            lax.ppermute(pieces[1], "depth", layers),
            line(pieces[2], across),
            lax.ppermute(pieces[3], ("grid", "depth"), opposite),
        ]

    done_at, rest_at = jnp.where(left, 3, 0), jnp.where(left, 0, 5)
    meta = jnp.stack([is_end, first_in, second_in, done_at, rest_at, *fourth]).astype(jnp.int32)
    *done, rest = half_products(meta, xs, total, [fwd_a, fwd_b], [far_a, far_b], fwd_second, 5)
    done = exchanged(done)
    far_second, done[1] = together(far_second, done[1])
    keep_wide = widen(keep_mask, block)
    out = assembled(jnp.stack([q, done_at]).astype(jnp.int32), keep_wide, done)
    meta = jnp.stack([is_end, last_in, rest_at, *fourth]).astype(jnp.int32)
    rest = exchanged(rest_products(meta, xs, rest, far_second, own_a.shape[1]))
    return assembled(jnp.stack([q, rest_at]).astype(jnp.int32), keep_wide, rest, out)


def solution(mesh):
    placed = (
        P(("groups", "grid"), None),
        P(("groups", "grid"), None),
        P(("groups", "grid"), None),
        P(("groups", "grid", "depth"), None),
    )

    def local(x_band, w_band, a_mask, keep_mask):
        panel, cols = x_band.shape
        pairs = mesh.shape["grid"] == 8 and mesh.shape["depth"] == 2
        pairs = pairs and cols == 8 * panel and panel == 4 * LANES
        return (pairs_in_line if pairs else ring)(x_band, w_band, a_mask, keep_mask)

    return jax.shard_map(
        local,
        mesh=mesh,
        in_specs=placed,
        out_specs=P(("groups", "grid", "depth"), None),
        check_vma=False,
    )
```

```python
import functools

import jax
import jax.numpy as jnp
from jax import lax
from jax.experimental import pallas as pl
from jax.experimental.pallas import tpu as pltpu
from jax.sharding import PartitionSpec as P

LANES = 128
MIB = 1 << 20
SMALL = pl.CostEstimate(flops=1000, bytes_accessed=1000, transcendentals=0)


def shifted(shard, axis, by):
    count = lax.axis_size(axis)
    return lax.ppermute(shard, axis, [(i, (i + by) % count) for i in range(count)])


def expand_blocks(mask, block):
    rows, cols = mask.shape
    wide = jnp.broadcast_to(mask[:, None, :, None], (rows, block, cols, block))
    return wide.reshape(rows * block, cols * block)


def ring(x_band, w_band, a_mask, keep_mask):
    panel = x_band.shape[0]
    block = panel // a_mask.shape[0]
    band_cols = x_band.shape[1]
    xm = x_band * expand_blocks(a_mask, block).astype(jnp.bfloat16)
    rows = lax.broadcasted_iota(jnp.int32, x_band.shape, 0)
    cols = lax.broadcasted_iota(jnp.int32, x_band.shape, 1)
    identity = jnp.where(cols == rows + 4 * panel, 1.0, 0.0).astype(jnp.float32)
    b_panel = (1.5 * identity - 0.5 * w_band.astype(jnp.float32)).astype(jnp.bfloat16)
    layer = lax.axis_index("depth")
    current = shifted(b_panel, ("grid", "depth"), -5)
    wide = jnp.zeros((panel, 2 * band_cols), jnp.float32)
    for step in range(4):
        offset = 6 + layer - 2 * step
        ablock = lax.dynamic_slice_in_dim(xm, offset * panel, panel, 1)
        term = jnp.dot(ablock, current, preferred_element_type=jnp.float32)
        region = lax.dynamic_slice_in_dim(wide, offset * panel, band_cols, 1)
        wide = lax.dynamic_update_slice_in_dim(wide, region + term, offset * panel, 1)
        if step < 3:
            current = shifted(current, "grid", 2)
    partial_band = wide[:, 4 * panel : 12 * panel]
    mine = lax.psum_scatter(partial_band, "depth", scatter_dimension=0, tiled=True)
    keep = expand_blocks(keep_mask, block).astype(jnp.float32)
    return (mine * keep).astype(jnp.bfloat16)


def strips_kernel(quarters_ref, w_ref, *refs):
    *b_refs, held, sems = refs
    _, panel, width = held.shape
    band = width // LANES

    def copy(k, j):
        at = pl.multiple_of(j * panel + quarters_ref[k] * LANES, LANES)
        to = held.at[k, :, j * LANES : (j + 1) * LANES]
        return pltpu.make_async_copy(w_ref.at[:, pl.ds(at, LANES)], to, sems.at[k, j])

    for k in range(len(b_refs)):
        for j in range(band):
            copy(k, j).start()
    for k, b_ref in enumerate(b_refs):
        for j in range(band):
            copy(k, j).wait()
            value = -0.5 * held[k, :, j * LANES : (j + 1) * LANES].astype(jnp.float32)
            if j == band // 2:
                rows = lax.broadcasted_iota(jnp.int32, value.shape, 0)
                cols = lax.broadcasted_iota(jnp.int32, value.shape, 1)
                value = value + jnp.where(rows == cols + quarters_ref[k] * LANES, 1.5, 0.0)
            b_ref[:, j * LANES : (j + 1) * LANES] = value.astype(jnp.bfloat16)


def b_strips(w_band, quarters):
    panel = w_band.shape[0]
    band = w_band.shape[1] // panel
    n = len(quarters)
    shape = (panel, band * LANES)
    return pl.pallas_call(
        strips_kernel,
        out_shape=[jax.ShapeDtypeStruct(shape, jnp.bfloat16)] * n,
        in_specs=[
            pl.BlockSpec(memory_space=pltpu.SMEM),
            pl.BlockSpec(memory_space=pltpu.HBM),
        ],
        out_specs=[pl.BlockSpec(memory_space=pltpu.VMEM)] * n,
        scratch_shapes=[pltpu.VMEM((n, *shape), jnp.bfloat16), pltpu.SemaphoreType.DMA((n, band))],
        compiler_params=pltpu.CompilerParams(vmem_limit_bytes=56 * MIB),
        cost_estimate=SMALL,
        name="b_strips",
    )(jnp.stack(quarters), w_band)


def mask_kernel(first_ref, mask_ref, x_ref, out_ref):
    out_ref[...] = (x_ref[...].astype(jnp.float32) * mask_ref[0]).astype(jnp.bfloat16)


def masked_rows(x_band, mask_wide, first, count):
    block = x_band.shape[0] // mask_wide.shape[0]
    cols = x_band.shape[1]
    return pl.pallas_call(
        mask_kernel,
        grid_spec=pltpu.PrefetchScalarGridSpec(
            num_scalar_prefetch=1,
            grid=(count,),
            in_specs=[
                pl.BlockSpec((1, 1, cols), lambda i, f: (f[0] + i, 0, 0)),
                pl.BlockSpec((block, cols), lambda i, f: (f[0] + i, 0)),
            ],
            out_specs=pl.BlockSpec((block, cols), lambda i, f: (i, 0)),
        ),
        out_shape=jax.ShapeDtypeStruct((count * block, cols), jnp.bfloat16),
        compiler_params=pltpu.CompilerParams(vmem_limit_bytes=58 * MIB),
        cost_estimate=SMALL,
        name="masked_rows",
    )(first.reshape(1), mask_wide, x_band)


PARTS = 8


def x_copies(x_refs, xv, sems, offset_of):
    n_b, _, rows, panel = xv.shape
    part = 2 * rows // PARTS
    copies = {}
    for p in range(n_b):
        for r in range(PARTS):
            g, k = divmod(r, PARTS // 2)
            at = pl.multiple_of(offset_of(p, g) * panel, panel)
            copies[p, r] = pltpu.make_async_copy(
                x_refs[r].at[:, pl.ds(at, panel)],
                xv.at[p, g, k * part : (k + 1) * part],
                sems.at[p, r],
            )
    return copies


def add_products(acc, xv, p, strips, offset_of, start):
    def step(g, carry):
        at = (offset_of(p, g) + start) * LANES
        cols = pl.ds(pl.multiple_of(at, LANES), strips.shape[1])
        acc[g, :, cols] += jnp.dot(xv[p, g], strips[...], preferred_element_type=jnp.float32)
        return carry

    lax.fori_loop(0, 2, step, 0)


def whole_kernel(plan, meta_ref, *refs):
    n_b = len(plan)
    x_refs, refs = refs[:PARTS], refs[PARTS:]
    b_refs, (out_ref, xv, bv, acc, x_sems, b_sems, out_sems) = refs[:-7], refs[-7:]
    quarter = bv.shape[2]
    low = quarter // 2
    is_end = meta_ref[0]

    def offset_of(p, g):
        return meta_ref[2 + 2 * p + g]

    def b_middle(p):
        return [pltpu.make_async_copy(b_refs[plan[p][0]].at[:, :quarter], bv.at[p], b_sems.at[p, 0])]

    def b_end(p):
        copies = []
        for k, (operand, first, count, at, to) in enumerate(plan[p][1]):
            to = meta_ref[1] if to is None else to
            source = b_refs[operand].at[:, first * LANES : (first + count) * LANES]
            copies.append(pltpu.make_async_copy(source, bv.at[to, :, at * LANES : (at + count) * LANES], b_sems.at[p, k]))
        return copies

    def on_each(p, do):
        @pl.when(is_end == 0)
        def _():
            for copy in b_middle(p):
                do(copy)

        @pl.when(is_end != 0)
        def _():
            for copy in b_end(p):
                do(copy)

    copies = x_copies(x_refs, xv, x_sems, offset_of)
    for p in range(n_b):
        on_each(p, lambda copy: copy.start())
        for r in range(PARTS):
            copies[p, r].start()
    acc[...] = jnp.zeros_like(acc)
    for p in range(n_b):
        for k in [p] if p < n_b - 2 else range(n_b - 2, n_b) if p == n_b - 2 else []:
            on_each(k, lambda copy: copy.wait())
        for r in range(PARTS):
            copies[p, r].wait()
        add_products(acc, xv, p, bv.at[p], offset_of, 0)
    outs = [
        pltpu.make_async_copy(acc.at[g, :, low : low + quarter], out_ref.at[g], out_sems.at[g]) for g in range(2)
    ]
    for out in outs:
        out.start()
    for out in outs:
        out.wait()


def whole_products(meta, xs, operands, plan):
    rows = PARTS // 4 * xs[0].shape[0]
    panel, quarter = operands[plan[0][0]].shape
    n_b = len(plan)
    any_spec = pl.BlockSpec(memory_space=pl.ANY)
    x_spec = pl.BlockSpec(memory_space=pltpu.HBM)
    return pl.pallas_call(
        functools.partial(whole_kernel, plan),
        out_shape=jax.ShapeDtypeStruct((2, 2 * rows, quarter), jnp.float32),
        in_specs=[pl.BlockSpec(memory_space=pltpu.SMEM)] + [x_spec] * PARTS + [any_spec] * len(operands),
        out_specs=any_spec,
        scratch_shapes=[
            pltpu.VMEM((n_b, 2, 2 * rows, panel), jnp.bfloat16),
            pltpu.VMEM((n_b, panel, quarter), jnp.bfloat16),
            pltpu.VMEM((2, 2 * rows, 2 * quarter), jnp.float32),
            pltpu.SemaphoreType.DMA((n_b, PARTS)),
            pltpu.SemaphoreType.DMA((n_b, 3)),
            pltpu.SemaphoreType.DMA((2,)),
        ],
        compiler_params=pltpu.CompilerParams(vmem_limit_bytes=59 * MIB),
        cost_estimate=SMALL,
        name="whole_products",
    )(meta, *xs, *operands)


def give_pieces(out_refs, acc, at):
    half, width = out_refs[0].shape
    cols = pl.ds(pl.multiple_of(at * LANES, LANES), width)
    for r in range(4):
        rows = slice((r % 2) * half, (r % 2 + 1) * half)
        out_refs[r][...] = acc[r // 2, rows, cols].astype(jnp.bfloat16)


def half_kernel(meta_ref, *refs):
    x_refs, (prev_ref, middle_ref, end_ref, second_ref), refs = refs[:PARTS], refs[PARTS : PARTS + 4], refs[PARTS + 4 :]
    out_refs, rest_ref, xv, bv, acc, x_sems, b_sems, prev_sem, rest_sem = refs[:4], *refs[4:]
    half = bv.shape[2]
    quarter = 2 * half
    low = quarter // 2
    band = quarter // LANES
    is_end = meta_ref[0]

    def offset_of(p, g):
        return meta_ref[5 + 2 * p + g]

    copies = x_copies(x_refs, xv, x_sems, offset_of)

    def b_copies(ref, first):
        return [
            pltpu.make_async_copy(ref.at[:, p * half : (p + 1) * half], bv.at[first + p], b_sems.at[first + p])
            for p in range(2)
        ]

    middle = b_copies(middle_ref, 0) + b_copies(second_ref, 2)
    end = b_copies(end_ref, 0)
    prev = pltpu.make_async_copy(prev_ref, acc.at[:, :, low : low + quarter], prev_sem)
    prev.start()

    @pl.when(is_end == 0)
    def _():
        for copy in middle:
            copy.start()

    @pl.when(is_end != 0)
    def _():
        for copy in end:
            copy.start()

    for copy in copies.values():
        copy.start()

    @pl.when(is_end == 0)
    def _():
        for copy in middle:
            copy.wait()

    @pl.when(is_end != 0)
    def _():
        for copy in end:
            copy.wait()

    for copy in copies.values():
        copy.wait()
    prev.wait()
    for p in range(2):
        add_products(acc, xv, p, bv.at[p], offset_of, meta_ref[1])

    @pl.when(is_end == 0)
    def _():
        for p in range(2):
            add_products(acc, xv, p, bv.at[2 + p], offset_of, meta_ref[2])

    at = pl.multiple_of((meta_ref[4] + band // 2) * LANES, LANES)
    rest = pltpu.make_async_copy(acc.at[:, :, pl.ds(at, rest_ref.shape[2])], rest_ref, rest_sem)
    rest.start()
    give_pieces(out_refs, acc, meta_ref[3] + band // 2)
    rest.wait()


def half_products(meta, xs, prev, middle, end, second, n_done):
    rows = PARTS // 4 * xs[0].shape[0]
    panel, quarter = second.shape
    any_spec = pl.BlockSpec(memory_space=pl.ANY)
    x_spec = pl.BlockSpec(memory_space=pltpu.HBM)
    n_rest = quarter // LANES - n_done
    return pl.pallas_call(
        half_kernel,
        out_shape=[jax.ShapeDtypeStruct((rows, n_done * LANES), jnp.bfloat16)] * 4
        + [jax.ShapeDtypeStruct((2, 2 * rows, n_rest * LANES), jnp.float32)],
        in_specs=[pl.BlockSpec(memory_space=pltpu.SMEM)] + [x_spec] * PARTS + [any_spec] * 4,
        out_specs=[pl.BlockSpec(memory_space=pltpu.VMEM)] * 4 + [any_spec],
        scratch_shapes=[
            pltpu.VMEM((2, 2, 2 * rows, panel), jnp.bfloat16),
            pltpu.VMEM((4, panel, quarter // 2), jnp.bfloat16),
            pltpu.VMEM((2, 2 * rows, 2 * quarter), jnp.float32),
            pltpu.SemaphoreType.DMA((2, PARTS)),
            pltpu.SemaphoreType.DMA((4,)),
            pltpu.SemaphoreType.DMA,
            pltpu.SemaphoreType.DMA,
        ],
        compiler_params=pltpu.CompilerParams(vmem_limit_bytes=59 * MIB),
        cost_estimate=SMALL,
        name="half_products",
    )(meta, *xs, prev, middle, end, second)


def rest_kernel(meta_ref, *refs):
    x_refs, (rest_ref, b_ref), refs = refs[:PARTS], refs[PARTS : PARTS + 2], refs[PARTS + 2 :]
    out_refs, xv, bv, acc, x_sems, b_sem, rest_sem = refs[:4], *refs[4:]
    band = acc.shape[2] // (2 * LANES)
    half = bv.shape[1] // 2
    is_end = meta_ref[0]

    def offset_of(p, g):
        return meta_ref[3 + 2 * p + g]

    at = pl.multiple_of((meta_ref[2] + band // 2) * LANES, LANES)
    rest = pltpu.make_async_copy(rest_ref, acc.at[:, :, pl.ds(at, rest_ref.shape[2])], rest_sem)
    rest.start()
    copies = x_copies(x_refs, xv, x_sems, offset_of)
    b_copy = pltpu.make_async_copy(b_ref, bv, b_sem)

    @pl.when(is_end != 0)
    def _():
        b_copy.start()
        for copy in copies.values():
            copy.start()

    rest.wait()

    @pl.when(is_end != 0)
    def _():
        b_copy.wait()
        for copy in copies.values():
            copy.wait()
        for p in range(2):
            add_products(acc, xv, p, bv.at[:, p * half : (p + 1) * half], offset_of, meta_ref[1])

    give_pieces(out_refs, acc, meta_ref[2] + band // 2)


def rest_products(meta, xs, rest, b, quarter):
    rows = PARTS // 4 * xs[0].shape[0]
    panel = b.shape[0]
    width = rest.shape[2]
    any_spec = pl.BlockSpec(memory_space=pl.ANY)
    x_spec = pl.BlockSpec(memory_space=pltpu.HBM)
    return pl.pallas_call(
        rest_kernel,
        out_shape=[jax.ShapeDtypeStruct((rows, width), jnp.bfloat16)] * 4,
        in_specs=[pl.BlockSpec(memory_space=pltpu.SMEM)] + [x_spec] * PARTS + [any_spec] * 2,
        out_specs=[pl.BlockSpec(memory_space=pltpu.VMEM)] * 4,
        scratch_shapes=[
            pltpu.VMEM((2, 2, 2 * rows, panel), jnp.bfloat16),
            pltpu.VMEM(b.shape, jnp.bfloat16),
            pltpu.VMEM((2, 2 * rows, 2 * quarter), jnp.float32),
            pltpu.SemaphoreType.DMA((2, PARTS)),
            pltpu.SemaphoreType.DMA,
            pltpu.SemaphoreType.DMA,
        ],
        compiler_params=pltpu.CompilerParams(vmem_limit_bytes=59 * MIB),
        cost_estimate=SMALL,
        name="rest_products",
    )(meta, *xs, rest, b)


def assemble_kernel(place_ref, mask_ref, *refs):
    n = 4
    pieces, (out_ref, made, sem) = refs[:n], refs[-3:]
    steps = mask_ref.shape[0]
    rows = made.shape[0] // steps
    panel = n * LANES
    first = pl.multiple_of(place_ref[1] * panel, panel)
    for r in range(n):
        t = jnp.bitwise_xor(place_ref[0], r)
        for j in range(made.shape[1] // panel):
            to = pl.multiple_of(j * panel + t * LANES, LANES)
            for i in range(steps):
                keep = mask_ref[i, :, pl.ds(pl.multiple_of(first + to, LANES), LANES)]
                value = pieces[r][i * rows : (i + 1) * rows, j * LANES : (j + 1) * LANES].astype(jnp.float32)
                made[i * rows : (i + 1) * rows, pl.ds(to, LANES)] = (value * keep).astype(jnp.bfloat16)
    copy = pltpu.make_async_copy(made, out_ref.at[:, pl.ds(first, made.shape[1])], sem)
    copy.start()
    copy.wait()


def assembled(place, keep_wide, pieces, out=None):
    rows, width = pieces[0].shape
    cols = keep_wide.shape[2]
    vmem_spec = pl.BlockSpec(memory_space=pltpu.VMEM)
    any_spec = pl.BlockSpec(memory_space=pltpu.HBM)
    operands = [place, keep_wide, *pieces] + ([] if out is None else [out])
    return pl.pallas_call(
        assemble_kernel,
        out_shape=jax.ShapeDtypeStruct((rows, cols), jnp.bfloat16),
        in_specs=[pl.BlockSpec(memory_space=pltpu.SMEM)] + [vmem_spec] * 5 + [any_spec] * (len(operands) - 6),
        out_specs=any_spec,
        scratch_shapes=[pltpu.VMEM((rows, width * len(pieces)), jnp.bfloat16), pltpu.SemaphoreType.DMA],
        input_output_aliases={} if out is None else {6: 0},
        compiler_params=pltpu.CompilerParams(vmem_limit_bytes=16 * MIB),
        cost_estimate=SMALL,
        name="assembled",
    )(*operands)


def widen(mask, block):
    rows, cols = mask.shape
    wide = jnp.broadcast_to(mask.astype(jnp.float32)[:, :, None], (rows, cols, block))
    return wide.reshape(rows, 1, cols * block)


def together(*values):
    return lax.optimization_barrier(values)


def pairs_in_line(x_band, w_band, a_mask, keep_mask):
    panel = x_band.shape[0]
    block = panel // a_mask.shape[0]
    g, c = lax.axis_index("grid"), lax.axis_index("depth")
    z, y = g // 2, g % 2
    left = z < 2
    is_end = ((z == 0) | (z == 3)).astype(jnp.int32)
    toward = jnp.where(left, 1, -1)
    q = 2 * y + c

    swap = [(0, 2), (1, 3), (2, 0), (3, 1), (4, 6), (5, 7), (6, 4), (7, 5)]
    outward = [(2, 0), (3, 1), (4, 6), (5, 7)]
    cross = [(2, 4), (3, 5), (4, 2), (5, 3)]
    across = [(i, i ^ 1) for i in range(8)]
    layers = [(0, 1), (1, 0)]
    opposite = [(i, i ^ 3) for i in range(16)]

    def line(value, pairs):
        return lax.ppermute(value, "grid", pairs)

    def strips(value, start, count):
        return lax.dynamic_slice_in_dim(value, start * LANES, count * LANES, 1)

    first_out, second_out = jnp.where(left, 0, 4), jnp.where(left, 4, 0)
    first_in, second_in = second_out, first_out
    last_in = jnp.where(left, 1, 4)

    sent_b, own_a = b_strips(w_band, [q ^ 2, q])
    own_b = line(sent_b, across)
    swap_a = line(own_a, swap)
    cross_a = line(own_a, cross)
    mask_wide = widen(a_mask, block)
    rows = a_mask.shape[0]
    x_mine = [masked_rows(x_band, mask_wide, c * rows // 2 + k * rows // 4, rows // 4) for k in range(2)]
    own_b, swap_a, cross_a, *x_mine = together(own_b, swap_a, cross_a, *x_mine)
    swap_b = line(jnp.concatenate([own_b, cross_a[:, 5 * LANES :]], 1), swap)
    cross_b = line(own_b, cross)
    x_across = [line(part, across) for part in x_mine]
    x_rest = [masked_rows(x_band, mask_wide, (1 - c) * rows // 2 + k * rows // 4, rows // 4) for k in range(2)]

    cross_a, cross_b = together(cross_a, cross_b)
    mid_b = jnp.concatenate(
        [
            jnp.where(y == 0, cross_a[:, : 3 * LANES], cross_b[:, : 3 * LANES]),
            cross_a[:, 3 * LANES : 5 * LANES],
            cross_b[:, 3 * LANES :],
        ],
        1,
    )
    fwd_first = jnp.concatenate([strips(v, first_out, 4) for v in (swap_a, swap_b)], 1)
    fwd_second = jnp.concatenate([strips(v, second_out, 4) for v in (swap_a, swap_b)], 1)
    mid_b, fwd_first, fwd_second = together(mid_b, fwd_first, fwd_second)
    mid_b = line(mid_b, outward)
    fwd_first = line(fwd_first, cross)
    fwd_first, fwd_second, *x_across = together(fwd_first, fwd_second, *x_across)
    far_first = line(fwd_first, outward)
    fwd_second = line(fwd_second, cross)
    x_opposite = [lax.ppermute(part, "depth", layers) for part in x_across]
    xs = x_mine + x_rest + x_across + x_opposite

    def offsets(delta):
        tilt = 2 * y - 1
        return [(2 * delta + 4) % 8, (2 * delta + tilt + 4) % 8, (2 * delta - tilt + 4) % 8, (2 * delta + 4) % 8]

    zero = jnp.zeros_like(z)
    third = offsets(jnp.where(is_end == 1, 2, -toward))
    fourth = offsets(jnp.where(is_end == 1, -toward, 2))
    meta = jnp.stack([is_end, 4 + y, *offsets(zero), *offsets(toward), *third]).astype(jnp.int32)
    plan = [
        (0, [(0, 0, 8, 0, 0)]),
        (1, [(1, 0, 8, 0, 1)]),
        (2, [(4, 0, 8, 0, 2)]),
        (3, [(5, 0, 8, 0, 3)]),
        (4, [(5, 8, 3, 5, 4), (6, 0, 3, 0, None), (6, 3, 2, 3, 4)]),
        (5, [(6, 5, 5, 3, 5)]),
    ]
    total = whole_products(meta, xs, [own_a, own_b, cross_a, cross_b, swap_a, swap_b, mid_b], plan)
    last_at = jnp.where(left, 1, 0)
    total, last_at = together(total, last_at)
    last = jnp.concatenate(
        [strips(fwd_second, last_at, 3), strips(fwd_second, last_at + 4, 3)], 1
    )
    far_second = line(last, outward)

    def exchanged(pieces):
        return [
            pieces[0],
            lax.ppermute(pieces[1], "depth", layers),
            line(pieces[2], across),
            lax.ppermute(pieces[3], ("grid", "depth"), opposite),
        ]

    done_at, rest_at = jnp.where(left, 3, 0), jnp.where(left, 0, 5)
    meta = jnp.stack([is_end, first_in, second_in, done_at, rest_at, *fourth]).astype(jnp.int32)
    *done, rest = half_products(meta, xs, total, fwd_first, far_first, fwd_second, 5)
    done = exchanged(done)
    far_second, done[1] = together(far_second, done[1])
    keep_wide = widen(keep_mask, block)
    out = assembled(jnp.stack([q, done_at]).astype(jnp.int32), keep_wide, done)
    meta = jnp.stack([is_end, last_in, rest_at, *fourth]).astype(jnp.int32)
    rest = exchanged(rest_products(meta, xs, rest, far_second, own_a.shape[1]))
    return assembled(jnp.stack([q, rest_at]).astype(jnp.int32), keep_wide, rest, out)


def solution(mesh):
    placed = (
        P(("groups", "grid"), None),
        P(("groups", "grid"), None),
        P(("groups", "grid"), None),
        P(("groups", "grid", "depth"), None),
    )

    def local(x_band, w_band, a_mask, keep_mask):
        panel, cols = x_band.shape
        pairs = mesh.shape["grid"] == 8 and mesh.shape["depth"] == 2
        pairs = pairs and cols == 8 * panel and panel == 4 * LANES
        return (pairs_in_line if pairs else ring)(x_band, w_band, a_mask, keep_mask)

    return jax.shard_map(
        local,
        mesh=mesh,
        in_specs=placed,
        out_specs=P(("groups", "grid", "depth"), None),
        check_vma=False,
    )
```

```python
import functools

import jax
import jax.numpy as jnp
from jax import lax
from jax.experimental import pallas as pl
from jax.experimental.pallas import tpu as pltpu
from jax.sharding import PartitionSpec as P

LANES = 128
MIB = 1 << 20
SMALL = pl.CostEstimate(flops=1000, bytes_accessed=1000, transcendentals=0)


def shifted(shard, axis, by):
    count = lax.axis_size(axis)
    return lax.ppermute(shard, axis, [(i, (i + by) % count) for i in range(count)])


def expand_blocks(mask, block):
    rows, cols = mask.shape
    wide = jnp.broadcast_to(mask[:, None, :, None], (rows, block, cols, block))
    return wide.reshape(rows * block, cols * block)


def ring(x_band, w_band, a_mask, keep_mask):
    panel = x_band.shape[0]
    block = panel // a_mask.shape[0]
    band_cols = x_band.shape[1]
    xm = x_band * expand_blocks(a_mask, block).astype(jnp.bfloat16)
    rows = lax.broadcasted_iota(jnp.int32, x_band.shape, 0)
    cols = lax.broadcasted_iota(jnp.int32, x_band.shape, 1)
    identity = jnp.where(cols == rows + 4 * panel, 1.0, 0.0).astype(jnp.float32)
    b_panel = (1.5 * identity - 0.5 * w_band.astype(jnp.float32)).astype(jnp.bfloat16)
    layer = lax.axis_index("depth")
    current = shifted(b_panel, ("grid", "depth"), -5)
    wide = jnp.zeros((panel, 2 * band_cols), jnp.float32)
    for step in range(4):
        offset = 6 + layer - 2 * step
        ablock = lax.dynamic_slice_in_dim(xm, offset * panel, panel, 1)
        term = jnp.dot(ablock, current, preferred_element_type=jnp.float32)
        region = lax.dynamic_slice_in_dim(wide, offset * panel, band_cols, 1)
        wide = lax.dynamic_update_slice_in_dim(wide, region + term, offset * panel, 1)
        if step < 3:
            current = shifted(current, "grid", 2)
    partial_band = wide[:, 4 * panel : 12 * panel]
    mine = lax.psum_scatter(partial_band, "depth", scatter_dimension=0, tiled=True)
    keep = expand_blocks(keep_mask, block).astype(jnp.float32)
    return (mine * keep).astype(jnp.bfloat16)


def strips_kernel(quarters_ref, w_ref, *refs):
    *b_refs, held, sems = refs
    _, panel, width = held.shape
    band = width // LANES

    def copy(k, j):
        at = pl.multiple_of(j * panel + quarters_ref[k] * LANES, LANES)
        to = held.at[k, :, j * LANES : (j + 1) * LANES]
        return pltpu.make_async_copy(w_ref.at[:, pl.ds(at, LANES)], to, sems.at[k, j])

    for k in range(len(b_refs)):
        for j in range(band):
            copy(k, j).start()
    for k, b_ref in enumerate(b_refs):
        for j in range(band):
            copy(k, j).wait()
            value = -0.5 * held[k, :, j * LANES : (j + 1) * LANES].astype(jnp.float32)
            if j == band // 2:
                rows = lax.broadcasted_iota(jnp.int32, value.shape, 0)
                cols = lax.broadcasted_iota(jnp.int32, value.shape, 1)
                value = value + jnp.where(rows == cols + quarters_ref[k] * LANES, 1.5, 0.0)
            b_ref[:, j * LANES : (j + 1) * LANES] = value.astype(jnp.bfloat16)


def b_strips(w_band, quarters, limit):
    panel = w_band.shape[0]
    band = w_band.shape[1] // panel
    n = len(quarters)
    shape = (panel, band * LANES)
    return pl.pallas_call(
        strips_kernel,
        out_shape=[jax.ShapeDtypeStruct(shape, jnp.bfloat16)] * n,
        in_specs=[
            pl.BlockSpec(memory_space=pltpu.SMEM),
            pl.BlockSpec(memory_space=pltpu.HBM),
        ],
        out_specs=[pl.BlockSpec(memory_space=pltpu.VMEM)] * n,
        scratch_shapes=[pltpu.VMEM((n, *shape), jnp.bfloat16), pltpu.SemaphoreType.DMA((n, band))],
        compiler_params=pltpu.CompilerParams(vmem_limit_bytes=limit * MIB),
        cost_estimate=SMALL,
        name="b_strips",
    )(jnp.stack(quarters), w_band)


def mask_kernel(first_ref, mask_ref, x_ref, out_ref):
    out_ref[...] = (x_ref[...].astype(jnp.float32) * mask_ref[0]).astype(jnp.bfloat16)


def masked_rows(x_band, mask_wide, first, count):
    block = x_band.shape[0] // mask_wide.shape[0]
    cols = x_band.shape[1]
    return pl.pallas_call(
        mask_kernel,
        grid_spec=pltpu.PrefetchScalarGridSpec(
            num_scalar_prefetch=1,
            grid=(count,),
            in_specs=[
                pl.BlockSpec((1, 1, cols), lambda i, f: (f[0] + i, 0, 0)),
                pl.BlockSpec((block, cols), lambda i, f: (f[0] + i, 0)),
            ],
            out_specs=pl.BlockSpec((block, cols), lambda i, f: (i, 0)),
        ),
        out_shape=jax.ShapeDtypeStruct((count * block, cols), jnp.bfloat16),
        compiler_params=pltpu.CompilerParams(vmem_limit_bytes=58 * MIB),
        cost_estimate=SMALL,
        name="masked_rows",
    )(first.reshape(1), mask_wide, x_band)


PARTS = 8


def x_copies(x_refs, xv, sems, offset_of):
    n_b, _, rows, panel = xv.shape
    part = 2 * rows // PARTS
    copies = {}
    for p in range(n_b):
        for r in range(PARTS):
            g, k = divmod(r, PARTS // 2)
            at = pl.multiple_of(offset_of(p, g) * panel, panel)
            copies[p, r] = pltpu.make_async_copy(
                x_refs[r].at[:, pl.ds(at, panel)],
                xv.at[p, g, k * part : (k + 1) * part],
                sems.at[p, r],
            )
    return copies


def add_products(acc, xv, p, strips, offset_of, start):
    def step(g, carry):
        at = (offset_of(p, g) + start) * LANES
        cols = pl.ds(pl.multiple_of(at, LANES), strips.shape[1])
        acc[g, :, cols] += jnp.dot(xv[p, g], strips[...], preferred_element_type=jnp.float32)
        return carry

    lax.fori_loop(0, 2, step, 0)


def whole_kernel(plan, meta_ref, *refs):
    n_b = len(plan)
    x_refs, refs = refs[:PARTS], refs[PARTS:]
    b_refs, (out_ref, xv, bv, acc, x_sems, b_sems, out_sems) = refs[:-7], refs[-7:]
    quarter = bv.shape[2]
    low = quarter // 2
    is_end = meta_ref[0]

    def offset_of(p, g):
        return meta_ref[2 + 2 * p + g]

    def b_middle(p):
        return [pltpu.make_async_copy(b_refs[plan[p][0]].at[:, :quarter], bv.at[p], b_sems.at[p, 0])]

    def b_end(p):
        copies = []
        for k, (operand, first, count, at, to) in enumerate(plan[p][1]):
            to = meta_ref[1] if to is None else to
            source = b_refs[operand].at[:, first * LANES : (first + count) * LANES]
            copies.append(pltpu.make_async_copy(source, bv.at[to, :, at * LANES : (at + count) * LANES], b_sems.at[p, k]))
        return copies

    def on_each(p, do):
        @pl.when(is_end == 0)
        def _():
            for copy in b_middle(p):
                do(copy)

        @pl.when(is_end != 0)
        def _():
            for copy in b_end(p):
                do(copy)

    copies = x_copies(x_refs, xv, x_sems, offset_of)
    for p in range(n_b):
        on_each(p, lambda copy: copy.start())
        for r in range(PARTS):
            copies[p, r].start()
    acc[...] = jnp.zeros_like(acc)
    for p in range(n_b):
        for k in [p] if p < n_b - 2 else range(n_b - 2, n_b) if p == n_b - 2 else []:
            on_each(k, lambda copy: copy.wait())
        for r in range(PARTS):
            copies[p, r].wait()
        add_products(acc, xv, p, bv.at[p], offset_of, 0)
    outs = [
        pltpu.make_async_copy(acc.at[g, :, low : low + quarter], out_ref.at[g], out_sems.at[g]) for g in range(2)
    ]
    for out in outs:
        out.start()
    for out in outs:
        out.wait()


def whole_products(meta, xs, operands, plan):
    rows = PARTS // 4 * xs[0].shape[0]
    panel, quarter = operands[plan[0][0]].shape
    n_b = len(plan)
    any_spec = pl.BlockSpec(memory_space=pl.ANY)
    x_spec = pl.BlockSpec(memory_space=pltpu.HBM)
    return pl.pallas_call(
        functools.partial(whole_kernel, plan),
        out_shape=jax.ShapeDtypeStruct((2, 2 * rows, quarter), jnp.float32),
        in_specs=[pl.BlockSpec(memory_space=pltpu.SMEM)] + [x_spec] * PARTS + [any_spec] * len(operands),
        out_specs=any_spec,
        scratch_shapes=[
            pltpu.VMEM((n_b, 2, 2 * rows, panel), jnp.bfloat16),
            pltpu.VMEM((n_b, panel, quarter), jnp.bfloat16),
            pltpu.VMEM((2, 2 * rows, 2 * quarter), jnp.float32),
            pltpu.SemaphoreType.DMA((n_b, PARTS)),
            pltpu.SemaphoreType.DMA((n_b, 2)),
            pltpu.SemaphoreType.DMA((2,)),
        ],
        compiler_params=pltpu.CompilerParams(vmem_limit_bytes=59 * MIB),
        cost_estimate=SMALL,
        name="whole_products",
    )(meta, *xs, *operands)


def give_pieces(out_refs, acc, at):
    half, width = out_refs[0].shape
    cols = pl.ds(pl.multiple_of(at * LANES, LANES), width)
    for r in range(4):
        rows = slice((r % 2) * half, (r % 2 + 1) * half)
        out_refs[r][...] = acc[r // 2, rows, cols].astype(jnp.bfloat16)


def half_kernel(meta_ref, *refs):
    x_refs, (prev_ref, middle_ref, end_ref, second_ref), refs = refs[:PARTS], refs[PARTS : PARTS + 4], refs[PARTS + 4 :]
    out_refs, rest_ref, xv, bv, acc, x_sems, b_sems, prev_sem, rest_sem = refs[:4], *refs[4:]
    half = bv.shape[2]
    quarter = 2 * half
    low = quarter // 2
    band = quarter // LANES
    is_end = meta_ref[0]

    def offset_of(p, g):
        return meta_ref[5 + 2 * p + g]

    copies = x_copies(x_refs, xv, x_sems, offset_of)

    def b_copies(ref, first):
        return [
            pltpu.make_async_copy(ref.at[:, p * half : (p + 1) * half], bv.at[first + p], b_sems.at[first + p])
            for p in range(2)
        ]

    middle = b_copies(middle_ref, 0) + b_copies(second_ref, 2)
    end = b_copies(end_ref, 0)
    prev = pltpu.make_async_copy(prev_ref, acc.at[:, :, low : low + quarter], prev_sem)
    prev.start()

    @pl.when(is_end == 0)
    def _():
        for copy in middle:
            copy.start()

    @pl.when(is_end != 0)
    def _():
        for copy in end:
            copy.start()

    for copy in copies.values():
        copy.start()

    @pl.when(is_end == 0)
    def _():
        for copy in middle:
            copy.wait()

    @pl.when(is_end != 0)
    def _():
        for copy in end:
            copy.wait()

    for copy in copies.values():
        copy.wait()
    prev.wait()
    for p in range(2):
        add_products(acc, xv, p, bv.at[p], offset_of, meta_ref[1])

    @pl.when(is_end == 0)
    def _():
        for p in range(2):
            add_products(acc, xv, p, bv.at[2 + p], offset_of, meta_ref[2])

    at = pl.multiple_of((meta_ref[4] + band // 2) * LANES, LANES)
    rest = pltpu.make_async_copy(acc.at[:, :, pl.ds(at, rest_ref.shape[2])], rest_ref, rest_sem)
    rest.start()
    give_pieces(out_refs, acc, meta_ref[3] + band // 2)
    rest.wait()


def half_products(meta, xs, prev, middle, end, second, n_done):
    rows = PARTS // 4 * xs[0].shape[0]
    panel, quarter = second.shape
    any_spec = pl.BlockSpec(memory_space=pl.ANY)
    x_spec = pl.BlockSpec(memory_space=pltpu.HBM)
    n_rest = quarter // LANES - n_done
    return pl.pallas_call(
        half_kernel,
        out_shape=[jax.ShapeDtypeStruct((rows, n_done * LANES), jnp.bfloat16)] * 4
        + [jax.ShapeDtypeStruct((2, 2 * rows, n_rest * LANES), jnp.float32)],
        in_specs=[pl.BlockSpec(memory_space=pltpu.SMEM)] + [x_spec] * PARTS + [any_spec] * 4,
        out_specs=[pl.BlockSpec(memory_space=pltpu.VMEM)] * 4 + [any_spec],
        scratch_shapes=[
            pltpu.VMEM((2, 2, 2 * rows, panel), jnp.bfloat16),
            pltpu.VMEM((4, panel, quarter // 2), jnp.bfloat16),
            pltpu.VMEM((2, 2 * rows, 2 * quarter), jnp.float32),
            pltpu.SemaphoreType.DMA((2, PARTS)),
            pltpu.SemaphoreType.DMA((4,)),
            pltpu.SemaphoreType.DMA,
            pltpu.SemaphoreType.DMA,
        ],
        compiler_params=pltpu.CompilerParams(vmem_limit_bytes=59 * MIB),
        cost_estimate=SMALL,
        name="half_products",
    )(meta, *xs, prev, middle, end, second)


def rest_kernel(meta_ref, *refs):
    x_refs, (rest_ref, b_ref), refs = refs[:PARTS], refs[PARTS : PARTS + 2], refs[PARTS + 2 :]
    out_refs, xv, bv, acc, x_sems, b_sem, rest_sem = refs[:4], *refs[4:]
    band = acc.shape[2] // (2 * LANES)
    half = bv.shape[1] // 2
    is_end = meta_ref[0]

    def offset_of(p, g):
        return meta_ref[3 + 2 * p + g]

    at = pl.multiple_of((meta_ref[2] + band // 2) * LANES, LANES)
    rest = pltpu.make_async_copy(rest_ref, acc.at[:, :, pl.ds(at, rest_ref.shape[2])], rest_sem)
    rest.start()
    copies = x_copies(x_refs, xv, x_sems, offset_of)
    b_copy = pltpu.make_async_copy(b_ref, bv, b_sem)

    @pl.when(is_end != 0)
    def _():
        b_copy.start()
        for copy in copies.values():
            copy.start()

    rest.wait()

    @pl.when(is_end != 0)
    def _():
        b_copy.wait()
        for copy in copies.values():
            copy.wait()
        for p in range(2):
            add_products(acc, xv, p, bv.at[:, p * half : (p + 1) * half], offset_of, meta_ref[1])

    give_pieces(out_refs, acc, meta_ref[2] + band // 2)


def rest_products(meta, xs, rest, b, quarter):
    rows = PARTS // 4 * xs[0].shape[0]
    panel = b.shape[0]
    width = rest.shape[2]
    any_spec = pl.BlockSpec(memory_space=pl.ANY)
    x_spec = pl.BlockSpec(memory_space=pltpu.HBM)
    return pl.pallas_call(
        rest_kernel,
        out_shape=[jax.ShapeDtypeStruct((rows, width), jnp.bfloat16)] * 4,
        in_specs=[pl.BlockSpec(memory_space=pltpu.SMEM)] + [x_spec] * PARTS + [any_spec] * 2,
        out_specs=[pl.BlockSpec(memory_space=pltpu.VMEM)] * 4,
        scratch_shapes=[
            pltpu.VMEM((2, 2, 2 * rows, panel), jnp.bfloat16),
            pltpu.VMEM(b.shape, jnp.bfloat16),
            pltpu.VMEM((2, 2 * rows, 2 * quarter), jnp.float32),
            pltpu.SemaphoreType.DMA((2, PARTS)),
            pltpu.SemaphoreType.DMA,
            pltpu.SemaphoreType.DMA,
        ],
        compiler_params=pltpu.CompilerParams(vmem_limit_bytes=59 * MIB),
        cost_estimate=SMALL,
        name="rest_products",
    )(meta, *xs, rest, b)


def assemble_kernel(place_ref, mask_ref, *refs):
    n = 4
    pieces, (out_ref, made, sem) = refs[:n], refs[-3:]
    steps = mask_ref.shape[0]
    rows = made.shape[0] // steps
    panel = n * LANES
    first = pl.multiple_of(place_ref[1] * panel, panel)
    for r in range(n):
        t = jnp.bitwise_xor(place_ref[0], r)
        for j in range(made.shape[1] // panel):
            to = pl.multiple_of(j * panel + t * LANES, LANES)
            for i in range(steps):
                keep = mask_ref[i, :, pl.ds(pl.multiple_of(first + to, LANES), LANES)]
                value = pieces[r][i * rows : (i + 1) * rows, j * LANES : (j + 1) * LANES].astype(jnp.float32)
                made[i * rows : (i + 1) * rows, pl.ds(to, LANES)] = (value * keep).astype(jnp.bfloat16)
    copy = pltpu.make_async_copy(made, out_ref.at[:, pl.ds(first, made.shape[1])], sem)
    copy.start()
    copy.wait()


def assembled(place, keep_wide, pieces, out=None):
    rows, width = pieces[0].shape
    cols = keep_wide.shape[2]
    vmem_spec = pl.BlockSpec(memory_space=pltpu.VMEM)
    any_spec = pl.BlockSpec(memory_space=pltpu.HBM)
    operands = [place, keep_wide, *pieces] + ([] if out is None else [out])
    return pl.pallas_call(
        assemble_kernel,
        out_shape=jax.ShapeDtypeStruct((rows, cols), jnp.bfloat16),
        in_specs=[pl.BlockSpec(memory_space=pltpu.SMEM)] + [vmem_spec] * 5 + [any_spec] * (len(operands) - 6),
        out_specs=any_spec,
        scratch_shapes=[pltpu.VMEM((rows, width * len(pieces)), jnp.bfloat16), pltpu.SemaphoreType.DMA],
        input_output_aliases={} if out is None else {6: 0},
        compiler_params=pltpu.CompilerParams(vmem_limit_bytes=16 * MIB),
        cost_estimate=SMALL,
        name="assembled",
    )(*operands)


def widen(mask, block):
    rows, cols = mask.shape
    wide = jnp.broadcast_to(mask.astype(jnp.float32)[:, :, None], (rows, cols, block))
    return wide.reshape(rows, 1, cols * block)


def together(*values):
    return lax.optimization_barrier(values)


def pairs_in_line(x_band, w_band, a_mask, keep_mask):
    panel = x_band.shape[0]
    block = panel // a_mask.shape[0]
    g, c = lax.axis_index("grid"), lax.axis_index("depth")
    z, y = g // 2, g % 2
    left = z < 2
    is_end = ((z == 0) | (z == 3)).astype(jnp.int32)
    toward = jnp.where(left, 1, -1)
    q = 2 * y + c

    swap = [(0, 2), (1, 3), (2, 0), (3, 1), (4, 6), (5, 7), (6, 4), (7, 5)]
    outward = [(2, 0), (3, 1), (4, 6), (5, 7)]
    cross = [(2, 4), (3, 5), (4, 2), (5, 3)]
    across = [(i, i ^ 1) for i in range(8)]
    layers = [(0, 1), (1, 0)]
    opposite = [(i, i ^ 3) for i in range(16)]

    def line(value, pairs):
        return lax.ppermute(value, "grid", pairs)

    def strips(value, start, count):
        return lax.dynamic_slice_in_dim(value, start * LANES, count * LANES, 1)

    first_out, second_out = jnp.where(left, 0, 4), jnp.where(left, 4, 0)
    first_in, second_in = second_out, first_out
    last_in = jnp.where(left, 1, 4)

    (sent_b,) = b_strips(w_band, [q ^ 2], 58)
    own_b = line(sent_b, across)
    sent_b, w_band = together(sent_b, w_band)
    (own_a,) = b_strips(w_band, [q], 48)
    swap_a = line(own_a, swap)
    cross_a = line(own_a, cross)
    mask_wide = widen(a_mask, block)
    rows = a_mask.shape[0]
    x_mine = [masked_rows(x_band, mask_wide, c * rows // 2 + k * rows // 4, rows // 4) for k in range(2)]
    own_b, *x_mine = together(own_b, *x_mine)
    own_b, swap_a = together(own_b, swap_a)
    own_b, cross_a = together(own_b, cross_a)
    swap_b = line(own_b, swap)
    cross_b = line(own_b, cross)
    x_across = [line(part, across) for part in x_mine]
    x_rest = [masked_rows(x_band, mask_wide, (1 - c) * rows // 2 + k * rows // 4, rows // 4) for k in range(2)]

    cross_a, cross_b = together(cross_a, cross_b)
    mid_b = jnp.concatenate(
        [
            jnp.where(y == 0, cross_a[:, : 3 * LANES], cross_b[:, : 3 * LANES]),
            cross_a[:, 3 * LANES :],
            cross_b[:, 3 * LANES :],
        ],
        1,
    )
    fwd_first = jnp.concatenate([strips(v, first_out, 4) for v in (swap_a, swap_b)], 1)
    fwd_second = jnp.concatenate([strips(v, second_out, 4) for v in (swap_a, swap_b)], 1)
    fwd_first, fwd_second = together(fwd_first, fwd_second)
    mid_b, fwd_first, fwd_second = together(mid_b, fwd_first, fwd_second)
    mid_b = line(mid_b, outward)
    fwd_first = line(fwd_first, cross)
    fwd_first, fwd_second, *x_across = together(fwd_first, fwd_second, *x_across)
    far_first = line(fwd_first, outward)
    fwd_second = line(fwd_second, cross)
    x_opposite = [lax.ppermute(part, "depth", layers) for part in x_across]
    xs = x_mine + x_rest + x_across + x_opposite

    def offsets(delta):
        tilt = 2 * y - 1
        return [(2 * delta + 4) % 8, (2 * delta + tilt + 4) % 8, (2 * delta - tilt + 4) % 8, (2 * delta + 4) % 8]

    zero = jnp.zeros_like(z)
    third = offsets(jnp.where(is_end == 1, 2, -toward))
    fourth = offsets(jnp.where(is_end == 1, -toward, 2))
    meta = jnp.stack([is_end, 4 + y, *offsets(zero), *offsets(toward), *third]).astype(jnp.int32)
    plan = [
        (0, [(0, 0, 8, 0, 0)]),
        (1, [(1, 0, 8, 0, 1)]),
        (2, [(4, 0, 8, 0, 2)]),
        (3, [(5, 0, 8, 0, 3)]),
        (4, [(6, 0, 3, 0, None), (6, 3, 5, 3, 4)]),
        (5, [(6, 8, 5, 3, 5)]),
    ]
    total = whole_products(meta, xs, [own_a, own_b, cross_a, cross_b, swap_a, swap_b, mid_b], plan)
    last_at = jnp.where(left, 1, 0)
    total, last_at = together(total, last_at)
    last = jnp.concatenate(
        [strips(fwd_second, last_at, 3), strips(fwd_second, last_at + 4, 3)], 1
    )
    far_second = line(last, outward)

    def exchanged(pieces):
        return [
            pieces[0],
            lax.ppermute(pieces[1], "depth", layers),
            line(pieces[2], across),
            lax.ppermute(pieces[3], ("grid", "depth"), opposite),
        ]

    done_at, rest_at = jnp.where(left, 3, 0), jnp.where(left, 0, 5)
    meta = jnp.stack([is_end, first_in, second_in, done_at, rest_at, *fourth]).astype(jnp.int32)
    *done, rest = half_products(meta, xs, total, fwd_first, far_first, fwd_second, 5)
    done = exchanged(done)
    far_second, done[1] = together(far_second, done[1])
    keep_wide = widen(keep_mask, block)
    out = assembled(jnp.stack([q, done_at]).astype(jnp.int32), keep_wide, done)
    meta = jnp.stack([is_end, last_in, rest_at, *fourth]).astype(jnp.int32)
    rest = exchanged(rest_products(meta, xs, rest, far_second, own_a.shape[1]))
    return assembled(jnp.stack([q, rest_at]).astype(jnp.int32), keep_wide, rest, out)


def solution(mesh):
    placed = (
        P(("groups", "grid"), None),
        P(("groups", "grid"), None),
        P(("groups", "grid"), None),
        P(("groups", "grid", "depth"), None),
    )

    def local(x_band, w_band, a_mask, keep_mask):
        panel, cols = x_band.shape
        pairs = mesh.shape["grid"] == 8 and mesh.shape["depth"] == 2
        pairs = pairs and cols == 8 * panel and panel == 4 * LANES
        return (pairs_in_line if pairs else ring)(x_band, w_band, a_mask, keep_mask)

    return jax.shard_map(
        local,
        mesh=mesh,
        in_specs=placed,
        out_specs=P(("groups", "grid", "depth"), None),
        check_vma=False,
    )
```

```python
import functools

import jax
import jax.numpy as jnp
from jax import lax
from jax.experimental import pallas as pl
from jax.experimental.pallas import tpu as pltpu
from jax.sharding import PartitionSpec as P

LANES = 128
MIB = 1 << 20
SMALL = pl.CostEstimate(flops=1000, bytes_accessed=1000, transcendentals=0)


def shifted(shard, axis, by):
    count = lax.axis_size(axis)
    return lax.ppermute(shard, axis, [(i, (i + by) % count) for i in range(count)])


def expand_blocks(mask, block):
    rows, cols = mask.shape
    wide = jnp.broadcast_to(mask[:, None, :, None], (rows, block, cols, block))
    return wide.reshape(rows * block, cols * block)


def ring(x_band, w_band, a_mask, keep_mask):
    panel = x_band.shape[0]
    block = panel // a_mask.shape[0]
    band_cols = x_band.shape[1]
    xm = x_band * expand_blocks(a_mask, block).astype(jnp.bfloat16)
    rows = lax.broadcasted_iota(jnp.int32, x_band.shape, 0)
    cols = lax.broadcasted_iota(jnp.int32, x_band.shape, 1)
    identity = jnp.where(cols == rows + 4 * panel, 1.0, 0.0).astype(jnp.float32)
    b_panel = (1.5 * identity - 0.5 * w_band.astype(jnp.float32)).astype(jnp.bfloat16)
    layer = lax.axis_index("depth")
    current = shifted(b_panel, ("grid", "depth"), -5)
    wide = jnp.zeros((panel, 2 * band_cols), jnp.float32)
    for step in range(4):
        offset = 6 + layer - 2 * step
        ablock = lax.dynamic_slice_in_dim(xm, offset * panel, panel, 1)
        term = jnp.dot(ablock, current, preferred_element_type=jnp.float32)
        region = lax.dynamic_slice_in_dim(wide, offset * panel, band_cols, 1)
        wide = lax.dynamic_update_slice_in_dim(wide, region + term, offset * panel, 1)
        if step < 3:
            current = shifted(current, "grid", 2)
    partial_band = wide[:, 4 * panel : 12 * panel]
    mine = lax.psum_scatter(partial_band, "depth", scatter_dimension=0, tiled=True)
    keep = expand_blocks(keep_mask, block).astype(jnp.float32)
    return (mine * keep).astype(jnp.bfloat16)


def strips_kernel(quarters_ref, w_ref, *refs):
    *b_refs, held, sems = refs
    _, panel, width = held.shape
    band = width // LANES

    def copy(k, j):
        at = pl.multiple_of(j * panel + quarters_ref[k] * LANES, LANES)
        to = held.at[k, :, j * LANES : (j + 1) * LANES]
        return pltpu.make_async_copy(w_ref.at[:, pl.ds(at, LANES)], to, sems.at[k, j])

    for k in range(len(b_refs)):
        for j in range(band):
            copy(k, j).start()
    for k, b_ref in enumerate(b_refs):
        for j in range(band):
            copy(k, j).wait()
            value = -0.5 * held[k, :, j * LANES : (j + 1) * LANES].astype(jnp.float32)
            if j == band // 2:
                rows = lax.broadcasted_iota(jnp.int32, value.shape, 0)
                cols = lax.broadcasted_iota(jnp.int32, value.shape, 1)
                value = value + jnp.where(rows == cols + quarters_ref[k] * LANES, 1.5, 0.0)
            b_ref[:, j * LANES : (j + 1) * LANES] = value.astype(jnp.bfloat16)


def b_strips(w_band, quarters, limit):
    panel = w_band.shape[0]
    band = w_band.shape[1] // panel
    n = len(quarters)
    shape = (panel, band * LANES)
    return pl.pallas_call(
        strips_kernel,
        out_shape=[jax.ShapeDtypeStruct(shape, jnp.bfloat16)] * n,
        in_specs=[
            pl.BlockSpec(memory_space=pltpu.SMEM),
            pl.BlockSpec(memory_space=pltpu.HBM),
        ],
        out_specs=[pl.BlockSpec(memory_space=pltpu.VMEM)] * n,
        scratch_shapes=[pltpu.VMEM((n, *shape), jnp.bfloat16), pltpu.SemaphoreType.DMA((n, band))],
        compiler_params=pltpu.CompilerParams(vmem_limit_bytes=limit * MIB),
        cost_estimate=SMALL,
        name="b_strips",
    )(jnp.stack(quarters), w_band)


def pack_kernel(plan, n_in, meta_ref, *refs):
    sources, outs, sems = refs[:n_in], refs[n_in:-1], refs[-1]

    def on_each(do):
        for k, (source, start, count, out, to, when) in enumerate(plan):
            at = start * LANES if isinstance(start, int) else pl.multiple_of(meta_ref[start[0]] * LANES, LANES)
            copy = pltpu.make_async_copy(
                sources[source].at[:, pl.ds(at, count * LANES)],
                outs[out].at[:, to * LANES : (to + count) * LANES],
                sems.at[k],
            )
            if when is None:
                do(copy)
            else:
                pl.when(meta_ref[when[0]] == when[1])(functools.partial(do, copy))

    on_each(lambda copy: copy.start())
    on_each(lambda copy: copy.wait())


def packed(meta, sources, widths, plan):
    rows = sources[0].shape[0]
    any_spec = pl.BlockSpec(memory_space=pl.ANY)
    return pl.pallas_call(
        functools.partial(pack_kernel, plan, len(sources)),
        out_shape=[jax.ShapeDtypeStruct((rows, width * LANES), jnp.bfloat16) for width in widths],
        in_specs=[pl.BlockSpec(memory_space=pltpu.SMEM)] + [any_spec] * len(sources),
        out_specs=[any_spec] * len(widths),
        scratch_shapes=[pltpu.SemaphoreType.DMA((len(plan),))],
        compiler_params=pltpu.CompilerParams(vmem_limit_bytes=59 * MIB),
        cost_estimate=SMALL,
        name="packed",
    )(jnp.stack(meta).astype(jnp.int32), *sources)


def mask_kernel(first_ref, mask_ref, x_ref, out_ref):
    out_ref[...] = (x_ref[...].astype(jnp.float32) * mask_ref[0]).astype(jnp.bfloat16)


def masked_rows(x_band, mask_wide, first, count):
    block = x_band.shape[0] // mask_wide.shape[0]
    cols = x_band.shape[1]
    return pl.pallas_call(
        mask_kernel,
        grid_spec=pltpu.PrefetchScalarGridSpec(
            num_scalar_prefetch=1,
            grid=(count,),
            in_specs=[
                pl.BlockSpec((1, 1, cols), lambda i, f: (f[0] + i, 0, 0)),
                pl.BlockSpec((block, cols), lambda i, f: (f[0] + i, 0)),
            ],
            out_specs=pl.BlockSpec((block, cols), lambda i, f: (i, 0)),
        ),
        out_shape=jax.ShapeDtypeStruct((count * block, cols), jnp.bfloat16),
        compiler_params=pltpu.CompilerParams(vmem_limit_bytes=58 * MIB),
        cost_estimate=SMALL,
        name="masked_rows",
    )(first.reshape(1), mask_wide, x_band)


PARTS = 8


def x_copies(x_refs, xv, sems, offset_of):
    n_b, _, rows, panel = xv.shape
    part = 2 * rows // PARTS
    copies = {}
    for p in range(n_b):
        for r in range(PARTS):
            g, k = divmod(r, PARTS // 2)
            at = pl.multiple_of(offset_of(p, g) * panel, panel)
            copies[p, r] = pltpu.make_async_copy(
                x_refs[r].at[:, pl.ds(at, panel)],
                xv.at[p, g, k * part : (k + 1) * part],
                sems.at[p, r],
            )
    return copies


def add_product(acc, x, strips, g, first):
    cols = pl.ds(pl.multiple_of(first * LANES, LANES), strips.shape[1])
    acc[g, :, cols] += jnp.dot(x, strips, preferred_element_type=jnp.float32)


def whole_kernel(plan, meta_ref, *refs):
    n_b = len(plan)
    x_refs, refs = refs[:PARTS], refs[PARTS:]
    b_refs, (out_ref, xv, bv, acc, x_sems, b_sems, out_sems) = refs[:-7], refs[-7:]
    quarter = bv.shape[2]
    low = quarter // 2
    is_end = meta_ref[0]

    def offset_of(p, g):
        return meta_ref[2 + 2 * p + g]

    def b_middle(p):
        return [pltpu.make_async_copy(b_refs[plan[p][0]].at[:, :quarter], bv.at[p], b_sems.at[p, 0])]

    def b_end(p):
        copies = []
        for k, (operand, first, count, at, to) in enumerate(plan[p][1]):
            to = meta_ref[1] if to is None else to
            source = b_refs[operand].at[:, first * LANES : (first + count) * LANES]
            copies.append(pltpu.make_async_copy(source, bv.at[to, :, at * LANES : (at + count) * LANES], b_sems.at[p, k]))
        return copies

    def on_each(p, do):
        @pl.when(is_end == 0)
        def _():
            for copy in b_middle(p):
                do(copy)

        @pl.when(is_end != 0)
        def _():
            for copy in b_end(p):
                do(copy)

    copies = x_copies(x_refs, xv, x_sems, offset_of)
    for p in range(n_b):
        on_each(p, lambda copy: copy.start())
        for r in range(PARTS):
            copies[p, r].start()
    acc[...] = jnp.zeros_like(acc)
    for p in range(n_b):
        for k in [p] if p < n_b - 2 else range(n_b - 2, n_b) if p == n_b - 2 else []:
            on_each(k, lambda copy: copy.wait())
        for r in range(PARTS):
            copies[p, r].wait()

        def step(g, carry):
            add_product(acc, xv[p, g], bv[p], g, offset_of(p, g))
            return carry

        lax.fori_loop(0, 2, step, 0)
    outs = [
        pltpu.make_async_copy(acc.at[g, :, low : low + quarter], out_ref.at[g], out_sems.at[g]) for g in range(2)
    ]
    for out in outs:
        out.start()
    for out in outs:
        out.wait()


def whole_products(meta, xs, operands, plan):
    rows = PARTS // 4 * xs[0].shape[0]
    panel, quarter = operands[plan[0][0]].shape
    n_b = len(plan)
    any_spec = pl.BlockSpec(memory_space=pl.ANY)
    x_spec = pl.BlockSpec(memory_space=pltpu.HBM)
    return pl.pallas_call(
        functools.partial(whole_kernel, plan),
        out_shape=jax.ShapeDtypeStruct((2, 2 * rows, quarter), jnp.float32),
        in_specs=[pl.BlockSpec(memory_space=pltpu.SMEM)] + [x_spec] * PARTS + [any_spec] * len(operands),
        out_specs=any_spec,
        scratch_shapes=[
            pltpu.VMEM((n_b, 2, 2 * rows, panel), jnp.bfloat16),
            pltpu.VMEM((n_b, panel, quarter), jnp.bfloat16),
            pltpu.VMEM((2, 2 * rows, 2 * quarter), jnp.float32),
            pltpu.SemaphoreType.DMA((n_b, PARTS)),
            pltpu.SemaphoreType.DMA((n_b, 2)),
            pltpu.SemaphoreType.DMA((2,)),
        ],
        compiler_params=pltpu.CompilerParams(vmem_limit_bytes=59 * MIB),
        cost_estimate=SMALL,
        name="whole_products",
    )(meta, *xs, *operands)


def finish(acc, wait_for, add, at, out_refs, pieces, sems, also=None):
    half, width = out_refs[0].shape
    cols = pl.ds(pl.multiple_of(at * LANES, LANES), width)
    outs = [pltpu.make_async_copy(pieces.at[r], out_refs[r], sems.at[r]) for r in range(4)]
    also = also or []

    def step(g, carry):
        for k in range(2):
            pl.when(g == k)(functools.partial(wait_for, k))
        add(g)
        for k in range(2):

            @pl.when(g == k)
            def _():
                for copy in also[k : k + 1]:
                    copy.start()
                for r in range(2 * k, 2 * k + 2):
                    rows = slice((r % 2) * half, (r % 2 + 1) * half)
                    pieces[r] = acc[k, rows, cols].astype(jnp.bfloat16)
                    outs[r].start()

        return carry

    lax.fori_loop(0, 2, step, 0)
    for copy in outs + also:
        copy.wait()


def half_kernel(meta_ref, *refs):
    x_refs, (prev_ref, middle_ref, end_ref, second_ref), refs = refs[:PARTS], refs[PARTS : PARTS + 4], refs[PARTS + 4 :]
    out_refs, rest_ref, xv, bv, acc, pieces, x_sems, b_sems, prev_sems, rest_sems, out_sems = refs[:4], *refs[4:]
    quarter = bv.shape[2]
    half = quarter // 2
    low = quarter // 2
    band = quarter // LANES
    is_end = meta_ref[0]

    def offset_of(p, g):
        return meta_ref[5 + 2 * p + g]

    x_loads = x_copies(x_refs, xv, x_sems, offset_of)
    middle = pltpu.make_async_copy(middle_ref, bv.at[0], b_sems.at[0])
    end = pltpu.make_async_copy(end_ref, bv.at[0], b_sems.at[0])
    second = pltpu.make_async_copy(second_ref, bv.at[1], b_sems.at[1])
    prev = [
        pltpu.make_async_copy(prev_ref.at[g], acc.at[g, :, low : low + quarter], prev_sems.at[g]) for g in range(2)
    ]
    at = pl.multiple_of((meta_ref[4] + band // 2) * LANES, LANES)
    rest = [
        pltpu.make_async_copy(acc.at[g, :, pl.ds(at, rest_ref.shape[2])], rest_ref.at[g], rest_sems.at[g])
        for g in range(2)
    ]

    @pl.when(is_end == 0)
    def _():
        middle.start()
        second.start()

    pl.when(is_end != 0)(end.start)

    def rows_loads(g):
        return [prev[g]] + [copy for (_, r), copy in x_loads.items() if r // (PARTS // 2) == g]

    for g in range(2):
        for copy in rows_loads(g):
            copy.start()

    def wait_for(g):
        for copy in rows_loads(g):
            copy.wait()
        if g == 0:

            @pl.when(is_end == 0)
            def _():
                middle.wait()
                second.wait()

            pl.when(is_end != 0)(end.wait)

    def add(g):
        for p in range(2):
            add_product(acc, xv[p, g], bv[0, :, p * half : (p + 1) * half], g, offset_of(p, g) + meta_ref[1])

        @pl.when(is_end == 0)
        def _():
            for p in range(2):
                add_product(acc, xv[p, g], bv[1, :, p * half : (p + 1) * half], g, offset_of(p, g) + meta_ref[2])

    finish(acc, wait_for, add, meta_ref[3] + band // 2, out_refs, pieces, out_sems, rest)


def half_products(meta, xs, prev, middle, end, second, n_done):
    rows = PARTS // 4 * xs[0].shape[0]
    panel, quarter = second.shape
    any_spec = pl.BlockSpec(memory_space=pl.ANY)
    x_spec = pl.BlockSpec(memory_space=pltpu.HBM)
    n_rest = quarter // LANES - n_done
    return pl.pallas_call(
        half_kernel,
        out_shape=[jax.ShapeDtypeStruct((rows, n_done * LANES), jnp.bfloat16)] * 4
        + [jax.ShapeDtypeStruct((2, 2 * rows, n_rest * LANES), jnp.float32)],
        in_specs=[pl.BlockSpec(memory_space=pltpu.SMEM)] + [x_spec] * PARTS + [any_spec] * 4,
        out_specs=[any_spec] * 5,
        scratch_shapes=[
            pltpu.VMEM((2, 2, 2 * rows, panel), jnp.bfloat16),
            pltpu.VMEM((2, panel, quarter), jnp.bfloat16),
            pltpu.VMEM((2, 2 * rows, 2 * quarter), jnp.float32),
            pltpu.VMEM((4, rows, n_done * LANES), jnp.bfloat16),
            pltpu.SemaphoreType.DMA((2, PARTS)),
            pltpu.SemaphoreType.DMA((2,)),
            pltpu.SemaphoreType.DMA((2,)),
            pltpu.SemaphoreType.DMA((2,)),
            pltpu.SemaphoreType.DMA((4,)),
        ],
        compiler_params=pltpu.CompilerParams(vmem_limit_bytes=59 * MIB),
        cost_estimate=SMALL,
        name="half_products",
    )(meta, *xs, prev, middle, end, second)


def rest_kernel(meta_ref, *refs):
    x_refs, (rest_ref, b_ref), refs = refs[:PARTS], refs[PARTS : PARTS + 2], refs[PARTS + 2 :]
    out_refs, xv, bv, acc, pieces, x_sems, b_sem, rest_sems, out_sems = refs[:4], *refs[4:]
    band = acc.shape[2] // (2 * LANES)
    half = bv.shape[1] // 2
    is_end = meta_ref[0]

    def offset_of(p, g):
        return meta_ref[3 + 2 * p + g]

    at = pl.multiple_of((meta_ref[2] + band // 2) * LANES, LANES)
    rest = [
        pltpu.make_async_copy(rest_ref.at[g], acc.at[g, :, pl.ds(at, rest_ref.shape[2])], rest_sems.at[g])
        for g in range(2)
    ]
    x_loads = x_copies(x_refs, xv, x_sems, offset_of)
    b_copy = pltpu.make_async_copy(b_ref, bv, b_sem)

    def x_loads_of(g):
        return [copy for (_, r), copy in x_loads.items() if r // (PARTS // 2) == g]

    pl.when(is_end != 0)(b_copy.start)
    for g in range(2):
        rest[g].start()

        @pl.when(is_end != 0)
        def _():
            for copy in x_loads_of(g):
                copy.start()

    def wait_for(g):
        rest[g].wait()

        @pl.when(is_end != 0)
        def _():
            for copy in x_loads_of(g):
                copy.wait()
            if g == 0:
                b_copy.wait()

    def add(g):
        @pl.when(is_end != 0)
        def _():
            for p in range(2):
                add_product(acc, xv[p, g], bv[:, p * half : (p + 1) * half], g, offset_of(p, g) + meta_ref[1])

    finish(acc, wait_for, add, meta_ref[2] + band // 2, out_refs, pieces, out_sems)


def rest_products(meta, xs, rest, b, quarter):
    rows = PARTS // 4 * xs[0].shape[0]
    panel = b.shape[0]
    width = rest.shape[2]
    any_spec = pl.BlockSpec(memory_space=pl.ANY)
    x_spec = pl.BlockSpec(memory_space=pltpu.HBM)
    return pl.pallas_call(
        rest_kernel,
        out_shape=[jax.ShapeDtypeStruct((rows, width), jnp.bfloat16)] * 4,
        in_specs=[pl.BlockSpec(memory_space=pltpu.SMEM)] + [x_spec] * PARTS + [any_spec] * 2,
        out_specs=[any_spec] * 4,
        scratch_shapes=[
            pltpu.VMEM((2, 2, 2 * rows, panel), jnp.bfloat16),
            pltpu.VMEM(b.shape, jnp.bfloat16),
            pltpu.VMEM((2, 2 * rows, 2 * quarter), jnp.float32),
            pltpu.VMEM((4, rows, width), jnp.bfloat16),
            pltpu.SemaphoreType.DMA((2, PARTS)),
            pltpu.SemaphoreType.DMA,
            pltpu.SemaphoreType.DMA((2,)),
            pltpu.SemaphoreType.DMA((4,)),
        ],
        compiler_params=pltpu.CompilerParams(vmem_limit_bytes=59 * MIB),
        cost_estimate=SMALL,
        name="rest_products",
    )(meta, *xs, rest, b)


def assemble_kernel(place_ref, mask_ref, *refs):
    n = 4
    pieces, (out_ref, made, sem) = refs[:n], refs[-3:]
    steps = mask_ref.shape[0]
    rows = made.shape[0] // steps
    panel = n * LANES
    first = pl.multiple_of(place_ref[1] * panel, panel)
    for r in range(n):
        t = jnp.bitwise_xor(place_ref[0], r)
        for j in range(made.shape[1] // panel):
            to = pl.multiple_of(j * panel + t * LANES, LANES)
            for i in range(steps):
                keep = mask_ref[i, :, pl.ds(pl.multiple_of(first + to, LANES), LANES)]
                value = pieces[r][i * rows : (i + 1) * rows, j * LANES : (j + 1) * LANES].astype(jnp.float32)
                made[i * rows : (i + 1) * rows, pl.ds(to, LANES)] = (value * keep).astype(jnp.bfloat16)
    copy = pltpu.make_async_copy(made, out_ref.at[:, pl.ds(first, made.shape[1])], sem)
    copy.start()
    copy.wait()


def assembled(place, keep_wide, pieces, out=None):
    rows, width = pieces[0].shape
    cols = keep_wide.shape[2]
    vmem_spec = pl.BlockSpec(memory_space=pltpu.VMEM)
    any_spec = pl.BlockSpec(memory_space=pltpu.HBM)
    operands = [place, keep_wide, *pieces] + ([] if out is None else [out])
    return pl.pallas_call(
        assemble_kernel,
        out_shape=jax.ShapeDtypeStruct((rows, cols), jnp.bfloat16),
        in_specs=[pl.BlockSpec(memory_space=pltpu.SMEM)] + [vmem_spec] * 5 + [any_spec] * (len(operands) - 6),
        out_specs=any_spec,
        scratch_shapes=[pltpu.VMEM((rows, width * len(pieces)), jnp.bfloat16), pltpu.SemaphoreType.DMA],
        input_output_aliases={} if out is None else {6: 0},
        compiler_params=pltpu.CompilerParams(vmem_limit_bytes=16 * MIB),
        cost_estimate=SMALL,
        name="assembled",
    )(*operands)


def widen(mask, block):
    rows, cols = mask.shape
    wide = jnp.broadcast_to(mask.astype(jnp.float32)[:, :, None], (rows, cols, block))
    return wide.reshape(rows, 1, cols * block)


def together(*values):
    return lax.optimization_barrier(values)


def pairs_in_line(x_band, w_band, a_mask, keep_mask):
    panel = x_band.shape[0]
    block = panel // a_mask.shape[0]
    g, c = lax.axis_index("grid"), lax.axis_index("depth")
    z, y = g // 2, g % 2
    left = z < 2
    is_end = ((z == 0) | (z == 3)).astype(jnp.int32)
    toward = jnp.where(left, 1, -1)
    q = 2 * y + c

    swap = [(0, 2), (1, 3), (2, 0), (3, 1), (4, 6), (5, 7), (6, 4), (7, 5)]
    outward = [(2, 0), (3, 1), (4, 6), (5, 7)]
    cross = [(2, 4), (3, 5), (4, 2), (5, 3)]
    across = [(i, i ^ 1) for i in range(8)]
    layers = [(0, 1), (1, 0)]
    opposite = [(i, i ^ 3) for i in range(16)]

    def line(value, pairs):
        return lax.ppermute(value, "grid", pairs)

    first_out, second_out = jnp.where(left, 0, 4), jnp.where(left, 4, 0)
    first_in, second_in = second_out, first_out
    last_in = jnp.where(left, 1, 4)

    (sent_b,) = b_strips(w_band, [q ^ 2], 58)
    own_b = line(sent_b, across)
    sent_b, w_band = together(sent_b, w_band)
    (own_a,) = b_strips(w_band, [q], 48)
    swap_a = line(own_a, swap)
    cross_a = line(own_a, cross)
    mask_wide = widen(a_mask, block)
    rows = a_mask.shape[0]
    x_mine = [masked_rows(x_band, mask_wide, c * rows // 2 + k * rows // 4, rows // 4) for k in range(2)]
    own_b, *x_mine = together(own_b, *x_mine)
    own_b, swap_a = together(own_b, swap_a)
    swap_b = line(own_b, swap)
    own_b, cross_a = together(own_b, cross_a)
    cross_b = line(own_b, cross)
    x_across = [line(part, across) for part in x_mine]
    x_rest = [masked_rows(x_band, mask_wide, (1 - c) * rows // 2 + k * rows // 4, rows // 4) for k in range(2)]

    mid_b, fwd_first = packed(
        [y, first_out],
        [cross_a, cross_b, swap_a, swap_b],
        [13, 8],
        [
            (0, 0, 3, 0, 0, (0, 0)),
            (1, 0, 3, 0, 0, (0, 1)),
            (0, 3, 5, 0, 3, None),
            (1, 3, 5, 0, 8, None),
            (2, (1,), 4, 1, 0, None),
            (3, (1,), 4, 1, 4, None),
        ],
    )
    (fwd_second,) = packed([second_out], [swap_a, swap_b], [8], [(0, (0,), 4, 0, 0, None), (1, (0,), 4, 0, 4, None)])
    mid_b = line(mid_b, outward)
    fwd_first = line(fwd_first, cross)
    fwd_first, fwd_second, *x_across = together(fwd_first, fwd_second, *x_across)
    far_first = line(fwd_first, outward)
    fwd_second = line(fwd_second, cross)
    x_opposite = [lax.ppermute(part, "depth", layers) for part in x_across]
    xs = x_mine + x_rest + x_across + x_opposite

    def offsets(delta):
        tilt = 2 * y - 1
        return [(2 * delta + 4) % 8, (2 * delta + tilt + 4) % 8, (2 * delta - tilt + 4) % 8, (2 * delta + 4) % 8]

    zero = jnp.zeros_like(z)
    third = offsets(jnp.where(is_end == 1, 2, -toward))
    fourth = offsets(jnp.where(is_end == 1, -toward, 2))
    meta = jnp.stack([is_end, 4 + y, *offsets(zero), *offsets(toward), *third]).astype(jnp.int32)
    plan = [
        (0, [(0, 0, 8, 0, 0)]),
        (1, [(1, 0, 8, 0, 1)]),
        (2, [(4, 0, 8, 0, 2)]),
        (3, [(5, 0, 8, 0, 3)]),
        (4, [(6, 0, 3, 0, None), (6, 3, 5, 3, 4)]),
        (5, [(6, 8, 5, 3, 5)]),
    ]
    total = whole_products(meta, xs, [own_a, own_b, cross_a, cross_b, swap_a, swap_b, mid_b], plan)
    last_at = jnp.where(left, 1, 0)
    total, last_at = together(total, last_at)
    (last,) = packed(
        [last_at, last_at + 4], [fwd_second], [6], [(0, (0,), 3, 0, 0, None), (0, (1,), 3, 0, 3, None)]
    )
    far_second = line(last, outward)

    def exchanged(pieces):
        return [
            pieces[0],
            lax.ppermute(pieces[1], "depth", layers),
            line(pieces[2], across),
            lax.ppermute(pieces[3], ("grid", "depth"), opposite),
        ]

    done_at, rest_at = jnp.where(left, 3, 0), jnp.where(left, 0, 5)
    meta = jnp.stack([is_end, first_in, second_in, done_at, rest_at, *fourth]).astype(jnp.int32)
    *done, rest = half_products(meta, xs, total, fwd_first, far_first, fwd_second, 5)
    done = exchanged(done)
    far_second, done[1] = together(far_second, done[1])
    keep_wide = widen(keep_mask, block)
    out = assembled(jnp.stack([q, done_at]).astype(jnp.int32), keep_wide, done)
    meta = jnp.stack([is_end, last_in, rest_at, *fourth]).astype(jnp.int32)
    rest = exchanged(rest_products(meta, xs, rest, far_second, own_a.shape[1]))
    return assembled(jnp.stack([q, rest_at]).astype(jnp.int32), keep_wide, rest, out)


def solution(mesh):
    placed = (
        P(("groups", "grid"), None),
        P(("groups", "grid"), None),
        P(("groups", "grid"), None),
        P(("groups", "grid", "depth"), None),
    )

    def local(x_band, w_band, a_mask, keep_mask):
        panel, cols = x_band.shape
        pairs = mesh.shape["grid"] == 8 and mesh.shape["depth"] == 2
        pairs = pairs and cols == 8 * panel and panel == 4 * LANES
        return (pairs_in_line if pairs else ring)(x_band, w_band, a_mask, keep_mask)

    return jax.shard_map(
        local,
        mesh=mesh,
        in_specs=placed,
        out_specs=P(("groups", "grid", "depth"), None),
        check_vma=False,
    )
```

```python
import functools

import jax
import jax.numpy as jnp
from jax import lax
from jax.experimental import pallas as pl
from jax.experimental.pallas import tpu as pltpu
from jax.sharding import PartitionSpec as P

LANES = 128
MIB = 1 << 20
SMALL = pl.CostEstimate(flops=1000, bytes_accessed=1000, transcendentals=0)


def shifted(shard, axis, by):
    count = lax.axis_size(axis)
    return lax.ppermute(shard, axis, [(i, (i + by) % count) for i in range(count)])


def expand_blocks(mask, block):
    rows, cols = mask.shape
    wide = jnp.broadcast_to(mask[:, None, :, None], (rows, block, cols, block))
    return wide.reshape(rows * block, cols * block)


def ring(x_band, w_band, a_mask, keep_mask):
    panel = x_band.shape[0]
    block = panel // a_mask.shape[0]
    band_cols = x_band.shape[1]
    xm = x_band * expand_blocks(a_mask, block).astype(jnp.bfloat16)
    rows = lax.broadcasted_iota(jnp.int32, x_band.shape, 0)
    cols = lax.broadcasted_iota(jnp.int32, x_band.shape, 1)
    identity = jnp.where(cols == rows + 4 * panel, 1.0, 0.0).astype(jnp.float32)
    b_panel = (1.5 * identity - 0.5 * w_band.astype(jnp.float32)).astype(jnp.bfloat16)
    layer = lax.axis_index("depth")
    current = shifted(b_panel, ("grid", "depth"), -5)
    wide = jnp.zeros((panel, 2 * band_cols), jnp.float32)
    for step in range(4):
        offset = 6 + layer - 2 * step
        ablock = lax.dynamic_slice_in_dim(xm, offset * panel, panel, 1)
        term = jnp.dot(ablock, current, preferred_element_type=jnp.float32)
        region = lax.dynamic_slice_in_dim(wide, offset * panel, band_cols, 1)
        wide = lax.dynamic_update_slice_in_dim(wide, region + term, offset * panel, 1)
        if step < 3:
            current = shifted(current, "grid", 2)
    partial_band = wide[:, 4 * panel : 12 * panel]
    mine = lax.psum_scatter(partial_band, "depth", scatter_dimension=0, tiled=True)
    keep = expand_blocks(keep_mask, block).astype(jnp.float32)
    return (mine * keep).astype(jnp.bfloat16)


def strips_kernel(quarters_ref, w_ref, *refs):
    *b_refs, held, sems = refs
    _, panel, width = held.shape
    band = width // LANES

    def copy(k, j):
        at = pl.multiple_of(j * panel + quarters_ref[k] * LANES, LANES)
        to = held.at[k, :, j * LANES : (j + 1) * LANES]
        return pltpu.make_async_copy(w_ref.at[:, pl.ds(at, LANES)], to, sems.at[k, j])

    for k in range(len(b_refs)):
        for j in range(band):
            copy(k, j).start()
    for k, b_ref in enumerate(b_refs):
        for j in range(band):
            copy(k, j).wait()
            value = -0.5 * held[k, :, j * LANES : (j + 1) * LANES].astype(jnp.float32)
            if j == band // 2:
                rows = lax.broadcasted_iota(jnp.int32, value.shape, 0)
                cols = lax.broadcasted_iota(jnp.int32, value.shape, 1)
                value = value + jnp.where(rows == cols + quarters_ref[k] * LANES, 1.5, 0.0)
            b_ref[:, j * LANES : (j + 1) * LANES] = value.astype(jnp.bfloat16)


def b_strips(w_band, quarters, limit):
    panel = w_band.shape[0]
    band = w_band.shape[1] // panel
    n = len(quarters)
    shape = (panel, band * LANES)
    return pl.pallas_call(
        strips_kernel,
        out_shape=[jax.ShapeDtypeStruct(shape, jnp.bfloat16)] * n,
        in_specs=[
            pl.BlockSpec(memory_space=pltpu.SMEM),
            pl.BlockSpec(memory_space=pltpu.HBM),
        ],
        out_specs=[pl.BlockSpec(memory_space=pltpu.VMEM)] * n,
        scratch_shapes=[pltpu.VMEM((n, *shape), jnp.bfloat16), pltpu.SemaphoreType.DMA((n, band))],
        compiler_params=pltpu.CompilerParams(vmem_limit_bytes=limit * MIB),
        cost_estimate=SMALL,
        name="b_strips",
    )(jnp.stack(quarters), w_band)


def pack_kernel(plan, n_in, meta_ref, *refs):
    sources, outs, sems = refs[:n_in], refs[n_in:-1], refs[-1]

    def on_each(do):
        for k, (source, start, count, out, to, when) in enumerate(plan):
            at = start * LANES if isinstance(start, int) else pl.multiple_of(meta_ref[start[0]] * LANES, LANES)
            copy = pltpu.make_async_copy(
                sources[source].at[:, pl.ds(at, count * LANES)],
                outs[out].at[:, to * LANES : (to + count) * LANES],
                sems.at[k],
            )
            if when is None:
                do(copy)
            else:
                pl.when(meta_ref[when[0]] == when[1])(functools.partial(do, copy))

    on_each(lambda copy: copy.start())
    on_each(lambda copy: copy.wait())


def packed(meta, sources, widths, plan):
    rows = sources[0].shape[0]
    any_spec = pl.BlockSpec(memory_space=pl.ANY)
    return pl.pallas_call(
        functools.partial(pack_kernel, plan, len(sources)),
        out_shape=[jax.ShapeDtypeStruct((rows, width * LANES), jnp.bfloat16) for width in widths],
        in_specs=[pl.BlockSpec(memory_space=pltpu.SMEM)] + [any_spec] * len(sources),
        out_specs=[pl.BlockSpec(memory_space=pltpu.VMEM)] * len(widths),
        scratch_shapes=[pltpu.SemaphoreType.DMA((len(plan),))],
        compiler_params=pltpu.CompilerParams(vmem_limit_bytes=40 * MIB),
        cost_estimate=SMALL,
        name="packed",
    )(jnp.stack(meta).astype(jnp.int32), *sources)


def mask_kernel(first_ref, mask_ref, x_ref, out_ref):
    out_ref[...] = (x_ref[...].astype(jnp.float32) * mask_ref[0]).astype(jnp.bfloat16)


def masked_rows(x_band, mask_wide, first, count):
    block = x_band.shape[0] // mask_wide.shape[0]
    cols = x_band.shape[1]
    return pl.pallas_call(
        mask_kernel,
        grid_spec=pltpu.PrefetchScalarGridSpec(
            num_scalar_prefetch=1,
            grid=(count,),
            in_specs=[
                pl.BlockSpec((1, 1, cols), lambda i, f: (f[0] + i, 0, 0)),
                pl.BlockSpec((block, cols), lambda i, f: (f[0] + i, 0)),
            ],
            out_specs=pl.BlockSpec((block, cols), lambda i, f: (i, 0)),
        ),
        out_shape=jax.ShapeDtypeStruct((count * block, cols), jnp.bfloat16),
        compiler_params=pltpu.CompilerParams(vmem_limit_bytes=58 * MIB),
        cost_estimate=SMALL,
        name="masked_rows",
    )(first.reshape(1), mask_wide, x_band)


PARTS = 8


def x_copies(x_refs, xv, sems, offset_of):
    n_b, _, rows, panel = xv.shape
    part = 2 * rows // PARTS
    copies = {}
    for p in range(n_b):
        for r in range(PARTS):
            g, k = divmod(r, PARTS // 2)
            at = pl.multiple_of(offset_of(p, g) * panel, panel)
            copies[p, r] = pltpu.make_async_copy(
                x_refs[r].at[:, pl.ds(at, panel)],
                xv.at[p, g, k * part : (k + 1) * part],
                sems.at[p, r],
            )
    return copies


def add_product(acc, x, strips, g, first):
    cols = pl.ds(pl.multiple_of(first * LANES, LANES), strips.shape[1])
    acc[g, :, cols] += jnp.dot(x, strips, preferred_element_type=jnp.float32)


def whole_kernel(plan, meta_ref, *refs):
    n_b = len(plan)
    x_refs, refs = refs[:PARTS], refs[PARTS:]
    b_refs, (out_ref, xv, bv, acc, x_sems, b_sems, out_sems) = refs[:-7], refs[-7:]
    quarter = bv.shape[2]
    low = quarter // 2
    is_end = meta_ref[0]

    def offset_of(p, g):
        return meta_ref[2 + 2 * p + g]

    def b_middle(p):
        return [pltpu.make_async_copy(b_refs[plan[p][0]].at[:, :quarter], bv.at[p], b_sems.at[p, 0])]

    def b_end(p):
        copies = []
        for k, (operand, first, count, at, to) in enumerate(plan[p][1]):
            to = meta_ref[1] if to is None else to
            source = b_refs[operand].at[:, first * LANES : (first + count) * LANES]
            copies.append(pltpu.make_async_copy(source, bv.at[to, :, at * LANES : (at + count) * LANES], b_sems.at[p, k]))
        return copies

    def on_each(p, do):
        @pl.when(is_end == 0)
        def _():
            for copy in b_middle(p):
                do(copy)

        @pl.when(is_end != 0)
        def _():
            for copy in b_end(p):
                do(copy)

    copies = x_copies(x_refs, xv, x_sems, offset_of)
    for p in range(n_b):
        on_each(p, lambda copy: copy.start())
        for r in range(PARTS):
            copies[p, r].start()
    acc[...] = jnp.zeros_like(acc)
    for p in range(n_b):
        for k in [p] if p < n_b - 2 else range(n_b - 2, n_b) if p == n_b - 2 else []:
            on_each(k, lambda copy: copy.wait())
        for r in range(PARTS):
            copies[p, r].wait()

        def step(g, carry):
            add_product(acc, xv[p, g], bv[p], g, offset_of(p, g))
            return carry

        lax.fori_loop(0, 2, step, 0)
    outs = [
        pltpu.make_async_copy(acc.at[g, :, low : low + quarter], out_ref.at[g], out_sems.at[g]) for g in range(2)
    ]
    for out in outs:
        out.start()
    for out in outs:
        out.wait()


def whole_products(meta, xs, operands, plan):
    rows = PARTS // 4 * xs[0].shape[0]
    panel, quarter = operands[plan[0][0]].shape
    n_b = len(plan)
    any_spec = pl.BlockSpec(memory_space=pl.ANY)
    x_spec = pl.BlockSpec(memory_space=pltpu.HBM)
    return pl.pallas_call(
        functools.partial(whole_kernel, plan),
        out_shape=jax.ShapeDtypeStruct((2, 2 * rows, quarter), jnp.float32),
        in_specs=[pl.BlockSpec(memory_space=pltpu.SMEM)] + [x_spec] * PARTS + [any_spec] * len(operands),
        out_specs=any_spec,
        scratch_shapes=[
            pltpu.VMEM((n_b, 2, 2 * rows, panel), jnp.bfloat16),
            pltpu.VMEM((n_b, panel, quarter), jnp.bfloat16),
            pltpu.VMEM((2, 2 * rows, 2 * quarter), jnp.float32),
            pltpu.SemaphoreType.DMA((n_b, PARTS)),
            pltpu.SemaphoreType.DMA((n_b, 2)),
            pltpu.SemaphoreType.DMA((2,)),
        ],
        compiler_params=pltpu.CompilerParams(vmem_limit_bytes=59 * MIB),
        cost_estimate=SMALL,
        name="whole_products",
    )(meta, *xs, *operands)


def finish(acc, wait_for, add, at, out_refs, pieces, sems, also=None):
    half, width = out_refs[0].shape
    cols = pl.ds(pl.multiple_of(at * LANES, LANES), width)
    outs = [pltpu.make_async_copy(pieces.at[r], out_refs[r], sems.at[r]) for r in range(4)]
    also = also or []

    def step(g, carry):
        for k in range(2):
            pl.when(g == k)(functools.partial(wait_for, k))
        add(g)
        for k in range(2):

            @pl.when(g == k)
            def _():
                for copy in also[k : k + 1]:
                    copy.start()
                for r in range(2 * k, 2 * k + 2):
                    rows = slice((r % 2) * half, (r % 2 + 1) * half)
                    pieces[r] = acc[k, rows, cols].astype(jnp.bfloat16)
                    outs[r].start()

        return carry

    lax.fori_loop(0, 2, step, 0)
    for copy in outs + also:
        copy.wait()


def half_kernel(meta_ref, *refs):
    x_refs, (prev_ref, middle_ref, end_ref, second_ref), refs = refs[:PARTS], refs[PARTS : PARTS + 4], refs[PARTS + 4 :]
    out_refs, rest_ref, xv, bv, acc, pieces, x_sems, b_sems, prev_sems, rest_sems, out_sems = refs[:4], *refs[4:]
    quarter = bv.shape[2]
    half = quarter // 2
    low = quarter // 2
    band = quarter // LANES
    is_end = meta_ref[0]

    def offset_of(p, g):
        return meta_ref[5 + 2 * p + g]

    x_loads = x_copies(x_refs, xv, x_sems, offset_of)
    middle = pltpu.make_async_copy(middle_ref, bv.at[0], b_sems.at[0])
    end = pltpu.make_async_copy(end_ref, bv.at[0], b_sems.at[0])
    second = pltpu.make_async_copy(second_ref, bv.at[1], b_sems.at[1])
    prev = [
        pltpu.make_async_copy(prev_ref.at[g], acc.at[g, :, low : low + quarter], prev_sems.at[g]) for g in range(2)
    ]
    at = pl.multiple_of((meta_ref[4] + band // 2) * LANES, LANES)
    rest = [
        pltpu.make_async_copy(acc.at[g, :, pl.ds(at, rest_ref.shape[2])], rest_ref.at[g], rest_sems.at[g])
        for g in range(2)
    ]

    @pl.when(is_end == 0)
    def _():
        middle.start()
        second.start()

    pl.when(is_end != 0)(end.start)

    def rows_loads(g):
        return [prev[g]] + [copy for (_, r), copy in x_loads.items() if r // (PARTS // 2) == g]

    for g in range(2):
        for copy in rows_loads(g):
            copy.start()

    def wait_for(g):
        for copy in rows_loads(g):
            copy.wait()
        if g == 0:

            @pl.when(is_end == 0)
            def _():
                middle.wait()
                second.wait()

            pl.when(is_end != 0)(end.wait)

    def add(g):
        for p in range(2):
            add_product(acc, xv[p, g], bv[0, :, p * half : (p + 1) * half], g, offset_of(p, g) + meta_ref[1])

        @pl.when(is_end == 0)
        def _():
            for p in range(2):
                add_product(acc, xv[p, g], bv[1, :, p * half : (p + 1) * half], g, offset_of(p, g) + meta_ref[2])

    finish(acc, wait_for, add, meta_ref[3] + band // 2, out_refs, pieces, out_sems, rest)


def half_products(meta, xs, prev, middle, end, second, n_done):
    rows = PARTS // 4 * xs[0].shape[0]
    panel, quarter = second.shape
    any_spec = pl.BlockSpec(memory_space=pl.ANY)
    x_spec = pl.BlockSpec(memory_space=pltpu.HBM)
    n_rest = quarter // LANES - n_done
    return pl.pallas_call(
        half_kernel,
        out_shape=[jax.ShapeDtypeStruct((rows, n_done * LANES), jnp.bfloat16)] * 4
        + [jax.ShapeDtypeStruct((2, 2 * rows, n_rest * LANES), jnp.float32)],
        in_specs=[pl.BlockSpec(memory_space=pltpu.SMEM)] + [x_spec] * PARTS + [any_spec] * 4,
        out_specs=[any_spec] * 5,
        scratch_shapes=[
            pltpu.VMEM((2, 2, 2 * rows, panel), jnp.bfloat16),
            pltpu.VMEM((2, panel, quarter), jnp.bfloat16),
            pltpu.VMEM((2, 2 * rows, 2 * quarter), jnp.float32),
            pltpu.VMEM((4, rows, n_done * LANES), jnp.bfloat16),
            pltpu.SemaphoreType.DMA((2, PARTS)),
            pltpu.SemaphoreType.DMA((2,)),
            pltpu.SemaphoreType.DMA((2,)),
            pltpu.SemaphoreType.DMA((2,)),
            pltpu.SemaphoreType.DMA((4,)),
        ],
        compiler_params=pltpu.CompilerParams(vmem_limit_bytes=59 * MIB),
        cost_estimate=SMALL,
        name="half_products",
    )(meta, *xs, prev, middle, end, second)


def rest_kernel(meta_ref, *refs):
    x_refs, (rest_ref, b_ref), refs = refs[:PARTS], refs[PARTS : PARTS + 2], refs[PARTS + 2 :]
    out_refs, xv, bv, acc, pieces, x_sems, b_sem, rest_sems, out_sems = refs[:4], *refs[4:]
    band = acc.shape[2] // (2 * LANES)
    half = bv.shape[1] // 2
    is_end = meta_ref[0]

    def offset_of(p, g):
        return meta_ref[3 + 2 * p + g]

    at = pl.multiple_of((meta_ref[2] + band // 2) * LANES, LANES)
    rest = [
        pltpu.make_async_copy(rest_ref.at[g], acc.at[g, :, pl.ds(at, rest_ref.shape[2])], rest_sems.at[g])
        for g in range(2)
    ]
    x_loads = x_copies(x_refs, xv, x_sems, offset_of)
    b_copy = pltpu.make_async_copy(b_ref, bv, b_sem)

    def x_loads_of(g):
        return [copy for (_, r), copy in x_loads.items() if r // (PARTS // 2) == g]

    pl.when(is_end != 0)(b_copy.start)
    for g in range(2):
        rest[g].start()

        @pl.when(is_end != 0)
        def _():
            for copy in x_loads_of(g):
                copy.start()

    def wait_for(g):
        rest[g].wait()

        @pl.when(is_end != 0)
        def _():
            for copy in x_loads_of(g):
                copy.wait()
            if g == 0:
                b_copy.wait()

    def add(g):
        @pl.when(is_end != 0)
        def _():
            for p in range(2):
                add_product(acc, xv[p, g], bv[:, p * half : (p + 1) * half], g, offset_of(p, g) + meta_ref[1])

    finish(acc, wait_for, add, meta_ref[2] + band // 2, out_refs, pieces, out_sems)


def rest_products(meta, xs, rest, b, quarter):
    rows = PARTS // 4 * xs[0].shape[0]
    panel = b.shape[0]
    width = rest.shape[2]
    any_spec = pl.BlockSpec(memory_space=pl.ANY)
    x_spec = pl.BlockSpec(memory_space=pltpu.HBM)
    return pl.pallas_call(
        rest_kernel,
        out_shape=[jax.ShapeDtypeStruct((rows, width), jnp.bfloat16)] * 4,
        in_specs=[pl.BlockSpec(memory_space=pltpu.SMEM)] + [x_spec] * PARTS + [any_spec] * 2,
        out_specs=[any_spec] * 4,
        scratch_shapes=[
            pltpu.VMEM((2, 2, 2 * rows, panel), jnp.bfloat16),
            pltpu.VMEM(b.shape, jnp.bfloat16),
            pltpu.VMEM((2, 2 * rows, 2 * quarter), jnp.float32),
            pltpu.VMEM((4, rows, width), jnp.bfloat16),
            pltpu.SemaphoreType.DMA((2, PARTS)),
            pltpu.SemaphoreType.DMA,
            pltpu.SemaphoreType.DMA((2,)),
            pltpu.SemaphoreType.DMA((4,)),
        ],
        compiler_params=pltpu.CompilerParams(vmem_limit_bytes=59 * MIB),
        cost_estimate=SMALL,
        name="rest_products",
    )(meta, *xs, rest, b)


def assemble_kernel(place_ref, mask_ref, *refs):
    n = 4
    pieces, (out_ref, made, sem) = refs[:n], refs[-3:]
    steps = mask_ref.shape[0]
    rows = made.shape[0] // steps
    panel = n * LANES
    first = pl.multiple_of(place_ref[1] * panel, panel)
    for r in range(n):
        t = jnp.bitwise_xor(place_ref[0], r)
        for j in range(made.shape[1] // panel):
            to = pl.multiple_of(j * panel + t * LANES, LANES)
            for i in range(steps):
                keep = mask_ref[i, :, pl.ds(pl.multiple_of(first + to, LANES), LANES)]
                value = pieces[r][i * rows : (i + 1) * rows, j * LANES : (j + 1) * LANES].astype(jnp.float32)
                made[i * rows : (i + 1) * rows, pl.ds(to, LANES)] = (value * keep).astype(jnp.bfloat16)
    copy = pltpu.make_async_copy(made, out_ref.at[:, pl.ds(first, made.shape[1])], sem)
    copy.start()
    copy.wait()


def assembled(place, keep_wide, pieces, out=None):
    rows, width = pieces[0].shape
    cols = keep_wide.shape[2]
    vmem_spec = pl.BlockSpec(memory_space=pltpu.VMEM)
    any_spec = pl.BlockSpec(memory_space=pltpu.HBM)
    operands = [place, keep_wide, *pieces] + ([] if out is None else [out])
    return pl.pallas_call(
        assemble_kernel,
        out_shape=jax.ShapeDtypeStruct((rows, cols), jnp.bfloat16),
        in_specs=[pl.BlockSpec(memory_space=pltpu.SMEM)] + [vmem_spec] * 5 + [any_spec] * (len(operands) - 6),
        out_specs=any_spec,
        scratch_shapes=[pltpu.VMEM((rows, width * len(pieces)), jnp.bfloat16), pltpu.SemaphoreType.DMA],
        input_output_aliases={} if out is None else {6: 0},
        compiler_params=pltpu.CompilerParams(vmem_limit_bytes=16 * MIB),
        cost_estimate=SMALL,
        name="assembled",
    )(*operands)


def widen(mask, block):
    rows, cols = mask.shape
    wide = jnp.broadcast_to(mask.astype(jnp.float32)[:, :, None], (rows, cols, block))
    return wide.reshape(rows, 1, cols * block)


def together(*values):
    return lax.optimization_barrier(values)


def pairs_in_line(x_band, w_band, a_mask, keep_mask):
    panel = x_band.shape[0]
    block = panel // a_mask.shape[0]
    g, c = lax.axis_index("grid"), lax.axis_index("depth")
    z, y = g // 2, g % 2
    left = z < 2
    is_end = ((z == 0) | (z == 3)).astype(jnp.int32)
    toward = jnp.where(left, 1, -1)
    q = 2 * y + c

    swap = [(0, 2), (1, 3), (2, 0), (3, 1), (4, 6), (5, 7), (6, 4), (7, 5)]
    outward = [(2, 0), (3, 1), (4, 6), (5, 7)]
    cross = [(2, 4), (3, 5), (4, 2), (5, 3)]
    across = [(i, i ^ 1) for i in range(8)]
    layers = [(0, 1), (1, 0)]
    opposite = [(i, i ^ 3) for i in range(16)]

    def line(value, pairs):
        return lax.ppermute(value, "grid", pairs)

    first_out, second_out = jnp.where(left, 0, 4), jnp.where(left, 4, 0)
    first_in, second_in = second_out, first_out
    last_in = jnp.where(left, 1, 4)

    (sent_b,) = b_strips(w_band, [q ^ 2], 58)
    own_b = line(sent_b, across)
    sent_b, w_band = together(sent_b, w_band)
    (own_a,) = b_strips(w_band, [q], 48)
    swap_a = line(own_a, swap)
    cross_a = line(own_a, cross)
    mask_wide = widen(a_mask, block)
    rows = a_mask.shape[0]
    x_mine = [masked_rows(x_band, mask_wide, c * rows // 2 + k * rows // 4, rows // 4) for k in range(2)]
    own_b, *x_mine = together(own_b, *x_mine)
    own_b, swap_a = together(own_b, swap_a)
    swap_b = line(own_b, swap)
    own_b, cross_a = together(own_b, cross_a)
    cross_b = line(own_b, cross)
    x_across = [line(part, across) for part in x_mine]
    x_rest = [masked_rows(x_band, mask_wide, (1 - c) * rows // 2 + k * rows // 4, rows // 4) for k in range(2)]

    mid_b, fwd_first = packed(
        [y, first_out],
        [cross_a, cross_b, swap_a, swap_b],
        [13, 8],
        [
            (0, 0, 3, 0, 0, (0, 0)),
            (1, 0, 3, 0, 0, (0, 1)),
            (0, 3, 5, 0, 3, None),
            (1, 3, 5, 0, 8, None),
            (2, (1,), 4, 1, 0, None),
            (3, (1,), 4, 1, 4, None),
        ],
    )
    (fwd_second,) = packed([second_out], [swap_a, swap_b], [8], [(0, (0,), 4, 0, 0, None), (1, (0,), 4, 0, 4, None)])
    mid_b = line(mid_b, outward)
    fwd_first = line(fwd_first, cross)
    fwd_first, fwd_second, *x_across = together(fwd_first, fwd_second, *x_across)
    far_first = line(fwd_first, outward)
    fwd_second = line(fwd_second, cross)
    x_opposite = [lax.ppermute(part, "depth", layers) for part in x_across]
    xs = x_mine + x_rest + x_across + x_opposite

    def offsets(delta):
        tilt = 2 * y - 1
        return [(2 * delta + 4) % 8, (2 * delta + tilt + 4) % 8, (2 * delta - tilt + 4) % 8, (2 * delta + 4) % 8]

    zero = jnp.zeros_like(z)
    third = offsets(jnp.where(is_end == 1, 2, -toward))
    fourth = offsets(jnp.where(is_end == 1, -toward, 2))
    meta = jnp.stack([is_end, 4 + y, *offsets(zero), *offsets(toward), *third]).astype(jnp.int32)
    plan = [
        (0, [(0, 0, 8, 0, 0)]),
        (1, [(1, 0, 8, 0, 1)]),
        (2, [(4, 0, 8, 0, 2)]),
        (3, [(5, 0, 8, 0, 3)]),
        (4, [(6, 0, 3, 0, None), (6, 3, 5, 3, 4)]),
        (5, [(6, 8, 5, 3, 5)]),
    ]
    total = whole_products(meta, xs, [own_a, own_b, cross_a, cross_b, swap_a, swap_b, mid_b], plan)
    last_at = jnp.where(left, 1, 0)
    total, last_at = together(total, last_at)
    (last,) = packed(
        [last_at, last_at + 4], [fwd_second], [6], [(0, (0,), 3, 0, 0, None), (0, (1,), 3, 0, 3, None)]
    )
    far_second = line(last, outward)

    def exchanged(pieces):
        return [
            pieces[0],
            lax.ppermute(pieces[1], "depth", layers),
            line(pieces[2], across),
            lax.ppermute(pieces[3], ("grid", "depth"), opposite),
        ]

    done_at, rest_at = jnp.where(left, 3, 0), jnp.where(left, 0, 5)
    meta = jnp.stack([is_end, first_in, second_in, done_at, rest_at, *fourth]).astype(jnp.int32)
    *done, rest = half_products(meta, xs, total, fwd_first, far_first, fwd_second, 5)
    done = exchanged(done)
    far_second, done[1] = together(far_second, done[1])
    keep_wide = widen(keep_mask, block)
    out = assembled(jnp.stack([q, done_at]).astype(jnp.int32), keep_wide, done)
    meta = jnp.stack([is_end, last_in, rest_at, *fourth]).astype(jnp.int32)
    rest = exchanged(rest_products(meta, xs, rest, far_second, own_a.shape[1]))
    return assembled(jnp.stack([q, rest_at]).astype(jnp.int32), keep_wide, rest, out)


def solution(mesh):
    placed = (
        P(("groups", "grid"), None),
        P(("groups", "grid"), None),
        P(("groups", "grid"), None),
        P(("groups", "grid", "depth"), None),
    )

    def local(x_band, w_band, a_mask, keep_mask):
        panel, cols = x_band.shape
        pairs = mesh.shape["grid"] == 8 and mesh.shape["depth"] == 2
        pairs = pairs and cols == 8 * panel and panel == 4 * LANES
        return (pairs_in_line if pairs else ring)(x_band, w_band, a_mask, keep_mask)

    return jax.shard_map(
        local,
        mesh=mesh,
        in_specs=placed,
        out_specs=P(("groups", "grid", "depth"), None),
        check_vma=False,
    )
```

```python
import functools

import jax
import jax.numpy as jnp
from jax import lax
from jax.experimental import pallas as pl
from jax.experimental.pallas import tpu as pltpu
from jax.sharding import PartitionSpec as P

LANES = 128
MIB = 1 << 20
SMALL = pl.CostEstimate(flops=1000, bytes_accessed=1000, transcendentals=0)


def shifted(shard, axis, by):
    count = lax.axis_size(axis)
    return lax.ppermute(shard, axis, [(i, (i + by) % count) for i in range(count)])


def expand_blocks(mask, block):
    rows, cols = mask.shape
    wide = jnp.broadcast_to(mask[:, None, :, None], (rows, block, cols, block))
    return wide.reshape(rows * block, cols * block)


def ring(x_band, w_band, a_mask, keep_mask):
    panel = x_band.shape[0]
    block = panel // a_mask.shape[0]
    band_cols = x_band.shape[1]
    xm = x_band * expand_blocks(a_mask, block).astype(jnp.bfloat16)
    rows = lax.broadcasted_iota(jnp.int32, x_band.shape, 0)
    cols = lax.broadcasted_iota(jnp.int32, x_band.shape, 1)
    identity = jnp.where(cols == rows + 4 * panel, 1.0, 0.0).astype(jnp.float32)
    b_panel = (1.5 * identity - 0.5 * w_band.astype(jnp.float32)).astype(jnp.bfloat16)
    layer = lax.axis_index("depth")
    current = shifted(b_panel, ("grid", "depth"), -5)
    wide = jnp.zeros((panel, 2 * band_cols), jnp.float32)
    for step in range(4):
        offset = 6 + layer - 2 * step
        ablock = lax.dynamic_slice_in_dim(xm, offset * panel, panel, 1)
        term = jnp.dot(ablock, current, preferred_element_type=jnp.float32)
        region = lax.dynamic_slice_in_dim(wide, offset * panel, band_cols, 1)
        wide = lax.dynamic_update_slice_in_dim(wide, region + term, offset * panel, 1)
        if step < 3:
            current = shifted(current, "grid", 2)
    partial_band = wide[:, 4 * panel : 12 * panel]
    mine = lax.psum_scatter(partial_band, "depth", scatter_dimension=0, tiled=True)
    keep = expand_blocks(keep_mask, block).astype(jnp.float32)
    return (mine * keep).astype(jnp.bfloat16)


def strips_kernel(quarters_ref, w_ref, *refs):
    *b_refs, held, sems = refs
    _, panel, width = held.shape
    band = width // LANES

    def copy(k, j):
        at = pl.multiple_of(j * panel + quarters_ref[k] * LANES, LANES)
        to = held.at[k, :, j * LANES : (j + 1) * LANES]
        return pltpu.make_async_copy(w_ref.at[:, pl.ds(at, LANES)], to, sems.at[k, j])

    for k in range(len(b_refs)):
        for j in range(band):
            copy(k, j).start()
    for k, b_ref in enumerate(b_refs):
        for j in range(band):
            copy(k, j).wait()
            value = -0.5 * held[k, :, j * LANES : (j + 1) * LANES].astype(jnp.float32)
            if j == band // 2:
                rows = lax.broadcasted_iota(jnp.int32, value.shape, 0)
                cols = lax.broadcasted_iota(jnp.int32, value.shape, 1)
                value = value + jnp.where(rows == cols + quarters_ref[k] * LANES, 1.5, 0.0)
            b_ref[:, j * LANES : (j + 1) * LANES] = value.astype(jnp.bfloat16)


def b_strips(w_band, quarters, limit):
    panel = w_band.shape[0]
    band = w_band.shape[1] // panel
    n = len(quarters)
    shape = (panel, band * LANES)
    return pl.pallas_call(
        strips_kernel,
        out_shape=[jax.ShapeDtypeStruct(shape, jnp.bfloat16)] * n,
        in_specs=[
            pl.BlockSpec(memory_space=pltpu.SMEM),
            pl.BlockSpec(memory_space=pltpu.HBM),
        ],
        out_specs=[pl.BlockSpec(memory_space=pltpu.VMEM)] * n,
        scratch_shapes=[pltpu.VMEM((n, *shape), jnp.bfloat16), pltpu.SemaphoreType.DMA((n, band))],
        compiler_params=pltpu.CompilerParams(vmem_limit_bytes=limit * MIB),
        cost_estimate=SMALL,
        name="b_strips",
    )(jnp.stack(quarters), w_band)


def pack_kernel(plan, n_in, meta_ref, *refs):
    sources, outs, sems = refs[:n_in], refs[n_in:-1], refs[-1]

    def on_each(do):
        for k, (source, start, count, out, to, when) in enumerate(plan):
            at = start * LANES if isinstance(start, int) else pl.multiple_of(meta_ref[start[0]] * LANES, LANES)
            copy = pltpu.make_async_copy(
                sources[source].at[:, pl.ds(at, count * LANES)],
                outs[out].at[:, to * LANES : (to + count) * LANES],
                sems.at[k],
            )
            if when is None:
                do(copy)
            else:
                pl.when(meta_ref[when[0]] == when[1])(functools.partial(do, copy))

    on_each(lambda copy: copy.start())
    on_each(lambda copy: copy.wait())


def packed(meta, sources, widths, plan):
    rows = sources[0].shape[0]
    any_spec = pl.BlockSpec(memory_space=pl.ANY)
    return pl.pallas_call(
        functools.partial(pack_kernel, plan, len(sources)),
        out_shape=[jax.ShapeDtypeStruct((rows, width * LANES), jnp.bfloat16) for width in widths],
        in_specs=[pl.BlockSpec(memory_space=pltpu.SMEM)] + [any_spec] * len(sources),
        out_specs=[pl.BlockSpec(memory_space=pltpu.VMEM)] * len(widths),
        scratch_shapes=[pltpu.SemaphoreType.DMA((len(plan),))],
        compiler_params=pltpu.CompilerParams(vmem_limit_bytes=40 * MIB),
        cost_estimate=SMALL,
        name="packed",
    )(jnp.stack(meta).astype(jnp.int32), *sources)


def mask_kernel(first_ref, mask_ref, x_ref, out_ref):
    out_ref[...] = (x_ref[...].astype(jnp.float32) * mask_ref[0]).astype(jnp.bfloat16)


def masked_rows(x_band, mask_wide, first, count):
    block = x_band.shape[0] // mask_wide.shape[0]
    cols = x_band.shape[1]
    return pl.pallas_call(
        mask_kernel,
        grid_spec=pltpu.PrefetchScalarGridSpec(
            num_scalar_prefetch=1,
            grid=(count,),
            in_specs=[
                pl.BlockSpec((1, 1, cols), lambda i, f: (f[0] + i, 0, 0)),
                pl.BlockSpec((block, cols), lambda i, f: (f[0] + i, 0)),
            ],
            out_specs=pl.BlockSpec((block, cols), lambda i, f: (i, 0)),
        ),
        out_shape=jax.ShapeDtypeStruct((count * block, cols), jnp.bfloat16),
        compiler_params=pltpu.CompilerParams(vmem_limit_bytes=58 * MIB),
        cost_estimate=SMALL,
        name="masked_rows",
    )(first.reshape(1), mask_wide, x_band)


PARTS = 8


def x_copies(x_refs, xv, sems, offset_of):
    n_b, _, rows, panel = xv.shape
    part = 2 * rows // PARTS
    copies = {}
    for p in range(n_b):
        for r in range(PARTS):
            g, k = divmod(r, PARTS // 2)
            at = pl.multiple_of(offset_of(p, g) * panel, panel)
            copies[p, r] = pltpu.make_async_copy(
                x_refs[r].at[:, pl.ds(at, panel)],
                xv.at[p, g, k * part : (k + 1) * part],
                sems.at[p, r],
            )
    return copies


def add_product(acc, x, strips, g, first):
    cols = pl.ds(pl.multiple_of(first * LANES, LANES), strips.shape[1])
    acc[g, :, cols] += jnp.dot(x, strips, preferred_element_type=jnp.float32)


def whole_kernel(plan, meta_ref, *refs):
    n_b = len(plan)
    x_refs, refs = refs[:PARTS], refs[PARTS:]
    b_refs, (out_ref, xv, bv, acc, x_sems, b_sems, out_sems) = refs[:-7], refs[-7:]
    quarter = bv.shape[2]
    low = quarter // 2
    is_end = meta_ref[0]

    def offset_of(p, g):
        return meta_ref[2 + 2 * p + g]

    def b_middle(p):
        return [pltpu.make_async_copy(b_refs[plan[p][0]].at[:, :quarter], bv.at[p], b_sems.at[p, 0])]

    def b_end(p):
        copies = []
        for k, (operand, first, count, at, to) in enumerate(plan[p][1]):
            to = meta_ref[1] if to is None else to
            source = b_refs[operand].at[:, first * LANES : (first + count) * LANES]
            copies.append(pltpu.make_async_copy(source, bv.at[to, :, at * LANES : (at + count) * LANES], b_sems.at[p, k]))
        return copies

    def on_each(p, do):
        @pl.when(is_end == 0)
        def _():
            for copy in b_middle(p):
                do(copy)

        @pl.when(is_end != 0)
        def _():
            for copy in b_end(p):
                do(copy)

    copies = x_copies(x_refs, xv, x_sems, offset_of)
    for p in range(n_b):
        on_each(p, lambda copy: copy.start())
        for r in range(PARTS):
            copies[p, r].start()
    acc[...] = jnp.zeros_like(acc)
    for p in range(n_b):
        for k in [p] if p < n_b - 2 else range(n_b - 2, n_b) if p == n_b - 2 else []:
            on_each(k, lambda copy: copy.wait())
        for r in range(PARTS):
            copies[p, r].wait()

        def step(g, carry):
            add_product(acc, xv[p, g], bv[p], g, offset_of(p, g))
            return carry

        lax.fori_loop(0, 2, step, 0)
    outs = [
        pltpu.make_async_copy(acc.at[g, :, low : low + quarter], out_ref.at[g], out_sems.at[g]) for g in range(2)
    ]
    for out in outs:
        out.start()
    for out in outs:
        out.wait()


def whole_products(meta, xs, operands, plan):
    rows = PARTS // 4 * xs[0].shape[0]
    panel, quarter = operands[plan[0][0]].shape
    n_b = len(plan)
    any_spec = pl.BlockSpec(memory_space=pl.ANY)
    x_spec = pl.BlockSpec(memory_space=pltpu.HBM)
    return pl.pallas_call(
        functools.partial(whole_kernel, plan),
        out_shape=jax.ShapeDtypeStruct((2, 2 * rows, quarter), jnp.float32),
        in_specs=[pl.BlockSpec(memory_space=pltpu.SMEM)] + [x_spec] * PARTS + [any_spec] * len(operands),
        out_specs=any_spec,
        scratch_shapes=[
            pltpu.VMEM((n_b, 2, 2 * rows, panel), jnp.bfloat16),
            pltpu.VMEM((n_b, panel, quarter), jnp.bfloat16),
            pltpu.VMEM((2, 2 * rows, 2 * quarter), jnp.float32),
            pltpu.SemaphoreType.DMA((n_b, PARTS)),
            pltpu.SemaphoreType.DMA((n_b, 3)),
            pltpu.SemaphoreType.DMA((2,)),
        ],
        compiler_params=pltpu.CompilerParams(vmem_limit_bytes=59 * MIB),
        cost_estimate=SMALL,
        name="whole_products",
    )(meta, *xs, *operands)


def finish(acc, wait_for, add, at, out_refs, pieces, sems, also=None):
    half, width = out_refs[0].shape
    cols = pl.ds(pl.multiple_of(at * LANES, LANES), width)
    outs = [pltpu.make_async_copy(pieces.at[r], out_refs[r], sems.at[r]) for r in range(4)]
    also = also or []

    def step(g, carry):
        for k in range(2):
            pl.when(g == k)(functools.partial(wait_for, k))
        add(g)
        for k in range(2):

            @pl.when(g == k)
            def _():
                for copy in also[k : k + 1]:
                    copy.start()
                for r in range(2 * k, 2 * k + 2):
                    rows = slice((r % 2) * half, (r % 2 + 1) * half)
                    pieces[r] = acc[k, rows, cols].astype(jnp.bfloat16)
                    outs[r].start()

        return carry

    lax.fori_loop(0, 2, step, 0)
    for copy in outs + also:
        copy.wait()


def half_kernel(meta_ref, *refs):
    x_refs, (prev_ref, middle_ref, end_ref, second_ref), refs = refs[:PARTS], refs[PARTS : PARTS + 4], refs[PARTS + 4 :]
    out_refs, rest_ref, xv, bv, acc, pieces, x_sems, b_sems, prev_sems, rest_sems, out_sems = refs[:4], *refs[4:]
    quarter = bv.shape[2]
    half = quarter // 2
    low = quarter // 2
    band = quarter // LANES
    is_end = meta_ref[0]

    def offset_of(p, g):
        return meta_ref[5 + 2 * p + g]

    x_loads = x_copies(x_refs, xv, x_sems, offset_of)
    middle = pltpu.make_async_copy(middle_ref, bv.at[0], b_sems.at[0])
    end = pltpu.make_async_copy(end_ref, bv.at[0], b_sems.at[0])
    second = pltpu.make_async_copy(second_ref, bv.at[1], b_sems.at[1])
    prev = [
        pltpu.make_async_copy(prev_ref.at[g], acc.at[g, :, low : low + quarter], prev_sems.at[g]) for g in range(2)
    ]
    at = pl.multiple_of((meta_ref[4] + band // 2) * LANES, LANES)
    rest = [
        pltpu.make_async_copy(acc.at[g, :, pl.ds(at, rest_ref.shape[2])], rest_ref.at[g], rest_sems.at[g])
        for g in range(2)
    ]

    @pl.when(is_end == 0)
    def _():
        middle.start()
        second.start()

    pl.when(is_end != 0)(end.start)

    def rows_loads(g):
        return [prev[g]] + [copy for (_, r), copy in x_loads.items() if r // (PARTS // 2) == g]

    for g in range(2):
        for copy in rows_loads(g):
            copy.start()

    def wait_for(g):
        for copy in rows_loads(g):
            copy.wait()
        if g == 0:

            @pl.when(is_end == 0)
            def _():
                middle.wait()
                second.wait()

            pl.when(is_end != 0)(end.wait)

    def add(g):
        for p in range(2):
            add_product(acc, xv[p, g], bv[0, :, p * half : (p + 1) * half], g, offset_of(p, g) + meta_ref[1])

        @pl.when(is_end == 0)
        def _():
            for p in range(2):
                add_product(acc, xv[p, g], bv[1, :, p * half : (p + 1) * half], g, offset_of(p, g) + meta_ref[2])

    finish(acc, wait_for, add, meta_ref[3] + band // 2, out_refs, pieces, out_sems, rest)


def half_products(meta, xs, prev, middle, end, second, n_done):
    rows = PARTS // 4 * xs[0].shape[0]
    panel, quarter = second.shape
    any_spec = pl.BlockSpec(memory_space=pl.ANY)
    x_spec = pl.BlockSpec(memory_space=pltpu.HBM)
    n_rest = quarter // LANES - n_done
    return pl.pallas_call(
        half_kernel,
        out_shape=[jax.ShapeDtypeStruct((rows, n_done * LANES), jnp.bfloat16)] * 4
        + [jax.ShapeDtypeStruct((2, 2 * rows, n_rest * LANES), jnp.float32)],
        in_specs=[pl.BlockSpec(memory_space=pltpu.SMEM)] + [x_spec] * PARTS + [any_spec] * 4,
        out_specs=[any_spec] * 5,
        scratch_shapes=[
            pltpu.VMEM((2, 2, 2 * rows, panel), jnp.bfloat16),
            pltpu.VMEM((2, panel, quarter), jnp.bfloat16),
            pltpu.VMEM((2, 2 * rows, 2 * quarter), jnp.float32),
            pltpu.VMEM((4, rows, n_done * LANES), jnp.bfloat16),
            pltpu.SemaphoreType.DMA((2, PARTS)),
            pltpu.SemaphoreType.DMA((2,)),
            pltpu.SemaphoreType.DMA((2,)),
            pltpu.SemaphoreType.DMA((2,)),
            pltpu.SemaphoreType.DMA((4,)),
        ],
        compiler_params=pltpu.CompilerParams(vmem_limit_bytes=59 * MIB),
        cost_estimate=SMALL,
        name="half_products",
    )(meta, *xs, prev, middle, end, second)


def rest_kernel(meta_ref, *refs):
    x_refs, (rest_ref, b_ref), refs = refs[:PARTS], refs[PARTS : PARTS + 2], refs[PARTS + 2 :]
    out_refs, xv, bv, acc, pieces, x_sems, b_sem, rest_sems, out_sems = refs[:4], *refs[4:]
    band = acc.shape[2] // (2 * LANES)
    half = bv.shape[1] // 2
    is_end = meta_ref[0]

    def offset_of(p, g):
        return meta_ref[3 + 2 * p + g]

    at = pl.multiple_of((meta_ref[2] + band // 2) * LANES, LANES)
    rest = [
        pltpu.make_async_copy(rest_ref.at[g], acc.at[g, :, pl.ds(at, rest_ref.shape[2])], rest_sems.at[g])
        for g in range(2)
    ]
    x_loads = x_copies(x_refs, xv, x_sems, offset_of)
    b_copy = pltpu.make_async_copy(b_ref, bv, b_sem)

    def x_loads_of(g):
        return [copy for (_, r), copy in x_loads.items() if r // (PARTS // 2) == g]

    pl.when(is_end != 0)(b_copy.start)
    for g in range(2):
        rest[g].start()

        @pl.when(is_end != 0)
        def _():
            for copy in x_loads_of(g):
                copy.start()

    def wait_for(g):
        rest[g].wait()

        @pl.when(is_end != 0)
        def _():
            for copy in x_loads_of(g):
                copy.wait()
            if g == 0:
                b_copy.wait()

    def add(g):
        @pl.when(is_end != 0)
        def _():
            for p in range(2):
                add_product(acc, xv[p, g], bv[:, p * half : (p + 1) * half], g, offset_of(p, g) + meta_ref[1])

    finish(acc, wait_for, add, meta_ref[2] + band // 2, out_refs, pieces, out_sems)


def rest_products(meta, xs, rest, b, quarter):
    rows = PARTS // 4 * xs[0].shape[0]
    panel = b.shape[0]
    width = rest.shape[2]
    any_spec = pl.BlockSpec(memory_space=pl.ANY)
    x_spec = pl.BlockSpec(memory_space=pltpu.HBM)
    return pl.pallas_call(
        rest_kernel,
        out_shape=[jax.ShapeDtypeStruct((rows, width), jnp.bfloat16)] * 4,
        in_specs=[pl.BlockSpec(memory_space=pltpu.SMEM)] + [x_spec] * PARTS + [any_spec] * 2,
        out_specs=[any_spec] * 4,
        scratch_shapes=[
            pltpu.VMEM((2, 2, 2 * rows, panel), jnp.bfloat16),
            pltpu.VMEM(b.shape, jnp.bfloat16),
            pltpu.VMEM((2, 2 * rows, 2 * quarter), jnp.float32),
            pltpu.VMEM((4, rows, width), jnp.bfloat16),
            pltpu.SemaphoreType.DMA((2, PARTS)),
            pltpu.SemaphoreType.DMA,
            pltpu.SemaphoreType.DMA((2,)),
            pltpu.SemaphoreType.DMA((4,)),
        ],
        compiler_params=pltpu.CompilerParams(vmem_limit_bytes=59 * MIB),
        cost_estimate=SMALL,
        name="rest_products",
    )(meta, *xs, rest, b)


def assemble_kernel(place_ref, mask_ref, *refs):
    n = 4
    pieces, (out_ref, made, sem) = refs[:n], refs[-3:]
    steps = mask_ref.shape[0]
    rows = made.shape[0] // steps
    panel = n * LANES
    first = pl.multiple_of(place_ref[1] * panel, panel)
    for r in range(n):
        t = jnp.bitwise_xor(place_ref[0], r)
        for j in range(made.shape[1] // panel):
            to = pl.multiple_of(j * panel + t * LANES, LANES)
            for i in range(steps):
                keep = mask_ref[i, :, pl.ds(pl.multiple_of(first + to, LANES), LANES)]
                value = pieces[r][i * rows : (i + 1) * rows, j * LANES : (j + 1) * LANES].astype(jnp.float32)
                made[i * rows : (i + 1) * rows, pl.ds(to, LANES)] = (value * keep).astype(jnp.bfloat16)
    copy = pltpu.make_async_copy(made, out_ref.at[:, pl.ds(first, made.shape[1])], sem)
    copy.start()
    copy.wait()


def assembled(place, keep_wide, pieces, out=None):
    rows, width = pieces[0].shape
    cols = keep_wide.shape[2]
    vmem_spec = pl.BlockSpec(memory_space=pltpu.VMEM)
    any_spec = pl.BlockSpec(memory_space=pltpu.HBM)
    operands = [place, keep_wide, *pieces] + ([] if out is None else [out])
    return pl.pallas_call(
        assemble_kernel,
        out_shape=jax.ShapeDtypeStruct((rows, cols), jnp.bfloat16),
        in_specs=[pl.BlockSpec(memory_space=pltpu.SMEM)] + [vmem_spec] * 5 + [any_spec] * (len(operands) - 6),
        out_specs=any_spec,
        scratch_shapes=[pltpu.VMEM((rows, width * len(pieces)), jnp.bfloat16), pltpu.SemaphoreType.DMA],
        input_output_aliases={} if out is None else {6: 0},
        compiler_params=pltpu.CompilerParams(vmem_limit_bytes=16 * MIB),
        cost_estimate=SMALL,
        name="assembled",
    )(*operands)


def widen(mask, block):
    rows, cols = mask.shape
    wide = jnp.broadcast_to(mask.astype(jnp.float32)[:, :, None], (rows, cols, block))
    return wide.reshape(rows, 1, cols * block)


def together(*values):
    return lax.optimization_barrier(values)


def pairs_in_line(x_band, w_band, a_mask, keep_mask):
    panel = x_band.shape[0]
    block = panel // a_mask.shape[0]
    g, c = lax.axis_index("grid"), lax.axis_index("depth")
    z, y = g // 2, g % 2
    left = z < 2
    is_end = ((z == 0) | (z == 3)).astype(jnp.int32)
    toward = jnp.where(left, 1, -1)
    q = 2 * y + c

    swap = [(0, 2), (1, 3), (2, 0), (3, 1), (4, 6), (5, 7), (6, 4), (7, 5)]
    outward = [(2, 0), (3, 1), (4, 6), (5, 7)]
    cross = [(2, 4), (3, 5), (4, 2), (5, 3)]
    across = [(i, i ^ 1) for i in range(8)]
    layers = [(0, 1), (1, 0)]
    opposite = [(i, i ^ 3) for i in range(16)]

    def line(value, pairs):
        return lax.ppermute(value, "grid", pairs)

    first_out, second_out = jnp.where(left, 0, 4), jnp.where(left, 4, 0)
    first_in, second_in = second_out, first_out
    last_in = jnp.where(left, 1, 4)

    (sent_b,) = b_strips(w_band, [q ^ 2], 58)
    own_b = line(sent_b, across)
    sent_b, w_band = together(sent_b, w_band)
    (own_a,) = b_strips(w_band, [q], 48)
    swap_a = line(own_a, swap)
    cross_a = line(own_a, cross)
    mask_wide = widen(a_mask, block)
    rows = a_mask.shape[0]
    x_mine = [masked_rows(x_band, mask_wide, c * rows // 2 + k * rows // 4, rows // 4) for k in range(2)]
    own_b, *x_mine = together(own_b, *x_mine)
    own_b, swap_a = together(own_b, swap_a)
    swap_b = line(own_b, swap)
    cross_b = line(own_b, cross)
    x_across = [line(part, across) for part in x_mine]
    x_rest = [masked_rows(x_band, mask_wide, (1 - c) * rows // 2 + k * rows // 4, rows // 4) for k in range(2)]

    mid_a = line(cross_a[:, 5 * LANES :], outward)
    mid_b, fwd_first = packed(
        [y, first_out],
        [cross_a, cross_b, swap_a, swap_b],
        [10, 8],
        [
            (0, 0, 3, 0, 0, (0, 0)),
            (1, 0, 3, 0, 0, (0, 1)),
            (0, 3, 2, 0, 3, None),
            (1, 3, 5, 0, 5, None),
            (2, (1,), 4, 1, 0, None),
            (3, (1,), 4, 1, 4, None),
        ],
    )
    (fwd_second,) = packed([second_out], [swap_a, swap_b], [8], [(0, (0,), 4, 0, 0, None), (1, (0,), 4, 0, 4, None)])
    mid_a, mid_b, fwd_first = together(mid_a, mid_b, fwd_first)
    mid_b = line(mid_b, outward)
    fwd_first = line(fwd_first, cross)
    fwd_first, fwd_second, *x_across = together(fwd_first, fwd_second, *x_across)
    far_first = line(fwd_first, outward)
    fwd_second = line(fwd_second, cross)
    x_opposite = [lax.ppermute(part, "depth", layers) for part in x_across]
    xs = x_mine + x_rest + x_across + x_opposite

    def offsets(delta):
        tilt = 2 * y - 1
        return [(2 * delta + 4) % 8, (2 * delta + tilt + 4) % 8, (2 * delta - tilt + 4) % 8, (2 * delta + 4) % 8]

    zero = jnp.zeros_like(z)
    third = offsets(jnp.where(is_end == 1, 2, -toward))
    fourth = offsets(jnp.where(is_end == 1, -toward, 2))
    meta = jnp.stack([is_end, 4 + y, *offsets(zero), *offsets(toward), *third]).astype(jnp.int32)
    plan = [
        (0, [(0, 0, 8, 0, 0)]),
        (1, [(1, 0, 8, 0, 1)]),
        (2, [(4, 0, 8, 0, 2)]),
        (3, [(5, 0, 8, 0, 3)]),
        (4, [(6, 0, 3, 0, None), (6, 3, 2, 3, 4), (7, 0, 3, 5, 4)]),
        (5, [(6, 5, 5, 3, 5)]),
    ]
    total = whole_products(meta, xs, [own_a, own_b, cross_a, cross_b, swap_a, swap_b, mid_b, mid_a], plan)
    last_at = jnp.where(left, 1, 0)
    total, last_at = together(total, last_at)
    (last,) = packed(
        [last_at, last_at + 4], [fwd_second], [6], [(0, (0,), 3, 0, 0, None), (0, (1,), 3, 0, 3, None)]
    )
    far_second = line(last, outward)

    def exchanged(pieces):
        return [
            pieces[0],
            lax.ppermute(pieces[1], "depth", layers),
            line(pieces[2], across),
            lax.ppermute(pieces[3], ("grid", "depth"), opposite),
        ]

    done_at, rest_at = jnp.where(left, 3, 0), jnp.where(left, 0, 5)
    meta = jnp.stack([is_end, first_in, second_in, done_at, rest_at, *fourth]).astype(jnp.int32)
    *done, rest = half_products(meta, xs, total, fwd_first, far_first, fwd_second, 5)
    done = exchanged(done)
    far_second, done[1] = together(far_second, done[1])
    keep_wide = widen(keep_mask, block)
    out = assembled(jnp.stack([q, done_at]).astype(jnp.int32), keep_wide, done)
    meta = jnp.stack([is_end, last_in, rest_at, *fourth]).astype(jnp.int32)
    rest = exchanged(rest_products(meta, xs, rest, far_second, own_a.shape[1]))
    return assembled(jnp.stack([q, rest_at]).astype(jnp.int32), keep_wide, rest, out)


def solution(mesh):
    placed = (
        P(("groups", "grid"), None),
        P(("groups", "grid"), None),
        P(("groups", "grid"), None),
        P(("groups", "grid", "depth"), None),
    )

    def local(x_band, w_band, a_mask, keep_mask):
        panel, cols = x_band.shape
        pairs = mesh.shape["grid"] == 8 and mesh.shape["depth"] == 2
        pairs = pairs and cols == 8 * panel and panel == 4 * LANES
        return (pairs_in_line if pairs else ring)(x_band, w_band, a_mask, keep_mask)

    return jax.shard_map(
        local,
        mesh=mesh,
        in_specs=placed,
        out_specs=P(("groups", "grid", "depth"), None),
        check_vma=False,
    )
```

```python
import functools

import jax
import jax.numpy as jnp
from jax import lax
from jax.experimental import pallas as pl
from jax.experimental.pallas import tpu as pltpu
from jax.sharding import PartitionSpec as P

LANES = 128
MIB = 1 << 20
SMALL = pl.CostEstimate(flops=1000, bytes_accessed=1000, transcendentals=0)


def shifted(shard, axis, by):
    count = lax.axis_size(axis)
    return lax.ppermute(shard, axis, [(i, (i + by) % count) for i in range(count)])


def expand_blocks(mask, block):
    rows, cols = mask.shape
    wide = jnp.broadcast_to(mask[:, None, :, None], (rows, block, cols, block))
    return wide.reshape(rows * block, cols * block)


def ring(x_band, w_band, a_mask, keep_mask):
    panel = x_band.shape[0]
    block = panel // a_mask.shape[0]
    band_cols = x_band.shape[1]
    xm = x_band * expand_blocks(a_mask, block).astype(jnp.bfloat16)
    rows = lax.broadcasted_iota(jnp.int32, x_band.shape, 0)
    cols = lax.broadcasted_iota(jnp.int32, x_band.shape, 1)
    identity = jnp.where(cols == rows + 4 * panel, 1.0, 0.0).astype(jnp.float32)
    b_panel = (1.5 * identity - 0.5 * w_band.astype(jnp.float32)).astype(jnp.bfloat16)
    layer = lax.axis_index("depth")
    current = shifted(b_panel, ("grid", "depth"), -5)
    wide = jnp.zeros((panel, 2 * band_cols), jnp.float32)
    for step in range(4):
        offset = 6 + layer - 2 * step
        ablock = lax.dynamic_slice_in_dim(xm, offset * panel, panel, 1)
        term = jnp.dot(ablock, current, preferred_element_type=jnp.float32)
        region = lax.dynamic_slice_in_dim(wide, offset * panel, band_cols, 1)
        wide = lax.dynamic_update_slice_in_dim(wide, region + term, offset * panel, 1)
        if step < 3:
            current = shifted(current, "grid", 2)
    partial_band = wide[:, 4 * panel : 12 * panel]
    mine = lax.psum_scatter(partial_band, "depth", scatter_dimension=0, tiled=True)
    keep = expand_blocks(keep_mask, block).astype(jnp.float32)
    return (mine * keep).astype(jnp.bfloat16)


def strips_kernel(quarter_ref, w_ref, b_ref, held, made, in_sems, out_sems):
    panel, width = held.shape
    quarter = quarter_ref[0]

    def strip(j):
        return slice(j * LANES, (j + 1) * LANES)

    def load(j):
        at = pl.multiple_of(j * panel + quarter * LANES, LANES)
        return pltpu.make_async_copy(w_ref.at[:, pl.ds(at, LANES)], held.at[:, strip(j)], in_sems.at[j])

    def give(j):
        return pltpu.make_async_copy(made.at[:, strip(j)], b_ref.at[:, strip(j)], out_sems.at[j])

    band = width // LANES
    for j in range(band):
        load(j).start()
    for j in range(band):
        load(j).wait()
        value = -0.5 * held[:, strip(j)].astype(jnp.float32)
        if j == band // 2:
            rows = lax.broadcasted_iota(jnp.int32, value.shape, 0)
            cols = lax.broadcasted_iota(jnp.int32, value.shape, 1)
            value = value + jnp.where(rows == cols + quarter * LANES, 1.5, 0.0)
        made[:, strip(j)] = value.astype(jnp.bfloat16)
        give(j).start()
    for j in range(band):
        give(j).wait()


def b_strips(w_band, quarter, limit):
    panel = w_band.shape[0]
    band = w_band.shape[1] // panel
    shape = (panel, band * LANES)
    return pl.pallas_call(
        strips_kernel,
        out_shape=jax.ShapeDtypeStruct(shape, jnp.bfloat16),
        in_specs=[
            pl.BlockSpec(memory_space=pltpu.SMEM),
            pl.BlockSpec(memory_space=pltpu.HBM),
        ],
        out_specs=pl.BlockSpec(memory_space=pl.ANY),
        scratch_shapes=[
            pltpu.VMEM(shape, jnp.bfloat16),
            pltpu.VMEM(shape, jnp.bfloat16),
            pltpu.SemaphoreType.DMA((band,)),
            pltpu.SemaphoreType.DMA((band,)),
        ],
        compiler_params=pltpu.CompilerParams(vmem_limit_bytes=limit * MIB),
        cost_estimate=SMALL,
        name="b_strips",
    )(quarter.reshape(1), w_band)


def pack_kernel(plan, n_in, meta_ref, *refs):
    sources, outs, sems = refs[:n_in], refs[n_in:-1], refs[-1]

    def on_each(do):
        for k, (source, start, count, out, to, when) in enumerate(plan):
            at = start * LANES if isinstance(start, int) else pl.multiple_of(meta_ref[start[0]] * LANES, LANES)
            copy = pltpu.make_async_copy(
                sources[source].at[:, pl.ds(at, count * LANES)],
                outs[out].at[:, to * LANES : (to + count) * LANES],
                sems.at[k],
            )
            if when is None:
                do(copy)
            else:
                pl.when(meta_ref[when[0]] == when[1])(functools.partial(do, copy))

    on_each(lambda copy: copy.start())
    on_each(lambda copy: copy.wait())


def packed(meta, sources, widths, plan):
    rows = sources[0].shape[0]
    any_spec = pl.BlockSpec(memory_space=pl.ANY)
    return pl.pallas_call(
        functools.partial(pack_kernel, plan, len(sources)),
        out_shape=[jax.ShapeDtypeStruct((rows, width * LANES), jnp.bfloat16) for width in widths],
        in_specs=[pl.BlockSpec(memory_space=pltpu.SMEM)] + [any_spec] * len(sources),
        out_specs=[pl.BlockSpec(memory_space=pltpu.VMEM)] * len(widths),
        scratch_shapes=[pltpu.SemaphoreType.DMA((len(plan),))],
        compiler_params=pltpu.CompilerParams(vmem_limit_bytes=40 * MIB),
        cost_estimate=SMALL,
        name="packed",
    )(jnp.stack(meta).astype(jnp.int32), *sources)


def mask_kernel(first_ref, mask_ref, x_ref, out_ref):
    out_ref[...] = (x_ref[...].astype(jnp.float32) * mask_ref[0]).astype(jnp.bfloat16)


def masked_rows(x_band, mask_wide, first, count):
    block = x_band.shape[0] // mask_wide.shape[0]
    cols = x_band.shape[1]
    return pl.pallas_call(
        mask_kernel,
        grid_spec=pltpu.PrefetchScalarGridSpec(
            num_scalar_prefetch=1,
            grid=(count,),
            in_specs=[
                pl.BlockSpec((1, 1, cols), lambda i, f: (f[0] + i, 0, 0)),
                pl.BlockSpec((block, cols), lambda i, f: (f[0] + i, 0)),
            ],
            out_specs=pl.BlockSpec((block, cols), lambda i, f: (i, 0)),
        ),
        out_shape=jax.ShapeDtypeStruct((count * block, cols), jnp.bfloat16),
        compiler_params=pltpu.CompilerParams(vmem_limit_bytes=58 * MIB),
        cost_estimate=SMALL,
        name="masked_rows",
    )(first.reshape(1), mask_wide, x_band)


PARTS = 8


def x_copies(x_refs, xv, sems, offset_of):
    n_b, _, rows, panel = xv.shape
    part = 2 * rows // PARTS
    copies = {}
    for p in range(n_b):
        for r in range(PARTS):
            g, k = divmod(r, PARTS // 2)
            at = pl.multiple_of(offset_of(p, g) * panel, panel)
            copies[p, r] = pltpu.make_async_copy(
                x_refs[r].at[:, pl.ds(at, panel)],
                xv.at[p, g, k * part : (k + 1) * part],
                sems.at[p, r],
            )
    return copies


def add_product(acc, x, strips, g, first):
    cols = pl.ds(pl.multiple_of(first * LANES, LANES), strips.shape[1])
    acc[g, :, cols] += jnp.dot(x, strips, preferred_element_type=jnp.float32)


def whole_kernel(plan, meta_ref, *refs):
    n_b = len(plan)
    x_refs, refs = refs[:PARTS], refs[PARTS:]
    b_refs, (out_ref, xv, bv, acc, x_sems, b_sems, out_sems) = refs[:-7], refs[-7:]
    quarter = bv.shape[2]
    low = quarter // 2
    is_end = meta_ref[0]

    def offset_of(p, g):
        return meta_ref[2 + 2 * p + g]

    def b_middle(p):
        return [pltpu.make_async_copy(b_refs[plan[p][0]].at[:, :quarter], bv.at[p], b_sems.at[p, 0])]

    def b_end(p):
        copies = []
        for k, (operand, first, count, at, to) in enumerate(plan[p][1]):
            to = meta_ref[1] if to is None else to
            source = b_refs[operand].at[:, first * LANES : (first + count) * LANES]
            copies.append(pltpu.make_async_copy(source, bv.at[to, :, at * LANES : (at + count) * LANES], b_sems.at[p, k]))
        return copies

    def on_each(p, do):
        @pl.when(is_end == 0)
        def _():
            for copy in b_middle(p):
                do(copy)

        @pl.when(is_end != 0)
        def _():
            for copy in b_end(p):
                do(copy)

    copies = x_copies(x_refs, xv, x_sems, offset_of)
    for p in range(n_b):
        on_each(p, lambda copy: copy.start())
        for r in range(PARTS):
            copies[p, r].start()
    acc[...] = jnp.zeros_like(acc)
    for p in range(n_b):
        for k in [p] if p < n_b - 2 else range(n_b - 2, n_b) if p == n_b - 2 else []:
            on_each(k, lambda copy: copy.wait())
        for r in range(PARTS):
            copies[p, r].wait()

        def step(g, carry):
            add_product(acc, xv[p, g], bv[p], g, offset_of(p, g))
            return carry

        lax.fori_loop(0, 2, step, 0)
    outs = [
        pltpu.make_async_copy(acc.at[g, :, low : low + quarter], out_ref.at[g], out_sems.at[g]) for g in range(2)
    ]
    for out in outs:
        out.start()
    for out in outs:
        out.wait()


def whole_products(meta, xs, operands, plan):
    rows = PARTS // 4 * xs[0].shape[0]
    panel, quarter = operands[plan[0][0]].shape
    n_b = len(plan)
    any_spec = pl.BlockSpec(memory_space=pl.ANY)
    x_spec = pl.BlockSpec(memory_space=pltpu.HBM)
    return pl.pallas_call(
        functools.partial(whole_kernel, plan),
        out_shape=jax.ShapeDtypeStruct((2, 2 * rows, quarter), jnp.float32),
        in_specs=[pl.BlockSpec(memory_space=pltpu.SMEM)] + [x_spec] * PARTS + [any_spec] * len(operands),
        out_specs=any_spec,
        scratch_shapes=[
            pltpu.VMEM((n_b, 2, 2 * rows, panel), jnp.bfloat16),
            pltpu.VMEM((n_b, panel, quarter), jnp.bfloat16),
            pltpu.VMEM((2, 2 * rows, 2 * quarter), jnp.float32),
            pltpu.SemaphoreType.DMA((n_b, PARTS)),
            pltpu.SemaphoreType.DMA((n_b, 3)),
            pltpu.SemaphoreType.DMA((2,)),
        ],
        compiler_params=pltpu.CompilerParams(vmem_limit_bytes=59 * MIB),
        cost_estimate=SMALL,
        name="whole_products",
    )(meta, *xs, *operands)


def finish(acc, wait_for, add, at, out_refs, pieces, sems, also=None):
    half, width = out_refs[0].shape
    cols = pl.ds(pl.multiple_of(at * LANES, LANES), width)
    outs = [pltpu.make_async_copy(pieces.at[r], out_refs[r], sems.at[r]) for r in range(4)]
    also = also or []

    def step(g, carry):
        for k in range(2):
            pl.when(g == k)(functools.partial(wait_for, k))
        add(g)
        for k in range(2):

            @pl.when(g == k)
            def _():
                for copy in also[k : k + 1]:
                    copy.start()
                for r in range(2 * k, 2 * k + 2):
                    rows = slice((r % 2) * half, (r % 2 + 1) * half)
                    pieces[r] = acc[k, rows, cols].astype(jnp.bfloat16)
                    outs[r].start()

        return carry

    lax.fori_loop(0, 2, step, 0)
    for copy in outs + also:
        copy.wait()


def half_kernel(meta_ref, *refs):
    x_refs, (prev_ref, middle_ref, end_ref, second_ref), refs = refs[:PARTS], refs[PARTS : PARTS + 4], refs[PARTS + 4 :]
    out_refs, rest_ref, xv, bv, acc, pieces, x_sems, b_sems, prev_sems, rest_sems, out_sems = refs[:4], *refs[4:]
    quarter = bv.shape[2]
    half = quarter // 2
    low = quarter // 2
    band = quarter // LANES
    is_end = meta_ref[0]

    def offset_of(p, g):
        return meta_ref[5 + 2 * p + g]

    x_loads = x_copies(x_refs, xv, x_sems, offset_of)
    middle = pltpu.make_async_copy(middle_ref, bv.at[0], b_sems.at[0])
    end = pltpu.make_async_copy(end_ref, bv.at[0], b_sems.at[0])
    second = pltpu.make_async_copy(second_ref, bv.at[1], b_sems.at[1])
    prev = [
        pltpu.make_async_copy(prev_ref.at[g], acc.at[g, :, low : low + quarter], prev_sems.at[g]) for g in range(2)
    ]
    at = pl.multiple_of((meta_ref[4] + band // 2) * LANES, LANES)
    rest = [
        pltpu.make_async_copy(acc.at[g, :, pl.ds(at, rest_ref.shape[2])], rest_ref.at[g], rest_sems.at[g])
        for g in range(2)
    ]

    @pl.when(is_end == 0)
    def _():
        middle.start()
        second.start()

    pl.when(is_end != 0)(end.start)

    def rows_loads(g):
        return [prev[g]] + [copy for (_, r), copy in x_loads.items() if r // (PARTS // 2) == g]

    for g in range(2):
        for copy in rows_loads(g):
            copy.start()

    def wait_for(g):
        for copy in rows_loads(g):
            copy.wait()
        if g == 0:

            @pl.when(is_end == 0)
            def _():
                middle.wait()
                second.wait()

            pl.when(is_end != 0)(end.wait)

    def add(g):
        for p in range(2):
            add_product(acc, xv[p, g], bv[0, :, p * half : (p + 1) * half], g, offset_of(p, g) + meta_ref[1])

        @pl.when(is_end == 0)
        def _():
            for p in range(2):
                add_product(acc, xv[p, g], bv[1, :, p * half : (p + 1) * half], g, offset_of(p, g) + meta_ref[2])

    finish(acc, wait_for, add, meta_ref[3] + band // 2, out_refs, pieces, out_sems, rest)


def half_products(meta, xs, prev, middle, end, second, n_done):
    rows = PARTS // 4 * xs[0].shape[0]
    panel, quarter = second.shape
    any_spec = pl.BlockSpec(memory_space=pl.ANY)
    x_spec = pl.BlockSpec(memory_space=pltpu.HBM)
    n_rest = quarter // LANES - n_done
    return pl.pallas_call(
        half_kernel,
        out_shape=[jax.ShapeDtypeStruct((rows, n_done * LANES), jnp.bfloat16)] * 4
        + [jax.ShapeDtypeStruct((2, 2 * rows, n_rest * LANES), jnp.float32)],
        in_specs=[pl.BlockSpec(memory_space=pltpu.SMEM)] + [x_spec] * PARTS + [any_spec] * 4,
        out_specs=[any_spec] * 5,
        scratch_shapes=[
            pltpu.VMEM((2, 2, 2 * rows, panel), jnp.bfloat16),
            pltpu.VMEM((2, panel, quarter), jnp.bfloat16),
            pltpu.VMEM((2, 2 * rows, 2 * quarter), jnp.float32),
            pltpu.VMEM((4, rows, n_done * LANES), jnp.bfloat16),
            pltpu.SemaphoreType.DMA((2, PARTS)),
            pltpu.SemaphoreType.DMA((2,)),
            pltpu.SemaphoreType.DMA((2,)),
            pltpu.SemaphoreType.DMA((2,)),
            pltpu.SemaphoreType.DMA((4,)),
        ],
        compiler_params=pltpu.CompilerParams(vmem_limit_bytes=59 * MIB),
        cost_estimate=SMALL,
        name="half_products",
    )(meta, *xs, prev, middle, end, second)


def rest_kernel(meta_ref, *refs):
    x_refs, (rest_ref, b_ref), refs = refs[:PARTS], refs[PARTS : PARTS + 2], refs[PARTS + 2 :]
    out_refs, xv, bv, acc, pieces, x_sems, b_sem, rest_sems, out_sems = refs[:4], *refs[4:]
    band = acc.shape[2] // (2 * LANES)
    half = (bv.shape[1] - LANES) // 2
    is_end = meta_ref[0]

    def offset_of(p, g):
        return meta_ref[3 + 2 * p + g]

    at = pl.multiple_of((meta_ref[2] + band // 2) * LANES, LANES)
    rest = [
        pltpu.make_async_copy(rest_ref.at[g], acc.at[g, :, pl.ds(at, rest_ref.shape[2])], rest_sems.at[g])
        for g in range(2)
    ]
    x_loads = x_copies(x_refs, xv, x_sems, offset_of)
    b_copy = pltpu.make_async_copy(b_ref, bv, b_sem)

    def x_loads_of(g):
        return [copy for (_, r), copy in x_loads.items() if r // (PARTS // 2) == g]

    pl.when(is_end != 0)(b_copy.start)
    for g in range(2):
        rest[g].start()

        @pl.when(is_end != 0)
        def _():
            for copy in x_loads_of(g):
                copy.start()

    def wait_for(g):
        rest[g].wait()

        @pl.when(is_end != 0)
        def _():
            for copy in x_loads_of(g):
                copy.wait()
            if g == 0:
                b_copy.wait()

    def add(g):
        @pl.when(is_end != 0)
        def _():
            for p in range(2):
                add_product(acc, xv[p, g], bv[:, p * half : (p + 1) * half], g, offset_of(p, g) + meta_ref[1])
            p = meta_ref[8]
            add_product(acc, xv[p, g], bv[:, 2 * half :], g, offset_of(p, g) + meta_ref[7])

    finish(acc, wait_for, add, meta_ref[2] + band // 2, out_refs, pieces, out_sems)


def rest_products(meta, xs, rest, b, quarter):
    rows = PARTS // 4 * xs[0].shape[0]
    panel = b.shape[0]
    width = rest.shape[2]
    any_spec = pl.BlockSpec(memory_space=pl.ANY)
    x_spec = pl.BlockSpec(memory_space=pltpu.HBM)
    return pl.pallas_call(
        rest_kernel,
        out_shape=[jax.ShapeDtypeStruct((rows, width), jnp.bfloat16)] * 4,
        in_specs=[pl.BlockSpec(memory_space=pltpu.SMEM)] + [x_spec] * PARTS + [any_spec] * 2,
        out_specs=[any_spec] * 4,
        scratch_shapes=[
            pltpu.VMEM((2, 2, 2 * rows, panel), jnp.bfloat16),
            pltpu.VMEM(b.shape, jnp.bfloat16),
            pltpu.VMEM((2, 2 * rows, 2 * quarter), jnp.float32),
            pltpu.VMEM((4, rows, width), jnp.bfloat16),
            pltpu.SemaphoreType.DMA((2, PARTS)),
            pltpu.SemaphoreType.DMA,
            pltpu.SemaphoreType.DMA((2,)),
            pltpu.SemaphoreType.DMA((4,)),
        ],
        compiler_params=pltpu.CompilerParams(vmem_limit_bytes=59 * MIB),
        cost_estimate=SMALL,
        name="rest_products",
    )(meta, *xs, rest, b)


def assemble_kernel(place_ref, mask_ref, *refs):
    n = 4
    pieces, (out_ref, made, sem) = refs[:n], refs[-3:]
    steps = mask_ref.shape[0]
    rows = made.shape[0] // steps
    panel = n * LANES
    first = pl.multiple_of(place_ref[1] * panel, panel)
    for r in range(n):
        t = jnp.bitwise_xor(place_ref[0], r)
        for j in range(made.shape[1] // panel):
            to = pl.multiple_of(j * panel + t * LANES, LANES)
            for i in range(steps):
                keep = mask_ref[i, :, pl.ds(pl.multiple_of(first + to, LANES), LANES)]
                value = pieces[r][i * rows : (i + 1) * rows, j * LANES : (j + 1) * LANES].astype(jnp.float32)
                made[i * rows : (i + 1) * rows, pl.ds(to, LANES)] = (value * keep).astype(jnp.bfloat16)
    copy = pltpu.make_async_copy(made, out_ref.at[:, pl.ds(first, made.shape[1])], sem)
    copy.start()
    copy.wait()


def assembled(place, keep_wide, pieces, out=None):
    rows, width = pieces[0].shape
    cols = keep_wide.shape[2]
    vmem_spec = pl.BlockSpec(memory_space=pltpu.VMEM)
    any_spec = pl.BlockSpec(memory_space=pltpu.HBM)
    operands = [place, keep_wide, *pieces] + ([] if out is None else [out])
    return pl.pallas_call(
        assemble_kernel,
        out_shape=jax.ShapeDtypeStruct((rows, cols), jnp.bfloat16),
        in_specs=[pl.BlockSpec(memory_space=pltpu.SMEM)] + [vmem_spec] * 5 + [any_spec] * (len(operands) - 6),
        out_specs=any_spec,
        scratch_shapes=[pltpu.VMEM((rows, width * len(pieces)), jnp.bfloat16), pltpu.SemaphoreType.DMA],
        input_output_aliases={} if out is None else {6: 0},
        compiler_params=pltpu.CompilerParams(vmem_limit_bytes=16 * MIB),
        cost_estimate=SMALL,
        name="assembled",
    )(*operands)


def widen(mask, block):
    rows, cols = mask.shape
    wide = jnp.broadcast_to(mask.astype(jnp.float32)[:, :, None], (rows, cols, block))
    return wide.reshape(rows, 1, cols * block)


def together(*values):
    return lax.optimization_barrier(values)


def pairs_in_line(x_band, w_band, a_mask, keep_mask):
    panel = x_band.shape[0]
    block = panel // a_mask.shape[0]
    g, c = lax.axis_index("grid"), lax.axis_index("depth")
    z, y = g // 2, g % 2
    left = z < 2
    is_end = ((z == 0) | (z == 3)).astype(jnp.int32)
    toward = jnp.where(left, 1, -1)
    q = 2 * y + c

    swap = [(0, 2), (1, 3), (2, 0), (3, 1), (4, 6), (5, 7), (6, 4), (7, 5)]
    outward = [(2, 0), (3, 1), (4, 6), (5, 7)]
    cross = [(2, 4), (3, 5), (4, 2), (5, 3)]
    across = [(i, i ^ 1) for i in range(8)]
    layers = [(0, 1), (1, 0)]
    opposite = [(i, i ^ 3) for i in range(16)]

    def line(value, pairs):
        return lax.ppermute(value, "grid", pairs)

    first_out, second_out = jnp.where(left, 0, 4), jnp.where(left, 4, 0)
    first_in, second_in = second_out, first_out
    last_in = jnp.where(left, 2, 4)

    sent_b = b_strips(w_band, q ^ 2, 58)
    own_b = line(sent_b, across)
    sent_b, w_band = together(sent_b, w_band)
    own_a = b_strips(w_band, q, 58)
    swap_a = line(own_a, swap)
    cross_a = line(own_a, cross)
    mask_wide = widen(a_mask, block)
    rows = a_mask.shape[0]
    x_mine = [masked_rows(x_band, mask_wide, c * rows // 2 + k * rows // 4, rows // 4) for k in range(2)]
    own_b, *x_mine = together(own_b, *x_mine)
    own_b, swap_a = together(own_b, swap_a)
    swap_b = line(own_b, swap)
    cross_b = line(own_b, cross)
    x_across = [line(part, across) for part in x_mine]
    x_rest = [masked_rows(x_band, mask_wide, (1 - c) * rows // 2 + k * rows // 4, rows // 4) for k in range(2)]

    mid_a = line(cross_a[:, 5 * LANES :], outward)
    mid_b, fwd_first = packed(
        [y, first_out],
        [cross_a, cross_b, swap_a, swap_b],
        [10, 8],
        [
            (0, 0, 3, 0, 0, (0, 0)),
            (1, 0, 3, 0, 0, (0, 1)),
            (0, 3, 2, 0, 3, None),
            (1, 3, 5, 0, 5, None),
            (2, (1,), 4, 1, 0, None),
            (3, (1,), 4, 1, 4, None),
        ],
    )
    (fwd_second,) = packed([second_out], [swap_a, swap_b], [8], [(0, (0,), 4, 0, 0, None), (1, (0,), 4, 0, 4, None)])
    mid_a, mid_b, fwd_first = together(mid_a, mid_b, fwd_first)
    mid_b = line(mid_b, outward)
    fwd_first = line(fwd_first, cross)
    fwd_first, fwd_second, *x_across = together(fwd_first, fwd_second, *x_across)
    far_first = line(fwd_first, outward)
    fwd_second = line(fwd_second, cross)
    x_opposite = [lax.ppermute(part, "depth", layers) for part in x_across]
    xs = x_mine + x_rest + x_across + x_opposite

    def offsets(delta):
        tilt = 2 * y - 1
        return [(2 * delta + 4) % 8, (2 * delta + tilt + 4) % 8, (2 * delta - tilt + 4) % 8, (2 * delta + 4) % 8]

    zero = jnp.zeros_like(z)
    third = offsets(jnp.where(is_end == 1, 2, -toward))
    fourth = offsets(jnp.where(is_end == 1, -toward, 2))
    meta = jnp.stack([is_end, 4 + y, *offsets(zero), *offsets(toward), *third]).astype(jnp.int32)
    plan = [
        (0, [(0, 0, 8, 0, 0)]),
        (1, [(1, 0, 8, 0, 1)]),
        (2, [(4, 0, 8, 0, 2)]),
        (3, [(5, 0, 8, 0, 3)]),
        (4, [(6, 0, 3, 0, None), (6, 3, 2, 3, 4), (7, 0, 3, 5, 4)]),
        (5, [(6, 5, 5, 3, 5)]),
    ]
    total = whole_products(meta, xs, [own_a, own_b, cross_a, cross_b, swap_a, swap_b, mid_b, mid_a], plan)
    last_at = jnp.where(left, 2, 0)
    total, last_at = together(total, last_at)
    extra_in, extra_panel = jnp.where(left, 1, 6), jnp.where(left, 1 - y, y)
    extra_at = jnp.where(left, 1, 2) + 4 * extra_panel
    (last,) = packed(
        [last_at, last_at + 4, extra_at],
        [fwd_second],
        [5],
        [(0, (0,), 2, 0, 0, None), (0, (1,), 2, 0, 2, None), (0, (2,), 1, 0, 4, None)],
    )
    far_second = line(last, outward)

    def exchanged(pieces):
        return [
            pieces[0],
            lax.ppermute(pieces[1], "depth", layers),
            line(pieces[2], across),
            lax.ppermute(pieces[3], ("grid", "depth"), opposite),
        ]

    done_at, rest_at = jnp.where(left, 3, 0), jnp.where(left, 0, 5)
    meta = jnp.stack([is_end, first_in, second_in, done_at, rest_at, *fourth]).astype(jnp.int32)
    *done, rest = half_products(meta, xs, total, fwd_first, far_first, fwd_second, 5)
    done = exchanged(done)
    far_second, done[1] = together(far_second, done[1])
    keep_wide = widen(keep_mask, block)
    out = assembled(jnp.stack([q, done_at]).astype(jnp.int32), keep_wide, done)
    meta = jnp.stack([is_end, last_in, rest_at, *fourth, extra_in, extra_panel]).astype(jnp.int32)
    rest = exchanged(rest_products(meta, xs, rest, far_second, own_a.shape[1]))
    return assembled(jnp.stack([q, rest_at]).astype(jnp.int32), keep_wide, rest, out)


def solution(mesh):
    placed = (
        P(("groups", "grid"), None),
        P(("groups", "grid"), None),
        P(("groups", "grid"), None),
        P(("groups", "grid", "depth"), None),
    )

    def local(x_band, w_band, a_mask, keep_mask):
        panel, cols = x_band.shape
        pairs = mesh.shape["grid"] == 8 and mesh.shape["depth"] == 2
        pairs = pairs and cols == 8 * panel and panel == 4 * LANES
        return (pairs_in_line if pairs else ring)(x_band, w_band, a_mask, keep_mask)

    return jax.shard_map(
        local,
        mesh=mesh,
        in_specs=placed,
        out_specs=P(("groups", "grid", "depth"), None),
        check_vma=False,
    )
```

```python
import functools

import jax
import jax.numpy as jnp
from jax import lax
from jax.experimental import pallas as pl
from jax.experimental.pallas import tpu as pltpu
from jax.sharding import PartitionSpec as P

LANES = 128
MIB = 1 << 20
SMALL = pl.CostEstimate(flops=1000, bytes_accessed=1000, transcendentals=0)


def shifted(shard, axis, by):
    count = lax.axis_size(axis)
    return lax.ppermute(shard, axis, [(i, (i + by) % count) for i in range(count)])


def expand_blocks(mask, block):
    rows, cols = mask.shape
    wide = jnp.broadcast_to(mask[:, None, :, None], (rows, block, cols, block))
    return wide.reshape(rows * block, cols * block)


def ring(x_band, w_band, a_mask, keep_mask):
    panel = x_band.shape[0]
    block = panel // a_mask.shape[0]
    band_cols = x_band.shape[1]
    xm = x_band * expand_blocks(a_mask, block).astype(jnp.bfloat16)
    rows = lax.broadcasted_iota(jnp.int32, x_band.shape, 0)
    cols = lax.broadcasted_iota(jnp.int32, x_band.shape, 1)
    identity = jnp.where(cols == rows + 4 * panel, 1.0, 0.0).astype(jnp.float32)
    b_panel = (1.5 * identity - 0.5 * w_band.astype(jnp.float32)).astype(jnp.bfloat16)
    layer = lax.axis_index("depth")
    current = shifted(b_panel, ("grid", "depth"), -5)
    wide = jnp.zeros((panel, 2 * band_cols), jnp.float32)
    for step in range(4):
        offset = 6 + layer - 2 * step
        ablock = lax.dynamic_slice_in_dim(xm, offset * panel, panel, 1)
        term = jnp.dot(ablock, current, preferred_element_type=jnp.float32)
        region = lax.dynamic_slice_in_dim(wide, offset * panel, band_cols, 1)
        wide = lax.dynamic_update_slice_in_dim(wide, region + term, offset * panel, 1)
        if step < 3:
            current = shifted(current, "grid", 2)
    partial_band = wide[:, 4 * panel : 12 * panel]
    mine = lax.psum_scatter(partial_band, "depth", scatter_dimension=0, tiled=True)
    keep = expand_blocks(keep_mask, block).astype(jnp.float32)
    return (mine * keep).astype(jnp.bfloat16)


def strips_kernel(quarter_ref, w_ref, b_ref, held, made, in_sems, out_sems):
    panel, width = held.shape
    quarter = quarter_ref[0]

    def strip(j):
        return slice(j * LANES, (j + 1) * LANES)

    def load(j):
        at = pl.multiple_of(j * panel + quarter * LANES, LANES)
        return pltpu.make_async_copy(w_ref.at[:, pl.ds(at, LANES)], held.at[:, strip(j)], in_sems.at[j])

    def give(j):
        return pltpu.make_async_copy(made.at[:, strip(j)], b_ref.at[:, strip(j)], out_sems.at[j])

    band = width // LANES
    for j in range(band):
        load(j).start()
    for j in range(band):
        load(j).wait()
        value = -0.5 * held[:, strip(j)].astype(jnp.float32)
        if j == band // 2:
            rows = lax.broadcasted_iota(jnp.int32, value.shape, 0)
            cols = lax.broadcasted_iota(jnp.int32, value.shape, 1)
            value = value + jnp.where(rows == cols + quarter * LANES, 1.5, 0.0)
        made[:, strip(j)] = value.astype(jnp.bfloat16)
        give(j).start()
    for j in range(band):
        give(j).wait()


def b_strips(w_band, quarter, limit):
    panel = w_band.shape[0]
    band = w_band.shape[1] // panel
    shape = (panel, band * LANES)
    return pl.pallas_call(
        strips_kernel,
        out_shape=jax.ShapeDtypeStruct(shape, jnp.bfloat16),
        in_specs=[
            pl.BlockSpec(memory_space=pltpu.SMEM),
            pl.BlockSpec(memory_space=pltpu.HBM),
        ],
        out_specs=pl.BlockSpec(memory_space=pl.ANY),
        scratch_shapes=[
            pltpu.VMEM(shape, jnp.bfloat16),
            pltpu.VMEM(shape, jnp.bfloat16),
            pltpu.SemaphoreType.DMA((band,)),
            pltpu.SemaphoreType.DMA((band,)),
        ],
        compiler_params=pltpu.CompilerParams(vmem_limit_bytes=limit * MIB),
        cost_estimate=SMALL,
        name="b_strips",
    )(quarter.reshape(1), w_band)


def pack_kernel(plan, n_in, meta_ref, *refs):
    sources, outs, sems = refs[:n_in], refs[n_in:-1], refs[-1]

    def on_each(do):
        for k, (source, start, count, out, to, when) in enumerate(plan):
            at = start * LANES if isinstance(start, int) else pl.multiple_of(meta_ref[start[0]] * LANES, LANES)
            copy = pltpu.make_async_copy(
                sources[source].at[:, pl.ds(at, count * LANES)],
                outs[out].at[:, to * LANES : (to + count) * LANES],
                sems.at[k],
            )
            if when is None:
                do(copy)
            else:
                pl.when(meta_ref[when[0]] == when[1])(functools.partial(do, copy))

    on_each(lambda copy: copy.start())
    on_each(lambda copy: copy.wait())


def packed(meta, sources, widths, plan):
    rows = sources[0].shape[0]
    any_spec = pl.BlockSpec(memory_space=pl.ANY)
    return pl.pallas_call(
        functools.partial(pack_kernel, plan, len(sources)),
        out_shape=[jax.ShapeDtypeStruct((rows, width * LANES), jnp.bfloat16) for width in widths],
        in_specs=[pl.BlockSpec(memory_space=pltpu.SMEM)] + [any_spec] * len(sources),
        out_specs=[pl.BlockSpec(memory_space=pltpu.VMEM)] * len(widths),
        scratch_shapes=[pltpu.SemaphoreType.DMA((len(plan),))],
        compiler_params=pltpu.CompilerParams(vmem_limit_bytes=40 * MIB),
        cost_estimate=SMALL,
        name="packed",
    )(jnp.stack(meta).astype(jnp.int32), *sources)


def mask_kernel(first_ref, mask_ref, x_ref, out_ref):
    out_ref[...] = (x_ref[...].astype(jnp.float32) * mask_ref[0]).astype(jnp.bfloat16)


def masked_rows(x_band, mask_wide, first, count):
    block = x_band.shape[0] // mask_wide.shape[0]
    cols = x_band.shape[1]
    return pl.pallas_call(
        mask_kernel,
        grid_spec=pltpu.PrefetchScalarGridSpec(
            num_scalar_prefetch=1,
            grid=(count,),
            in_specs=[
                pl.BlockSpec((1, 1, cols), lambda i, f: (f[0] + i, 0, 0)),
                pl.BlockSpec((block, cols), lambda i, f: (f[0] + i, 0)),
            ],
            out_specs=pl.BlockSpec((block, cols), lambda i, f: (i, 0)),
        ),
        out_shape=jax.ShapeDtypeStruct((count * block, cols), jnp.bfloat16),
        compiler_params=pltpu.CompilerParams(vmem_limit_bytes=58 * MIB),
        cost_estimate=SMALL,
        name="masked_rows",
    )(first.reshape(1), mask_wide, x_band)


PARTS = 8


def x_copies(x_refs, xv, sems, offset_of):
    n_b, _, rows, panel = xv.shape
    part = 2 * rows // PARTS
    copies = {}
    for p in range(n_b):
        for r in range(PARTS):
            g, k = divmod(r, PARTS // 2)
            at = pl.multiple_of(offset_of(p, g) * panel, panel)
            copies[p, r] = pltpu.make_async_copy(
                x_refs[r].at[:, pl.ds(at, panel)],
                xv.at[p, g, k * part : (k + 1) * part],
                sems.at[p, r],
            )
    return copies


def add_product(acc, x, strips, g, first):
    cols = pl.ds(pl.multiple_of(first * LANES, LANES), strips.shape[1])
    acc[g, :, cols] += jnp.dot(x, strips, preferred_element_type=jnp.float32)


def whole_kernel(plan, meta_ref, *refs):
    n_b = len(plan)
    x_refs, refs = refs[:PARTS], refs[PARTS:]
    b_refs, (out_ref, xv, bv, acc, x_sems, b_sems, out_sems) = refs[:-7], refs[-7:]
    quarter = bv.shape[2]
    low = quarter // 2
    is_end = meta_ref[0]

    def offset_of(p, g):
        return meta_ref[2 + 2 * p + g]

    def b_middle(p):
        return [pltpu.make_async_copy(b_refs[plan[p][0]].at[:, :quarter], bv.at[p], b_sems.at[p, 0])]

    def b_end(p):
        copies = []
        for k, (operand, first, count, at, to) in enumerate(plan[p][1]):
            to = meta_ref[1] if to is None else to
            source = b_refs[operand].at[:, first * LANES : (first + count) * LANES]
            copies.append(pltpu.make_async_copy(source, bv.at[to, :, at * LANES : (at + count) * LANES], b_sems.at[p, k]))
        return copies

    def on_each(p, do):
        @pl.when(is_end == 0)
        def _():
            for copy in b_middle(p):
                do(copy)

        @pl.when(is_end != 0)
        def _():
            for copy in b_end(p):
                do(copy)

    copies = x_copies(x_refs, xv, x_sems, offset_of)
    for p in range(n_b):
        on_each(p, lambda copy: copy.start())
        for r in range(PARTS):
            copies[p, r].start()
    outs = [
        pltpu.make_async_copy(acc.at[g, :, low : low + quarter], out_ref.at[g], out_sems.at[g]) for g in range(2)
    ]

    def wait_for(p):
        for k in [p] if p < n_b - 2 else range(n_b - 2, n_b) if p == n_b - 2 else []:
            on_each(k, lambda copy: copy.wait())
        for r in range(PARTS):
            copies[p, r].wait()

    middle = quarter // LANES // 2

    def own(g, carry):
        acc[g, :, low : low + quarter] = jnp.dot(xv[g, g], bv[g], preferred_element_type=jnp.float32)
        return carry

    def step(i, carry):
        p = jnp.where(i < 4, i % 2, i // 2)
        g = jnp.where(i < 4, 1 - i % 2, i % 2)
        for k in range(2, n_b):
            pl.when(i == 2 * k)(functools.partial(wait_for, k))
        pl.when(i == 2 * n_b - 1)(outs[0].start)
        offset = offset_of(p, g)
        for k in range(2 * middle):
            if k == middle:
                continue
            first, last = max(0, middle - k), min(2 * middle, 3 * middle - k)

            @pl.when(offset == k)
            def _():
                strips = bv[p, :, first * LANES : last * LANES]
                acc[g, :, (k + first) * LANES : (k + last) * LANES] += jnp.dot(
                    xv[p, g], strips, preferred_element_type=jnp.float32
                )

        return carry

    for p in range(2):
        wait_for(p)
    lax.fori_loop(0, 2, own, 0)
    lax.fori_loop(2, 2 * n_b, step, 0)
    outs[1].start()
    for out in outs:
        out.wait()


def whole_products(meta, xs, operands, plan):
    rows = PARTS // 4 * xs[0].shape[0]
    panel, quarter = operands[plan[0][0]].shape
    n_b = len(plan)
    any_spec = pl.BlockSpec(memory_space=pl.ANY)
    x_spec = pl.BlockSpec(memory_space=pltpu.HBM)
    return pl.pallas_call(
        functools.partial(whole_kernel, plan),
        out_shape=jax.ShapeDtypeStruct((2, 2 * rows, quarter), jnp.float32),
        in_specs=[pl.BlockSpec(memory_space=pltpu.SMEM)] + [x_spec] * PARTS + [any_spec] * len(operands),
        out_specs=any_spec,
        scratch_shapes=[
            pltpu.VMEM((n_b, 2, 2 * rows, panel), jnp.bfloat16),
            pltpu.VMEM((n_b, panel, quarter), jnp.bfloat16),
            pltpu.VMEM((2, 2 * rows, 2 * quarter), jnp.float32),
            pltpu.SemaphoreType.DMA((n_b, PARTS)),
            pltpu.SemaphoreType.DMA((n_b, 3)),
            pltpu.SemaphoreType.DMA((2,)),
        ],
        compiler_params=pltpu.CompilerParams(vmem_limit_bytes=59 * MIB),
        cost_estimate=pl.CostEstimate(flops=6 * 10**9, bytes_accessed=36 * MIB, transcendentals=0),
        name="whole_products",
    )(meta, *xs, *operands)


def finish(acc, wait_for, add, at, out_refs, pieces, sems, also=None):
    half, width = out_refs[0].shape
    cols = pl.ds(pl.multiple_of(at * LANES, LANES), width)
    outs = [pltpu.make_async_copy(pieces.at[r], out_refs[r], sems.at[r]) for r in range(4)]
    also = also or []

    def step(g, carry):
        for k in range(2):
            pl.when(g == k)(functools.partial(wait_for, k))
        add(g)
        for k in range(2):

            @pl.when(g == k)
            def _():
                for copy in also[k : k + 1]:
                    copy.start()
                for r in range(2 * k, 2 * k + 2):
                    rows = slice((r % 2) * half, (r % 2 + 1) * half)
                    pieces[r] = acc[k, rows, cols].astype(jnp.bfloat16)
                    outs[r].start()

        return carry

    lax.fori_loop(0, 2, step, 0)
    for copy in outs + also:
        copy.wait()


def half_kernel(meta_ref, *refs):
    x_refs, (prev_ref, middle_ref, end_ref, second_ref), refs = refs[:PARTS], refs[PARTS : PARTS + 4], refs[PARTS + 4 :]
    out_refs, rest_ref, xv, bv, acc, pieces, x_sems, b_sems, prev_sems, rest_sems, out_sems = refs[:4], *refs[4:]
    quarter = bv.shape[2]
    half = quarter // 2
    low = quarter // 2
    band = quarter // LANES
    is_end = meta_ref[0]

    def offset_of(p, g):
        return meta_ref[5 + 2 * p + g]

    x_loads = x_copies(x_refs, xv, x_sems, offset_of)
    middle = pltpu.make_async_copy(middle_ref, bv.at[0], b_sems.at[0])
    end = pltpu.make_async_copy(end_ref, bv.at[0], b_sems.at[0])
    second = pltpu.make_async_copy(second_ref, bv.at[1], b_sems.at[1])
    prev = [
        pltpu.make_async_copy(prev_ref.at[g], acc.at[g, :, low : low + quarter], prev_sems.at[g]) for g in range(2)
    ]
    at = pl.multiple_of((meta_ref[4] + band // 2) * LANES, LANES)
    rest = [
        pltpu.make_async_copy(acc.at[g, :, pl.ds(at, rest_ref.shape[2])], rest_ref.at[g], rest_sems.at[g])
        for g in range(2)
    ]

    @pl.when(is_end == 0)
    def _():
        middle.start()
        second.start()

    pl.when(is_end != 0)(end.start)

    def rows_loads(g):
        return [prev[g]] + [copy for (_, r), copy in x_loads.items() if r // (PARTS // 2) == g]

    for g in range(2):
        for copy in rows_loads(g):
            copy.start()

    def wait_for(g):
        for copy in rows_loads(g):
            copy.wait()
        if g == 0:

            @pl.when(is_end == 0)
            def _():
                middle.wait()
                second.wait()

            pl.when(is_end != 0)(end.wait)

    def add(g):
        for p in range(2):
            add_product(acc, xv[p, g], bv[0, :, p * half : (p + 1) * half], g, offset_of(p, g) + meta_ref[1])

        @pl.when(is_end == 0)
        def _():
            for p in range(2):
                add_product(acc, xv[p, g], bv[1, :, p * half : (p + 1) * half], g, offset_of(p, g) + meta_ref[2])

    finish(acc, wait_for, add, meta_ref[3] + band // 2, out_refs, pieces, out_sems, rest)


def half_products(meta, xs, prev, middle, end, second, n_done):
    rows = PARTS // 4 * xs[0].shape[0]
    panel, quarter = second.shape
    any_spec = pl.BlockSpec(memory_space=pl.ANY)
    x_spec = pl.BlockSpec(memory_space=pltpu.HBM)
    n_rest = quarter // LANES - n_done
    return pl.pallas_call(
        half_kernel,
        out_shape=[jax.ShapeDtypeStruct((rows, n_done * LANES), jnp.bfloat16)] * 4
        + [jax.ShapeDtypeStruct((2, 2 * rows, n_rest * LANES), jnp.float32)],
        in_specs=[pl.BlockSpec(memory_space=pltpu.SMEM)] + [x_spec] * PARTS + [any_spec] * 4,
        out_specs=[any_spec] * 5,
        scratch_shapes=[
            pltpu.VMEM((2, 2, 2 * rows, panel), jnp.bfloat16),
            pltpu.VMEM((2, panel, quarter), jnp.bfloat16),
            pltpu.VMEM((2, 2 * rows, 2 * quarter), jnp.float32),
            pltpu.VMEM((4, rows, n_done * LANES), jnp.bfloat16),
            pltpu.SemaphoreType.DMA((2, PARTS)),
            pltpu.SemaphoreType.DMA((2,)),
            pltpu.SemaphoreType.DMA((2,)),
            pltpu.SemaphoreType.DMA((2,)),
            pltpu.SemaphoreType.DMA((4,)),
        ],
        compiler_params=pltpu.CompilerParams(vmem_limit_bytes=59 * MIB),
        cost_estimate=SMALL,
        name="half_products",
    )(meta, *xs, prev, middle, end, second)


def rest_kernel(meta_ref, *refs):
    x_refs, (rest_ref, b_ref), refs = refs[:PARTS], refs[PARTS : PARTS + 2], refs[PARTS + 2 :]
    out_refs, xv, bv, acc, pieces, x_sems, b_sem, rest_sems, out_sems = refs[:4], *refs[4:]
    band = acc.shape[2] // (2 * LANES)
    half = (bv.shape[1] - LANES) // 2
    is_end = meta_ref[0]

    def offset_of(p, g):
        return meta_ref[3 + 2 * p + g]

    at = pl.multiple_of((meta_ref[2] + band // 2) * LANES, LANES)
    rest = [
        pltpu.make_async_copy(rest_ref.at[g], acc.at[g, :, pl.ds(at, rest_ref.shape[2])], rest_sems.at[g])
        for g in range(2)
    ]
    x_loads = x_copies(x_refs, xv, x_sems, offset_of)
    b_copy = pltpu.make_async_copy(b_ref, bv, b_sem)

    def x_loads_of(g):
        return [copy for (_, r), copy in x_loads.items() if r // (PARTS // 2) == g]

    pl.when(is_end != 0)(b_copy.start)
    for g in range(2):
        rest[g].start()

        @pl.when(is_end != 0)
        def _():
            for copy in x_loads_of(g):
                copy.start()

    def wait_for(g):
        rest[g].wait()

        @pl.when(is_end != 0)
        def _():
            for copy in x_loads_of(g):
                copy.wait()
            if g == 0:
                b_copy.wait()

    def add(g):
        @pl.when(is_end != 0)
        def _():
            for p in range(2):
                add_product(acc, xv[p, g], bv[:, p * half : (p + 1) * half], g, offset_of(p, g) + meta_ref[1])
            p = meta_ref[8]
            add_product(acc, xv[p, g], bv[:, 2 * half :], g, offset_of(p, g) + meta_ref[7])

    finish(acc, wait_for, add, meta_ref[2] + band // 2, out_refs, pieces, out_sems)


def rest_products(meta, xs, rest, b, quarter):
    rows = PARTS // 4 * xs[0].shape[0]
    panel = b.shape[0]
    width = rest.shape[2]
    any_spec = pl.BlockSpec(memory_space=pl.ANY)
    x_spec = pl.BlockSpec(memory_space=pltpu.HBM)
    return pl.pallas_call(
        rest_kernel,
        out_shape=[jax.ShapeDtypeStruct((rows, width), jnp.bfloat16)] * 4,
        in_specs=[pl.BlockSpec(memory_space=pltpu.SMEM)] + [x_spec] * PARTS + [any_spec] * 2,
        out_specs=[any_spec] * 4,
        scratch_shapes=[
            pltpu.VMEM((2, 2, 2 * rows, panel), jnp.bfloat16),
            pltpu.VMEM(b.shape, jnp.bfloat16),
            pltpu.VMEM((2, 2 * rows, 2 * quarter), jnp.float32),
            pltpu.VMEM((4, rows, width), jnp.bfloat16),
            pltpu.SemaphoreType.DMA((2, PARTS)),
            pltpu.SemaphoreType.DMA,
            pltpu.SemaphoreType.DMA((2,)),
            pltpu.SemaphoreType.DMA((4,)),
        ],
        compiler_params=pltpu.CompilerParams(vmem_limit_bytes=59 * MIB),
        cost_estimate=SMALL,
        name="rest_products",
    )(meta, *xs, rest, b)


def assemble_kernel(place_ref, mask_ref, *refs):
    n = 4
    pieces, (out_ref, made, sem) = refs[:n], refs[-3:]
    steps = mask_ref.shape[0]
    rows = made.shape[0] // steps
    panel = n * LANES
    first = pl.multiple_of(place_ref[1] * panel, panel)
    for r in range(n):
        t = jnp.bitwise_xor(place_ref[0], r)
        for j in range(made.shape[1] // panel):
            to = pl.multiple_of(j * panel + t * LANES, LANES)
            for i in range(steps):
                keep = mask_ref[i, :, pl.ds(pl.multiple_of(first + to, LANES), LANES)]
                value = pieces[r][i * rows : (i + 1) * rows, j * LANES : (j + 1) * LANES].astype(jnp.float32)
                made[i * rows : (i + 1) * rows, pl.ds(to, LANES)] = (value * keep).astype(jnp.bfloat16)
    copy = pltpu.make_async_copy(made, out_ref.at[:, pl.ds(first, made.shape[1])], sem)
    copy.start()
    copy.wait()


def assembled(place, keep_wide, pieces, out=None):
    rows, width = pieces[0].shape
    cols = keep_wide.shape[2]
    vmem_spec = pl.BlockSpec(memory_space=pltpu.VMEM)
    any_spec = pl.BlockSpec(memory_space=pltpu.HBM)
    operands = [place, keep_wide, *pieces] + ([] if out is None else [out])
    return pl.pallas_call(
        assemble_kernel,
        out_shape=jax.ShapeDtypeStruct((rows, cols), jnp.bfloat16),
        in_specs=[pl.BlockSpec(memory_space=pltpu.SMEM)] + [vmem_spec] * 5 + [any_spec] * (len(operands) - 6),
        out_specs=any_spec,
        scratch_shapes=[pltpu.VMEM((rows, width * len(pieces)), jnp.bfloat16), pltpu.SemaphoreType.DMA],
        input_output_aliases={} if out is None else {6: 0},
        compiler_params=pltpu.CompilerParams(vmem_limit_bytes=16 * MIB),
        cost_estimate=SMALL,
        name="assembled",
    )(*operands)


def widen(mask, block):
    rows, cols = mask.shape
    wide = jnp.broadcast_to(mask.astype(jnp.float32)[:, :, None], (rows, cols, block))
    return wide.reshape(rows, 1, cols * block)


def together(*values):
    return lax.optimization_barrier(values)


def pairs_in_line(x_band, w_band, a_mask, keep_mask):
    panel = x_band.shape[0]
    block = panel // a_mask.shape[0]
    g, c = lax.axis_index("grid"), lax.axis_index("depth")
    z, y = g // 2, g % 2
    left = z < 2
    is_end = ((z == 0) | (z == 3)).astype(jnp.int32)
    toward = jnp.where(left, 1, -1)
    q = 2 * y + c

    swap = [(0, 2), (1, 3), (2, 0), (3, 1), (4, 6), (5, 7), (6, 4), (7, 5)]
    outward = [(2, 0), (3, 1), (4, 6), (5, 7)]
    cross = [(2, 4), (3, 5), (4, 2), (5, 3)]
    across = [(i, i ^ 1) for i in range(8)]
    layers = [(0, 1), (1, 0)]
    opposite = [(i, i ^ 3) for i in range(16)]

    def line(value, pairs):
        return lax.ppermute(value, "grid", pairs)

    first_out, second_out = jnp.where(left, 0, 4), jnp.where(left, 4, 0)
    first_in, second_in = second_out, first_out
    last_in = jnp.where(left, 2, 4)

    sent_b = b_strips(w_band, q ^ 2, 58)
    own_b = line(sent_b, across)
    sent_b, w_band = together(sent_b, w_band)
    own_a = b_strips(w_band, q, 58)
    swap_a = line(own_a, swap)
    cross_a = line(own_a, cross)
    mask_wide = widen(a_mask, block)
    rows = a_mask.shape[0]
    x_mine = [masked_rows(x_band, mask_wide, c * rows // 2 + k * rows // 4, rows // 4) for k in range(2)]
    own_b, *x_mine = together(own_b, *x_mine)
    own_b, swap_a = together(own_b, swap_a)
    swap_b = line(own_b, swap)
    cross_b = line(own_b, cross)
    x_across = [line(part, across) for part in x_mine]
    x_rest = [masked_rows(x_band, mask_wide, (1 - c) * rows // 2 + k * rows // 4, rows // 4) for k in range(2)]

    mid_a = line(cross_a[:, 5 * LANES :], outward)
    mid_b, fwd_first = packed(
        [y, first_out],
        [cross_a, cross_b, swap_a, swap_b],
        [10, 8],
        [
            (0, 0, 3, 0, 0, (0, 0)),
            (1, 0, 3, 0, 0, (0, 1)),
            (0, 3, 2, 0, 3, None),
            (1, 3, 5, 0, 5, None),
            (2, (1,), 4, 1, 0, None),
            (3, (1,), 4, 1, 4, None),
        ],
    )
    (fwd_second,) = packed([second_out], [swap_a, swap_b], [8], [(0, (0,), 4, 0, 0, None), (1, (0,), 4, 0, 4, None)])
    mid_a, mid_b, fwd_first = together(mid_a, mid_b, fwd_first)
    mid_b = line(mid_b, outward)
    fwd_first = line(fwd_first, cross)
    fwd_second, *x_across = together(fwd_second, *x_across)
    far_first = line(fwd_first, outward)
    fwd_second = line(fwd_second, cross)
    x_opposite = [lax.ppermute(part, "depth", layers) for part in x_across]
    xs = x_mine + x_rest + x_across + x_opposite

    def offsets(delta):
        tilt = 2 * y - 1
        return [(2 * delta + 4) % 8, (2 * delta + tilt + 4) % 8, (2 * delta - tilt + 4) % 8, (2 * delta + 4) % 8]

    zero = jnp.zeros_like(z)
    third = offsets(jnp.where(is_end == 1, 2, -toward))
    fourth = offsets(jnp.where(is_end == 1, -toward, 2))
    meta = jnp.stack([is_end, 4 + y, *offsets(zero), *offsets(toward), *third]).astype(jnp.int32)
    plan = [
        (0, [(0, 0, 8, 0, 0)]),
        (1, [(1, 0, 8, 0, 1)]),
        (2, [(4, 0, 8, 0, 2)]),
        (3, [(5, 0, 8, 0, 3)]),
        (4, [(6, 0, 3, 0, None), (6, 3, 2, 3, 4), (7, 0, 3, 5, 4)]),
        (5, [(6, 5, 5, 3, 5)]),
    ]
    total = whole_products(meta, xs, [own_a, own_b, cross_a, cross_b, swap_a, swap_b, mid_b, mid_a], plan)
    last_at = jnp.where(left, 2, 0)
    total, last_at = together(total, last_at)
    extra_in, extra_panel = jnp.where(left, 1, 6), jnp.where(left, 1 - y, y)
    extra_at = jnp.where(left, 1, 2) + 4 * extra_panel
    (last,) = packed(
        [last_at, last_at + 4, extra_at],
        [fwd_second],
        [5],
        [(0, (0,), 2, 0, 0, None), (0, (1,), 2, 0, 2, None), (0, (2,), 1, 0, 4, None)],
    )
    far_second = line(last, outward)

    def exchanged(pieces):
        return [
            pieces[0],
            lax.ppermute(pieces[1], "depth", layers),
            line(pieces[2], across),
            lax.ppermute(pieces[3], ("grid", "depth"), opposite),
        ]

    done_at, rest_at = jnp.where(left, 3, 0), jnp.where(left, 0, 5)
    meta = jnp.stack([is_end, first_in, second_in, done_at, rest_at, *fourth]).astype(jnp.int32)
    *done, rest = half_products(meta, xs, total, fwd_first, far_first, fwd_second, 5)
    done = exchanged(done)
    far_second, done[1] = together(far_second, done[1])
    keep_wide = widen(keep_mask, block)
    out = assembled(jnp.stack([q, done_at]).astype(jnp.int32), keep_wide, done)
    meta = jnp.stack([is_end, last_in, rest_at, *fourth, extra_in, extra_panel]).astype(jnp.int32)
    rest = exchanged(rest_products(meta, xs, rest, far_second, own_a.shape[1]))
    return assembled(jnp.stack([q, rest_at]).astype(jnp.int32), keep_wide, rest, out)


def solution(mesh):
    placed = (
        P(("groups", "grid"), None),
        P(("groups", "grid"), None),
        P(("groups", "grid"), None),
        P(("groups", "grid", "depth"), None),
    )

    def local(x_band, w_band, a_mask, keep_mask):
        panel, cols = x_band.shape
        pairs = mesh.shape["grid"] == 8 and mesh.shape["depth"] == 2
        pairs = pairs and cols == 8 * panel and panel == 4 * LANES
        return (pairs_in_line if pairs else ring)(x_band, w_band, a_mask, keep_mask)

    return jax.shard_map(
        local,
        mesh=mesh,
        in_specs=placed,
        out_specs=P(("groups", "grid", "depth"), None),
        check_vma=False,
    )
```

```python
import functools

import jax
import jax.numpy as jnp
from jax import lax
from jax.experimental import pallas as pl
from jax.experimental.pallas import tpu as pltpu
from jax.sharding import PartitionSpec as P

LANES = 128
MIB = 1 << 20
SMALL = pl.CostEstimate(flops=1000, bytes_accessed=1000, transcendentals=0)


def shifted(shard, axis, by):
    count = lax.axis_size(axis)
    return lax.ppermute(shard, axis, [(i, (i + by) % count) for i in range(count)])


def expand_blocks(mask, block):
    rows, cols = mask.shape
    wide = jnp.broadcast_to(mask[:, None, :, None], (rows, block, cols, block))
    return wide.reshape(rows * block, cols * block)


def ring(x_band, w_band, a_mask, keep_mask):
    panel = x_band.shape[0]
    block = panel // a_mask.shape[0]
    band_cols = x_band.shape[1]
    xm = x_band * expand_blocks(a_mask, block).astype(jnp.bfloat16)
    rows = lax.broadcasted_iota(jnp.int32, x_band.shape, 0)
    cols = lax.broadcasted_iota(jnp.int32, x_band.shape, 1)
    identity = jnp.where(cols == rows + 4 * panel, 1.0, 0.0).astype(jnp.float32)
    b_panel = (1.5 * identity - 0.5 * w_band.astype(jnp.float32)).astype(jnp.bfloat16)
    layer = lax.axis_index("depth")
    current = shifted(b_panel, ("grid", "depth"), -5)
    wide = jnp.zeros((panel, 2 * band_cols), jnp.float32)
    for step in range(4):
        offset = 6 + layer - 2 * step
        ablock = lax.dynamic_slice_in_dim(xm, offset * panel, panel, 1)
        term = jnp.dot(ablock, current, preferred_element_type=jnp.float32)
        region = lax.dynamic_slice_in_dim(wide, offset * panel, band_cols, 1)
        wide = lax.dynamic_update_slice_in_dim(wide, region + term, offset * panel, 1)
        if step < 3:
            current = shifted(current, "grid", 2)
    partial_band = wide[:, 4 * panel : 12 * panel]
    mine = lax.psum_scatter(partial_band, "depth", scatter_dimension=0, tiled=True)
    keep = expand_blocks(keep_mask, block).astype(jnp.float32)
    return (mine * keep).astype(jnp.bfloat16)


def strips_kernel(quarter_ref, w_ref, b_ref, held, made, in_sems, out_sems):
    panel, width = held.shape
    quarter = quarter_ref[0]

    def strip(j):
        return slice(j * LANES, (j + 1) * LANES)

    def load(j):
        at = pl.multiple_of(j * panel + quarter * LANES, LANES)
        return pltpu.make_async_copy(w_ref.at[:, pl.ds(at, LANES)], held.at[:, strip(j)], in_sems.at[j])

    def give(j):
        return pltpu.make_async_copy(made.at[:, strip(j)], b_ref.at[:, strip(j)], out_sems.at[j])

    band = width // LANES
    for j in range(band):
        load(j).start()
    for j in range(band):
        load(j).wait()
        value = -0.5 * held[:, strip(j)].astype(jnp.float32)
        if j == band // 2:
            rows = lax.broadcasted_iota(jnp.int32, value.shape, 0)
            cols = lax.broadcasted_iota(jnp.int32, value.shape, 1)
            value = value + jnp.where(rows == cols + quarter * LANES, 1.5, 0.0)
        made[:, strip(j)] = value.astype(jnp.bfloat16)
        give(j).start()
    for j in range(band):
        give(j).wait()


def b_strips(w_band, quarter, limit):
    panel = w_band.shape[0]
    band = w_band.shape[1] // panel
    shape = (panel, band * LANES)
    return pl.pallas_call(
        strips_kernel,
        out_shape=jax.ShapeDtypeStruct(shape, jnp.bfloat16),
        in_specs=[
            pl.BlockSpec(memory_space=pltpu.SMEM),
            pl.BlockSpec(memory_space=pltpu.HBM),
        ],
        out_specs=pl.BlockSpec(memory_space=pl.ANY),
        scratch_shapes=[
            pltpu.VMEM(shape, jnp.bfloat16),
            pltpu.VMEM(shape, jnp.bfloat16),
            pltpu.SemaphoreType.DMA((band,)),
            pltpu.SemaphoreType.DMA((band,)),
        ],
        compiler_params=pltpu.CompilerParams(vmem_limit_bytes=limit * MIB),
        cost_estimate=SMALL,
        name="b_strips",
    )(quarter.reshape(1), w_band)


def pack_kernel(plan, n_in, meta_ref, *refs):
    sources, outs, sems = refs[:n_in], refs[n_in:-1], refs[-1]

    def on_each(do):
        for k, (source, start, count, out, to, when) in enumerate(plan):
            at = start * LANES if isinstance(start, int) else pl.multiple_of(meta_ref[start[0]] * LANES, LANES)
            copy = pltpu.make_async_copy(
                sources[source].at[:, pl.ds(at, count * LANES)],
                outs[out].at[:, to * LANES : (to + count) * LANES],
                sems.at[k],
            )
            if when is None:
                do(copy)
            else:
                pl.when(meta_ref[when[0]] == when[1])(functools.partial(do, copy))

    on_each(lambda copy: copy.start())
    on_each(lambda copy: copy.wait())


def packed(meta, sources, widths, plan):
    rows = sources[0].shape[0]
    any_spec = pl.BlockSpec(memory_space=pl.ANY)
    return pl.pallas_call(
        functools.partial(pack_kernel, plan, len(sources)),
        out_shape=[jax.ShapeDtypeStruct((rows, width * LANES), jnp.bfloat16) for width in widths],
        in_specs=[pl.BlockSpec(memory_space=pltpu.SMEM)] + [any_spec] * len(sources),
        out_specs=[pl.BlockSpec(memory_space=pltpu.VMEM)] * len(widths),
        scratch_shapes=[pltpu.SemaphoreType.DMA((len(plan),))],
        compiler_params=pltpu.CompilerParams(vmem_limit_bytes=40 * MIB),
        cost_estimate=SMALL,
        name="packed",
    )(jnp.stack(meta).astype(jnp.int32), *sources)


def mask_kernel(first_ref, mask_ref, x_ref, out_ref):
    out_ref[...] = (x_ref[...].astype(jnp.float32) * mask_ref[0]).astype(jnp.bfloat16)


def masked_rows(x_band, mask_wide, first, count):
    block = x_band.shape[0] // mask_wide.shape[0]
    cols = x_band.shape[1]
    return pl.pallas_call(
        mask_kernel,
        grid_spec=pltpu.PrefetchScalarGridSpec(
            num_scalar_prefetch=1,
            grid=(count,),
            in_specs=[
                pl.BlockSpec((1, 1, cols), lambda i, f: (f[0] + i, 0, 0)),
                pl.BlockSpec((block, cols), lambda i, f: (f[0] + i, 0)),
            ],
            out_specs=pl.BlockSpec((block, cols), lambda i, f: (i, 0)),
        ),
        out_shape=jax.ShapeDtypeStruct((count * block, cols), jnp.bfloat16),
        compiler_params=pltpu.CompilerParams(vmem_limit_bytes=58 * MIB),
        cost_estimate=SMALL,
        name="masked_rows",
    )(first.reshape(1), mask_wide, x_band)


PARTS = 8


def x_copies(x_refs, xv, sems, offset_of):
    n_b, _, rows, panel = xv.shape
    part = 2 * rows // PARTS
    copies = {}
    for p in range(n_b):
        for r in range(PARTS):
            g, k = divmod(r, PARTS // 2)
            at = pl.multiple_of(offset_of(p, g) * panel, panel)
            copies[p, r] = pltpu.make_async_copy(
                x_refs[r].at[:, pl.ds(at, panel)],
                xv.at[p, g, k * part : (k + 1) * part],
                sems.at[p, r],
            )
    return copies


def add_product(acc, x, strips, g, first):
    cols = pl.ds(pl.multiple_of(first * LANES, LANES), strips.shape[1])
    acc[g, :, cols] += jnp.dot(x, strips, preferred_element_type=jnp.float32)


def whole_kernel(plan, meta_ref, *refs):
    n_b = len(plan)
    x_refs, refs = refs[:PARTS], refs[PARTS:]
    b_refs, (out_ref, xv, bv, acc, x_sems, b_sems, out_sems) = refs[:-7], refs[-7:]
    quarter = bv.shape[2]
    low = quarter // 2
    is_end = meta_ref[0]

    def offset_of(p, g):
        return meta_ref[2 + 2 * p + g]

    def b_middle(p):
        return [pltpu.make_async_copy(b_refs[plan[p][0]].at[:, :quarter], bv.at[p], b_sems.at[p, 0])]

    def b_end(p):
        copies = []
        for k, (operand, first, count, at, to) in enumerate(plan[p][1]):
            to = meta_ref[1] if to is None else to
            source = b_refs[operand].at[:, first * LANES : (first + count) * LANES]
            copies.append(pltpu.make_async_copy(source, bv.at[to, :, at * LANES : (at + count) * LANES], b_sems.at[p, k]))
        return copies

    def on_each(p, do):
        @pl.when(is_end == 0)
        def _():
            for copy in b_middle(p):
                do(copy)

        @pl.when(is_end != 0)
        def _():
            for copy in b_end(p):
                do(copy)

    copies = x_copies(x_refs, xv, x_sems, offset_of)
    for p in range(n_b):
        on_each(p, lambda copy: copy.start())
        for r in range(PARTS):
            copies[p, r].start()
    outs = [
        pltpu.make_async_copy(acc.at[g, :, low : low + quarter], out_ref.at[g], out_sems.at[g]) for g in range(2)
    ]

    def wait_for(p):
        for k in [p] if p < n_b - 2 else range(n_b - 2, n_b) if p == n_b - 2 else []:
            on_each(k, lambda copy: copy.wait())
        for r in range(PARTS):
            copies[p, r].wait()

    middle = quarter // LANES // 2

    def own(g, carry):
        acc[g, :, low : low + quarter] = jnp.dot(xv[g, g], bv[g], preferred_element_type=jnp.float32)
        return carry

    def step(i, carry):
        p = jnp.where(i < 4, i % 2, i // 2)
        g = jnp.where(i < 4, 1 - i % 2, i % 2)
        for k in range(2, n_b):
            pl.when(i == 2 * k)(functools.partial(wait_for, k))
        pl.when(i == 2 * n_b - 1)(outs[0].start)
        offset = offset_of(p, g)
        for k in range(2 * middle):
            if k == middle:
                continue
            first, last = max(0, middle - k), min(2 * middle, 3 * middle - k)

            @pl.when(offset == k)
            def _():
                strips = bv[p, :, first * LANES : last * LANES]
                acc[g, :, (k + first) * LANES : (k + last) * LANES] += jnp.dot(
                    xv[p, g], strips, preferred_element_type=jnp.float32
                )

        return carry

    for p in range(2):
        wait_for(p)
    lax.fori_loop(0, 2, own, 0)
    lax.fori_loop(2, 2 * n_b, step, 0)
    outs[1].start()
    for out in outs:
        out.wait()


def whole_products(meta, xs, operands, plan):
    rows = PARTS // 4 * xs[0].shape[0]
    panel, quarter = operands[plan[0][0]].shape
    n_b = len(plan)
    any_spec = pl.BlockSpec(memory_space=pl.ANY)
    x_spec = pl.BlockSpec(memory_space=pltpu.HBM)
    return pl.pallas_call(
        functools.partial(whole_kernel, plan),
        out_shape=jax.ShapeDtypeStruct((2, 2 * rows, quarter), jnp.float32),
        in_specs=[pl.BlockSpec(memory_space=pltpu.SMEM)] + [x_spec] * PARTS + [any_spec] * len(operands),
        out_specs=any_spec,
        scratch_shapes=[
            pltpu.VMEM((n_b, 2, 2 * rows, panel), jnp.bfloat16),
            pltpu.VMEM((n_b, panel, quarter), jnp.bfloat16),
            pltpu.VMEM((2, 2 * rows, 2 * quarter), jnp.float32),
            pltpu.SemaphoreType.DMA((n_b, PARTS)),
            pltpu.SemaphoreType.DMA((n_b, 3)),
            pltpu.SemaphoreType.DMA((2,)),
        ],
        compiler_params=pltpu.CompilerParams(vmem_limit_bytes=59 * MIB),
        cost_estimate=pl.CostEstimate(flops=6 * 10**9, bytes_accessed=36 * MIB, transcendentals=0),
        name="whole_products",
    )(meta, *xs, *operands)


def finish(acc, wait_for, add, at, out_refs, pieces, sems, also=None):
    half, width = out_refs[0].shape
    cols = pl.ds(pl.multiple_of(at * LANES, LANES), width)
    outs = [pltpu.make_async_copy(pieces.at[r], out_refs[r], sems.at[r]) for r in range(4)]
    also = also or []

    def step(g, carry):
        for k in range(2):
            pl.when(g == k)(functools.partial(wait_for, k))
        add(g)
        for k in range(2):

            @pl.when(g == k)
            def _():
                for copy in also[k : k + 1]:
                    copy.start()
                for r in range(2 * k, 2 * k + 2):
                    rows = slice((r % 2) * half, (r % 2 + 1) * half)
                    pieces[r] = acc[k, rows, cols].astype(jnp.bfloat16)
                    outs[r].start()

        return carry

    lax.fori_loop(0, 2, step, 0)
    for copy in outs + also:
        copy.wait()


def half_kernel(meta_ref, *refs):
    x_refs, (prev_ref, middle_ref, end_ref, second_ref), refs = refs[:PARTS], refs[PARTS : PARTS + 4], refs[PARTS + 4 :]
    out_refs, rest_ref, xv, bv, acc, pieces, x_sems, b_sems, prev_sems, rest_sems, out_sems = refs[:4], *refs[4:]
    quarter = bv.shape[2]
    half = quarter // 2
    low = quarter // 2
    band = quarter // LANES
    is_end = meta_ref[0]

    def offset_of(p, g):
        return meta_ref[5 + 2 * p + g]

    x_loads = x_copies(x_refs, xv, x_sems, offset_of)
    middle = pltpu.make_async_copy(middle_ref, bv.at[0], b_sems.at[0])
    end = pltpu.make_async_copy(end_ref, bv.at[0], b_sems.at[0])
    second = pltpu.make_async_copy(second_ref, bv.at[1], b_sems.at[1])
    prev = [
        pltpu.make_async_copy(prev_ref.at[g], acc.at[g, :, low : low + quarter], prev_sems.at[g]) for g in range(2)
    ]
    at = pl.multiple_of((meta_ref[4] + band // 2) * LANES, LANES)
    rest = [
        pltpu.make_async_copy(acc.at[g, :, pl.ds(at, rest_ref.shape[2])], rest_ref.at[g], rest_sems.at[g])
        for g in range(2)
    ]

    @pl.when(is_end == 0)
    def _():
        middle.start()
        second.start()

    pl.when(is_end != 0)(end.start)

    def rows_loads(g):
        return [prev[g]] + [copy for (_, r), copy in x_loads.items() if r // (PARTS // 2) == g]

    for g in range(2):
        for copy in rows_loads(g):
            copy.start()

    def wait_for(g):
        for copy in rows_loads(g):
            copy.wait()
        if g == 0:

            @pl.when(is_end == 0)
            def _():
                middle.wait()
                second.wait()

            pl.when(is_end != 0)(end.wait)

    def add(g):
        for p in range(2):
            add_product(acc, xv[p, g], bv[0, :, p * half : (p + 1) * half], g, offset_of(p, g) + meta_ref[1])

        @pl.when(is_end == 0)
        def _():
            for p in range(2):
                add_product(acc, xv[p, g], bv[1, :, p * half : (p + 1) * half], g, offset_of(p, g) + meta_ref[2])

    finish(acc, wait_for, add, meta_ref[3] + band // 2, out_refs, pieces, out_sems, rest)


def half_products(meta, xs, prev, middle, end, second, n_done):
    rows = PARTS // 4 * xs[0].shape[0]
    panel, quarter = second.shape
    any_spec = pl.BlockSpec(memory_space=pl.ANY)
    x_spec = pl.BlockSpec(memory_space=pltpu.HBM)
    n_rest = quarter // LANES - n_done
    return pl.pallas_call(
        half_kernel,
        out_shape=[jax.ShapeDtypeStruct((rows, n_done * LANES), jnp.bfloat16)] * 4
        + [jax.ShapeDtypeStruct((2, 2 * rows, n_rest * LANES), jnp.float32)],
        in_specs=[pl.BlockSpec(memory_space=pltpu.SMEM)] + [x_spec] * PARTS + [any_spec] * 4,
        out_specs=[any_spec] * 5,
        scratch_shapes=[
            pltpu.VMEM((2, 2, 2 * rows, panel), jnp.bfloat16),
            pltpu.VMEM((2, panel, quarter), jnp.bfloat16),
            pltpu.VMEM((2, 2 * rows, 2 * quarter), jnp.float32),
            pltpu.VMEM((4, rows, n_done * LANES), jnp.bfloat16),
            pltpu.SemaphoreType.DMA((2, PARTS)),
            pltpu.SemaphoreType.DMA((2,)),
            pltpu.SemaphoreType.DMA((2,)),
            pltpu.SemaphoreType.DMA((2,)),
            pltpu.SemaphoreType.DMA((4,)),
        ],
        compiler_params=pltpu.CompilerParams(vmem_limit_bytes=59 * MIB),
        cost_estimate=SMALL,
        name="half_products",
    )(meta, *xs, prev, middle, end, second)


def rest_kernel(meta_ref, *refs):
    x_refs, (rest_ref, b_ref), refs = refs[:PARTS], refs[PARTS : PARTS + 2], refs[PARTS + 2 :]
    out_refs, xv, bv, acc, pieces, x_sems, b_sem, rest_sems, out_sems = refs[:4], *refs[4:]
    band = acc.shape[2] // (2 * LANES)
    half = (bv.shape[1] - LANES) // 2
    is_end = meta_ref[0]

    def offset_of(p, g):
        return meta_ref[3 + 2 * p + g]

    at = pl.multiple_of((meta_ref[2] + band // 2) * LANES, LANES)
    rest = [
        pltpu.make_async_copy(rest_ref.at[g], acc.at[g, :, pl.ds(at, rest_ref.shape[2])], rest_sems.at[g])
        for g in range(2)
    ]
    x_loads = x_copies(x_refs, xv, x_sems, offset_of)
    b_copy = pltpu.make_async_copy(b_ref, bv, b_sem)

    def x_loads_of(g):
        return [copy for (_, r), copy in x_loads.items() if r // (PARTS // 2) == g]

    pl.when(is_end != 0)(b_copy.start)
    for g in range(2):
        rest[g].start()

        @pl.when(is_end != 0)
        def _():
            for copy in x_loads_of(g):
                copy.start()

    def wait_for(g):
        rest[g].wait()

        @pl.when(is_end != 0)
        def _():
            for copy in x_loads_of(g):
                copy.wait()
            if g == 0:
                b_copy.wait()

    def add(g):
        @pl.when(is_end != 0)
        def _():
            for p in range(2):
                add_product(acc, xv[p, g], bv[:, p * half : (p + 1) * half], g, offset_of(p, g) + meta_ref[1])
            p = meta_ref[8]
            add_product(acc, xv[p, g], bv[:, 2 * half :], g, offset_of(p, g) + meta_ref[7])

    finish(acc, wait_for, add, meta_ref[2] + band // 2, out_refs, pieces, out_sems)


def rest_products(meta, xs, rest, b, quarter):
    rows = PARTS // 4 * xs[0].shape[0]
    panel = b.shape[0]
    width = rest.shape[2]
    any_spec = pl.BlockSpec(memory_space=pl.ANY)
    x_spec = pl.BlockSpec(memory_space=pltpu.HBM)
    return pl.pallas_call(
        rest_kernel,
        out_shape=[jax.ShapeDtypeStruct((rows, width), jnp.bfloat16)] * 4,
        in_specs=[pl.BlockSpec(memory_space=pltpu.SMEM)] + [x_spec] * PARTS + [any_spec] * 2,
        out_specs=[any_spec] * 4,
        scratch_shapes=[
            pltpu.VMEM((2, 2, 2 * rows, panel), jnp.bfloat16),
            pltpu.VMEM(b.shape, jnp.bfloat16),
            pltpu.VMEM((2, 2 * rows, 2 * quarter), jnp.float32),
            pltpu.VMEM((4, rows, width), jnp.bfloat16),
            pltpu.SemaphoreType.DMA((2, PARTS)),
            pltpu.SemaphoreType.DMA,
            pltpu.SemaphoreType.DMA((2,)),
            pltpu.SemaphoreType.DMA((4,)),
        ],
        compiler_params=pltpu.CompilerParams(vmem_limit_bytes=59 * MIB),
        cost_estimate=SMALL,
        name="rest_products",
    )(meta, *xs, rest, b)


def assemble_kernel(place_ref, mask_ref, *refs):
    n = 4
    pieces, (out_ref, made, sem) = refs[:n], refs[-3:]
    steps = mask_ref.shape[0]
    rows = made.shape[0] // steps
    panel = n * LANES
    first = pl.multiple_of(place_ref[1] * panel, panel)
    for r in range(n):
        t = jnp.bitwise_xor(place_ref[0], r)
        for j in range(made.shape[1] // panel):
            to = pl.multiple_of(j * panel + t * LANES, LANES)
            for i in range(steps):
                keep = mask_ref[i, :, pl.ds(pl.multiple_of(first + to, LANES), LANES)]
                value = pieces[r][i * rows : (i + 1) * rows, j * LANES : (j + 1) * LANES].astype(jnp.float32)
                made[i * rows : (i + 1) * rows, pl.ds(to, LANES)] = (value * keep).astype(jnp.bfloat16)
    copy = pltpu.make_async_copy(made, out_ref.at[:, pl.ds(first, made.shape[1])], sem)
    copy.start()
    copy.wait()


def assembled(place, keep_wide, pieces, out=None):
    rows, width = pieces[0].shape
    cols = keep_wide.shape[2]
    vmem_spec = pl.BlockSpec(memory_space=pltpu.VMEM)
    any_spec = pl.BlockSpec(memory_space=pltpu.HBM)
    operands = [place, keep_wide, *pieces] + ([] if out is None else [out])
    return pl.pallas_call(
        assemble_kernel,
        out_shape=jax.ShapeDtypeStruct((rows, cols), jnp.bfloat16),
        in_specs=[pl.BlockSpec(memory_space=pltpu.SMEM)] + [vmem_spec] * 5 + [any_spec] * (len(operands) - 6),
        out_specs=any_spec,
        scratch_shapes=[pltpu.VMEM((rows, width * len(pieces)), jnp.bfloat16), pltpu.SemaphoreType.DMA],
        input_output_aliases={} if out is None else {6: 0},
        compiler_params=pltpu.CompilerParams(vmem_limit_bytes=16 * MIB),
        cost_estimate=SMALL,
        name="assembled",
    )(*operands)


def widen(mask, block):
    rows, cols = mask.shape
    wide = jnp.broadcast_to(mask.astype(jnp.float32)[:, :, None], (rows, cols, block))
    return wide.reshape(rows, 1, cols * block)


def together(*values):
    return lax.optimization_barrier(values)


def pairs_in_line(x_band, w_band, a_mask, keep_mask):
    panel = x_band.shape[0]
    block = panel // a_mask.shape[0]
    g, c = lax.axis_index("grid"), lax.axis_index("depth")
    z, y = g // 2, g % 2
    left = z < 2
    is_end = ((z == 0) | (z == 3)).astype(jnp.int32)
    toward = jnp.where(left, 1, -1)
    q = 2 * y + c

    swap = [(0, 2), (1, 3), (2, 0), (3, 1), (4, 6), (5, 7), (6, 4), (7, 5)]
    outward = [(2, 0), (3, 1), (4, 6), (5, 7)]
    cross = [(2, 4), (3, 5), (4, 2), (5, 3)]
    across = [(i, i ^ 1) for i in range(8)]
    layers = [(0, 1), (1, 0)]
    opposite = [(i, i ^ 3) for i in range(16)]

    def line(value, pairs):
        return lax.ppermute(value, "grid", pairs)

    first_out, second_out = jnp.where(left, 0, 4), jnp.where(left, 4, 0)
    first_in, second_in = second_out, first_out
    last_in = jnp.where(left, 2, 4)

    sent_b = b_strips(w_band, q ^ 2, 58)
    own_b = line(sent_b, across)
    sent_b, w_band = together(sent_b, w_band)
    own_a = b_strips(w_band, q, 58)
    swap_a = line(own_a, swap)
    cross_a = line(own_a, cross)
    mask_wide = widen(a_mask, block)
    rows = a_mask.shape[0]
    x_mine = [masked_rows(x_band, mask_wide, c * rows // 2 + k * rows // 4, rows // 4) for k in range(2)]
    own_b, *x_mine = together(own_b, *x_mine)
    own_b, swap_a = together(own_b, swap_a)
    swap_b = line(own_b, swap)
    cross_b = line(own_b, cross)
    x_across = [line(part, across) for part in x_mine]
    x_rest = [masked_rows(x_band, mask_wide, (1 - c) * rows // 2 + k * rows // 4, rows // 4) for k in range(2)]

    mid_a = line(cross_a[:, 5 * LANES :], outward)
    mid_b, fwd_first = packed(
        [y, first_out],
        [cross_a, cross_b, swap_a, swap_b],
        [10, 8],
        [
            (0, 0, 3, 0, 0, (0, 0)),
            (1, 0, 3, 0, 0, (0, 1)),
            (0, 3, 2, 0, 3, None),
            (1, 3, 5, 0, 5, None),
            (2, (1,), 4, 1, 0, None),
            (3, (1,), 4, 1, 4, None),
        ],
    )
    (fwd_second,) = packed([second_out], [swap_a, swap_b], [8], [(0, (0,), 4, 0, 0, None), (1, (0,), 4, 0, 4, None)])
    mid_a, mid_b, fwd_first, *x_rest = together(mid_a, mid_b, fwd_first, *x_rest)
    mid_b = line(mid_b, outward)
    fwd_first = line(fwd_first, cross)
    fwd_second, *x_across = together(fwd_second, *x_across)
    far_first = line(fwd_first, outward)
    fwd_second = line(fwd_second, cross)
    x_opposite = [lax.ppermute(part, "depth", layers) for part in x_across]
    xs = x_mine + x_rest + x_across + x_opposite

    def offsets(delta):
        tilt = 2 * y - 1
        return [(2 * delta + 4) % 8, (2 * delta + tilt + 4) % 8, (2 * delta - tilt + 4) % 8, (2 * delta + 4) % 8]

    zero = jnp.zeros_like(z)
    third = offsets(jnp.where(is_end == 1, 2, -toward))
    fourth = offsets(jnp.where(is_end == 1, -toward, 2))
    meta = jnp.stack([is_end, 4 + y, *offsets(zero), *offsets(toward), *third]).astype(jnp.int32)
    plan = [
        (0, [(0, 0, 8, 0, 0)]),
        (1, [(1, 0, 8, 0, 1)]),
        (2, [(4, 0, 8, 0, 2)]),
        (3, [(5, 0, 8, 0, 3)]),
        (4, [(6, 0, 3, 0, None), (6, 3, 2, 3, 4), (7, 0, 3, 5, 4)]),
        (5, [(6, 5, 5, 3, 5)]),
    ]
    total = whole_products(meta, xs, [own_a, own_b, cross_a, cross_b, swap_a, swap_b, mid_b, mid_a], plan)
    last_at = jnp.where(left, 2, 0)
    total, last_at = together(total, last_at)
    extra_in, extra_panel = jnp.where(left, 1, 6), jnp.where(left, 1 - y, y)
    extra_at = jnp.where(left, 1, 2) + 4 * extra_panel
    (last,) = packed(
        [last_at, last_at + 4, extra_at],
        [fwd_second],
        [5],
        [(0, (0,), 2, 0, 0, None), (0, (1,), 2, 0, 2, None), (0, (2,), 1, 0, 4, None)],
    )
    far_second = line(last, outward)

    def exchanged(pieces):
        return [
            pieces[0],
            lax.ppermute(pieces[1], "depth", layers),
            line(pieces[2], across),
            lax.ppermute(pieces[3], ("grid", "depth"), opposite),
        ]

    done_at, rest_at = jnp.where(left, 3, 0), jnp.where(left, 0, 5)
    meta = jnp.stack([is_end, first_in, second_in, done_at, rest_at, *fourth]).astype(jnp.int32)
    *done, rest = half_products(meta, xs, total, fwd_first, far_first, fwd_second, 5)
    done = exchanged(done)
    far_second, done[1] = together(far_second, done[1])
    keep_wide = widen(keep_mask, block)
    out = assembled(jnp.stack([q, done_at]).astype(jnp.int32), keep_wide, done)
    meta = jnp.stack([is_end, last_in, rest_at, *fourth, extra_in, extra_panel]).astype(jnp.int32)
    rest = exchanged(rest_products(meta, xs, rest, far_second, own_a.shape[1]))
    return assembled(jnp.stack([q, rest_at]).astype(jnp.int32), keep_wide, rest, out)


def solution(mesh):
    placed = (
        P(("groups", "grid"), None),
        P(("groups", "grid"), None),
        P(("groups", "grid"), None),
        P(("groups", "grid", "depth"), None),
    )

    def local(x_band, w_band, a_mask, keep_mask):
        panel, cols = x_band.shape
        pairs = mesh.shape["grid"] == 8 and mesh.shape["depth"] == 2
        pairs = pairs and cols == 8 * panel and panel == 4 * LANES
        return (pairs_in_line if pairs else ring)(x_band, w_band, a_mask, keep_mask)

    return jax.shard_map(
        local,
        mesh=mesh,
        in_specs=placed,
        out_specs=P(("groups", "grid", "depth"), None),
        check_vma=False,
    )
```

```python
import functools

import jax
import jax.numpy as jnp
from jax import lax
from jax.experimental import pallas as pl
from jax.experimental.pallas import tpu as pltpu
from jax.sharding import PartitionSpec as P

LANES = 128
MIB = 1 << 20
SMALL = pl.CostEstimate(flops=1000, bytes_accessed=1000, transcendentals=0)


def shifted(shard, axis, by):
    count = lax.axis_size(axis)
    return lax.ppermute(shard, axis, [(i, (i + by) % count) for i in range(count)])


def expand_blocks(mask, block):
    rows, cols = mask.shape
    wide = jnp.broadcast_to(mask[:, None, :, None], (rows, block, cols, block))
    return wide.reshape(rows * block, cols * block)


def ring(x_band, w_band, a_mask, keep_mask):
    panel = x_band.shape[0]
    block = panel // a_mask.shape[0]
    band_cols = x_band.shape[1]
    xm = x_band * expand_blocks(a_mask, block).astype(jnp.bfloat16)
    rows = lax.broadcasted_iota(jnp.int32, x_band.shape, 0)
    cols = lax.broadcasted_iota(jnp.int32, x_band.shape, 1)
    identity = jnp.where(cols == rows + 4 * panel, 1.0, 0.0).astype(jnp.float32)
    b_panel = (1.5 * identity - 0.5 * w_band.astype(jnp.float32)).astype(jnp.bfloat16)
    layer = lax.axis_index("depth")
    current = shifted(b_panel, ("grid", "depth"), -5)
    wide = jnp.zeros((panel, 2 * band_cols), jnp.float32)
    for step in range(4):
        offset = 6 + layer - 2 * step
        ablock = lax.dynamic_slice_in_dim(xm, offset * panel, panel, 1)
        term = jnp.dot(ablock, current, preferred_element_type=jnp.float32)
        region = lax.dynamic_slice_in_dim(wide, offset * panel, band_cols, 1)
        wide = lax.dynamic_update_slice_in_dim(wide, region + term, offset * panel, 1)
        if step < 3:
            current = shifted(current, "grid", 2)
    partial_band = wide[:, 4 * panel : 12 * panel]
    mine = lax.psum_scatter(partial_band, "depth", scatter_dimension=0, tiled=True)
    keep = expand_blocks(keep_mask, block).astype(jnp.float32)
    return (mine * keep).astype(jnp.bfloat16)


def strips_kernel(quarter_ref, w_ref, b_ref, held, made, in_sems, out_sems):
    panel, width = held.shape
    quarter = quarter_ref[0]

    def strip(j):
        return slice(j * LANES, (j + 1) * LANES)

    def load(j):
        at = pl.multiple_of(j * panel + quarter * LANES, LANES)
        return pltpu.make_async_copy(w_ref.at[:, pl.ds(at, LANES)], held.at[:, strip(j)], in_sems.at[j])

    def give(j):
        return pltpu.make_async_copy(made.at[:, strip(j)], b_ref.at[:, strip(j)], out_sems.at[j])

    band = width // LANES
    for j in range(band):
        load(j).start()
    for j in range(band):
        load(j).wait()
        value = -0.5 * held[:, strip(j)].astype(jnp.float32)
        if j == band // 2:
            rows = lax.broadcasted_iota(jnp.int32, value.shape, 0)
            cols = lax.broadcasted_iota(jnp.int32, value.shape, 1)
            value = value + jnp.where(rows == cols + quarter * LANES, 1.5, 0.0)
        made[:, strip(j)] = value.astype(jnp.bfloat16)
        give(j).start()
    for j in range(band):
        give(j).wait()


def b_strips(w_band, quarter, limit):
    panel = w_band.shape[0]
    band = w_band.shape[1] // panel
    shape = (panel, band * LANES)
    return pl.pallas_call(
        strips_kernel,
        out_shape=jax.ShapeDtypeStruct(shape, jnp.bfloat16),
        in_specs=[
            pl.BlockSpec(memory_space=pltpu.SMEM),
            pl.BlockSpec(memory_space=pltpu.HBM),
        ],
        out_specs=pl.BlockSpec(memory_space=pl.ANY),
        scratch_shapes=[
            pltpu.VMEM(shape, jnp.bfloat16),
            pltpu.VMEM(shape, jnp.bfloat16),
            pltpu.SemaphoreType.DMA((band,)),
            pltpu.SemaphoreType.DMA((band,)),
        ],
        compiler_params=pltpu.CompilerParams(vmem_limit_bytes=limit * MIB),
        cost_estimate=SMALL,
        name="b_strips",
    )(quarter.reshape(1), w_band)


def pack_kernel(plan, n_in, meta_ref, *refs):
    sources, outs, sems = refs[:n_in], refs[n_in:-1], refs[-1]

    def on_each(do):
        for k, (source, start, count, out, to, when) in enumerate(plan):
            at = start * LANES if isinstance(start, int) else pl.multiple_of(meta_ref[start[0]] * LANES, LANES)
            copy = pltpu.make_async_copy(
                sources[source].at[:, pl.ds(at, count * LANES)],
                outs[out].at[:, to * LANES : (to + count) * LANES],
                sems.at[k],
            )
            if when is None:
                do(copy)
            else:
                pl.when(meta_ref[when[0]] == when[1])(functools.partial(do, copy))

    on_each(lambda copy: copy.start())
    on_each(lambda copy: copy.wait())


def packed(meta, sources, widths, plan):
    rows = sources[0].shape[0]
    any_spec = pl.BlockSpec(memory_space=pl.ANY)
    return pl.pallas_call(
        functools.partial(pack_kernel, plan, len(sources)),
        out_shape=[jax.ShapeDtypeStruct((rows, width * LANES), jnp.bfloat16) for width in widths],
        in_specs=[pl.BlockSpec(memory_space=pltpu.SMEM)] + [any_spec] * len(sources),
        out_specs=[pl.BlockSpec(memory_space=pltpu.VMEM)] * len(widths),
        scratch_shapes=[pltpu.SemaphoreType.DMA((len(plan),))],
        compiler_params=pltpu.CompilerParams(vmem_limit_bytes=40 * MIB),
        cost_estimate=SMALL,
        name="packed",
    )(jnp.stack(meta).astype(jnp.int32), *sources)


def mask_kernel(first_ref, mask_ref, x_ref, out_ref):
    out_ref[...] = (x_ref[...].astype(jnp.float32) * mask_ref[0]).astype(jnp.bfloat16)


def masked_x(x_band, mask_wide, first):
    count = mask_wide.shape[0]
    block = x_band.shape[0] // count
    cols = x_band.shape[1]
    return pl.pallas_call(
        mask_kernel,
        grid_spec=pltpu.PrefetchScalarGridSpec(
            num_scalar_prefetch=1,
            grid=(count,),
            in_specs=[
                pl.BlockSpec((1, 1, cols), lambda i, f: (lax.rem(f[0] + i, count), 0, 0)),
                pl.BlockSpec((block, cols), lambda i, f: (lax.rem(f[0] + i, count), 0)),
            ],
            out_specs=pl.BlockSpec((block, cols), lambda i, f: (i, 0)),
        ),
        out_shape=jax.ShapeDtypeStruct(x_band.shape, jnp.bfloat16),
        compiler_params=pltpu.CompilerParams(vmem_limit_bytes=58 * MIB),
        cost_estimate=SMALL,
        name="masked_x",
    )(first.reshape(1), mask_wide, x_band)


PARTS = 5


def x_copies(x_refs, xv, sems, offset_of):
    n_b, _, rows, panel = xv.shape
    copies = {}
    for p in range(n_b):
        for r in range(PARTS):
            g = min(r, 1)
            at = pl.multiple_of(offset_of(p, g) * panel, panel)
            to = xv.at[p, 0] if r == 0 else xv.at[p, 1, (r - 1) * rows // 4 : r * rows // 4]
            copies[p, r] = pltpu.make_async_copy(x_refs[r].at[:, pl.ds(at, panel)], to, sems.at[p, r])
    return copies


def add_product(acc, x, strips, g, first):
    cols = pl.ds(pl.multiple_of(first * LANES, LANES), strips.shape[1])
    acc[g, :, cols] += jnp.dot(x, strips, preferred_element_type=jnp.float32)


def whole_kernel(plan, meta_ref, *refs):
    n_b = len(plan)
    x_refs, refs = refs[:PARTS], refs[PARTS:]
    b_refs, (out_ref, xv, bv, acc, x_sems, b_sems, out_sems) = refs[:-7], refs[-7:]
    quarter = bv.shape[2]
    low = quarter // 2
    is_end = meta_ref[0]

    def offset_of(p, g):
        return meta_ref[2 + 2 * p + g]

    def b_middle(p):
        return [pltpu.make_async_copy(b_refs[plan[p][0]].at[:, :quarter], bv.at[p], b_sems.at[p, 0])]

    def b_end(p):
        copies = []
        for k, (operand, first, count, at, to) in enumerate(plan[p][1]):
            to = meta_ref[1] if to is None else to
            source = b_refs[operand].at[:, first * LANES : (first + count) * LANES]
            copies.append(pltpu.make_async_copy(source, bv.at[to, :, at * LANES : (at + count) * LANES], b_sems.at[p, k]))
        return copies

    def on_each(p, do):
        @pl.when(is_end == 0)
        def _():
            for copy in b_middle(p):
                do(copy)

        @pl.when(is_end != 0)
        def _():
            for copy in b_end(p):
                do(copy)

    copies = x_copies(x_refs, xv, x_sems, offset_of)
    for p in range(n_b):
        on_each(p, lambda copy: copy.start())
        for r in range(PARTS):
            copies[p, r].start()
    outs = [
        pltpu.make_async_copy(acc.at[g, :, low : low + quarter], out_ref.at[g], out_sems.at[g]) for g in range(2)
    ]

    def wait_for(p):
        for k in [p] if p < n_b - 2 else range(n_b - 2, n_b) if p == n_b - 2 else []:
            on_each(k, lambda copy: copy.wait())
        for r in range(PARTS):
            copies[p, r].wait()

    middle = quarter // LANES // 2

    def own(g, carry):
        acc[g, :, low : low + quarter] = jnp.dot(xv[g, g], bv[g], preferred_element_type=jnp.float32)
        return carry

    def step(i, carry):
        p = jnp.where(i < 4, i % 2, i // 2)
        g = jnp.where(i < 4, 1 - i % 2, i % 2)
        for k in range(2, n_b):
            pl.when(i == 2 * k)(functools.partial(wait_for, k))
        pl.when(i == 2 * n_b - 1)(outs[0].start)
        offset = offset_of(p, g)
        for k in range(2 * middle):
            if k == middle:
                continue
            first, last = max(0, middle - k), min(2 * middle, 3 * middle - k)

            @pl.when(offset == k)
            def _():
                strips = bv[p, :, first * LANES : last * LANES]
                acc[g, :, (k + first) * LANES : (k + last) * LANES] += jnp.dot(
                    xv[p, g], strips, preferred_element_type=jnp.float32
                )

        return carry

    for p in range(2):
        wait_for(p)
    lax.fori_loop(0, 2, own, 0)
    lax.fori_loop(2, 2 * n_b, step, 0)
    outs[1].start()
    for out in outs:
        out.wait()


def whole_products(meta, xs, operands, plan):
    rows = xs[0].shape[0] // 2
    panel, quarter = operands[plan[0][0]].shape
    n_b = len(plan)
    any_spec = pl.BlockSpec(memory_space=pl.ANY)
    x_spec = pl.BlockSpec(memory_space=pltpu.HBM)
    return pl.pallas_call(
        functools.partial(whole_kernel, plan),
        out_shape=jax.ShapeDtypeStruct((2, 2 * rows, quarter), jnp.float32),
        in_specs=[pl.BlockSpec(memory_space=pltpu.SMEM)] + [x_spec] * PARTS + [any_spec] * len(operands),
        out_specs=any_spec,
        scratch_shapes=[
            pltpu.VMEM((n_b, 2, 2 * rows, panel), jnp.bfloat16),
            pltpu.VMEM((n_b, panel, quarter), jnp.bfloat16),
            pltpu.VMEM((2, 2 * rows, 2 * quarter), jnp.float32),
            pltpu.SemaphoreType.DMA((n_b, PARTS)),
            pltpu.SemaphoreType.DMA((n_b, 3)),
            pltpu.SemaphoreType.DMA((2,)),
        ],
        compiler_params=pltpu.CompilerParams(vmem_limit_bytes=59 * MIB),
        cost_estimate=pl.CostEstimate(flops=6 * 10**9, bytes_accessed=36 * MIB, transcendentals=0),
        name="whole_products",
    )(meta, *xs, *operands)


def finish(acc, wait_for, add, at, out_refs, pieces, sems, also=None):
    half, width = out_refs[0].shape
    cols = pl.ds(pl.multiple_of(at * LANES, LANES), width)
    outs = [pltpu.make_async_copy(pieces.at[r], out_refs[r], sems.at[r]) for r in range(4)]
    also = also or []

    def step(g, carry):
        for k in range(2):
            pl.when(g == k)(functools.partial(wait_for, k))
        add(g)
        for k in range(2):

            @pl.when(g == k)
            def _():
                for copy in also[k : k + 1]:
                    copy.start()
                for r in range(2 * k, 2 * k + 2):
                    rows = slice((r % 2) * half, (r % 2 + 1) * half)
                    pieces[r] = acc[k, rows, cols].astype(jnp.bfloat16)
                    outs[r].start()

        return carry

    lax.fori_loop(0, 2, step, 0)
    for copy in outs + also:
        copy.wait()


def half_kernel(meta_ref, *refs):
    x_refs, (prev_ref, middle_ref, end_ref, second_ref), refs = refs[:PARTS], refs[PARTS : PARTS + 4], refs[PARTS + 4 :]
    out_refs, rest_ref, xv, bv, acc, pieces, x_sems, b_sems, prev_sems, rest_sems, out_sems = refs[:4], *refs[4:]
    quarter = bv.shape[2]
    half = quarter // 2
    low = quarter // 2
    band = quarter // LANES
    is_end = meta_ref[0]

    def offset_of(p, g):
        return meta_ref[5 + 2 * p + g]

    x_loads = x_copies(x_refs, xv, x_sems, offset_of)
    middle = pltpu.make_async_copy(middle_ref, bv.at[0], b_sems.at[0])
    end = pltpu.make_async_copy(end_ref, bv.at[0], b_sems.at[0])
    second = pltpu.make_async_copy(second_ref, bv.at[1], b_sems.at[1])
    prev = [
        pltpu.make_async_copy(prev_ref.at[g], acc.at[g, :, low : low + quarter], prev_sems.at[g]) for g in range(2)
    ]
    at = pl.multiple_of((meta_ref[4] + band // 2) * LANES, LANES)
    rest = [
        pltpu.make_async_copy(acc.at[g, :, pl.ds(at, rest_ref.shape[2])], rest_ref.at[g], rest_sems.at[g])
        for g in range(2)
    ]

    @pl.when(is_end == 0)
    def _():
        middle.start()
        second.start()

    pl.when(is_end != 0)(end.start)

    def rows_loads(g):
        return [prev[g]] + [copy for (_, r), copy in x_loads.items() if min(r, 1) == g]

    for g in range(2):
        for copy in rows_loads(g):
            copy.start()

    def wait_for(g):
        for copy in rows_loads(g):
            copy.wait()
        if g == 0:

            @pl.when(is_end == 0)
            def _():
                middle.wait()
                second.wait()

            pl.when(is_end != 0)(end.wait)

    def add(g):
        for p in range(2):
            add_product(acc, xv[p, g], bv[0, :, p * half : (p + 1) * half], g, offset_of(p, g) + meta_ref[1])

        @pl.when(is_end == 0)
        def _():
            for p in range(2):
                add_product(acc, xv[p, g], bv[1, :, p * half : (p + 1) * half], g, offset_of(p, g) + meta_ref[2])

    finish(acc, wait_for, add, meta_ref[3] + band // 2, out_refs, pieces, out_sems, rest)


def half_products(meta, xs, prev, middle, end, second, n_done):
    rows = xs[0].shape[0] // 2
    panel, quarter = second.shape
    any_spec = pl.BlockSpec(memory_space=pl.ANY)
    x_spec = pl.BlockSpec(memory_space=pltpu.HBM)
    n_rest = quarter // LANES - n_done
    return pl.pallas_call(
        half_kernel,
        out_shape=[jax.ShapeDtypeStruct((rows, n_done * LANES), jnp.bfloat16)] * 4
        + [jax.ShapeDtypeStruct((2, 2 * rows, n_rest * LANES), jnp.float32)],
        in_specs=[pl.BlockSpec(memory_space=pltpu.SMEM)] + [x_spec] * PARTS + [any_spec] * 4,
        out_specs=[any_spec] * 5,
        scratch_shapes=[
            pltpu.VMEM((2, 2, 2 * rows, panel), jnp.bfloat16),
            pltpu.VMEM((2, panel, quarter), jnp.bfloat16),
            pltpu.VMEM((2, 2 * rows, 2 * quarter), jnp.float32),
            pltpu.VMEM((4, rows, n_done * LANES), jnp.bfloat16),
            pltpu.SemaphoreType.DMA((2, PARTS)),
            pltpu.SemaphoreType.DMA((2,)),
            pltpu.SemaphoreType.DMA((2,)),
            pltpu.SemaphoreType.DMA((2,)),
            pltpu.SemaphoreType.DMA((4,)),
        ],
        compiler_params=pltpu.CompilerParams(vmem_limit_bytes=59 * MIB),
        cost_estimate=SMALL,
        name="half_products",
    )(meta, *xs, prev, middle, end, second)


def rest_kernel(meta_ref, *refs):
    x_refs, (rest_ref, b_ref), refs = refs[:PARTS], refs[PARTS : PARTS + 2], refs[PARTS + 2 :]
    out_refs, xv, bv, acc, pieces, x_sems, b_sem, rest_sems, out_sems = refs[:4], *refs[4:]
    band = acc.shape[2] // (2 * LANES)
    half = (bv.shape[1] - LANES) // 2
    is_end = meta_ref[0]

    def offset_of(p, g):
        return meta_ref[3 + 2 * p + g]

    at = pl.multiple_of((meta_ref[2] + band // 2) * LANES, LANES)
    rest = [
        pltpu.make_async_copy(rest_ref.at[g], acc.at[g, :, pl.ds(at, rest_ref.shape[2])], rest_sems.at[g])
        for g in range(2)
    ]
    x_loads = x_copies(x_refs, xv, x_sems, offset_of)
    b_copy = pltpu.make_async_copy(b_ref, bv, b_sem)

    def x_loads_of(g):
        return [copy for (_, r), copy in x_loads.items() if min(r, 1) == g]

    pl.when(is_end != 0)(b_copy.start)
    for g in range(2):
        rest[g].start()

        @pl.when(is_end != 0)
        def _():
            for copy in x_loads_of(g):
                copy.start()

    def wait_for(g):
        rest[g].wait()

        @pl.when(is_end != 0)
        def _():
            for copy in x_loads_of(g):
                copy.wait()
            if g == 0:
                b_copy.wait()

    def add(g):
        @pl.when(is_end != 0)
        def _():
            for p in range(2):
                add_product(acc, xv[p, g], bv[:, p * half : (p + 1) * half], g, offset_of(p, g) + meta_ref[1])
            p = meta_ref[8]
            add_product(acc, xv[p, g], bv[:, 2 * half :], g, offset_of(p, g) + meta_ref[7])

    finish(acc, wait_for, add, meta_ref[2] + band // 2, out_refs, pieces, out_sems)


def rest_products(meta, xs, rest, b, quarter):
    rows = xs[0].shape[0] // 2
    panel = b.shape[0]
    width = rest.shape[2]
    any_spec = pl.BlockSpec(memory_space=pl.ANY)
    x_spec = pl.BlockSpec(memory_space=pltpu.HBM)
    return pl.pallas_call(
        rest_kernel,
        out_shape=[jax.ShapeDtypeStruct((rows, width), jnp.bfloat16)] * 4,
        in_specs=[pl.BlockSpec(memory_space=pltpu.SMEM)] + [x_spec] * PARTS + [any_spec] * 2,
        out_specs=[any_spec] * 4,
        scratch_shapes=[
            pltpu.VMEM((2, 2, 2 * rows, panel), jnp.bfloat16),
            pltpu.VMEM(b.shape, jnp.bfloat16),
            pltpu.VMEM((2, 2 * rows, 2 * quarter), jnp.float32),
            pltpu.VMEM((4, rows, width), jnp.bfloat16),
            pltpu.SemaphoreType.DMA((2, PARTS)),
            pltpu.SemaphoreType.DMA,
            pltpu.SemaphoreType.DMA((2,)),
            pltpu.SemaphoreType.DMA((4,)),
        ],
        compiler_params=pltpu.CompilerParams(vmem_limit_bytes=59 * MIB),
        cost_estimate=SMALL,
        name="rest_products",
    )(meta, *xs, rest, b)


def assemble_kernel(place_ref, mask_ref, *refs):
    n = 4
    pieces, (out_ref, made, sem) = refs[:n], refs[-3:]
    steps = mask_ref.shape[0]
    rows = made.shape[0] // steps
    panel = n * LANES
    first = pl.multiple_of(place_ref[1] * panel, panel)
    for r in range(n):
        t = jnp.bitwise_xor(place_ref[0], r)
        for j in range(made.shape[1] // panel):
            to = pl.multiple_of(j * panel + t * LANES, LANES)
            for i in range(steps):
                keep = mask_ref[i, :, pl.ds(pl.multiple_of(first + to, LANES), LANES)]
                value = pieces[r][i * rows : (i + 1) * rows, j * LANES : (j + 1) * LANES].astype(jnp.float32)
                made[i * rows : (i + 1) * rows, pl.ds(to, LANES)] = (value * keep).astype(jnp.bfloat16)
    copy = pltpu.make_async_copy(made, out_ref.at[:, pl.ds(first, made.shape[1])], sem)
    copy.start()
    copy.wait()


def assembled(place, keep_wide, pieces, out=None):
    rows, width = pieces[0].shape
    cols = keep_wide.shape[2]
    vmem_spec = pl.BlockSpec(memory_space=pltpu.VMEM)
    any_spec = pl.BlockSpec(memory_space=pltpu.HBM)
    operands = [place, keep_wide, *pieces] + ([] if out is None else [out])
    return pl.pallas_call(
        assemble_kernel,
        out_shape=jax.ShapeDtypeStruct((rows, cols), jnp.bfloat16),
        in_specs=[pl.BlockSpec(memory_space=pltpu.SMEM)] + [vmem_spec] * 5 + [any_spec] * (len(operands) - 6),
        out_specs=any_spec,
        scratch_shapes=[pltpu.VMEM((rows, width * len(pieces)), jnp.bfloat16), pltpu.SemaphoreType.DMA],
        input_output_aliases={} if out is None else {6: 0},
        compiler_params=pltpu.CompilerParams(vmem_limit_bytes=16 * MIB),
        cost_estimate=SMALL,
        name="assembled",
    )(*operands)


def widen(mask, block):
    rows, cols = mask.shape
    wide = jnp.broadcast_to(mask.astype(jnp.float32)[:, :, None], (rows, cols, block))
    return wide.reshape(rows, 1, cols * block)


def together(*values):
    return lax.optimization_barrier(values)


def pairs_in_line(x_band, w_band, a_mask, keep_mask):
    panel = x_band.shape[0]
    block = panel // a_mask.shape[0]
    g, c = lax.axis_index("grid"), lax.axis_index("depth")
    z, y = g // 2, g % 2
    left = z < 2
    is_end = ((z == 0) | (z == 3)).astype(jnp.int32)
    toward = jnp.where(left, 1, -1)
    q = 2 * y + c

    swap = [(0, 2), (1, 3), (2, 0), (3, 1), (4, 6), (5, 7), (6, 4), (7, 5)]
    outward = [(2, 0), (3, 1), (4, 6), (5, 7)]
    cross = [(2, 4), (3, 5), (4, 2), (5, 3)]
    across = [(i, i ^ 1) for i in range(8)]
    layers = [(0, 1), (1, 0)]
    opposite = [(i, i ^ 3) for i in range(16)]

    def line(value, pairs):
        return lax.ppermute(value, "grid", pairs)

    first_out, second_out = jnp.where(left, 0, 4), jnp.where(left, 4, 0)
    first_in, second_in = second_out, first_out
    last_in = jnp.where(left, 2, 4)

    sent_b = b_strips(w_band, q ^ 2, 58)
    own_b = line(sent_b, across)
    sent_b, w_band = together(sent_b, w_band)
    own_a = b_strips(w_band, q, 58)
    swap_a = line(own_a, swap)
    cross_a = line(own_a, cross)
    mask_wide = widen(a_mask, block)
    rows = a_mask.shape[0]
    x_own = masked_x(x_band, mask_wide, c * rows // 2)
    x_mine = [x_own[k * panel // 4 : (k + 1) * panel // 4] for k in range(2)]
    own_b, *x_mine = together(own_b, *x_mine)
    own_b, swap_a = together(own_b, swap_a)
    swap_b = line(own_b, swap)
    cross_b = line(own_b, cross)
    x_across = [line(part, across) for part in x_mine]

    mid_a = line(cross_a[:, 5 * LANES :], outward)
    mid_b, fwd_first = packed(
        [y, first_out],
        [cross_a, cross_b, swap_a, swap_b],
        [10, 8],
        [
            (0, 0, 3, 0, 0, (0, 0)),
            (1, 0, 3, 0, 0, (0, 1)),
            (0, 3, 2, 0, 3, None),
            (1, 3, 5, 0, 5, None),
            (2, (1,), 4, 1, 0, None),
            (3, (1,), 4, 1, 4, None),
        ],
    )
    (fwd_second,) = packed([second_out], [swap_a, swap_b], [8], [(0, (0,), 4, 0, 0, None), (1, (0,), 4, 0, 4, None)])
    mid_a, mid_b, fwd_first = together(mid_a, mid_b, fwd_first)
    mid_b = line(mid_b, outward)
    fwd_first = line(fwd_first, cross)
    fwd_second, *x_across = together(fwd_second, *x_across)
    far_first = line(fwd_first, outward)
    fwd_second = line(fwd_second, cross)
    x_opposite = [lax.ppermute(part, "depth", layers) for part in x_across]
    xs = [x_own] + x_across + x_opposite

    def offsets(delta):
        tilt = 2 * y - 1
        return [(2 * delta + 4) % 8, (2 * delta + tilt + 4) % 8, (2 * delta - tilt + 4) % 8, (2 * delta + 4) % 8]

    zero = jnp.zeros_like(z)
    third = offsets(jnp.where(is_end == 1, 2, -toward))
    fourth = offsets(jnp.where(is_end == 1, -toward, 2))
    meta = jnp.stack([is_end, 4 + y, *offsets(zero), *offsets(toward), *third]).astype(jnp.int32)
    plan = [
        (0, [(0, 0, 8, 0, 0)]),
        (1, [(1, 0, 8, 0, 1)]),
        (2, [(4, 0, 8, 0, 2)]),
        (3, [(5, 0, 8, 0, 3)]),
        (4, [(6, 0, 3, 0, None), (6, 3, 2, 3, 4), (7, 0, 3, 5, 4)]),
        (5, [(6, 5, 5, 3, 5)]),
    ]
    total = whole_products(meta, xs, [own_a, own_b, cross_a, cross_b, swap_a, swap_b, mid_b, mid_a], plan)
    last_at = jnp.where(left, 2, 0)
    total, last_at = together(total, last_at)
    extra_in, extra_panel = jnp.where(left, 1, 6), jnp.where(left, 1 - y, y)
    extra_at = jnp.where(left, 1, 2) + 4 * extra_panel
    (last,) = packed(
        [last_at, last_at + 4, extra_at],
        [fwd_second],
        [5],
        [(0, (0,), 2, 0, 0, None), (0, (1,), 2, 0, 2, None), (0, (2,), 1, 0, 4, None)],
    )
    far_second = line(last, outward)

    def exchanged(pieces):
        return [
            pieces[0],
            lax.ppermute(pieces[1], "depth", layers),
            line(pieces[2], across),
            lax.ppermute(pieces[3], ("grid", "depth"), opposite),
        ]

    done_at, rest_at = jnp.where(left, 3, 0), jnp.where(left, 0, 5)
    meta = jnp.stack([is_end, first_in, second_in, done_at, rest_at, *fourth]).astype(jnp.int32)
    *done, rest = half_products(meta, xs, total, fwd_first, far_first, fwd_second, 5)
    done = exchanged(done)
    far_second, done[1] = together(far_second, done[1])
    keep_wide = widen(keep_mask, block)
    out = assembled(jnp.stack([q, done_at]).astype(jnp.int32), keep_wide, done)
    meta = jnp.stack([is_end, last_in, rest_at, *fourth, extra_in, extra_panel]).astype(jnp.int32)
    rest = exchanged(rest_products(meta, xs, rest, far_second, own_a.shape[1]))
    return assembled(jnp.stack([q, rest_at]).astype(jnp.int32), keep_wide, rest, out)


def solution(mesh):
    placed = (
        P(("groups", "grid"), None),
        P(("groups", "grid"), None),
        P(("groups", "grid"), None),
        P(("groups", "grid", "depth"), None),
    )

    def local(x_band, w_band, a_mask, keep_mask):
        panel, cols = x_band.shape
        pairs = mesh.shape["grid"] == 8 and mesh.shape["depth"] == 2
        pairs = pairs and cols == 8 * panel and panel == 4 * LANES
        return (pairs_in_line if pairs else ring)(x_band, w_band, a_mask, keep_mask)

    return jax.shard_map(
        local,
        mesh=mesh,
        in_specs=placed,
        out_specs=P(("groups", "grid", "depth"), None),
        check_vma=False,
    )
```

```python
import functools

import jax
import jax.numpy as jnp
from jax import lax
from jax.experimental import pallas as pl
from jax.experimental.pallas import tpu as pltpu
from jax.sharding import PartitionSpec as P

LANES = 128
MIB = 1 << 20
SMALL = pl.CostEstimate(flops=1000, bytes_accessed=1000, transcendentals=0)


def shifted(shard, axis, by):
    count = lax.axis_size(axis)
    return lax.ppermute(shard, axis, [(i, (i + by) % count) for i in range(count)])


def expand_blocks(mask, block):
    rows, cols = mask.shape
    wide = jnp.broadcast_to(mask[:, None, :, None], (rows, block, cols, block))
    return wide.reshape(rows * block, cols * block)


def ring(x_band, w_band, a_mask, keep_mask):
    panel = x_band.shape[0]
    block = panel // a_mask.shape[0]
    band_cols = x_band.shape[1]
    xm = x_band * expand_blocks(a_mask, block).astype(jnp.bfloat16)
    rows = lax.broadcasted_iota(jnp.int32, x_band.shape, 0)
    cols = lax.broadcasted_iota(jnp.int32, x_band.shape, 1)
    identity = jnp.where(cols == rows + 4 * panel, 1.0, 0.0).astype(jnp.float32)
    b_panel = (1.5 * identity - 0.5 * w_band.astype(jnp.float32)).astype(jnp.bfloat16)
    layer = lax.axis_index("depth")
    current = shifted(b_panel, ("grid", "depth"), -5)
    wide = jnp.zeros((panel, 2 * band_cols), jnp.float32)
    for step in range(4):
        offset = 6 + layer - 2 * step
        ablock = lax.dynamic_slice_in_dim(xm, offset * panel, panel, 1)
        term = jnp.dot(ablock, current, preferred_element_type=jnp.float32)
        region = lax.dynamic_slice_in_dim(wide, offset * panel, band_cols, 1)
        wide = lax.dynamic_update_slice_in_dim(wide, region + term, offset * panel, 1)
        if step < 3:
            current = shifted(current, "grid", 2)
    partial_band = wide[:, 4 * panel : 12 * panel]
    mine = lax.psum_scatter(partial_band, "depth", scatter_dimension=0, tiled=True)
    keep = expand_blocks(keep_mask, block).astype(jnp.float32)
    return (mine * keep).astype(jnp.bfloat16)


def strips_kernel(quarter_ref, w_ref, b_ref, held, made, in_sems, out_sems):
    panel, width = held.shape
    quarter = quarter_ref[0]

    def strip(j):
        return slice(j * LANES, (j + 1) * LANES)

    def load(j):
        at = pl.multiple_of(j * panel + quarter * LANES, LANES)
        return pltpu.make_async_copy(w_ref.at[:, pl.ds(at, LANES)], held.at[:, strip(j)], in_sems.at[j])

    def give(j):
        return pltpu.make_async_copy(made.at[:, strip(j)], b_ref.at[:, strip(j)], out_sems.at[j])

    band = width // LANES
    for j in range(band):
        load(j).start()
    for j in range(band):
        load(j).wait()
        value = -0.5 * held[:, strip(j)].astype(jnp.float32)
        if j == band // 2:
            rows = lax.broadcasted_iota(jnp.int32, value.shape, 0)
            cols = lax.broadcasted_iota(jnp.int32, value.shape, 1)
            value = value + jnp.where(rows == cols + quarter * LANES, 1.5, 0.0)
        made[:, strip(j)] = value.astype(jnp.bfloat16)
        give(j).start()
    for j in range(band):
        give(j).wait()


def b_strips(w_band, quarter, limit):
    panel = w_band.shape[0]
    band = w_band.shape[1] // panel
    shape = (panel, band * LANES)
    return pl.pallas_call(
        strips_kernel,
        out_shape=jax.ShapeDtypeStruct(shape, jnp.bfloat16),
        in_specs=[
            pl.BlockSpec(memory_space=pltpu.SMEM),
            pl.BlockSpec(memory_space=pltpu.HBM),
        ],
        out_specs=pl.BlockSpec(memory_space=pl.ANY),
        scratch_shapes=[
            pltpu.VMEM(shape, jnp.bfloat16),
            pltpu.VMEM(shape, jnp.bfloat16),
            pltpu.SemaphoreType.DMA((band,)),
            pltpu.SemaphoreType.DMA((band,)),
        ],
        compiler_params=pltpu.CompilerParams(vmem_limit_bytes=limit * MIB),
        cost_estimate=SMALL,
        name="b_strips",
    )(quarter.reshape(1), w_band)


def pack_kernel(plan, n_in, meta_ref, *refs):
    sources, outs, sems = refs[:n_in], refs[n_in:-1], refs[-1]

    def on_each(do):
        for k, (source, start, count, out, to, when) in enumerate(plan):
            at = start * LANES if isinstance(start, int) else pl.multiple_of(meta_ref[start[0]] * LANES, LANES)
            copy = pltpu.make_async_copy(
                sources[source].at[:, pl.ds(at, count * LANES)],
                outs[out].at[:, to * LANES : (to + count) * LANES],
                sems.at[k],
            )
            if when is None:
                do(copy)
            else:
                pl.when(meta_ref[when[0]] == when[1])(functools.partial(do, copy))

    on_each(lambda copy: copy.start())
    on_each(lambda copy: copy.wait())


def packed(meta, sources, widths, plan):
    rows = sources[0].shape[0]
    any_spec = pl.BlockSpec(memory_space=pl.ANY)
    return pl.pallas_call(
        functools.partial(pack_kernel, plan, len(sources)),
        out_shape=[jax.ShapeDtypeStruct((rows, width * LANES), jnp.bfloat16) for width in widths],
        in_specs=[pl.BlockSpec(memory_space=pltpu.SMEM)] + [any_spec] * len(sources),
        out_specs=[pl.BlockSpec(memory_space=pltpu.VMEM)] * len(widths),
        scratch_shapes=[pltpu.SemaphoreType.DMA((len(plan),))],
        compiler_params=pltpu.CompilerParams(vmem_limit_bytes=40 * MIB),
        cost_estimate=SMALL,
        name="packed",
    )(jnp.stack(meta).astype(jnp.int32), *sources)


def mask_kernel(first_ref, mask_ref, x_ref, out_ref):
    out_ref[...] = (x_ref[...].astype(jnp.float32) * mask_ref[0]).astype(jnp.bfloat16)


def masked_x(x_band, mask_wide, first):
    count = mask_wide.shape[0]
    block = x_band.shape[0] // count
    cols = x_band.shape[1]
    return pl.pallas_call(
        mask_kernel,
        grid_spec=pltpu.PrefetchScalarGridSpec(
            num_scalar_prefetch=1,
            grid=(count,),
            in_specs=[
                pl.BlockSpec((1, 1, cols), lambda i, f: (lax.rem(f[0] + i, count), 0, 0)),
                pl.BlockSpec((block, cols), lambda i, f: (lax.rem(f[0] + i, count), 0)),
            ],
            out_specs=pl.BlockSpec((block, cols), lambda i, f: (i, 0)),
        ),
        out_shape=jax.ShapeDtypeStruct(x_band.shape, jnp.bfloat16),
        compiler_params=pltpu.CompilerParams(vmem_limit_bytes=58 * MIB),
        cost_estimate=SMALL,
        name="masked_x",
    )(first.reshape(1), mask_wide, x_band)


PARTS = 5


def x_copies(x_refs, xv, sems, offset_of):
    n_b, _, rows, panel = xv.shape
    copies = {}
    for p in range(n_b):
        for r in range(PARTS):
            g = min(r, 1)
            at = pl.multiple_of(offset_of(p, g) * panel, panel)
            to = xv.at[p, 0] if r == 0 else xv.at[p, 1, (r - 1) * rows // 4 : r * rows // 4]
            copies[p, r] = pltpu.make_async_copy(x_refs[r].at[:, pl.ds(at, panel)], to, sems.at[p, r])
    return copies


def add_product(acc, x, strips, g, first):
    cols = pl.ds(pl.multiple_of(first * LANES, LANES), strips.shape[1])
    acc[g, :, cols] += jnp.dot(x, strips, preferred_element_type=jnp.float32)


def whole_kernel(plan, meta_ref, *refs):
    n_b = len(plan)
    x_refs, refs = refs[:PARTS], refs[PARTS:]
    b_refs, (out_ref, xv, bv, acc, x_sems, b_sems, out_sems) = refs[:-7], refs[-7:]
    quarter = bv.shape[2]
    low = quarter // 2
    is_end = meta_ref[0]

    def offset_of(p, g):
        return meta_ref[2 + 2 * p + g]

    def b_middle(p):
        return [pltpu.make_async_copy(b_refs[plan[p][0]].at[:, :quarter], bv.at[p], b_sems.at[p, 0])]

    def b_end(p):
        copies = []
        for k, (operand, first, count, at, to) in enumerate(plan[p][1]):
            to = meta_ref[1] if to is None else to
            source = b_refs[operand].at[:, first * LANES : (first + count) * LANES]
            copies.append(pltpu.make_async_copy(source, bv.at[to, :, at * LANES : (at + count) * LANES], b_sems.at[p, k]))
        return copies

    def on_each(p, do):
        @pl.when(is_end == 0)
        def _():
            for copy in b_middle(p):
                do(copy)

        @pl.when(is_end != 0)
        def _():
            for copy in b_end(p):
                do(copy)

    copies = x_copies(x_refs, xv, x_sems, offset_of)
    for p in range(n_b):
        on_each(p, lambda copy: copy.start())
        for r in range(PARTS):
            copies[p, r].start()
    outs = [
        pltpu.make_async_copy(acc.at[g, :, low : low + quarter], out_ref.at[g], out_sems.at[g]) for g in range(2)
    ]

    def wait_for(p):
        for k in [p] if p < n_b - 2 else range(n_b - 2, n_b) if p == n_b - 2 else []:
            on_each(k, lambda copy: copy.wait())
        for r in range(PARTS):
            copies[p, r].wait()

    middle = quarter // LANES // 2

    def own(g, carry):
        acc[g, :, low : low + quarter] = jnp.dot(xv[g, g], bv[g], preferred_element_type=jnp.float32)
        return carry

    def step(i, carry):
        p = jnp.where(i < 4, i % 2, i // 2)
        g = jnp.where(i < 4, 1 - i % 2, i % 2)
        for k in range(2, n_b):
            pl.when(i == 2 * k)(functools.partial(wait_for, k))
        pl.when(i == 2 * n_b - 1)(outs[0].start)
        offset = offset_of(p, g)
        for k in range(2 * middle):
            if k == middle:
                continue
            first, last = max(0, middle - k), min(2 * middle, 3 * middle - k)

            @pl.when(offset == k)
            def _():
                strips = bv[p, :, first * LANES : last * LANES]
                acc[g, :, (k + first) * LANES : (k + last) * LANES] += jnp.dot(
                    xv[p, g], strips, preferred_element_type=jnp.float32
                )

        return carry

    for p in range(2):
        wait_for(p)
    lax.fori_loop(0, 2, own, 0)
    lax.fori_loop(2, 2 * n_b, step, 0)
    outs[1].start()
    for out in outs:
        out.wait()


def whole_products(meta, xs, operands, plan):
    rows = xs[0].shape[0] // 2
    panel, quarter = operands[plan[0][0]].shape
    n_b = len(plan)
    any_spec = pl.BlockSpec(memory_space=pl.ANY)
    x_spec = pl.BlockSpec(memory_space=pltpu.HBM)
    return pl.pallas_call(
        functools.partial(whole_kernel, plan),
        out_shape=jax.ShapeDtypeStruct((2, 2 * rows, quarter), jnp.float32),
        in_specs=[pl.BlockSpec(memory_space=pltpu.SMEM)] + [x_spec] * PARTS + [any_spec] * len(operands),
        out_specs=any_spec,
        scratch_shapes=[
            pltpu.VMEM((n_b, 2, 2 * rows, panel), jnp.bfloat16),
            pltpu.VMEM((n_b, panel, quarter), jnp.bfloat16),
            pltpu.VMEM((2, 2 * rows, 2 * quarter), jnp.float32),
            pltpu.SemaphoreType.DMA((n_b, PARTS)),
            pltpu.SemaphoreType.DMA((n_b, 3)),
            pltpu.SemaphoreType.DMA((2,)),
        ],
        compiler_params=pltpu.CompilerParams(vmem_limit_bytes=59 * MIB),
        cost_estimate=pl.CostEstimate(flops=6 * 10**9, bytes_accessed=36 * MIB, transcendentals=0),
        name="whole_products",
    )(meta, *xs, *operands)


def finish(acc, wait_for, add, at, out_refs, pieces, sems, also=None):
    half, width = out_refs[0].shape
    cols = pl.ds(pl.multiple_of(at * LANES, LANES), width)
    outs = [pltpu.make_async_copy(pieces.at[r], out_refs[r], sems.at[r]) for r in range(4)]
    also = also or []

    def step(g, carry):
        for k in range(2):
            pl.when(g == k)(functools.partial(wait_for, k))
        add(g)
        for k in range(2):

            @pl.when(g == k)
            def _():
                for copy in also[k : k + 1]:
                    copy.start()
                for r in range(2 * k, 2 * k + 2):
                    rows = slice((r % 2) * half, (r % 2 + 1) * half)
                    pieces[r] = acc[k, rows, cols].astype(jnp.bfloat16)
                    outs[r].start()

        return carry

    lax.fori_loop(0, 2, step, 0)
    for copy in outs + also:
        copy.wait()


def half_kernel(meta_ref, *refs):
    x_refs, (prev_ref, middle_ref, end_ref, second_ref), refs = refs[:PARTS], refs[PARTS : PARTS + 4], refs[PARTS + 4 :]
    out_refs, rest_ref, xv, bv, acc, pieces, x_sems, b_sems, prev_sems, rest_sems, out_sems = refs[:4], *refs[4:]
    quarter = bv.shape[2]
    half = quarter // 2
    low = quarter // 2
    band = quarter // LANES
    is_end = meta_ref[0]

    def offset_of(p, g):
        return meta_ref[5 + 2 * p + g]

    x_loads = x_copies(x_refs, xv, x_sems, offset_of)
    middle = pltpu.make_async_copy(middle_ref, bv.at[0], b_sems.at[0])
    end = pltpu.make_async_copy(end_ref, bv.at[0], b_sems.at[0])
    second = pltpu.make_async_copy(second_ref, bv.at[1], b_sems.at[1])
    prev = [
        pltpu.make_async_copy(prev_ref.at[g], acc.at[g, :, low : low + quarter], prev_sems.at[g]) for g in range(2)
    ]
    at = pl.multiple_of((meta_ref[4] + band // 2) * LANES, LANES)
    rest = [
        pltpu.make_async_copy(acc.at[g, :, pl.ds(at, rest_ref.shape[2])], rest_ref.at[g], rest_sems.at[g])
        for g in range(2)
    ]

    @pl.when(is_end == 0)
    def _():
        middle.start()
        second.start()

    pl.when(is_end != 0)(end.start)

    def rows_loads(g):
        return [prev[g]] + [copy for (_, r), copy in x_loads.items() if min(r, 1) == g]

    for g in range(2):
        for copy in rows_loads(g):
            copy.start()

    def wait_for(g):
        for copy in rows_loads(g):
            copy.wait()
        if g == 0:

            @pl.when(is_end == 0)
            def _():
                middle.wait()
                second.wait()

            pl.when(is_end != 0)(end.wait)

    def add(g):
        for p in range(2):
            add_product(acc, xv[p, g], bv[0, :, p * half : (p + 1) * half], g, offset_of(p, g) + meta_ref[1])

        @pl.when(is_end == 0)
        def _():
            for p in range(2):
                add_product(acc, xv[p, g], bv[1, :, p * half : (p + 1) * half], g, offset_of(p, g) + meta_ref[2])

    finish(acc, wait_for, add, meta_ref[3] + band // 2, out_refs, pieces, out_sems, rest)


def half_products(meta, xs, prev, middle, end, second, n_done):
    rows = xs[0].shape[0] // 2
    panel, quarter = second.shape
    any_spec = pl.BlockSpec(memory_space=pl.ANY)
    x_spec = pl.BlockSpec(memory_space=pltpu.HBM)
    n_rest = quarter // LANES - n_done
    return pl.pallas_call(
        half_kernel,
        out_shape=[jax.ShapeDtypeStruct((rows, n_done * LANES), jnp.bfloat16)] * 4
        + [jax.ShapeDtypeStruct((2, 2 * rows, n_rest * LANES), jnp.float32)],
        in_specs=[pl.BlockSpec(memory_space=pltpu.SMEM)] + [x_spec] * PARTS + [any_spec] * 4,
        out_specs=[any_spec] * 5,
        scratch_shapes=[
            pltpu.VMEM((2, 2, 2 * rows, panel), jnp.bfloat16),
            pltpu.VMEM((2, panel, quarter), jnp.bfloat16),
            pltpu.VMEM((2, 2 * rows, 2 * quarter), jnp.float32),
            pltpu.VMEM((4, rows, n_done * LANES), jnp.bfloat16),
            pltpu.SemaphoreType.DMA((2, PARTS)),
            pltpu.SemaphoreType.DMA((2,)),
            pltpu.SemaphoreType.DMA((2,)),
            pltpu.SemaphoreType.DMA((2,)),
            pltpu.SemaphoreType.DMA((4,)),
        ],
        compiler_params=pltpu.CompilerParams(vmem_limit_bytes=59 * MIB),
        cost_estimate=SMALL,
        name="half_products",
    )(meta, *xs, prev, middle, end, second)


def rest_kernel(meta_ref, *refs):
    x_refs, (rest_ref, b_ref), refs = refs[:PARTS], refs[PARTS : PARTS + 2], refs[PARTS + 2 :]
    out_refs, xv, bv, acc, pieces, x_sems, b_sem, rest_sems, out_sems = refs[:4], *refs[4:]
    band = acc.shape[2] // (2 * LANES)
    half = (bv.shape[1] - LANES) // 2
    is_end = meta_ref[0]

    def offset_of(p, g):
        return meta_ref[3 + 2 * p + g]

    at = pl.multiple_of((meta_ref[2] + band // 2) * LANES, LANES)
    rest = [
        pltpu.make_async_copy(rest_ref.at[g], acc.at[g, :, pl.ds(at, rest_ref.shape[2])], rest_sems.at[g])
        for g in range(2)
    ]
    x_loads = x_copies(x_refs, xv, x_sems, offset_of)
    b_copy = pltpu.make_async_copy(b_ref, bv, b_sem)

    def x_loads_of(g):
        return [copy for (_, r), copy in x_loads.items() if min(r, 1) == g]

    pl.when(is_end != 0)(b_copy.start)
    for g in range(2):
        rest[g].start()

        @pl.when(is_end != 0)
        def _():
            for copy in x_loads_of(g):
                copy.start()

    def wait_for(g):
        rest[g].wait()

        @pl.when(is_end != 0)
        def _():
            for copy in x_loads_of(g):
                copy.wait()
            if g == 0:
                b_copy.wait()

    def add(g):
        @pl.when(is_end != 0)
        def _():
            for p in range(2):
                add_product(acc, xv[p, g], bv[:, p * half : (p + 1) * half], g, offset_of(p, g) + meta_ref[1])
            p = meta_ref[8]
            add_product(acc, xv[p, g], bv[:, 2 * half :], g, offset_of(p, g) + meta_ref[7])

    finish(acc, wait_for, add, meta_ref[2] + band // 2, out_refs, pieces, out_sems)


def rest_products(meta, xs, rest, b, quarter):
    rows = xs[0].shape[0] // 2
    panel = b.shape[0]
    width = rest.shape[2]
    any_spec = pl.BlockSpec(memory_space=pl.ANY)
    x_spec = pl.BlockSpec(memory_space=pltpu.HBM)
    return pl.pallas_call(
        rest_kernel,
        out_shape=[jax.ShapeDtypeStruct((rows, width), jnp.bfloat16)] * 4,
        in_specs=[pl.BlockSpec(memory_space=pltpu.SMEM)] + [x_spec] * PARTS + [any_spec] * 2,
        out_specs=[any_spec] * 4,
        scratch_shapes=[
            pltpu.VMEM((2, 2, 2 * rows, panel), jnp.bfloat16),
            pltpu.VMEM(b.shape, jnp.bfloat16),
            pltpu.VMEM((2, 2 * rows, 2 * quarter), jnp.float32),
            pltpu.VMEM((4, rows, width), jnp.bfloat16),
            pltpu.SemaphoreType.DMA((2, PARTS)),
            pltpu.SemaphoreType.DMA,
            pltpu.SemaphoreType.DMA((2,)),
            pltpu.SemaphoreType.DMA((4,)),
        ],
        compiler_params=pltpu.CompilerParams(vmem_limit_bytes=59 * MIB),
        cost_estimate=SMALL,
        name="rest_products",
    )(meta, *xs, rest, b)


def assemble_kernel(place_ref, mask_ref, *refs):
    n = 4
    pieces, (out_ref, made, sem) = refs[:n], refs[-3:]
    steps = mask_ref.shape[0]
    rows = made.shape[0] // steps
    panel = n * LANES
    first = pl.multiple_of(place_ref[1] * panel, panel)
    for r in range(n):
        t = jnp.bitwise_xor(place_ref[0], r)
        for j in range(made.shape[1] // panel):
            to = pl.multiple_of(j * panel + t * LANES, LANES)
            for i in range(steps):
                keep = mask_ref[i, :, pl.ds(pl.multiple_of(first + to, LANES), LANES)]
                value = pieces[r][i * rows : (i + 1) * rows, j * LANES : (j + 1) * LANES].astype(jnp.float32)
                made[i * rows : (i + 1) * rows, pl.ds(to, LANES)] = (value * keep).astype(jnp.bfloat16)
    copy = pltpu.make_async_copy(made, out_ref.at[:, pl.ds(first, made.shape[1])], sem)
    copy.start()
    copy.wait()


def assembled(place, keep_wide, pieces, out=None):
    rows, width = pieces[0].shape
    cols = keep_wide.shape[2]
    vmem_spec = pl.BlockSpec(memory_space=pltpu.VMEM)
    any_spec = pl.BlockSpec(memory_space=pltpu.HBM)
    operands = [place, keep_wide, *pieces] + ([] if out is None else [out])
    return pl.pallas_call(
        assemble_kernel,
        out_shape=jax.ShapeDtypeStruct((rows, cols), jnp.bfloat16),
        in_specs=[pl.BlockSpec(memory_space=pltpu.SMEM)] + [vmem_spec] * 5 + [any_spec] * (len(operands) - 6),
        out_specs=any_spec,
        scratch_shapes=[pltpu.VMEM((rows, width * len(pieces)), jnp.bfloat16), pltpu.SemaphoreType.DMA],
        input_output_aliases={} if out is None else {6: 0},
        compiler_params=pltpu.CompilerParams(vmem_limit_bytes=16 * MIB),
        cost_estimate=SMALL,
        name="assembled",
    )(*operands)


def widen(mask, block):
    rows, cols = mask.shape
    wide = jnp.broadcast_to(mask.astype(jnp.float32)[:, :, None], (rows, cols, block))
    return wide.reshape(rows, 1, cols * block)


def together(*values):
    return lax.optimization_barrier(values)


def pairs_in_line(x_band, w_band, a_mask, keep_mask):
    panel = x_band.shape[0]
    block = panel // a_mask.shape[0]
    g, c = lax.axis_index("grid"), lax.axis_index("depth")
    z, y = g // 2, g % 2
    left = z < 2
    is_end = ((z == 0) | (z == 3)).astype(jnp.int32)
    toward = jnp.where(left, 1, -1)
    q = 2 * y + c

    swap = [(0, 2), (1, 3), (2, 0), (3, 1), (4, 6), (5, 7), (6, 4), (7, 5)]
    outward = [(2, 0), (3, 1), (4, 6), (5, 7)]
    cross = [(2, 4), (3, 5), (4, 2), (5, 3)]
    across = [(i, i ^ 1) for i in range(8)]
    layers = [(0, 1), (1, 0)]
    opposite = [(i, i ^ 3) for i in range(16)]

    def line(value, pairs):
        return lax.ppermute(value, "grid", pairs)

    first_out, second_out = jnp.where(left, 0, 4), jnp.where(left, 4, 0)
    first_in, second_in = second_out, first_out
    last_in = jnp.where(left, 2, 4)

    sent_b = b_strips(w_band, q ^ 2, 58)
    own_b = line(sent_b, across)
    sent_b, w_band = together(sent_b, w_band)
    own_a = b_strips(w_band, q, 58)
    swap_a = line(own_a, swap)
    cross_a = line(own_a, cross)
    mask_wide = widen(a_mask, block)
    rows = a_mask.shape[0]
    x_own = masked_x(x_band, mask_wide, c * rows // 2)
    x_mine = [x_own[k * panel // 4 : (k + 1) * panel // 4] for k in range(2)]
    own_b, *x_mine = together(own_b, *x_mine)
    own_b, swap_a = together(own_b, swap_a)
    swap_b = line(own_b, swap)
    cross_b = line(own_b, cross)
    x_across = [line(part, across) for part in x_mine]

    mid_a = line(cross_a[:, 6 * LANES :], outward)
    mid_b, fwd_first = packed(
        [y, first_out],
        [cross_a, cross_b, swap_a, swap_b],
        [11, 8],
        [
            (0, 0, 3, 0, 0, (0, 0)),
            (1, 0, 3, 0, 0, (0, 1)),
            (0, 3, 3, 0, 3, None),
            (1, 3, 5, 0, 6, None),
            (2, (1,), 4, 1, 0, None),
            (3, (1,), 4, 1, 4, None),
        ],
    )
    (fwd_second,) = packed([second_out], [swap_a, swap_b], [8], [(0, (0,), 4, 0, 0, None), (1, (0,), 4, 0, 4, None)])
    mid_a, mid_b, fwd_first = together(mid_a, mid_b, fwd_first)
    mid_b = line(mid_b, outward)
    fwd_first = line(fwd_first, cross)
    fwd_second, *x_across = together(fwd_second, *x_across)
    far_first = line(fwd_first, outward)
    fwd_second = line(fwd_second, cross)
    x_opposite = [lax.ppermute(part, "depth", layers) for part in x_across]
    xs = [x_own] + x_across + x_opposite

    def offsets(delta):
        tilt = 2 * y - 1
        return [(2 * delta + 4) % 8, (2 * delta + tilt + 4) % 8, (2 * delta - tilt + 4) % 8, (2 * delta + 4) % 8]

    zero = jnp.zeros_like(z)
    third = offsets(jnp.where(is_end == 1, 2, -toward))
    fourth = offsets(jnp.where(is_end == 1, -toward, 2))
    meta = jnp.stack([is_end, 4 + y, *offsets(zero), *offsets(toward), *third]).astype(jnp.int32)
    plan = [
        (0, [(0, 0, 8, 0, 0)]),
        (1, [(1, 0, 8, 0, 1)]),
        (2, [(4, 0, 8, 0, 2)]),
        (3, [(5, 0, 8, 0, 3)]),
        (4, [(6, 0, 3, 0, None), (6, 3, 3, 3, 4), (7, 0, 2, 6, 4)]),
        (5, [(6, 6, 5, 3, 5)]),
    ]
    total = whole_products(meta, xs, [own_a, own_b, cross_a, cross_b, swap_a, swap_b, mid_b, mid_a], plan)
    last_at = jnp.where(left, 2, 0)
    total, last_at = together(total, last_at)
    extra_in, extra_panel = jnp.where(left, 1, 6), jnp.where(left, 1 - y, y)
    extra_at = jnp.where(left, 1, 2) + 4 * extra_panel
    (last,) = packed(
        [last_at, last_at + 4, extra_at],
        [fwd_second],
        [5],
        [(0, (0,), 2, 0, 0, None), (0, (1,), 2, 0, 2, None), (0, (2,), 1, 0, 4, None)],
    )
    far_second = line(last, outward)

    def exchanged(pieces):
        return [
            pieces[0],
            lax.ppermute(pieces[1], "depth", layers),
            line(pieces[2], across),
            lax.ppermute(pieces[3], ("grid", "depth"), opposite),
        ]

    done_at, rest_at = jnp.where(left, 3, 0), jnp.where(left, 0, 5)
    meta = jnp.stack([is_end, first_in, second_in, done_at, rest_at, *fourth]).astype(jnp.int32)
    *done, rest = half_products(meta, xs, total, fwd_first, far_first, fwd_second, 5)
    done = exchanged(done)
    far_second, done[1] = together(far_second, done[1])
    keep_wide = widen(keep_mask, block)
    out = assembled(jnp.stack([q, done_at]).astype(jnp.int32), keep_wide, done)
    meta = jnp.stack([is_end, last_in, rest_at, *fourth, extra_in, extra_panel]).astype(jnp.int32)
    rest = exchanged(rest_products(meta, xs, rest, far_second, own_a.shape[1]))
    return assembled(jnp.stack([q, rest_at]).astype(jnp.int32), keep_wide, rest, out)


def solution(mesh):
    placed = (
        P(("groups", "grid"), None),
        P(("groups", "grid"), None),
        P(("groups", "grid"), None),
        P(("groups", "grid", "depth"), None),
    )

    def local(x_band, w_band, a_mask, keep_mask):
        panel, cols = x_band.shape
        pairs = mesh.shape["grid"] == 8 and mesh.shape["depth"] == 2
        pairs = pairs and cols == 8 * panel and panel == 4 * LANES
        return (pairs_in_line if pairs else ring)(x_band, w_band, a_mask, keep_mask)

    return jax.shard_map(
        local,
        mesh=mesh,
        in_specs=placed,
        out_specs=P(("groups", "grid", "depth"), None),
        check_vma=False,
    )
```

```python
import functools

import jax
import jax.numpy as jnp
from jax import lax
from jax.experimental import pallas as pl
from jax.experimental.pallas import tpu as pltpu
from jax.sharding import PartitionSpec as P

LANES = 128
MIB = 1 << 20
SMALL = pl.CostEstimate(flops=1000, bytes_accessed=1000, transcendentals=0)


def shifted(shard, axis, by):
    count = lax.axis_size(axis)
    return lax.ppermute(shard, axis, [(i, (i + by) % count) for i in range(count)])


def expand_blocks(mask, block):
    rows, cols = mask.shape
    wide = jnp.broadcast_to(mask[:, None, :, None], (rows, block, cols, block))
    return wide.reshape(rows * block, cols * block)


def ring(x_band, w_band, a_mask, keep_mask):
    panel = x_band.shape[0]
    block = panel // a_mask.shape[0]
    band_cols = x_band.shape[1]
    xm = x_band * expand_blocks(a_mask, block).astype(jnp.bfloat16)
    rows = lax.broadcasted_iota(jnp.int32, x_band.shape, 0)
    cols = lax.broadcasted_iota(jnp.int32, x_band.shape, 1)
    identity = jnp.where(cols == rows + 4 * panel, 1.0, 0.0).astype(jnp.float32)
    b_panel = (1.5 * identity - 0.5 * w_band.astype(jnp.float32)).astype(jnp.bfloat16)
    layer = lax.axis_index("depth")
    current = shifted(b_panel, ("grid", "depth"), -5)
    wide = jnp.zeros((panel, 2 * band_cols), jnp.float32)
    for step in range(4):
        offset = 6 + layer - 2 * step
        ablock = lax.dynamic_slice_in_dim(xm, offset * panel, panel, 1)
        term = jnp.dot(ablock, current, preferred_element_type=jnp.float32)
        region = lax.dynamic_slice_in_dim(wide, offset * panel, band_cols, 1)
        wide = lax.dynamic_update_slice_in_dim(wide, region + term, offset * panel, 1)
        if step < 3:
            current = shifted(current, "grid", 2)
    partial_band = wide[:, 4 * panel : 12 * panel]
    mine = lax.psum_scatter(partial_band, "depth", scatter_dimension=0, tiled=True)
    keep = expand_blocks(keep_mask, block).astype(jnp.float32)
    return (mine * keep).astype(jnp.bfloat16)


def strips_kernel(quarter_ref, w_ref, b_ref, held, made, in_sems, out_sems):
    panel, width = held.shape
    quarter = quarter_ref[0]

    def strip(j):
        return slice(j * LANES, (j + 1) * LANES)

    def load(j):
        at = pl.multiple_of(j * panel + quarter * LANES, LANES)
        return pltpu.make_async_copy(w_ref.at[:, pl.ds(at, LANES)], held.at[:, strip(j)], in_sems.at[j])

    def give(j):
        return pltpu.make_async_copy(made.at[:, strip(j)], b_ref.at[:, strip(j)], out_sems.at[j])

    band = width // LANES
    for j in range(band):
        load(j).start()
    for j in range(band):
        load(j).wait()
        value = -0.5 * held[:, strip(j)].astype(jnp.float32)
        if j == band // 2:
            rows = lax.broadcasted_iota(jnp.int32, value.shape, 0)
            cols = lax.broadcasted_iota(jnp.int32, value.shape, 1)
            value = value + jnp.where(rows == cols + quarter * LANES, 1.5, 0.0)
        made[:, strip(j)] = value.astype(jnp.bfloat16)
        give(j).start()
    for j in range(band):
        give(j).wait()


def b_strips(w_band, quarter, limit):
    panel = w_band.shape[0]
    band = w_band.shape[1] // panel
    shape = (panel, band * LANES)
    return pl.pallas_call(
        strips_kernel,
        out_shape=jax.ShapeDtypeStruct(shape, jnp.bfloat16),
        in_specs=[
            pl.BlockSpec(memory_space=pltpu.SMEM),
            pl.BlockSpec(memory_space=pltpu.HBM),
        ],
        out_specs=pl.BlockSpec(memory_space=pl.ANY),
        scratch_shapes=[
            pltpu.VMEM(shape, jnp.bfloat16),
            pltpu.VMEM(shape, jnp.bfloat16),
            pltpu.SemaphoreType.DMA((band,)),
            pltpu.SemaphoreType.DMA((band,)),
        ],
        compiler_params=pltpu.CompilerParams(vmem_limit_bytes=limit * MIB),
        cost_estimate=SMALL,
        name="b_strips",
    )(quarter.reshape(1), w_band)


def pack_kernel(plan, n_in, meta_ref, *refs):
    sources, outs, sems = refs[:n_in], refs[n_in:-1], refs[-1]

    def on_each(do):
        for k, (source, start, count, out, to, when) in enumerate(plan):
            at = start * LANES if isinstance(start, int) else pl.multiple_of(meta_ref[start[0]] * LANES, LANES)
            copy = pltpu.make_async_copy(
                sources[source].at[:, pl.ds(at, count * LANES)],
                outs[out].at[:, to * LANES : (to + count) * LANES],
                sems.at[k],
            )
            if when is None:
                do(copy)
            else:
                pl.when(meta_ref[when[0]] == when[1])(functools.partial(do, copy))

    on_each(lambda copy: copy.start())
    on_each(lambda copy: copy.wait())


def packed(meta, sources, widths, plan):
    rows = sources[0].shape[0]
    any_spec = pl.BlockSpec(memory_space=pl.ANY)
    return pl.pallas_call(
        functools.partial(pack_kernel, plan, len(sources)),
        out_shape=[jax.ShapeDtypeStruct((rows, width * LANES), jnp.bfloat16) for width in widths],
        in_specs=[pl.BlockSpec(memory_space=pltpu.SMEM)] + [any_spec] * len(sources),
        out_specs=[pl.BlockSpec(memory_space=pltpu.VMEM)] * len(widths),
        scratch_shapes=[pltpu.SemaphoreType.DMA((len(plan),))],
        compiler_params=pltpu.CompilerParams(vmem_limit_bytes=40 * MIB),
        cost_estimate=SMALL,
        name="packed",
    )(jnp.stack(meta).astype(jnp.int32), *sources)


def mask_kernel(first_ref, mask_ref, x_ref, out_ref):
    out_ref[...] = (x_ref[...].astype(jnp.float32) * mask_ref[0]).astype(jnp.bfloat16)


def masked_x(x_band, mask_wide, first):
    count = mask_wide.shape[0]
    block = x_band.shape[0] // count
    cols = x_band.shape[1]
    return pl.pallas_call(
        mask_kernel,
        grid_spec=pltpu.PrefetchScalarGridSpec(
            num_scalar_prefetch=1,
            grid=(count,),
            in_specs=[
                pl.BlockSpec((1, 1, cols), lambda i, f: (lax.rem(f[0] + i, count), 0, 0)),
                pl.BlockSpec((block, cols), lambda i, f: (lax.rem(f[0] + i, count), 0)),
            ],
            out_specs=pl.BlockSpec((block, cols), lambda i, f: (i, 0)),
        ),
        out_shape=jax.ShapeDtypeStruct(x_band.shape, jnp.bfloat16),
        compiler_params=pltpu.CompilerParams(vmem_limit_bytes=58 * MIB),
        cost_estimate=SMALL,
        name="masked_x",
    )(first.reshape(1), mask_wide, x_band)


PARTS = 5


def x_copies(x_refs, xv, sems, offset_of):
    n_b, _, rows, panel = xv.shape
    copies = {}
    for p in range(n_b):
        for r in range(PARTS):
            g = min(r, 1)
            at = pl.multiple_of(offset_of(p, g) * panel, panel)
            to = xv.at[p, 0] if r == 0 else xv.at[p, 1, (r - 1) * rows // 4 : r * rows // 4]
            copies[p, r] = pltpu.make_async_copy(x_refs[r].at[:, pl.ds(at, panel)], to, sems.at[p, r])
    return copies


def add_product(acc, x, strips, g, first, start=False):
    width = strips.shape[1]
    for n in range(0, width, 2 * LANES):
        block = min(2 * LANES, width - n)
        at = first * LANES + n
        cols = slice(at, at + block) if isinstance(at, int) else pl.ds(pl.multiple_of(at, LANES), block)
        value = jnp.dot(x[...], strips[:, n : n + block], preferred_element_type=jnp.float32)
        acc[g, :, cols] = value if start else acc[g, :, cols] + value


def whole_kernel(plan, meta_ref, *refs):
    n_b = len(plan)
    x_refs, refs = refs[:PARTS], refs[PARTS:]
    b_refs, (out_ref, xv, bv, acc, x_sems, b_sems, out_sems) = refs[:-7], refs[-7:]
    quarter = bv.shape[2]
    low = quarter // 2
    is_end = meta_ref[0]

    def offset_of(p, g):
        return meta_ref[2 + 2 * p + g]

    def b_middle(p):
        return [pltpu.make_async_copy(b_refs[plan[p][0]].at[:, :quarter], bv.at[p], b_sems.at[p, 0])]

    def b_end(p):
        copies = []
        for k, (operand, first, count, at, to) in enumerate(plan[p][1]):
            to = meta_ref[1] if to is None else to
            source = b_refs[operand].at[:, first * LANES : (first + count) * LANES]
            copies.append(pltpu.make_async_copy(source, bv.at[to, :, at * LANES : (at + count) * LANES], b_sems.at[p, k]))
        return copies

    def on_each(p, do):
        @pl.when(is_end == 0)
        def _():
            for copy in b_middle(p):
                do(copy)

        @pl.when(is_end != 0)
        def _():
            for copy in b_end(p):
                do(copy)

    copies = x_copies(x_refs, xv, x_sems, offset_of)
    for p in range(n_b):
        on_each(p, lambda copy: copy.start())
        for r in range(PARTS):
            copies[p, r].start()
    outs = [
        pltpu.make_async_copy(acc.at[g, :, low : low + quarter], out_ref.at[g], out_sems.at[g]) for g in range(2)
    ]

    def wait_for(p):
        for k in [p] if p < n_b - 2 else range(n_b - 2, n_b) if p == n_b - 2 else []:
            on_each(k, lambda copy: copy.wait())
        for r in range(PARTS):
            copies[p, r].wait()

    middle = quarter // LANES // 2

    def own(g, carry):
        add_product(acc, xv.at[g, g], bv.at[g], g, low // LANES, True)
        return carry

    def step(i, carry):
        p = jnp.where(i < 4, i % 2, i // 2)
        g = jnp.where(i < 4, 1 - i % 2, i % 2)
        for k in range(2, n_b):
            pl.when(i == 2 * k)(functools.partial(wait_for, k))
        pl.when(i == 2 * n_b - 1)(outs[0].start)
        offset = offset_of(p, g)
        for k in range(2 * middle):
            if k == middle:
                continue
            first, last = max(0, middle - k), min(2 * middle, 3 * middle - k)

            @pl.when(offset == k)
            def _():
                add_product(acc, xv.at[p, g], bv.at[p, :, first * LANES : last * LANES], g, k + first)

        return carry

    for p in range(2):
        wait_for(p)
    lax.fori_loop(0, 2, own, 0)
    lax.fori_loop(2, 2 * n_b, step, 0)
    outs[1].start()
    for out in outs:
        out.wait()


def whole_products(meta, xs, operands, plan):
    rows = xs[0].shape[0] // 2
    panel, quarter = operands[plan[0][0]].shape
    n_b = len(plan)
    any_spec = pl.BlockSpec(memory_space=pl.ANY)
    x_spec = pl.BlockSpec(memory_space=pltpu.HBM)
    return pl.pallas_call(
        functools.partial(whole_kernel, plan),
        out_shape=jax.ShapeDtypeStruct((2, 2 * rows, quarter), jnp.float32),
        in_specs=[pl.BlockSpec(memory_space=pltpu.SMEM)] + [x_spec] * PARTS + [any_spec] * len(operands),
        out_specs=any_spec,
        scratch_shapes=[
            pltpu.VMEM((n_b, 2, 2 * rows, panel), jnp.bfloat16),
            pltpu.VMEM((n_b, panel, quarter), jnp.bfloat16),
            pltpu.VMEM((2, 2 * rows, 2 * quarter), jnp.float32),
            pltpu.SemaphoreType.DMA((n_b, PARTS)),
            pltpu.SemaphoreType.DMA((n_b, 3)),
            pltpu.SemaphoreType.DMA((2,)),
        ],
        compiler_params=pltpu.CompilerParams(vmem_limit_bytes=59 * MIB),
        cost_estimate=pl.CostEstimate(flops=6 * 10**9, bytes_accessed=36 * MIB, transcendentals=0),
        name="whole_products",
    )(meta, *xs, *operands)


def finish(acc, wait_for, add, at, out_refs, pieces, sems, also=None):
    half, width = out_refs[0].shape
    cols = pl.ds(pl.multiple_of(at * LANES, LANES), width)
    outs = [pltpu.make_async_copy(pieces.at[r], out_refs[r], sems.at[r]) for r in range(4)]
    also = also or []

    def step(g, carry):
        for k in range(2):
            pl.when(g == k)(functools.partial(wait_for, k))
        add(g)
        for k in range(2):

            @pl.when(g == k)
            def _():
                for copy in also[k : k + 1]:
                    copy.start()
                for r in range(2 * k, 2 * k + 2):
                    rows = slice((r % 2) * half, (r % 2 + 1) * half)
                    pieces[r] = acc[k, rows, cols].astype(jnp.bfloat16)
                    outs[r].start()

        return carry

    lax.fori_loop(0, 2, step, 0)
    for copy in outs + also:
        copy.wait()


def half_kernel(meta_ref, *refs):
    x_refs, (prev_ref, middle_ref, end_ref, second_ref), refs = refs[:PARTS], refs[PARTS : PARTS + 4], refs[PARTS + 4 :]
    out_refs, rest_ref, xv, bv, acc, pieces, x_sems, b_sems, prev_sems, rest_sems, out_sems = refs[:4], *refs[4:]
    quarter = bv.shape[2]
    half = quarter // 2
    low = quarter // 2
    band = quarter // LANES
    is_end = meta_ref[0]

    def offset_of(p, g):
        return meta_ref[5 + 2 * p + g]

    x_loads = x_copies(x_refs, xv, x_sems, offset_of)
    middle = pltpu.make_async_copy(middle_ref, bv.at[0], b_sems.at[0])
    end = pltpu.make_async_copy(end_ref, bv.at[0], b_sems.at[0])
    second = pltpu.make_async_copy(second_ref, bv.at[1], b_sems.at[1])
    prev = [
        pltpu.make_async_copy(prev_ref.at[g], acc.at[g, :, low : low + quarter], prev_sems.at[g]) for g in range(2)
    ]
    at = pl.multiple_of((meta_ref[4] + band // 2) * LANES, LANES)
    rest = [
        pltpu.make_async_copy(acc.at[g, :, pl.ds(at, rest_ref.shape[2])], rest_ref.at[g], rest_sems.at[g])
        for g in range(2)
    ]

    @pl.when(is_end == 0)
    def _():
        middle.start()
        second.start()

    pl.when(is_end != 0)(end.start)

    def rows_loads(g):
        return [prev[g]] + [copy for (_, r), copy in x_loads.items() if min(r, 1) == g]

    for g in range(2):
        for copy in rows_loads(g):
            copy.start()

    def wait_for(g):
        for copy in rows_loads(g):
            copy.wait()
        if g == 0:

            @pl.when(is_end == 0)
            def _():
                middle.wait()
                second.wait()

            pl.when(is_end != 0)(end.wait)

    def add(g):
        for p in range(2):
            add_product(acc, xv.at[p, g], bv.at[0, :, p * half : (p + 1) * half], g, offset_of(p, g) + meta_ref[1])

        @pl.when(is_end == 0)
        def _():
            for p in range(2):
                add_product(acc, xv.at[p, g], bv.at[1, :, p * half : (p + 1) * half], g, offset_of(p, g) + meta_ref[2])

    finish(acc, wait_for, add, meta_ref[3] + band // 2, out_refs, pieces, out_sems, rest)


def half_products(meta, xs, prev, middle, end, second, n_done):
    rows = xs[0].shape[0] // 2
    panel, quarter = second.shape
    any_spec = pl.BlockSpec(memory_space=pl.ANY)
    x_spec = pl.BlockSpec(memory_space=pltpu.HBM)
    n_rest = quarter // LANES - n_done
    return pl.pallas_call(
        half_kernel,
        out_shape=[jax.ShapeDtypeStruct((rows, n_done * LANES), jnp.bfloat16)] * 4
        + [jax.ShapeDtypeStruct((2, 2 * rows, n_rest * LANES), jnp.float32)],
        in_specs=[pl.BlockSpec(memory_space=pltpu.SMEM)] + [x_spec] * PARTS + [any_spec] * 4,
        out_specs=[any_spec] * 5,
        scratch_shapes=[
            pltpu.VMEM((2, 2, 2 * rows, panel), jnp.bfloat16),
            pltpu.VMEM((2, panel, quarter), jnp.bfloat16),
            pltpu.VMEM((2, 2 * rows, 2 * quarter), jnp.float32),
            pltpu.VMEM((4, rows, n_done * LANES), jnp.bfloat16),
            pltpu.SemaphoreType.DMA((2, PARTS)),
            pltpu.SemaphoreType.DMA((2,)),
            pltpu.SemaphoreType.DMA((2,)),
            pltpu.SemaphoreType.DMA((2,)),
            pltpu.SemaphoreType.DMA((4,)),
        ],
        compiler_params=pltpu.CompilerParams(vmem_limit_bytes=59 * MIB),
        cost_estimate=SMALL,
        name="half_products",
    )(meta, *xs, prev, middle, end, second)


def rest_kernel(meta_ref, *refs):
    x_refs, (rest_ref, b_ref), refs = refs[:PARTS], refs[PARTS : PARTS + 2], refs[PARTS + 2 :]
    out_refs, xv, bv, acc, pieces, x_sems, b_sem, rest_sems, out_sems = refs[:4], *refs[4:]
    band = acc.shape[2] // (2 * LANES)
    half = (bv.shape[1] - LANES) // 2
    is_end = meta_ref[0]

    def offset_of(p, g):
        return meta_ref[3 + 2 * p + g]

    at = pl.multiple_of((meta_ref[2] + band // 2) * LANES, LANES)
    rest = [
        pltpu.make_async_copy(rest_ref.at[g], acc.at[g, :, pl.ds(at, rest_ref.shape[2])], rest_sems.at[g])
        for g in range(2)
    ]
    x_loads = x_copies(x_refs, xv, x_sems, offset_of)
    b_copy = pltpu.make_async_copy(b_ref, bv, b_sem)

    def x_loads_of(g):
        return [copy for (_, r), copy in x_loads.items() if min(r, 1) == g]

    pl.when(is_end != 0)(b_copy.start)
    for g in range(2):
        rest[g].start()

        @pl.when(is_end != 0)
        def _():
            for copy in x_loads_of(g):
                copy.start()

    def wait_for(g):
        rest[g].wait()

        @pl.when(is_end != 0)
        def _():
            for copy in x_loads_of(g):
                copy.wait()
            if g == 0:
                b_copy.wait()

    def add(g):
        @pl.when(is_end != 0)
        def _():
            for p in range(2):
                add_product(acc, xv.at[p, g], bv.at[:, p * half : (p + 1) * half], g, offset_of(p, g) + meta_ref[1])
            p = meta_ref[8]
            add_product(acc, xv.at[p, g], bv.at[:, 2 * half :], g, offset_of(p, g) + meta_ref[7])

    finish(acc, wait_for, add, meta_ref[2] + band // 2, out_refs, pieces, out_sems)


def rest_products(meta, xs, rest, b, quarter):
    rows = xs[0].shape[0] // 2
    panel = b.shape[0]
    width = rest.shape[2]
    any_spec = pl.BlockSpec(memory_space=pl.ANY)
    x_spec = pl.BlockSpec(memory_space=pltpu.HBM)
    return pl.pallas_call(
        rest_kernel,
        out_shape=[jax.ShapeDtypeStruct((rows, width), jnp.bfloat16)] * 4,
        in_specs=[pl.BlockSpec(memory_space=pltpu.SMEM)] + [x_spec] * PARTS + [any_spec] * 2,
        out_specs=[any_spec] * 4,
        scratch_shapes=[
            pltpu.VMEM((2, 2, 2 * rows, panel), jnp.bfloat16),
            pltpu.VMEM(b.shape, jnp.bfloat16),
            pltpu.VMEM((2, 2 * rows, 2 * quarter), jnp.float32),
            pltpu.VMEM((4, rows, width), jnp.bfloat16),
            pltpu.SemaphoreType.DMA((2, PARTS)),
            pltpu.SemaphoreType.DMA,
            pltpu.SemaphoreType.DMA((2,)),
            pltpu.SemaphoreType.DMA((4,)),
        ],
        compiler_params=pltpu.CompilerParams(vmem_limit_bytes=59 * MIB),
        cost_estimate=SMALL,
        name="rest_products",
    )(meta, *xs, rest, b)


def assemble_kernel(place_ref, mask_ref, *refs):
    n = 4
    pieces, (out_ref, made, sem) = refs[:n], refs[-3:]
    steps = mask_ref.shape[0]
    rows = made.shape[0] // steps
    panel = n * LANES
    first = pl.multiple_of(place_ref[1] * panel, panel)
    for r in range(n):
        t = jnp.bitwise_xor(place_ref[0], r)
        for j in range(made.shape[1] // panel):
            to = pl.multiple_of(j * panel + t * LANES, LANES)
            for i in range(steps):
                keep = mask_ref[i, :, pl.ds(pl.multiple_of(first + to, LANES), LANES)]
                value = pieces[r][i * rows : (i + 1) * rows, j * LANES : (j + 1) * LANES].astype(jnp.float32)
                made[i * rows : (i + 1) * rows, pl.ds(to, LANES)] = (value * keep).astype(jnp.bfloat16)
    copy = pltpu.make_async_copy(made, out_ref.at[:, pl.ds(first, made.shape[1])], sem)
    copy.start()
    copy.wait()


def assembled(place, keep_wide, pieces, out=None):
    rows, width = pieces[0].shape
    cols = keep_wide.shape[2]
    vmem_spec = pl.BlockSpec(memory_space=pltpu.VMEM)
    any_spec = pl.BlockSpec(memory_space=pltpu.HBM)
    operands = [place, keep_wide, *pieces] + ([] if out is None else [out])
    return pl.pallas_call(
        assemble_kernel,
        out_shape=jax.ShapeDtypeStruct((rows, cols), jnp.bfloat16),
        in_specs=[pl.BlockSpec(memory_space=pltpu.SMEM)] + [vmem_spec] * 5 + [any_spec] * (len(operands) - 6),
        out_specs=any_spec,
        scratch_shapes=[pltpu.VMEM((rows, width * len(pieces)), jnp.bfloat16), pltpu.SemaphoreType.DMA],
        input_output_aliases={} if out is None else {6: 0},
        compiler_params=pltpu.CompilerParams(vmem_limit_bytes=16 * MIB),
        cost_estimate=SMALL,
        name="assembled",
    )(*operands)


def widen(mask, block):
    rows, cols = mask.shape
    wide = jnp.broadcast_to(mask.astype(jnp.float32)[:, :, None], (rows, cols, block))
    return wide.reshape(rows, 1, cols * block)


def together(*values):
    return lax.optimization_barrier(values)


def pairs_in_line(x_band, w_band, a_mask, keep_mask):
    panel = x_band.shape[0]
    block = panel // a_mask.shape[0]
    g, c = lax.axis_index("grid"), lax.axis_index("depth")
    z, y = g // 2, g % 2
    left = z < 2
    is_end = ((z == 0) | (z == 3)).astype(jnp.int32)
    toward = jnp.where(left, 1, -1)
    q = 2 * y + c

    swap = [(0, 2), (1, 3), (2, 0), (3, 1), (4, 6), (5, 7), (6, 4), (7, 5)]
    outward = [(2, 0), (3, 1), (4, 6), (5, 7)]
    cross = [(2, 4), (3, 5), (4, 2), (5, 3)]
    across = [(i, i ^ 1) for i in range(8)]
    layers = [(0, 1), (1, 0)]
    opposite = [(i, i ^ 3) for i in range(16)]

    def line(value, pairs):
        return lax.ppermute(value, "grid", pairs)

    first_out, second_out = jnp.where(left, 0, 4), jnp.where(left, 4, 0)
    first_in, second_in = second_out, first_out
    last_in = jnp.where(left, 2, 4)

    sent_b = b_strips(w_band, q ^ 2, 58)
    own_b = line(sent_b, across)
    sent_b, w_band = together(sent_b, w_band)
    own_a = b_strips(w_band, q, 58)
    swap_a = line(own_a, swap)
    cross_a = line(own_a, cross)
    mask_wide = widen(a_mask, block)
    rows = a_mask.shape[0]
    x_own = masked_x(x_band, mask_wide, c * rows // 2)
    x_mine = [x_own[k * panel // 4 : (k + 1) * panel // 4] for k in range(2)]
    own_b, *x_mine = together(own_b, *x_mine)
    own_b, swap_a = together(own_b, swap_a)
    swap_b = line(own_b, swap)
    cross_b = line(own_b, cross)
    x_across = [line(part, across) for part in x_mine]

    mid_a = line(cross_a[:, 5 * LANES :], outward)
    mid_b, fwd_first = packed(
        [y, first_out],
        [cross_a, cross_b, swap_a, swap_b],
        [10, 8],
        [
            (0, 0, 3, 0, 0, (0, 0)),
            (1, 0, 3, 0, 0, (0, 1)),
            (0, 3, 2, 0, 3, None),
            (1, 3, 5, 0, 5, None),
            (2, (1,), 4, 1, 0, None),
            (3, (1,), 4, 1, 4, None),
        ],
    )
    (fwd_second,) = packed([second_out], [swap_a, swap_b], [8], [(0, (0,), 4, 0, 0, None), (1, (0,), 4, 0, 4, None)])
    mid_a, mid_b, fwd_first = together(mid_a, mid_b, fwd_first)
    mid_b = line(mid_b, outward)
    fwd_first = line(fwd_first, cross)
    fwd_second, *x_across = together(fwd_second, *x_across)
    far_first = line(fwd_first, outward)
    fwd_second = line(fwd_second, cross)
    x_opposite = [lax.ppermute(part, "depth", layers) for part in x_across]
    xs = [x_own] + x_across + x_opposite

    def offsets(delta):
        tilt = 2 * y - 1
        return [(2 * delta + 4) % 8, (2 * delta + tilt + 4) % 8, (2 * delta - tilt + 4) % 8, (2 * delta + 4) % 8]

    zero = jnp.zeros_like(z)
    third = offsets(jnp.where(is_end == 1, 2, -toward))
    fourth = offsets(jnp.where(is_end == 1, -toward, 2))
    meta = jnp.stack([is_end, 4 + y, *offsets(zero), *offsets(toward), *third]).astype(jnp.int32)
    plan = [
        (0, [(0, 0, 8, 0, 0)]),
        (1, [(1, 0, 8, 0, 1)]),
        (2, [(4, 0, 8, 0, 2)]),
        (3, [(5, 0, 8, 0, 3)]),
        (4, [(6, 0, 3, 0, None), (6, 3, 2, 3, 4), (7, 0, 3, 5, 4)]),
        (5, [(6, 5, 5, 3, 5)]),
    ]
    total = whole_products(meta, xs, [own_a, own_b, cross_a, cross_b, swap_a, swap_b, mid_b, mid_a], plan)
    last_at = jnp.where(left, 2, 0)
    total, last_at = together(total, last_at)
    extra_in, extra_panel = jnp.where(left, 1, 6), jnp.where(left, 1 - y, y)
    extra_at = jnp.where(left, 1, 2) + 4 * extra_panel
    (last,) = packed(
        [last_at, last_at + 4, extra_at],
        [fwd_second],
        [5],
        [(0, (0,), 2, 0, 0, None), (0, (1,), 2, 0, 2, None), (0, (2,), 1, 0, 4, None)],
    )
    far_second = line(last, outward)

    def exchanged(pieces):
        return [
            pieces[0],
            lax.ppermute(pieces[1], "depth", layers),
            line(pieces[2], across),
            lax.ppermute(pieces[3], ("grid", "depth"), opposite),
        ]

    done_at, rest_at = jnp.where(left, 3, 0), jnp.where(left, 0, 5)
    meta = jnp.stack([is_end, first_in, second_in, done_at, rest_at, *fourth]).astype(jnp.int32)
    *done, rest = half_products(meta, xs, total, fwd_first, far_first, fwd_second, 5)
    done = exchanged(done)
    far_second, done[1] = together(far_second, done[1])
    keep_wide = widen(keep_mask, block)
    out = assembled(jnp.stack([q, done_at]).astype(jnp.int32), keep_wide, done)
    meta = jnp.stack([is_end, last_in, rest_at, *fourth, extra_in, extra_panel]).astype(jnp.int32)
    rest = exchanged(rest_products(meta, xs, rest, far_second, own_a.shape[1]))
    return assembled(jnp.stack([q, rest_at]).astype(jnp.int32), keep_wide, rest, out)


def solution(mesh):
    placed = (
        P(("groups", "grid"), None),
        P(("groups", "grid"), None),
        P(("groups", "grid"), None),
        P(("groups", "grid", "depth"), None),
    )

    def local(x_band, w_band, a_mask, keep_mask):
        panel, cols = x_band.shape
        pairs = mesh.shape["grid"] == 8 and mesh.shape["depth"] == 2
        pairs = pairs and cols == 8 * panel and panel == 4 * LANES
        return (pairs_in_line if pairs else ring)(x_band, w_band, a_mask, keep_mask)

    return jax.shard_map(
        local,
        mesh=mesh,
        in_specs=placed,
        out_specs=P(("groups", "grid", "depth"), None),
        check_vma=False,
    )
```

```python
import functools

import jax
import jax.numpy as jnp
from jax import lax
from jax.experimental import pallas as pl
from jax.experimental.pallas import tpu as pltpu
from jax.sharding import PartitionSpec as P

LANES = 128
MIB = 1 << 20
SMALL = pl.CostEstimate(flops=1000, bytes_accessed=1000, transcendentals=0)


def shifted(shard, axis, by):
    count = lax.axis_size(axis)
    return lax.ppermute(shard, axis, [(i, (i + by) % count) for i in range(count)])


def expand_blocks(mask, block):
    rows, cols = mask.shape
    wide = jnp.broadcast_to(mask[:, None, :, None], (rows, block, cols, block))
    return wide.reshape(rows * block, cols * block)


def ring(x_band, w_band, a_mask, keep_mask):
    panel = x_band.shape[0]
    block = panel // a_mask.shape[0]
    band_cols = x_band.shape[1]
    xm = x_band * expand_blocks(a_mask, block).astype(jnp.bfloat16)
    rows = lax.broadcasted_iota(jnp.int32, x_band.shape, 0)
    cols = lax.broadcasted_iota(jnp.int32, x_band.shape, 1)
    identity = jnp.where(cols == rows + 4 * panel, 1.0, 0.0).astype(jnp.float32)
    b_panel = (1.5 * identity - 0.5 * w_band.astype(jnp.float32)).astype(jnp.bfloat16)
    layer = lax.axis_index("depth")
    current = shifted(b_panel, ("grid", "depth"), -5)
    wide = jnp.zeros((panel, 2 * band_cols), jnp.float32)
    for step in range(4):
        offset = 6 + layer - 2 * step
        ablock = lax.dynamic_slice_in_dim(xm, offset * panel, panel, 1)
        term = jnp.dot(ablock, current, preferred_element_type=jnp.float32)
        region = lax.dynamic_slice_in_dim(wide, offset * panel, band_cols, 1)
        wide = lax.dynamic_update_slice_in_dim(wide, region + term, offset * panel, 1)
        if step < 3:
            current = shifted(current, "grid", 2)
    partial_band = wide[:, 4 * panel : 12 * panel]
    mine = lax.psum_scatter(partial_band, "depth", scatter_dimension=0, tiled=True)
    keep = expand_blocks(keep_mask, block).astype(jnp.float32)
    return (mine * keep).astype(jnp.bfloat16)


def strips_kernel(quarter_ref, w_ref, b_ref, held, made, in_sems, out_sems):
    panel, width = held.shape
    quarter = quarter_ref[0]

    def strip(j):
        return slice(j * LANES, (j + 1) * LANES)

    def load(j):
        at = pl.multiple_of(j * panel + quarter * LANES, LANES)
        return pltpu.make_async_copy(w_ref.at[:, pl.ds(at, LANES)], held.at[:, strip(j)], in_sems.at[j])

    def give(j):
        return pltpu.make_async_copy(made.at[:, strip(j)], b_ref.at[:, strip(j)], out_sems.at[j])

    band = width // LANES
    for j in range(band):
        load(j).start()
    for j in range(band):
        load(j).wait()
        value = -0.5 * held[:, strip(j)].astype(jnp.float32)
        if j == band // 2:
            rows = lax.broadcasted_iota(jnp.int32, value.shape, 0)
            cols = lax.broadcasted_iota(jnp.int32, value.shape, 1)
            value = value + jnp.where(rows == cols + quarter * LANES, 1.5, 0.0)
        made[:, strip(j)] = value.astype(jnp.bfloat16)
        give(j).start()
    for j in range(band):
        give(j).wait()


def b_strips(w_band, quarter, limit):
    panel = w_band.shape[0]
    band = w_band.shape[1] // panel
    shape = (panel, band * LANES)
    return pl.pallas_call(
        strips_kernel,
        out_shape=jax.ShapeDtypeStruct(shape, jnp.bfloat16),
        in_specs=[
            pl.BlockSpec(memory_space=pltpu.SMEM),
            pl.BlockSpec(memory_space=pltpu.HBM),
        ],
        out_specs=pl.BlockSpec(memory_space=pl.ANY),
        scratch_shapes=[
            pltpu.VMEM(shape, jnp.bfloat16),
            pltpu.VMEM(shape, jnp.bfloat16),
            pltpu.SemaphoreType.DMA((band,)),
            pltpu.SemaphoreType.DMA((band,)),
        ],
        compiler_params=pltpu.CompilerParams(vmem_limit_bytes=limit * MIB),
        cost_estimate=SMALL,
        name="b_strips",
    )(quarter.reshape(1), w_band)


def pack_kernel(plan, n_in, meta_ref, *refs):
    sources, outs, sems = refs[:n_in], refs[n_in:-1], refs[-1]

    def on_each(do):
        for k, (source, start, count, out, to, when) in enumerate(plan):
            at = start * LANES if isinstance(start, int) else pl.multiple_of(meta_ref[start[0]] * LANES, LANES)
            copy = pltpu.make_async_copy(
                sources[source].at[:, pl.ds(at, count * LANES)],
                outs[out].at[:, to * LANES : (to + count) * LANES],
                sems.at[k],
            )
            if when is None:
                do(copy)
            else:
                pl.when(meta_ref[when[0]] == when[1])(functools.partial(do, copy))

    on_each(lambda copy: copy.start())
    on_each(lambda copy: copy.wait())


def packed(meta, sources, widths, plan):
    rows = sources[0].shape[0]
    any_spec = pl.BlockSpec(memory_space=pl.ANY)
    return pl.pallas_call(
        functools.partial(pack_kernel, plan, len(sources)),
        out_shape=[jax.ShapeDtypeStruct((rows, width * LANES), jnp.bfloat16) for width in widths],
        in_specs=[pl.BlockSpec(memory_space=pltpu.SMEM)] + [any_spec] * len(sources),
        out_specs=[pl.BlockSpec(memory_space=pltpu.VMEM)] * len(widths),
        scratch_shapes=[pltpu.SemaphoreType.DMA((len(plan),))],
        compiler_params=pltpu.CompilerParams(vmem_limit_bytes=40 * MIB),
        cost_estimate=SMALL,
        name="packed",
    )(jnp.stack(meta).astype(jnp.int32), *sources)


def mask_kernel(first_ref, mask_ref, x_ref, out_ref):
    out_ref[...] = (x_ref[...].astype(jnp.float32) * mask_ref[0]).astype(jnp.bfloat16)


def masked_x(x_band, mask_wide, first):
    count = mask_wide.shape[0]
    block = x_band.shape[0] // count
    cols = x_band.shape[1]
    return pl.pallas_call(
        mask_kernel,
        grid_spec=pltpu.PrefetchScalarGridSpec(
            num_scalar_prefetch=1,
            grid=(count,),
            in_specs=[
                pl.BlockSpec((1, 1, cols), lambda i, f: (lax.rem(f[0] + i, count), 0, 0)),
                pl.BlockSpec((block, cols), lambda i, f: (lax.rem(f[0] + i, count), 0)),
            ],
            out_specs=pl.BlockSpec((block, cols), lambda i, f: (i, 0)),
        ),
        out_shape=jax.ShapeDtypeStruct(x_band.shape, jnp.bfloat16),
        compiler_params=pltpu.CompilerParams(vmem_limit_bytes=58 * MIB),
        cost_estimate=SMALL,
        name="masked_x",
    )(first.reshape(1), mask_wide, x_band)


PARTS = 5


def x_copies(x_refs, xv, sems, offset_of):
    n_b, _, rows, panel = xv.shape
    copies = {}
    for p in range(n_b):
        for r in range(PARTS):
            g = min(r, 1)
            at = pl.multiple_of(offset_of(p, g) * panel, panel)
            to = xv.at[p, 0] if r == 0 else xv.at[p, 1, (r - 1) * rows // 4 : r * rows // 4]
            copies[p, r] = pltpu.make_async_copy(x_refs[r].at[:, pl.ds(at, panel)], to, sems.at[p, r])
    return copies


def add_product(acc, x, strips, g, first):
    cols = pl.ds(pl.multiple_of(first * LANES, LANES), strips.shape[1])
    acc[g, :, cols] += jnp.dot(x, strips, preferred_element_type=jnp.float32)


def whole_kernel(plan, meta_ref, *refs):
    n_b = len(plan)
    x_refs, refs = refs[:PARTS], refs[PARTS:]
    b_refs, (out_ref, xv, bv, acc, x_sems, b_sems, out_sems) = refs[:-7], refs[-7:]
    quarter = bv.shape[2]
    low = quarter // 2
    is_end = meta_ref[0]

    def offset_of(p, g):
        return meta_ref[2 + 2 * p + g]

    def b_middle(p):
        return [pltpu.make_async_copy(b_refs[plan[p][0]].at[:, :quarter], bv.at[p], b_sems.at[p, 0])]

    def b_end(p):
        copies = []
        for k, (operand, first, count, at, to) in enumerate(plan[p][1]):
            to = meta_ref[1] if to is None else to
            source = b_refs[operand].at[:, first * LANES : (first + count) * LANES]
            copies.append(pltpu.make_async_copy(source, bv.at[to, :, at * LANES : (at + count) * LANES], b_sems.at[p, k]))
        return copies

    def on_each(p, do):
        @pl.when(is_end == 0)
        def _():
            for copy in b_middle(p):
                do(copy)

        @pl.when(is_end != 0)
        def _():
            for copy in b_end(p):
                do(copy)

    copies = x_copies(x_refs, xv, x_sems, offset_of)
    for p in range(n_b):
        on_each(p, lambda copy: copy.start())
        for r in range(PARTS):
            copies[p, r].start()
    outs = [
        pltpu.make_async_copy(acc.at[g, :, low : low + quarter], out_ref.at[g], out_sems.at[g]) for g in range(2)
    ]

    def wait_for(p):
        for k in [p] if p < n_b - 2 else range(n_b - 2, n_b) if p == n_b - 2 else []:
            on_each(k, lambda copy: copy.wait())
        for r in range(PARTS):
            copies[p, r].wait()

    middle = quarter // LANES // 2

    def own(g, carry):
        acc[g, :, low : low + quarter] = jnp.dot(xv[g, g], bv[g], preferred_element_type=jnp.float32)
        return carry

    def step(i, carry):
        p = jnp.where(i < 4, i % 2, i // 2)
        g = jnp.where(i < 4, 1 - i % 2, i % 2)
        for k in range(2, n_b):
            pl.when(i == 2 * k)(functools.partial(wait_for, k))
        pl.when(i == 2 * n_b - 1)(outs[0].start)
        offset = offset_of(p, g)
        for k in range(2 * middle):
            if k == middle:
                continue
            first, last = max(0, middle - k), min(2 * middle, 3 * middle - k)

            @pl.when(offset == k)
            def _():
                strips = bv[p, :, first * LANES : last * LANES]
                acc[g, :, (k + first) * LANES : (k + last) * LANES] += jnp.dot(
                    xv[p, g], strips, preferred_element_type=jnp.float32
                )

        return carry

    for p in range(2):
        wait_for(p)
    lax.fori_loop(0, 2, own, 0)
    lax.fori_loop(2, 2 * n_b, step, 0)
    outs[1].start()
    for out in outs:
        out.wait()


def whole_products(meta, xs, operands, plan):
    rows = xs[0].shape[0] // 2
    panel, quarter = operands[plan[0][0]].shape
    n_b = len(plan)
    any_spec = pl.BlockSpec(memory_space=pl.ANY)
    x_spec = pl.BlockSpec(memory_space=pltpu.HBM)
    return pl.pallas_call(
        functools.partial(whole_kernel, plan),
        out_shape=jax.ShapeDtypeStruct((2, 2 * rows, quarter), jnp.float32),
        in_specs=[pl.BlockSpec(memory_space=pltpu.SMEM)] + [x_spec] * PARTS + [any_spec] * len(operands),
        out_specs=any_spec,
        scratch_shapes=[
            pltpu.VMEM((n_b, 2, 2 * rows, panel), jnp.bfloat16),
            pltpu.VMEM((n_b, panel, quarter), jnp.bfloat16),
            pltpu.VMEM((2, 2 * rows, 2 * quarter), jnp.float32),
            pltpu.SemaphoreType.DMA((n_b, PARTS)),
            pltpu.SemaphoreType.DMA((n_b, 3)),
            pltpu.SemaphoreType.DMA((2,)),
        ],
        compiler_params=pltpu.CompilerParams(vmem_limit_bytes=59 * MIB),
        cost_estimate=pl.CostEstimate(flops=6 * 10**9, bytes_accessed=36 * MIB, transcendentals=0),
        name="whole_products",
    )(meta, *xs, *operands)


def finish(acc, wait_for, add, at, out_refs, pieces, sems):
    half, width = out_refs[0].shape
    cols = pl.ds(pl.multiple_of(at * LANES, LANES), width)
    outs = [pltpu.make_async_copy(pieces.at[r], out_refs[r], sems.at[r]) for r in range(4)]

    def step(g, carry):
        for k in range(2):
            pl.when(g == k)(functools.partial(wait_for, k))
        add(g)
        for k in range(2):

            @pl.when(g == k)
            def _():
                for r in range(2 * k, 2 * k + 2):
                    rows = slice((r % 2) * half, (r % 2 + 1) * half)
                    pieces[r] = acc[k, rows, cols].astype(jnp.bfloat16)
                    outs[r].start()

        return carry

    lax.fori_loop(0, 2, step, 0)
    for copy in outs:
        copy.wait()


def last_kernel(has_b, meta_ref, *refs):
    x_refs, (prev_ref, middle_ref, end_ref, second_ref), refs = refs[:PARTS], refs[PARTS : PARTS + 4], refs[PARTS + 4 :]
    b_ref, refs = (refs[0], refs[1:]) if has_b else (None, refs)
    out_refs, xv, bv, acc, pieces, x_sems, b_sems, prev_sems, out_sems = refs[:4], *refs[4:]
    quarter = bv.shape[2]
    half = quarter // 2
    band = quarter // LANES
    width = out_refs[0].shape[1]
    is_end = meta_ref[0]

    def offset_of(p, g):
        return meta_ref[4 + 2 * p + g]

    def strips(first):
        return pl.ds(pl.multiple_of(first * LANES, LANES), width)

    x_loads = x_copies(x_refs, xv, x_sems, offset_of)
    middle = [
        pltpu.make_async_copy(middle_ref, bv.at[0], b_sems.at[0]),
        pltpu.make_async_copy(second_ref, bv.at[1], b_sems.at[1]),
    ]
    end = [pltpu.make_async_copy(end_ref, bv.at[0], b_sems.at[0])]
    if has_b:
        n_b = b_ref.shape[1]
        few = (n_b - LANES) // 2
        end.append(pltpu.make_async_copy(b_ref, bv.at[1, :, :n_b], b_sems.at[1]))
    prev = [
        pltpu.make_async_copy(
            prev_ref.at[g, :, strips(meta_ref[3])], acc.at[g, :, strips(meta_ref[3] + band // 2)], prev_sems.at[g]
        )
        for g in range(2)
    ]

    def on_b(do):
        @pl.when(is_end == 0)
        def _():
            for copy in middle:
                do(copy)

        @pl.when(is_end != 0)
        def _():
            for copy in end:
                do(copy)

    def rows_loads(g):
        return [prev[g]] + [copy for (_, r), copy in x_loads.items() if min(r, 1) == g]

    on_b(lambda copy: copy.start())
    for g in range(2):
        for copy in rows_loads(g):
            copy.start()

    def wait_for(g):
        for copy in rows_loads(g):
            copy.wait()
        if g == 0:
            on_b(lambda copy: copy.wait())

    def add(g):
        for p in range(2):
            add_product(acc, xv[p, g], bv[0, :, p * half : (p + 1) * half], g, offset_of(p, g) + meta_ref[1])

        @pl.when(is_end == 0)
        def _():
            for p in range(2):
                add_product(acc, xv[p, g], bv[1, :, p * half : (p + 1) * half], g, offset_of(p, g) + meta_ref[2])

        if has_b:

            @pl.when(is_end != 0)
            def _():
                for p in range(2):
                    add_product(acc, xv[p, g], bv[1, :, p * few : (p + 1) * few], g, offset_of(p, g) + meta_ref[8])
                p = meta_ref[10]
                add_product(acc, xv[p, g], bv[1, :, 2 * few : n_b], g, offset_of(p, g) + meta_ref[9])

    finish(acc, wait_for, add, meta_ref[3] + band // 2, out_refs, pieces, out_sems)


def last_products(meta, xs, prev, middle, end, second, b, count, name):
    rows = xs[0].shape[0] // 2
    panel, quarter = second.shape
    any_spec = pl.BlockSpec(memory_space=pl.ANY)
    x_spec = pl.BlockSpec(memory_space=pltpu.HBM)
    operands = [prev, middle, end, second] + ([] if b is None else [b])
    width = count * LANES
    return pl.pallas_call(
        functools.partial(last_kernel, b is not None),
        out_shape=[jax.ShapeDtypeStruct((rows, width), jnp.bfloat16)] * 4,
        in_specs=[pl.BlockSpec(memory_space=pltpu.SMEM)] + [x_spec] * PARTS + [any_spec] * len(operands),
        out_specs=[any_spec] * 4,
        scratch_shapes=[
            pltpu.VMEM((2, 2, 2 * rows, panel), jnp.bfloat16),
            pltpu.VMEM((2, panel, quarter), jnp.bfloat16),
            pltpu.VMEM((2, 2 * rows, 2 * quarter), jnp.float32),
            pltpu.VMEM((4, rows, width), jnp.bfloat16),
            pltpu.SemaphoreType.DMA((2, PARTS)),
            pltpu.SemaphoreType.DMA((2,)),
            pltpu.SemaphoreType.DMA((2,)),
            pltpu.SemaphoreType.DMA((4,)),
        ],
        compiler_params=pltpu.CompilerParams(vmem_limit_bytes=59 * MIB),
        cost_estimate=SMALL,
        name=name,
    )(meta, *xs, *operands)


def assemble_kernel(place_ref, mask_ref, *refs):
    n = 4
    pieces, (out_ref, made, sem) = refs[:n], refs[-3:]
    steps = mask_ref.shape[0]
    rows = made.shape[0] // steps
    panel = n * LANES
    first = pl.multiple_of(place_ref[1] * panel, panel)
    for r in range(n):
        t = jnp.bitwise_xor(place_ref[0], r)
        for j in range(made.shape[1] // panel):
            to = pl.multiple_of(j * panel + t * LANES, LANES)
            for i in range(steps):
                keep = mask_ref[i, :, pl.ds(pl.multiple_of(first + to, LANES), LANES)]
                value = pieces[r][i * rows : (i + 1) * rows, j * LANES : (j + 1) * LANES].astype(jnp.float32)
                made[i * rows : (i + 1) * rows, pl.ds(to, LANES)] = (value * keep).astype(jnp.bfloat16)
    copy = pltpu.make_async_copy(made, out_ref.at[:, pl.ds(first, made.shape[1])], sem)
    copy.start()
    copy.wait()


def assembled(place, keep_wide, pieces, out=None):
    rows, width = pieces[0].shape
    cols = keep_wide.shape[2]
    vmem_spec = pl.BlockSpec(memory_space=pltpu.VMEM)
    any_spec = pl.BlockSpec(memory_space=pltpu.HBM)
    operands = [place, keep_wide, *pieces] + ([] if out is None else [out])
    return pl.pallas_call(
        assemble_kernel,
        out_shape=jax.ShapeDtypeStruct((rows, cols), jnp.bfloat16),
        in_specs=[pl.BlockSpec(memory_space=pltpu.SMEM)] + [vmem_spec] * 5 + [any_spec] * (len(operands) - 6),
        out_specs=any_spec,
        scratch_shapes=[pltpu.VMEM((rows, width * len(pieces)), jnp.bfloat16), pltpu.SemaphoreType.DMA],
        input_output_aliases={} if out is None else {6: 0},
        compiler_params=pltpu.CompilerParams(vmem_limit_bytes=16 * MIB),
        cost_estimate=SMALL,
        name="assembled",
    )(*operands)


def widen(mask, block):
    rows, cols = mask.shape
    wide = jnp.broadcast_to(mask.astype(jnp.float32)[:, :, None], (rows, cols, block))
    return wide.reshape(rows, 1, cols * block)


def together(*values):
    return lax.optimization_barrier(values)


def pairs_in_line(x_band, w_band, a_mask, keep_mask):
    panel = x_band.shape[0]
    block = panel // a_mask.shape[0]
    g, c = lax.axis_index("grid"), lax.axis_index("depth")
    z, y = g // 2, g % 2
    left = z < 2
    is_end = ((z == 0) | (z == 3)).astype(jnp.int32)
    toward = jnp.where(left, 1, -1)
    q = 2 * y + c

    swap = [(0, 2), (1, 3), (2, 0), (3, 1), (4, 6), (5, 7), (6, 4), (7, 5)]
    outward = [(2, 0), (3, 1), (4, 6), (5, 7)]
    cross = [(2, 4), (3, 5), (4, 2), (5, 3)]
    across = [(i, i ^ 1) for i in range(8)]
    layers = [(0, 1), (1, 0)]
    opposite = [(i, i ^ 3) for i in range(16)]

    def line(value, pairs):
        return lax.ppermute(value, "grid", pairs)

    first_out, second_out = jnp.where(left, 0, 4), jnp.where(left, 4, 0)
    first_in, second_in = second_out, first_out
    last_in = jnp.where(left, 2, 4)

    sent_b = b_strips(w_band, q ^ 2, 58)
    own_b = line(sent_b, across)
    sent_b, w_band = together(sent_b, w_band)
    own_a = b_strips(w_band, q, 58)
    swap_a = line(own_a, swap)
    cross_a = line(own_a, cross)
    mask_wide = widen(a_mask, block)
    rows = a_mask.shape[0]
    x_own = masked_x(x_band, mask_wide, c * rows // 2)
    x_mine = [x_own[k * panel // 4 : (k + 1) * panel // 4] for k in range(2)]
    own_b, *x_mine = together(own_b, *x_mine)
    own_b, swap_a = together(own_b, swap_a)
    swap_b = line(own_b, swap)
    cross_b = line(own_b, cross)
    x_across = [line(part, across) for part in x_mine]

    mid_a = line(cross_a[:, 5 * LANES :], outward)
    mid_b, fwd_first = packed(
        [y, first_out],
        [cross_a, cross_b, swap_a, swap_b],
        [10, 8],
        [
            (0, 0, 3, 0, 0, (0, 0)),
            (1, 0, 3, 0, 0, (0, 1)),
            (0, 3, 2, 0, 3, None),
            (1, 3, 5, 0, 5, None),
            (2, (1,), 4, 1, 0, None),
            (3, (1,), 4, 1, 4, None),
        ],
    )
    (fwd_second,) = packed([second_out], [swap_a, swap_b], [8], [(0, (0,), 4, 0, 0, None), (1, (0,), 4, 0, 4, None)])
    mid_a, mid_b, fwd_first = together(mid_a, mid_b, fwd_first)
    mid_b = line(mid_b, outward)
    fwd_first = line(fwd_first, cross)
    fwd_second, *x_across = together(fwd_second, *x_across)
    far_first = line(fwd_first, outward)
    fwd_second = line(fwd_second, cross)
    x_opposite = [lax.ppermute(part, "depth", layers) for part in x_across]
    xs = [x_own] + x_across + x_opposite

    def offsets(delta):
        tilt = 2 * y - 1
        return [(2 * delta + 4) % 8, (2 * delta + tilt + 4) % 8, (2 * delta - tilt + 4) % 8, (2 * delta + 4) % 8]

    zero = jnp.zeros_like(z)
    third = offsets(jnp.where(is_end == 1, 2, -toward))
    fourth = offsets(jnp.where(is_end == 1, -toward, 2))
    meta = jnp.stack([is_end, 4 + y, *offsets(zero), *offsets(toward), *third]).astype(jnp.int32)
    plan = [
        (0, [(0, 0, 8, 0, 0)]),
        (1, [(1, 0, 8, 0, 1)]),
        (2, [(4, 0, 8, 0, 2)]),
        (3, [(5, 0, 8, 0, 3)]),
        (4, [(6, 0, 3, 0, None), (6, 3, 2, 3, 4), (7, 0, 3, 5, 4)]),
        (5, [(6, 5, 5, 3, 5)]),
    ]
    total = whole_products(meta, xs, [own_a, own_b, cross_a, cross_b, swap_a, swap_b, mid_b, mid_a], plan)
    last_at = jnp.where(left, 2, 0)
    total, last_at = together(total, last_at)
    extra_in, extra_panel = jnp.where(left, 1, 6), jnp.where(left, 1 - y, y)
    extra_at = jnp.where(left, 1, 2) + 4 * extra_panel
    (last,) = packed(
        [last_at, last_at + 4, extra_at],
        [fwd_second],
        [5],
        [(0, (0,), 2, 0, 0, None), (0, (1,), 2, 0, 2, None), (0, (2,), 1, 0, 4, None)],
    )
    far_second = line(last, outward)

    def exchanged(pieces):
        return [
            pieces[0],
            lax.ppermute(pieces[1], "depth", layers),
            line(pieces[2], across),
            lax.ppermute(pieces[3], ("grid", "depth"), opposite),
        ]

    done_at, rest_at = jnp.where(left, 3, 0), jnp.where(left, 0, 5)
    halves = [total, fwd_first, far_first, fwd_second]
    meta = jnp.stack([is_end, first_in, second_in, done_at, *fourth]).astype(jnp.int32)
    done = exchanged(last_products(meta, xs, *halves, None, 5, "half_products"))
    far_second, done[1] = together(far_second, done[1])
    keep_wide = widen(keep_mask, block)
    out = assembled(jnp.stack([q, done_at]).astype(jnp.int32), keep_wide, done)
    meta = [is_end, first_in, second_in, rest_at, *fourth, last_in, extra_in, extra_panel]
    meta = jnp.stack(meta).astype(jnp.int32)
    rest = exchanged(last_products(meta, xs, *halves, far_second, 3, "rest_products"))
    return assembled(jnp.stack([q, rest_at]).astype(jnp.int32), keep_wide, rest, out)


def solution(mesh):
    placed = (
        P(("groups", "grid"), None),
        P(("groups", "grid"), None),
        P(("groups", "grid"), None),
        P(("groups", "grid", "depth"), None),
    )

    def local(x_band, w_band, a_mask, keep_mask):
        panel, cols = x_band.shape
        pairs = mesh.shape["grid"] == 8 and mesh.shape["depth"] == 2
        pairs = pairs and cols == 8 * panel and panel == 4 * LANES
        return (pairs_in_line if pairs else ring)(x_band, w_band, a_mask, keep_mask)

    return jax.shard_map(
        local,
        mesh=mesh,
        in_specs=placed,
        out_specs=P(("groups", "grid", "depth"), None),
        check_vma=False,
    )
```

```python
import functools

import jax
import jax.numpy as jnp
from jax import lax
from jax.experimental import pallas as pl
from jax.experimental.pallas import tpu as pltpu
from jax.sharding import PartitionSpec as P

LANES = 128
MIB = 1 << 20
SMALL = pl.CostEstimate(flops=1000, bytes_accessed=1000, transcendentals=0)


def shifted(shard, axis, by):
    count = lax.axis_size(axis)
    return lax.ppermute(shard, axis, [(i, (i + by) % count) for i in range(count)])


def expand_blocks(mask, block):
    rows, cols = mask.shape
    wide = jnp.broadcast_to(mask[:, None, :, None], (rows, block, cols, block))
    return wide.reshape(rows * block, cols * block)


def ring(x_band, w_band, a_mask, keep_mask):
    panel = x_band.shape[0]
    block = panel // a_mask.shape[0]
    band_cols = x_band.shape[1]
    xm = x_band * expand_blocks(a_mask, block).astype(jnp.bfloat16)
    rows = lax.broadcasted_iota(jnp.int32, x_band.shape, 0)
    cols = lax.broadcasted_iota(jnp.int32, x_band.shape, 1)
    identity = jnp.where(cols == rows + 4 * panel, 1.0, 0.0).astype(jnp.float32)
    b_panel = (1.5 * identity - 0.5 * w_band.astype(jnp.float32)).astype(jnp.bfloat16)
    layer = lax.axis_index("depth")
    current = shifted(b_panel, ("grid", "depth"), -5)
    wide = jnp.zeros((panel, 2 * band_cols), jnp.float32)
    for step in range(4):
        offset = 6 + layer - 2 * step
        ablock = lax.dynamic_slice_in_dim(xm, offset * panel, panel, 1)
        term = jnp.dot(ablock, current, preferred_element_type=jnp.float32)
        region = lax.dynamic_slice_in_dim(wide, offset * panel, band_cols, 1)
        wide = lax.dynamic_update_slice_in_dim(wide, region + term, offset * panel, 1)
        if step < 3:
            current = shifted(current, "grid", 2)
    partial_band = wide[:, 4 * panel : 12 * panel]
    mine = lax.psum_scatter(partial_band, "depth", scatter_dimension=0, tiled=True)
    keep = expand_blocks(keep_mask, block).astype(jnp.float32)
    return (mine * keep).astype(jnp.bfloat16)


def strips_kernel(quarter_ref, w_ref, b_ref, held, made, in_sems, out_sems):
    panel, width = held.shape
    quarter = quarter_ref[0]

    def strip(j):
        return slice(j * LANES, (j + 1) * LANES)

    def load(j):
        at = pl.multiple_of(j * panel + quarter * LANES, LANES)
        return pltpu.make_async_copy(w_ref.at[:, pl.ds(at, LANES)], held.at[:, strip(j)], in_sems.at[j])

    def give(j):
        return pltpu.make_async_copy(made.at[:, strip(j)], b_ref.at[:, strip(j)], out_sems.at[j])

    band = width // LANES
    for j in range(band):
        load(j).start()
    for j in range(band):
        load(j).wait()
        value = -0.5 * held[:, strip(j)].astype(jnp.float32)
        if j == band // 2:
            rows = lax.broadcasted_iota(jnp.int32, value.shape, 0)
            cols = lax.broadcasted_iota(jnp.int32, value.shape, 1)
            value = value + jnp.where(rows == cols + quarter * LANES, 1.5, 0.0)
        made[:, strip(j)] = value.astype(jnp.bfloat16)
        give(j).start()
    for j in range(band):
        give(j).wait()


def b_strips(w_band, quarter, limit):
    panel = w_band.shape[0]
    band = w_band.shape[1] // panel
    shape = (panel, band * LANES)
    return pl.pallas_call(
        strips_kernel,
        out_shape=jax.ShapeDtypeStruct(shape, jnp.bfloat16),
        in_specs=[
            pl.BlockSpec(memory_space=pltpu.SMEM),
            pl.BlockSpec(memory_space=pltpu.HBM),
        ],
        out_specs=pl.BlockSpec(memory_space=pl.ANY),
        scratch_shapes=[
            pltpu.VMEM(shape, jnp.bfloat16),
            pltpu.VMEM(shape, jnp.bfloat16),
            pltpu.SemaphoreType.DMA((band,)),
            pltpu.SemaphoreType.DMA((band,)),
        ],
        compiler_params=pltpu.CompilerParams(vmem_limit_bytes=limit * MIB),
        cost_estimate=SMALL,
        name="b_strips",
    )(quarter.reshape(1), w_band)


def pack_kernel(plan, n_in, meta_ref, *refs):
    sources, outs, sems = refs[:n_in], refs[n_in:-1], refs[-1]

    def on_each(do):
        for k, (source, start, count, out, to, when) in enumerate(plan):
            at = start * LANES if isinstance(start, int) else pl.multiple_of(meta_ref[start[0]] * LANES, LANES)
            copy = pltpu.make_async_copy(
                sources[source].at[:, pl.ds(at, count * LANES)],
                outs[out].at[:, to * LANES : (to + count) * LANES],
                sems.at[k],
            )
            if when is None:
                do(copy)
            else:
                pl.when(meta_ref[when[0]] == when[1])(functools.partial(do, copy))

    on_each(lambda copy: copy.start())
    on_each(lambda copy: copy.wait())


def packed(meta, sources, widths, plan):
    rows = sources[0].shape[0]
    any_spec = pl.BlockSpec(memory_space=pl.ANY)
    return pl.pallas_call(
        functools.partial(pack_kernel, plan, len(sources)),
        out_shape=[jax.ShapeDtypeStruct((rows, width * LANES), jnp.bfloat16) for width in widths],
        in_specs=[pl.BlockSpec(memory_space=pltpu.SMEM)] + [any_spec] * len(sources),
        out_specs=[pl.BlockSpec(memory_space=pltpu.VMEM)] * len(widths),
        scratch_shapes=[pltpu.SemaphoreType.DMA((len(plan),))],
        compiler_params=pltpu.CompilerParams(vmem_limit_bytes=40 * MIB),
        cost_estimate=SMALL,
        name="packed",
    )(jnp.stack(meta).astype(jnp.int32), *sources)


def mask_kernel(first_ref, mask_ref, x_ref, out_ref):
    out_ref[...] = (x_ref[...].astype(jnp.float32) * mask_ref[0]).astype(jnp.bfloat16)


def masked_x(x_band, mask_wide, first):
    count = mask_wide.shape[0]
    block = x_band.shape[0] // count
    cols = x_band.shape[1]
    return pl.pallas_call(
        mask_kernel,
        grid_spec=pltpu.PrefetchScalarGridSpec(
            num_scalar_prefetch=1,
            grid=(count,),
            in_specs=[
                pl.BlockSpec((1, 1, cols), lambda i, f: (lax.rem(f[0] + i, count), 0, 0)),
                pl.BlockSpec((block, cols), lambda i, f: (lax.rem(f[0] + i, count), 0)),
            ],
            out_specs=pl.BlockSpec((block, cols), lambda i, f: (i, 0)),
        ),
        out_shape=jax.ShapeDtypeStruct(x_band.shape, jnp.bfloat16),
        compiler_params=pltpu.CompilerParams(vmem_limit_bytes=58 * MIB),
        cost_estimate=SMALL,
        name="masked_x",
    )(first.reshape(1), mask_wide, x_band)


PARTS = 5


def x_copies(x_refs, xv, sems, offset_of):
    n_b, _, rows, panel = xv.shape
    copies = {}
    for p in range(n_b):
        for r in range(PARTS):
            g = min(r, 1)
            at = pl.multiple_of(offset_of(p, g) * panel, panel)
            to = xv.at[p, 0] if r == 0 else xv.at[p, 1, (r - 1) * rows // 4 : r * rows // 4]
            copies[p, r] = pltpu.make_async_copy(x_refs[r].at[:, pl.ds(at, panel)], to, sems.at[p, r])
    return copies


def add_product(acc, x, strips, g, first):
    cols = pl.ds(pl.multiple_of(first * LANES, LANES), strips.shape[1])
    acc[g, :, cols] += jnp.dot(x, strips, preferred_element_type=jnp.float32)


def whole_kernel(plan, meta_ref, *refs):
    n_b = len(plan)
    x_refs, refs = refs[:PARTS], refs[PARTS:]
    b_refs, (out_ref, xv, bv, acc, x_sems, b_sems, out_sems) = refs[:-7], refs[-7:]
    quarter = bv.shape[2]
    low = quarter // 2
    is_end = meta_ref[0]

    def offset_of(p, g):
        return meta_ref[2 + 2 * p + g]

    def b_middle(p):
        return [pltpu.make_async_copy(b_refs[plan[p][0]].at[:, :quarter], bv.at[p], b_sems.at[p, 0])]

    def b_end(p):
        copies = []
        for k, (operand, first, count, at, to) in enumerate(plan[p][1]):
            to = meta_ref[1] if to is None else to
            source = b_refs[operand].at[:, first * LANES : (first + count) * LANES]
            copies.append(pltpu.make_async_copy(source, bv.at[to, :, at * LANES : (at + count) * LANES], b_sems.at[p, k]))
        return copies

    def on_each(p, do):
        @pl.when(is_end == 0)
        def _():
            for copy in b_middle(p):
                do(copy)

        @pl.when(is_end != 0)
        def _():
            for copy in b_end(p):
                do(copy)

    copies = x_copies(x_refs, xv, x_sems, offset_of)
    for p in range(n_b):
        on_each(p, lambda copy: copy.start())
        for r in range(PARTS):
            copies[p, r].start()
    outs = [
        pltpu.make_async_copy(acc.at[g, :, low : low + quarter], out_ref.at[g], out_sems.at[g]) for g in range(2)
    ]

    def wait_for(p):
        for k in [p] if p < n_b - 2 else range(n_b - 2, n_b) if p == n_b - 2 else []:
            on_each(k, lambda copy: copy.wait())
        for r in range(PARTS):
            copies[p, r].wait()

    middle = quarter // LANES // 2

    def own(g, carry):
        acc[g, :, low : low + quarter] = jnp.dot(xv[g, g], bv[g], preferred_element_type=jnp.float32)
        return carry

    def step(i, carry):
        p = jnp.where(i < 4, i % 2, i // 2)
        g = jnp.where(i < 4, 1 - i % 2, i % 2)
        for k in range(2, n_b):
            pl.when(i == 2 * k)(functools.partial(wait_for, k))
        pl.when(i == 2 * n_b - 1)(outs[0].start)
        offset = offset_of(p, g)
        for k in range(2 * middle):
            if k == middle:
                continue
            first, last = max(0, middle - k), min(2 * middle, 3 * middle - k)

            @pl.when(offset == k)
            def _():
                strips = bv[p, :, first * LANES : last * LANES]
                acc[g, :, (k + first) * LANES : (k + last) * LANES] += jnp.dot(
                    xv[p, g], strips, preferred_element_type=jnp.float32
                )

        return carry

    for p in range(2):
        wait_for(p)
    lax.fori_loop(0, 2, own, 0)
    lax.fori_loop(2, 2 * n_b, step, 0)
    outs[1].start()
    for out in outs:
        out.wait()


def whole_products(meta, xs, operands, plan):
    rows = xs[0].shape[0] // 2
    panel, quarter = operands[plan[0][0]].shape
    n_b = len(plan)
    any_spec = pl.BlockSpec(memory_space=pl.ANY)
    x_spec = pl.BlockSpec(memory_space=pltpu.HBM)
    return pl.pallas_call(
        functools.partial(whole_kernel, plan),
        out_shape=jax.ShapeDtypeStruct((2, 2 * rows, quarter), jnp.float32),
        in_specs=[pl.BlockSpec(memory_space=pltpu.SMEM)] + [x_spec] * PARTS + [any_spec] * len(operands),
        out_specs=any_spec,
        scratch_shapes=[
            pltpu.VMEM((n_b, 2, 2 * rows, panel), jnp.bfloat16),
            pltpu.VMEM((n_b, panel, quarter), jnp.bfloat16),
            pltpu.VMEM((2, 2 * rows, 2 * quarter), jnp.float32),
            pltpu.SemaphoreType.DMA((n_b, PARTS)),
            pltpu.SemaphoreType.DMA((n_b, 3)),
            pltpu.SemaphoreType.DMA((2,)),
        ],
        compiler_params=pltpu.CompilerParams(vmem_limit_bytes=59 * MIB),
        cost_estimate=pl.CostEstimate(flops=6 * 10**9, bytes_accessed=36 * MIB, transcendentals=0),
        name="whole_products",
    )(meta, *xs, *operands)


def finish(acc, wait_for, add, at, out_refs, pieces, sems):
    half, width = out_refs[0].shape
    cols = pl.ds(pl.multiple_of(at * LANES, LANES), width)
    outs = [pltpu.make_async_copy(pieces.at[r], out_refs[r], sems.at[r]) for r in range(4)]

    def step(g, carry):
        for k in range(2):
            pl.when(g == k)(functools.partial(wait_for, k))
        add(g)
        for k in range(2):

            @pl.when(g == k)
            def _():
                for r in range(2 * k, 2 * k + 2):
                    rows = slice((r % 2) * half, (r % 2 + 1) * half)
                    pieces[r] = acc[k, rows, cols].astype(jnp.bfloat16)
                    outs[r].start()

        return carry

    lax.fori_loop(0, 2, step, 0)
    for copy in outs:
        copy.wait()


def last_kernel(has_b, meta_ref, *refs):
    x_refs, (prev_ref, middle_ref, end_ref, second_ref), refs = refs[:PARTS], refs[PARTS : PARTS + 4], refs[PARTS + 4 :]
    b_ref, refs = (refs[0], refs[1:]) if has_b else (None, refs)
    out_refs, xv, bv, acc, pieces, x_sems, b_sems, prev_sems, out_sems = refs[:4], *refs[4:]
    quarter = bv.shape[2]
    half = quarter // 2
    band = quarter // LANES
    width = out_refs[0].shape[1]
    is_end = meta_ref[0]

    def offset_of(p, g):
        return meta_ref[4 + 2 * p + g]

    def strips(first):
        return pl.ds(pl.multiple_of(first * LANES, LANES), width)

    x_loads = x_copies(x_refs, xv, x_sems, offset_of)
    middle = [
        pltpu.make_async_copy(middle_ref, bv.at[0], b_sems.at[0]),
        pltpu.make_async_copy(second_ref, bv.at[1], b_sems.at[1]),
    ]
    end = [pltpu.make_async_copy(end_ref, bv.at[0], b_sems.at[0])]
    if has_b:
        n_b = b_ref.shape[1]
        few = (n_b - LANES) // 2
        end.append(pltpu.make_async_copy(b_ref, bv.at[1, :, :n_b], b_sems.at[1]))
    prev = [
        pltpu.make_async_copy(
            prev_ref.at[g, :, strips(meta_ref[3])], acc.at[g, :, strips(meta_ref[3] + band // 2)], prev_sems.at[g]
        )
        for g in range(2)
    ]

    def on_b(do):
        @pl.when(is_end == 0)
        def _():
            for copy in middle:
                do(copy)

        @pl.when(is_end != 0)
        def _():
            for copy in end:
                do(copy)

    def rows_loads(g):
        return [prev[g]] + [copy for (_, r), copy in x_loads.items() if min(r, 1) == g]

    on_b(lambda copy: copy.start())
    for g in range(2):
        for copy in rows_loads(g):
            copy.start()

    def wait_for(g):
        for copy in rows_loads(g):
            copy.wait()
        if g == 0:
            on_b(lambda copy: copy.wait())

    def add(g):
        for p in range(2):
            add_product(acc, xv[p, g], bv[0, :, p * half : (p + 1) * half], g, offset_of(p, g) + meta_ref[1])

        @pl.when(is_end == 0)
        def _():
            for p in range(2):
                add_product(acc, xv[p, g], bv[1, :, p * half : (p + 1) * half], g, offset_of(p, g) + meta_ref[2])

        if has_b:

            @pl.when(is_end != 0)
            def _():
                for p in range(2):
                    add_product(acc, xv[p, g], bv[1, :, p * few : (p + 1) * few], g, offset_of(p, g) + meta_ref[8])
                p = meta_ref[10]
                add_product(acc, xv[p, g], bv[1, :, 2 * few : n_b], g, offset_of(p, g) + meta_ref[9])

    finish(acc, wait_for, add, meta_ref[3] + band // 2, out_refs, pieces, out_sems)


def last_products(meta, xs, prev, middle, end, second, b, count, name):
    rows = xs[0].shape[0] // 2
    panel, quarter = second.shape
    any_spec = pl.BlockSpec(memory_space=pl.ANY)
    x_spec = pl.BlockSpec(memory_space=pltpu.HBM)
    operands = [prev, middle, end, second] + ([] if b is None else [b])
    width = count * LANES
    return pl.pallas_call(
        functools.partial(last_kernel, b is not None),
        out_shape=[jax.ShapeDtypeStruct((rows, width), jnp.bfloat16)] * 4,
        in_specs=[pl.BlockSpec(memory_space=pltpu.SMEM)] + [x_spec] * PARTS + [any_spec] * len(operands),
        out_specs=[any_spec] * 4,
        scratch_shapes=[
            pltpu.VMEM((2, 2, 2 * rows, panel), jnp.bfloat16),
            pltpu.VMEM((2, panel, quarter), jnp.bfloat16),
            pltpu.VMEM((2, 2 * rows, 2 * quarter), jnp.float32),
            pltpu.VMEM((4, rows, width), jnp.bfloat16),
            pltpu.SemaphoreType.DMA((2, PARTS)),
            pltpu.SemaphoreType.DMA((2,)),
            pltpu.SemaphoreType.DMA((2,)),
            pltpu.SemaphoreType.DMA((4,)),
        ],
        compiler_params=pltpu.CompilerParams(vmem_limit_bytes=59 * MIB),
        cost_estimate=SMALL,
        name=name,
    )(meta, *xs, *operands)


def assemble_kernel(place_ref, mask_ref, *refs):
    n = 4
    pieces, (out_ref, made, sem) = refs[:n], refs[-3:]
    steps = mask_ref.shape[0]
    rows = made.shape[0] // steps
    panel = n * LANES
    first = pl.multiple_of(place_ref[1] * panel, panel)
    for r in range(n):
        t = jnp.bitwise_xor(place_ref[0], r)
        for j in range(made.shape[1] // panel):
            to = pl.multiple_of(j * panel + t * LANES, LANES)
            for i in range(steps):
                keep = mask_ref[i, :, pl.ds(pl.multiple_of(first + to, LANES), LANES)]
                value = pieces[r][i * rows : (i + 1) * rows, j * LANES : (j + 1) * LANES].astype(jnp.float32)
                made[i * rows : (i + 1) * rows, pl.ds(to, LANES)] = (value * keep).astype(jnp.bfloat16)
    copy = pltpu.make_async_copy(made, out_ref.at[:, pl.ds(first, made.shape[1])], sem)
    copy.start()
    copy.wait()


def assembled(place, keep_wide, pieces, out=None):
    rows, width = pieces[0].shape
    cols = keep_wide.shape[2]
    vmem_spec = pl.BlockSpec(memory_space=pltpu.VMEM)
    any_spec = pl.BlockSpec(memory_space=pltpu.HBM)
    operands = [place, keep_wide, *pieces] + ([] if out is None else [out])
    return pl.pallas_call(
        assemble_kernel,
        out_shape=jax.ShapeDtypeStruct((rows, cols), jnp.bfloat16),
        in_specs=[pl.BlockSpec(memory_space=pltpu.SMEM)] + [vmem_spec] * 5 + [any_spec] * (len(operands) - 6),
        out_specs=any_spec,
        scratch_shapes=[pltpu.VMEM((rows, width * len(pieces)), jnp.bfloat16), pltpu.SemaphoreType.DMA],
        input_output_aliases={} if out is None else {6: 0},
        compiler_params=pltpu.CompilerParams(vmem_limit_bytes=16 * MIB),
        cost_estimate=SMALL,
        name="assembled",
    )(*operands)


def widen(mask, block):
    rows, cols = mask.shape
    wide = jnp.broadcast_to(mask.astype(jnp.float32)[:, :, None], (rows, cols, block))
    return wide.reshape(rows, 1, cols * block)


def together(*values):
    return lax.optimization_barrier(values)


def pairs_in_line(x_band, w_band, a_mask, keep_mask):
    panel = x_band.shape[0]
    block = panel // a_mask.shape[0]
    g, c = lax.axis_index("grid"), lax.axis_index("depth")
    z, y = g // 2, g % 2
    left = z < 2
    is_end = ((z == 0) | (z == 3)).astype(jnp.int32)
    toward = jnp.where(left, 1, -1)
    q = 2 * y + c

    swap = [(0, 2), (1, 3), (2, 0), (3, 1), (4, 6), (5, 7), (6, 4), (7, 5)]
    outward = [(2, 0), (3, 1), (4, 6), (5, 7)]
    cross = [(2, 4), (3, 5), (4, 2), (5, 3)]
    across = [(i, i ^ 1) for i in range(8)]
    layers = [(0, 1), (1, 0)]
    opposite = [(i, i ^ 3) for i in range(16)]

    def line(value, pairs):
        return lax.ppermute(value, "grid", pairs)

    first_out, second_out = jnp.where(left, 0, 4), jnp.where(left, 4, 0)
    first_in, second_in = second_out, first_out
    last_in = jnp.where(left, 2, 4)

    sent_b = b_strips(w_band, q ^ 2, 58)
    own_b = line(sent_b, across)
    sent_b, w_band = together(sent_b, w_band)
    own_a = b_strips(w_band, q, 58)
    swap_a = line(own_a, swap)
    cross_a = line(own_a, cross)
    mask_wide = widen(a_mask, block)
    rows = a_mask.shape[0]
    x_own = masked_x(x_band, mask_wide, c * rows // 2)
    x_mine = [x_own[k * panel // 4 : (k + 1) * panel // 4] for k in range(2)]
    own_b, *x_mine = together(own_b, *x_mine)
    own_b, swap_a = together(own_b, swap_a)
    swap_b = line(own_b, swap)
    cross_b = line(own_b, cross)
    x_across = [line(part, across) for part in x_mine]

    mid_a = line(cross_a[:, 5 * LANES :], outward)
    mid_b, fwd_first = packed(
        [y, first_out],
        [cross_a, cross_b, swap_a, swap_b],
        [10, 8],
        [
            (0, 0, 3, 0, 0, (0, 0)),
            (1, 0, 3, 0, 0, (0, 1)),
            (0, 3, 2, 0, 3, None),
            (1, 3, 5, 0, 5, None),
            (2, (1,), 4, 1, 0, None),
            (3, (1,), 4, 1, 4, None),
        ],
    )
    (fwd_second,) = packed([second_out], [swap_a, swap_b], [8], [(0, (0,), 4, 0, 0, None), (1, (0,), 4, 0, 4, None)])
    mid_a, mid_b, fwd_first = together(mid_a, mid_b, fwd_first)
    mid_b = line(mid_b, outward)
    fwd_first = line(fwd_first, cross)
    fwd_second, *x_across = together(fwd_second, *x_across)
    far_first = line(fwd_first, outward)
    fwd_second = line(fwd_second, cross)
    x_opposite = [lax.ppermute(part, "depth", layers) for part in x_across]
    xs = [x_own] + x_across + x_opposite

    def offsets(delta):
        tilt = 2 * y - 1
        return [(2 * delta + 4) % 8, (2 * delta + tilt + 4) % 8, (2 * delta - tilt + 4) % 8, (2 * delta + 4) % 8]

    zero = jnp.zeros_like(z)
    third = offsets(jnp.where(is_end == 1, 2, -toward))
    fourth = offsets(jnp.where(is_end == 1, -toward, 2))
    meta = jnp.stack([is_end, 4 + y, *offsets(zero), *offsets(toward), *third]).astype(jnp.int32)
    plan = [
        (0, [(0, 0, 8, 0, 0)]),
        (1, [(1, 0, 8, 0, 1)]),
        (2, [(4, 0, 8, 0, 2)]),
        (3, [(5, 0, 8, 0, 3)]),
        (4, [(6, 0, 3, 0, None), (6, 3, 2, 3, 4), (7, 0, 3, 5, 4)]),
        (5, [(6, 5, 5, 3, 5)]),
    ]
    total = whole_products(meta, xs, [own_a, own_b, cross_a, cross_b, swap_a, swap_b, mid_b, mid_a], plan)
    last_at = jnp.where(left, 2, 0)
    total, last_at = together(total, last_at)
    extra_in, extra_panel = jnp.where(left, 1, 6), jnp.where(left, 1 - y, y)
    extra_at = jnp.where(left, 1, 2) + 4 * extra_panel
    (last,) = packed(
        [last_at, last_at + 4, extra_at],
        [fwd_second],
        [5],
        [(0, (0,), 2, 0, 0, None), (0, (1,), 2, 0, 2, None), (0, (2,), 1, 0, 4, None)],
    )
    far_second = line(last, outward)

    def exchanged(pieces):
        return [
            pieces[0],
            lax.ppermute(pieces[1], "depth", layers),
            line(pieces[2], across),
            lax.ppermute(pieces[3], ("grid", "depth"), opposite),
        ]

    done_at, rest_at = jnp.where(left, 3, 0), jnp.where(left, 0, 5)
    halves = [total, fwd_first, far_first, fwd_second]
    meta = jnp.stack([is_end, first_in, second_in, done_at, *fourth]).astype(jnp.int32)
    done = exchanged(last_products(meta, xs, *halves, None, 5, "half_products"))
    far_second, done[1] = together(far_second, done[1])
    keep_wide = widen(keep_mask, block)
    out = assembled(jnp.stack([q, done_at]).astype(jnp.int32), keep_wide, done)
    meta = [is_end, first_in, second_in, rest_at, *fourth, last_in, extra_in, extra_panel]
    meta = jnp.stack(meta).astype(jnp.int32)
    rest = exchanged(last_products(meta, xs, *halves, far_second, 3, "rest_products"))
    rest[2], rest[3] = together(rest[2], rest[3])
    rest[0], rest[1], rest[2] = together(rest[0], rest[1], rest[2])
    return assembled(jnp.stack([q, rest_at]).astype(jnp.int32), keep_wide, rest, out)


def solution(mesh):
    placed = (
        P(("groups", "grid"), None),
        P(("groups", "grid"), None),
        P(("groups", "grid"), None),
        P(("groups", "grid", "depth"), None),
    )

    def local(x_band, w_band, a_mask, keep_mask):
        panel, cols = x_band.shape
        pairs = mesh.shape["grid"] == 8 and mesh.shape["depth"] == 2
        pairs = pairs and cols == 8 * panel and panel == 4 * LANES
        return (pairs_in_line if pairs else ring)(x_band, w_band, a_mask, keep_mask)

    return jax.shard_map(
        local,
        mesh=mesh,
        in_specs=placed,
        out_specs=P(("groups", "grid", "depth"), None),
        check_vma=False,
    )
```

```python
import functools

import jax
import jax.numpy as jnp
from jax import lax
from jax.experimental import pallas as pl
from jax.experimental.pallas import tpu as pltpu
from jax.sharding import PartitionSpec as P

LANES = 128
MIB = 1 << 20
SMALL = pl.CostEstimate(flops=1000, bytes_accessed=1000, transcendentals=0)


def shifted(shard, axis, by):
    count = lax.axis_size(axis)
    return lax.ppermute(shard, axis, [(i, (i + by) % count) for i in range(count)])


def expand_blocks(mask, block):
    rows, cols = mask.shape
    wide = jnp.broadcast_to(mask[:, None, :, None], (rows, block, cols, block))
    return wide.reshape(rows * block, cols * block)


def ring(x_band, w_band, a_mask, keep_mask):
    panel = x_band.shape[0]
    block = panel // a_mask.shape[0]
    band_cols = x_band.shape[1]
    xm = x_band * expand_blocks(a_mask, block).astype(jnp.bfloat16)
    rows = lax.broadcasted_iota(jnp.int32, x_band.shape, 0)
    cols = lax.broadcasted_iota(jnp.int32, x_band.shape, 1)
    identity = jnp.where(cols == rows + 4 * panel, 1.0, 0.0).astype(jnp.float32)
    b_panel = (1.5 * identity - 0.5 * w_band.astype(jnp.float32)).astype(jnp.bfloat16)
    layer = lax.axis_index("depth")
    current = shifted(b_panel, ("grid", "depth"), -5)
    wide = jnp.zeros((panel, 2 * band_cols), jnp.float32)
    for step in range(4):
        offset = 6 + layer - 2 * step
        ablock = lax.dynamic_slice_in_dim(xm, offset * panel, panel, 1)
        term = jnp.dot(ablock, current, preferred_element_type=jnp.float32)
        region = lax.dynamic_slice_in_dim(wide, offset * panel, band_cols, 1)
        wide = lax.dynamic_update_slice_in_dim(wide, region + term, offset * panel, 1)
        if step < 3:
            current = shifted(current, "grid", 2)
    partial_band = wide[:, 4 * panel : 12 * panel]
    mine = lax.psum_scatter(partial_band, "depth", scatter_dimension=0, tiled=True)
    keep = expand_blocks(keep_mask, block).astype(jnp.float32)
    return (mine * keep).astype(jnp.bfloat16)


def strips_kernel(quarter_ref, w_ref, b_ref, held, made, in_sems, out_sems):
    panel, width = held.shape
    quarter = quarter_ref[0]

    def strip(j):
        return slice(j * LANES, (j + 1) * LANES)

    def load(j):
        at = pl.multiple_of(j * panel + quarter * LANES, LANES)
        return pltpu.make_async_copy(w_ref.at[:, pl.ds(at, LANES)], held.at[:, strip(j)], in_sems.at[j])

    def give(j):
        return pltpu.make_async_copy(made.at[:, strip(j)], b_ref.at[:, strip(j)], out_sems.at[j])

    band = width // LANES
    for j in range(band):
        load(j).start()
    for j in range(band):
        load(j).wait()
        value = -0.5 * held[:, strip(j)].astype(jnp.float32)
        if j == band // 2:
            rows = lax.broadcasted_iota(jnp.int32, value.shape, 0)
            cols = lax.broadcasted_iota(jnp.int32, value.shape, 1)
            value = value + jnp.where(rows == cols + quarter * LANES, 1.5, 0.0)
        made[:, strip(j)] = value.astype(jnp.bfloat16)
        give(j).start()
    for j in range(band):
        give(j).wait()


def b_strips(w_band, quarter, limit):
    panel = w_band.shape[0]
    band = w_band.shape[1] // panel
    shape = (panel, band * LANES)
    return pl.pallas_call(
        strips_kernel,
        out_shape=jax.ShapeDtypeStruct(shape, jnp.bfloat16),
        in_specs=[
            pl.BlockSpec(memory_space=pltpu.SMEM),
            pl.BlockSpec(memory_space=pltpu.HBM),
        ],
        out_specs=pl.BlockSpec(memory_space=pl.ANY),
        scratch_shapes=[
            pltpu.VMEM(shape, jnp.bfloat16),
            pltpu.VMEM(shape, jnp.bfloat16),
            pltpu.SemaphoreType.DMA((band,)),
            pltpu.SemaphoreType.DMA((band,)),
        ],
        compiler_params=pltpu.CompilerParams(vmem_limit_bytes=limit * MIB),
        cost_estimate=SMALL,
        name="b_strips",
    )(quarter.reshape(1), w_band)


def pack_kernel(plan, n_in, meta_ref, *refs):
    sources, outs, sems = refs[:n_in], refs[n_in:-1], refs[-1]

    def on_each(do):
        for k, (source, start, count, out, to, when) in enumerate(plan):
            at = start * LANES if isinstance(start, int) else pl.multiple_of(meta_ref[start[0]] * LANES, LANES)
            copy = pltpu.make_async_copy(
                sources[source].at[:, pl.ds(at, count * LANES)],
                outs[out].at[:, to * LANES : (to + count) * LANES],
                sems.at[k],
            )
            if when is None:
                do(copy)
            else:
                pl.when(meta_ref[when[0]] == when[1])(functools.partial(do, copy))

    on_each(lambda copy: copy.start())
    on_each(lambda copy: copy.wait())


def packed(meta, sources, widths, plan):
    rows = sources[0].shape[0]
    any_spec = pl.BlockSpec(memory_space=pl.ANY)
    return pl.pallas_call(
        functools.partial(pack_kernel, plan, len(sources)),
        out_shape=[jax.ShapeDtypeStruct((rows, width * LANES), jnp.bfloat16) for width in widths],
        in_specs=[pl.BlockSpec(memory_space=pltpu.SMEM)] + [any_spec] * len(sources),
        out_specs=[pl.BlockSpec(memory_space=pltpu.VMEM)] * len(widths),
        scratch_shapes=[pltpu.SemaphoreType.DMA((len(plan),))],
        compiler_params=pltpu.CompilerParams(vmem_limit_bytes=40 * MIB),
        cost_estimate=SMALL,
        name="packed",
    )(jnp.stack(meta).astype(jnp.int32), *sources)


def mask_kernel(first_ref, mask_ref, x_ref, out_ref):
    out_ref[...] = (x_ref[...].astype(jnp.float32) * mask_ref[0]).astype(jnp.bfloat16)


def masked_rows(x_band, mask_wide, first, count):
    block = x_band.shape[0] // mask_wide.shape[0]
    cols = x_band.shape[1]
    return pl.pallas_call(
        mask_kernel,
        grid_spec=pltpu.PrefetchScalarGridSpec(
            num_scalar_prefetch=1,
            grid=(count,),
            in_specs=[
                pl.BlockSpec((1, 1, cols), lambda i, f: (f[0] + i, 0, 0)),
                pl.BlockSpec((block, cols), lambda i, f: (f[0] + i, 0)),
            ],
            out_specs=pl.BlockSpec((block, cols), lambda i, f: (i, 0)),
        ),
        out_shape=jax.ShapeDtypeStruct((count * block, cols), jnp.bfloat16),
        compiler_params=pltpu.CompilerParams(vmem_limit_bytes=58 * MIB),
        cost_estimate=SMALL,
        name="masked_rows",
    )(first.reshape(1), mask_wide, x_band)


PARTS = 8


def x_copies(x_refs, xv, sems, offset_of):
    n_b, _, rows, panel = xv.shape
    part = 2 * rows // PARTS
    copies = {}
    for p in range(n_b):
        for r in range(PARTS):
            g, k = divmod(r, PARTS // 2)
            at = pl.multiple_of(offset_of(p, g) * panel, panel)
            copies[p, r] = pltpu.make_async_copy(
                x_refs[r].at[:, pl.ds(at, panel)],
                xv.at[p, g, k * part : (k + 1) * part],
                sems.at[p, r],
            )
    return copies


def add_product(acc, x, strips, g, first):
    cols = pl.ds(pl.multiple_of(first * LANES, LANES), strips.shape[1])
    acc[g, :, cols] += jnp.dot(x, strips, preferred_element_type=jnp.float32)


def whole_kernel(plan, meta_ref, *refs):
    n_b = len(plan)
    x_refs, refs = refs[:PARTS], refs[PARTS:]
    b_refs, (out_ref, xv, bv, acc, x_sems, b_sems, out_sems) = refs[:-7], refs[-7:]
    quarter = bv.shape[2]
    low = quarter // 2
    is_end = meta_ref[0]

    def offset_of(p, g):
        return meta_ref[2 + 2 * p + g]

    def b_middle(p):
        return [pltpu.make_async_copy(b_refs[plan[p][0]].at[:, :quarter], bv.at[p], b_sems.at[p, 0])]

    def b_end(p):
        copies = []
        for k, (operand, first, count, at, to) in enumerate(plan[p][1]):
            to = meta_ref[1] if to is None else to
            source = b_refs[operand].at[:, first * LANES : (first + count) * LANES]
            copies.append(pltpu.make_async_copy(source, bv.at[to, :, at * LANES : (at + count) * LANES], b_sems.at[p, k]))
        return copies

    def on_each(p, do):
        @pl.when(is_end == 0)
        def _():
            for copy in b_middle(p):
                do(copy)

        @pl.when(is_end != 0)
        def _():
            for copy in b_end(p):
                do(copy)

    copies = x_copies(x_refs, xv, x_sems, offset_of)
    for p in range(n_b):
        on_each(p, lambda copy: copy.start())
        for r in range(PARTS):
            copies[p, r].start()
    outs = [
        pltpu.make_async_copy(acc.at[g, :, low : low + quarter], out_ref.at[g], out_sems.at[g]) for g in range(2)
    ]

    def wait_for(p):
        for k in [p] if p < n_b - 2 else range(n_b - 2, n_b) if p == n_b - 2 else []:
            on_each(k, lambda copy: copy.wait())
        for r in range(PARTS):
            copies[p, r].wait()

    middle = quarter // LANES // 2

    def own(g, carry):
        acc[g, :, low : low + quarter] = jnp.dot(xv[g, g], bv[g], preferred_element_type=jnp.float32)
        return carry

    def step(i, carry):
        p = jnp.where(i < 4, i % 2, i // 2)
        g = jnp.where(i < 4, 1 - i % 2, i % 2)
        for k in range(2, n_b):
            pl.when(i == 2 * k)(functools.partial(wait_for, k))
        pl.when(i == 2 * n_b - 1)(outs[0].start)
        offset = offset_of(p, g)
        for k in range(2 * middle):
            if k == middle:
                continue
            first, last = max(0, middle - k), min(2 * middle, 3 * middle - k)

            @pl.when(offset == k)
            def _():
                strips = bv[p, :, first * LANES : last * LANES]
                acc[g, :, (k + first) * LANES : (k + last) * LANES] += jnp.dot(
                    xv[p, g], strips, preferred_element_type=jnp.float32
                )

        return carry

    for p in range(2):
        wait_for(p)
    lax.fori_loop(0, 2, own, 0)
    lax.fori_loop(2, 2 * n_b, step, 0)
    outs[1].start()
    for out in outs:
        out.wait()


def whole_products(meta, xs, operands, plan):
    rows = PARTS // 4 * xs[0].shape[0]
    panel, quarter = operands[plan[0][0]].shape
    n_b = len(plan)
    any_spec = pl.BlockSpec(memory_space=pl.ANY)
    x_spec = pl.BlockSpec(memory_space=pltpu.HBM)
    return pl.pallas_call(
        functools.partial(whole_kernel, plan),
        out_shape=jax.ShapeDtypeStruct((2, 2 * rows, quarter), jnp.float32),
        in_specs=[pl.BlockSpec(memory_space=pltpu.SMEM)] + [x_spec] * PARTS + [any_spec] * len(operands),
        out_specs=any_spec,
        scratch_shapes=[
            pltpu.VMEM((n_b, 2, 2 * rows, panel), jnp.bfloat16),
            pltpu.VMEM((n_b, panel, quarter), jnp.bfloat16),
            pltpu.VMEM((2, 2 * rows, 2 * quarter), jnp.float32),
            pltpu.SemaphoreType.DMA((n_b, PARTS)),
            pltpu.SemaphoreType.DMA((n_b, 3)),
            pltpu.SemaphoreType.DMA((2,)),
        ],
        compiler_params=pltpu.CompilerParams(vmem_limit_bytes=59 * MIB),
        cost_estimate=pl.CostEstimate(flops=6 * 10**9, bytes_accessed=36 * MIB, transcendentals=0),
        name="whole_products",
    )(meta, *xs, *operands)


def finish(acc, wait_for, add, at, out_refs, pieces, sems):
    half, width = out_refs[0].shape
    cols = pl.ds(pl.multiple_of(at * LANES, LANES), width)
    outs = [pltpu.make_async_copy(pieces.at[r], out_refs[r], sems.at[r]) for r in range(4)]

    def step(g, carry):
        for k in range(2):
            pl.when(g == k)(functools.partial(wait_for, k))
        add(g)
        for k in range(2):

            @pl.when(g == k)
            def _():
                for r in range(2 * k, 2 * k + 2):
                    rows = slice((r % 2) * half, (r % 2 + 1) * half)
                    pieces[r] = acc[k, rows, cols].astype(jnp.bfloat16)
                    outs[r].start()

        return carry

    lax.fori_loop(0, 2, step, 0)
    for copy in outs:
        copy.wait()


def last_kernel(has_b, meta_ref, *refs):
    x_refs, (prev_ref, middle_ref, end_ref, second_ref), refs = refs[:PARTS], refs[PARTS : PARTS + 4], refs[PARTS + 4 :]
    b_ref, refs = (refs[0], refs[1:]) if has_b else (None, refs)
    out_refs, xv, bv, acc, pieces, x_sems, b_sems, prev_sems, out_sems = refs[:4], *refs[4:]
    quarter = bv.shape[2]
    half = quarter // 2
    band = quarter // LANES
    width = out_refs[0].shape[1]
    is_end = meta_ref[0]

    def offset_of(p, g):
        return meta_ref[4 + 2 * p + g]

    def strips(first):
        return pl.ds(pl.multiple_of(first * LANES, LANES), width)

    x_loads = x_copies(x_refs, xv, x_sems, offset_of)
    middle = [
        pltpu.make_async_copy(middle_ref, bv.at[0], b_sems.at[0]),
        pltpu.make_async_copy(second_ref, bv.at[1], b_sems.at[1]),
    ]
    end = [pltpu.make_async_copy(end_ref, bv.at[0], b_sems.at[0])]
    if has_b:
        n_b = b_ref.shape[1]
        few = (n_b - LANES) // 2
        end.append(pltpu.make_async_copy(b_ref, bv.at[1, :, :n_b], b_sems.at[1]))
    prev = [
        pltpu.make_async_copy(
            prev_ref.at[g, :, strips(meta_ref[3])], acc.at[g, :, strips(meta_ref[3] + band // 2)], prev_sems.at[g]
        )
        for g in range(2)
    ]

    def on_b(do):
        @pl.when(is_end == 0)
        def _():
            for copy in middle:
                do(copy)

        @pl.when(is_end != 0)
        def _():
            for copy in end:
                do(copy)

    def rows_loads(g):
        return [prev[g]] + [copy for (_, r), copy in x_loads.items() if r // (PARTS // 2) == g]

    on_b(lambda copy: copy.start())
    for g in range(2):
        for copy in rows_loads(g):
            copy.start()

    def wait_for(g):
        for copy in rows_loads(g):
            copy.wait()
        if g == 0:
            on_b(lambda copy: copy.wait())

    def add(g):
        for p in range(2):
            add_product(acc, xv[p, g], bv[0, :, p * half : (p + 1) * half], g, offset_of(p, g) + meta_ref[1])

        @pl.when(is_end == 0)
        def _():
            for p in range(2):
                add_product(acc, xv[p, g], bv[1, :, p * half : (p + 1) * half], g, offset_of(p, g) + meta_ref[2])

        if has_b:

            @pl.when(is_end != 0)
            def _():
                for p in range(2):
                    add_product(acc, xv[p, g], bv[1, :, p * few : (p + 1) * few], g, offset_of(p, g) + meta_ref[8])
                p = meta_ref[10]
                add_product(acc, xv[p, g], bv[1, :, 2 * few : n_b], g, offset_of(p, g) + meta_ref[9])

    finish(acc, wait_for, add, meta_ref[3] + band // 2, out_refs, pieces, out_sems)


def last_products(meta, xs, prev, middle, end, second, b, count, name):
    rows = PARTS // 4 * xs[0].shape[0]
    panel, quarter = second.shape
    any_spec = pl.BlockSpec(memory_space=pl.ANY)
    x_spec = pl.BlockSpec(memory_space=pltpu.HBM)
    operands = [prev, middle, end, second] + ([] if b is None else [b])
    width = count * LANES
    return pl.pallas_call(
        functools.partial(last_kernel, b is not None),
        out_shape=[jax.ShapeDtypeStruct((rows, width), jnp.bfloat16)] * 4,
        in_specs=[pl.BlockSpec(memory_space=pltpu.SMEM)] + [x_spec] * PARTS + [any_spec] * len(operands),
        out_specs=[any_spec] * 4,
        scratch_shapes=[
            pltpu.VMEM((2, 2, 2 * rows, panel), jnp.bfloat16),
            pltpu.VMEM((2, panel, quarter), jnp.bfloat16),
            pltpu.VMEM((2, 2 * rows, 2 * quarter), jnp.float32),
            pltpu.VMEM((4, rows, width), jnp.bfloat16),
            pltpu.SemaphoreType.DMA((2, PARTS)),
            pltpu.SemaphoreType.DMA((2,)),
            pltpu.SemaphoreType.DMA((2,)),
            pltpu.SemaphoreType.DMA((4,)),
        ],
        compiler_params=pltpu.CompilerParams(vmem_limit_bytes=59 * MIB),
        cost_estimate=SMALL,
        name=name,
    )(meta, *xs, *operands)


def assemble_kernel(place_ref, mask_ref, *refs):
    n = 4
    pieces, (out_ref, made, sem) = refs[:n], refs[-3:]
    steps = mask_ref.shape[0]
    rows = made.shape[0] // steps
    panel = n * LANES
    first = pl.multiple_of(place_ref[1] * panel, panel)
    for r in range(n):
        t = jnp.bitwise_xor(place_ref[0], r)
        for j in range(made.shape[1] // panel):
            to = pl.multiple_of(j * panel + t * LANES, LANES)
            for i in range(steps):
                keep = mask_ref[i, :, pl.ds(pl.multiple_of(first + to, LANES), LANES)]
                value = pieces[r][i * rows : (i + 1) * rows, j * LANES : (j + 1) * LANES].astype(jnp.float32)
                made[i * rows : (i + 1) * rows, pl.ds(to, LANES)] = (value * keep).astype(jnp.bfloat16)
    copy = pltpu.make_async_copy(made, out_ref.at[:, pl.ds(first, made.shape[1])], sem)
    copy.start()
    copy.wait()


def assembled(place, keep_wide, pieces, out=None):
    rows, width = pieces[0].shape
    cols = keep_wide.shape[2]
    vmem_spec = pl.BlockSpec(memory_space=pltpu.VMEM)
    any_spec = pl.BlockSpec(memory_space=pltpu.HBM)
    operands = [place, keep_wide, *pieces] + ([] if out is None else [out])
    return pl.pallas_call(
        assemble_kernel,
        out_shape=jax.ShapeDtypeStruct((rows, cols), jnp.bfloat16),
        in_specs=[pl.BlockSpec(memory_space=pltpu.SMEM)] + [vmem_spec] * 5 + [any_spec] * (len(operands) - 6),
        out_specs=any_spec,
        scratch_shapes=[pltpu.VMEM((rows, width * len(pieces)), jnp.bfloat16), pltpu.SemaphoreType.DMA],
        input_output_aliases={} if out is None else {6: 0},
        compiler_params=pltpu.CompilerParams(vmem_limit_bytes=16 * MIB),
        cost_estimate=SMALL,
        name="assembled",
    )(*operands)


def widen(mask, block):
    rows, cols = mask.shape
    wide = jnp.broadcast_to(mask.astype(jnp.float32)[:, :, None], (rows, cols, block))
    return wide.reshape(rows, 1, cols * block)


def together(*values):
    return lax.optimization_barrier(values)


def pairs_in_line(x_band, w_band, a_mask, keep_mask):
    panel = x_band.shape[0]
    block = panel // a_mask.shape[0]
    g, c = lax.axis_index("grid"), lax.axis_index("depth")
    z, y = g // 2, g % 2
    left = z < 2
    is_end = ((z == 0) | (z == 3)).astype(jnp.int32)
    toward = jnp.where(left, 1, -1)
    q = 2 * y + c

    swap = [(0, 2), (1, 3), (2, 0), (3, 1), (4, 6), (5, 7), (6, 4), (7, 5)]
    outward = [(2, 0), (3, 1), (4, 6), (5, 7)]
    cross = [(2, 4), (3, 5), (4, 2), (5, 3)]
    across = [(i, i ^ 1) for i in range(8)]
    layers = [(0, 1), (1, 0)]
    opposite = [(i, i ^ 3) for i in range(16)]

    def line(value, pairs):
        return lax.ppermute(value, "grid", pairs)

    first_out, second_out = jnp.where(left, 0, 4), jnp.where(left, 4, 0)
    first_in, second_in = second_out, first_out
    last_in = jnp.where(left, 2, 4)

    sent_b = b_strips(w_band, q ^ 2, 58)
    own_b = line(sent_b, across)
    sent_b, w_band = together(sent_b, w_band)
    own_a = b_strips(w_band, q, 58)
    swap_a = line(own_a, swap)
    cross_a = line(own_a, cross)
    mask_wide = widen(a_mask, block)
    rows = a_mask.shape[0]
    x_mine = [masked_rows(x_band, mask_wide, c * rows // 2 + k * rows // 4, rows // 4) for k in range(2)]
    own_b, *x_mine = together(own_b, *x_mine)
    own_b, swap_a = together(own_b, swap_a)
    swap_b = line(own_b, swap)
    cross_b = line(own_b, cross)
    x_across = [line(part, across) for part in x_mine]
    x_rest = [masked_rows(x_band, mask_wide, (1 - c) * rows // 2 + k * rows // 4, rows // 4) for k in range(2)]

    mid_a = line(cross_a[:, 5 * LANES :], outward)
    mid_b, fwd_first = packed(
        [y, first_out],
        [cross_a, cross_b, swap_a, swap_b],
        [10, 8],
        [
            (0, 0, 3, 0, 0, (0, 0)),
            (1, 0, 3, 0, 0, (0, 1)),
            (0, 3, 2, 0, 3, None),
            (1, 3, 5, 0, 5, None),
            (2, (1,), 4, 1, 0, None),
            (3, (1,), 4, 1, 4, None),
        ],
    )
    (fwd_second,) = packed([second_out], [swap_a, swap_b], [8], [(0, (0,), 4, 0, 0, None), (1, (0,), 4, 0, 4, None)])
    mid_a, mid_b, fwd_first, *x_rest = together(mid_a, mid_b, fwd_first, *x_rest)
    mid_b = line(mid_b, outward)
    fwd_first = line(fwd_first, cross)
    fwd_second, *x_across = together(fwd_second, *x_across)
    far_first = line(fwd_first, outward)
    fwd_second = line(fwd_second, cross)
    x_opposite = [lax.ppermute(part, "depth", layers) for part in x_across]
    xs = x_mine + x_rest + x_across + x_opposite

    def offsets(delta):
        tilt = 2 * y - 1
        return [(2 * delta + 4) % 8, (2 * delta + tilt + 4) % 8, (2 * delta - tilt + 4) % 8, (2 * delta + 4) % 8]

    zero = jnp.zeros_like(z)
    third = offsets(jnp.where(is_end == 1, 2, -toward))
    fourth = offsets(jnp.where(is_end == 1, -toward, 2))
    meta = jnp.stack([is_end, 4 + y, *offsets(zero), *offsets(toward), *third]).astype(jnp.int32)
    plan = [
        (0, [(0, 0, 8, 0, 0)]),
        (1, [(1, 0, 8, 0, 1)]),
        (2, [(4, 0, 8, 0, 2)]),
        (3, [(5, 0, 8, 0, 3)]),
        (4, [(6, 0, 3, 0, None), (6, 3, 2, 3, 4), (7, 0, 3, 5, 4)]),
        (5, [(6, 5, 5, 3, 5)]),
    ]
    total = whole_products(meta, xs, [own_a, own_b, cross_a, cross_b, swap_a, swap_b, mid_b, mid_a], plan)
    last_at = jnp.where(left, 2, 0)
    total, last_at = together(total, last_at)
    extra_in, extra_panel = jnp.where(left, 1, 6), jnp.where(left, 1 - y, y)
    extra_at = jnp.where(left, 1, 2) + 4 * extra_panel
    (last,) = packed(
        [last_at, last_at + 4, extra_at],
        [fwd_second],
        [5],
        [(0, (0,), 2, 0, 0, None), (0, (1,), 2, 0, 2, None), (0, (2,), 1, 0, 4, None)],
    )
    far_second = line(last, outward)

    def exchanged(pieces):
        return [
            pieces[0],
            lax.ppermute(pieces[1], "depth", layers),
            line(pieces[2], across),
            lax.ppermute(pieces[3], ("grid", "depth"), opposite),
        ]

    done_at, rest_at = jnp.where(left, 3, 0), jnp.where(left, 0, 5)
    halves = [total, fwd_first, far_first, fwd_second]
    meta = jnp.stack([is_end, first_in, second_in, done_at, *fourth]).astype(jnp.int32)
    done = exchanged(last_products(meta, xs, *halves, None, 5, "half_products"))
    far_second, done[1] = together(far_second, done[1])
    keep_wide = widen(keep_mask, block)
    out = assembled(jnp.stack([q, done_at]).astype(jnp.int32), keep_wide, done)
    meta = [is_end, first_in, second_in, rest_at, *fourth, last_in, extra_in, extra_panel]
    meta = jnp.stack(meta).astype(jnp.int32)
    rest = exchanged(last_products(meta, xs, *halves, far_second, 3, "rest_products"))
    return assembled(jnp.stack([q, rest_at]).astype(jnp.int32), keep_wide, rest, out)


def solution(mesh):
    placed = (
        P(("groups", "grid"), None),
        P(("groups", "grid"), None),
        P(("groups", "grid"), None),
        P(("groups", "grid", "depth"), None),
    )

    def local(x_band, w_band, a_mask, keep_mask):
        panel, cols = x_band.shape
        pairs = mesh.shape["grid"] == 8 and mesh.shape["depth"] == 2
        pairs = pairs and cols == 8 * panel and panel == 4 * LANES
        return (pairs_in_line if pairs else ring)(x_band, w_band, a_mask, keep_mask)

    return jax.shard_map(
        local,
        mesh=mesh,
        in_specs=placed,
        out_specs=P(("groups", "grid", "depth"), None),
        check_vma=False,
    )
```

```python
import functools

import jax
import jax.numpy as jnp
from jax import lax
from jax.experimental import pallas as pl
from jax.experimental.pallas import tpu as pltpu
from jax.sharding import PartitionSpec as P

LANES = 128
MIB = 1 << 20
SMALL = pl.CostEstimate(flops=1000, bytes_accessed=1000, transcendentals=0)


def shifted(shard, axis, by):
    count = lax.axis_size(axis)
    return lax.ppermute(shard, axis, [(i, (i + by) % count) for i in range(count)])


def expand_blocks(mask, block):
    rows, cols = mask.shape
    wide = jnp.broadcast_to(mask[:, None, :, None], (rows, block, cols, block))
    return wide.reshape(rows * block, cols * block)


def ring(x_band, w_band, a_mask, keep_mask):
    panel = x_band.shape[0]
    block = panel // a_mask.shape[0]
    band_cols = x_band.shape[1]
    xm = x_band * expand_blocks(a_mask, block).astype(jnp.bfloat16)
    rows = lax.broadcasted_iota(jnp.int32, x_band.shape, 0)
    cols = lax.broadcasted_iota(jnp.int32, x_band.shape, 1)
    identity = jnp.where(cols == rows + 4 * panel, 1.0, 0.0).astype(jnp.float32)
    b_panel = (1.5 * identity - 0.5 * w_band.astype(jnp.float32)).astype(jnp.bfloat16)
    layer = lax.axis_index("depth")
    current = shifted(b_panel, ("grid", "depth"), -5)
    wide = jnp.zeros((panel, 2 * band_cols), jnp.float32)
    for step in range(4):
        offset = 6 + layer - 2 * step
        ablock = lax.dynamic_slice_in_dim(xm, offset * panel, panel, 1)
        term = jnp.dot(ablock, current, preferred_element_type=jnp.float32)
        region = lax.dynamic_slice_in_dim(wide, offset * panel, band_cols, 1)
        wide = lax.dynamic_update_slice_in_dim(wide, region + term, offset * panel, 1)
        if step < 3:
            current = shifted(current, "grid", 2)
    partial_band = wide[:, 4 * panel : 12 * panel]
    mine = lax.psum_scatter(partial_band, "depth", scatter_dimension=0, tiled=True)
    keep = expand_blocks(keep_mask, block).astype(jnp.float32)
    return (mine * keep).astype(jnp.bfloat16)


def strips_kernel(quarter_ref, w_ref, b_ref, held, made, in_sems, out_sems):
    panel, width = held.shape
    quarter = quarter_ref[0]

    def strip(j):
        return slice(j * LANES, (j + 1) * LANES)

    def load(j):
        at = pl.multiple_of(j * panel + quarter * LANES, LANES)
        return pltpu.make_async_copy(w_ref.at[:, pl.ds(at, LANES)], held.at[:, strip(j)], in_sems.at[j])

    def give(j):
        return pltpu.make_async_copy(made.at[:, strip(j)], b_ref.at[:, strip(j)], out_sems.at[j])

    band = width // LANES
    for j in range(band):
        load(j).start()
    for j in range(band):
        load(j).wait()
        value = -0.5 * held[:, strip(j)].astype(jnp.float32)
        if j == band // 2:
            rows = lax.broadcasted_iota(jnp.int32, value.shape, 0)
            cols = lax.broadcasted_iota(jnp.int32, value.shape, 1)
            value = value + jnp.where(rows == cols + quarter * LANES, 1.5, 0.0)
        made[:, strip(j)] = value.astype(jnp.bfloat16)
        give(j).start()
    for j in range(band):
        give(j).wait()


def b_strips(w_band, quarter, limit):
    panel = w_band.shape[0]
    band = w_band.shape[1] // panel
    shape = (panel, band * LANES)
    return pl.pallas_call(
        strips_kernel,
        out_shape=jax.ShapeDtypeStruct(shape, jnp.bfloat16),
        in_specs=[
            pl.BlockSpec(memory_space=pltpu.SMEM),
            pl.BlockSpec(memory_space=pltpu.HBM),
        ],
        out_specs=pl.BlockSpec(memory_space=pl.ANY),
        scratch_shapes=[
            pltpu.VMEM(shape, jnp.bfloat16),
            pltpu.VMEM(shape, jnp.bfloat16),
            pltpu.SemaphoreType.DMA((band,)),
            pltpu.SemaphoreType.DMA((band,)),
        ],
        compiler_params=pltpu.CompilerParams(vmem_limit_bytes=limit * MIB),
        cost_estimate=SMALL,
        name="b_strips",
    )(quarter.reshape(1), w_band)


def pack_kernel(plan, n_in, meta_ref, *refs):
    sources, outs, sems = refs[:n_in], refs[n_in:-1], refs[-1]

    def on_each(do):
        for k, (source, start, count, out, to, when) in enumerate(plan):
            at = start * LANES if isinstance(start, int) else pl.multiple_of(meta_ref[start[0]] * LANES, LANES)
            copy = pltpu.make_async_copy(
                sources[source].at[:, pl.ds(at, count * LANES)],
                outs[out].at[:, to * LANES : (to + count) * LANES],
                sems.at[k],
            )
            if when is None:
                do(copy)
            else:
                pl.when(meta_ref[when[0]] == when[1])(functools.partial(do, copy))

    on_each(lambda copy: copy.start())
    on_each(lambda copy: copy.wait())


def packed(meta, sources, widths, plan):
    rows = sources[0].shape[0]
    any_spec = pl.BlockSpec(memory_space=pl.ANY)
    return pl.pallas_call(
        functools.partial(pack_kernel, plan, len(sources)),
        out_shape=[jax.ShapeDtypeStruct((rows, width * LANES), jnp.bfloat16) for width in widths],
        in_specs=[pl.BlockSpec(memory_space=pltpu.SMEM)] + [any_spec] * len(sources),
        out_specs=[pl.BlockSpec(memory_space=pltpu.VMEM)] * len(widths),
        scratch_shapes=[pltpu.SemaphoreType.DMA((len(plan),))],
        compiler_params=pltpu.CompilerParams(vmem_limit_bytes=40 * MIB),
        cost_estimate=SMALL,
        name="packed",
    )(jnp.stack(meta).astype(jnp.int32), *sources)


def mask_kernel(first_ref, mask_ref, x_ref, out_ref):
    out_ref[...] = (x_ref[...].astype(jnp.float32) * mask_ref[0]).astype(jnp.bfloat16)


def masked_rows(x_band, mask_wide, first, count):
    block = x_band.shape[0] // mask_wide.shape[0]
    cols = x_band.shape[1]
    return pl.pallas_call(
        mask_kernel,
        grid_spec=pltpu.PrefetchScalarGridSpec(
            num_scalar_prefetch=1,
            grid=(count,),
            in_specs=[
                pl.BlockSpec((1, 1, cols), lambda i, f: (f[0] + i, 0, 0)),
                pl.BlockSpec((block, cols), lambda i, f: (f[0] + i, 0)),
            ],
            out_specs=pl.BlockSpec((block, cols), lambda i, f: (i, 0)),
        ),
        out_shape=jax.ShapeDtypeStruct((count * block, cols), jnp.bfloat16),
        compiler_params=pltpu.CompilerParams(vmem_limit_bytes=58 * MIB),
        cost_estimate=SMALL,
        name="masked_rows",
    )(first.reshape(1), mask_wide, x_band)


PARTS = 8


def x_copies(x_refs, xv, sems, offset_of):
    n_b, _, rows, panel = xv.shape
    part = 2 * rows // PARTS
    copies = {}
    for p in range(n_b):
        for r in range(PARTS):
            g, k = divmod(r, PARTS // 2)
            at = pl.multiple_of(offset_of(p, g) * panel, panel)
            copies[p, r] = pltpu.make_async_copy(
                x_refs[r].at[:, pl.ds(at, panel)],
                xv.at[p, g, k * part : (k + 1) * part],
                sems.at[p, r],
            )
    return copies


def add_product(acc, x, strips, g, first):
    cols = pl.ds(pl.multiple_of(first * LANES, LANES), strips.shape[1])
    acc[g, :, cols] += jnp.dot(x, strips, preferred_element_type=jnp.float32)


def whole_kernel(plan, meta_ref, *refs):
    n_b = len(plan)
    x_refs, refs = refs[:PARTS], refs[PARTS:]
    b_refs, (out_ref, xv, bv, acc, x_sems, b_sems, out_sems) = refs[:-7], refs[-7:]
    quarter = bv.shape[2]
    low = quarter // 2
    is_end = meta_ref[0]

    def offset_of(p, g):
        return meta_ref[3 + 2 * p + g]

    def b_middle(p):
        if p < 2:
            return [pltpu.make_async_copy(b_refs[p], bv.at[p], b_sems.at[p, 0])]
        first = meta_ref[2] if p < 4 else 1 - meta_ref[2]
        cols = pl.ds(pl.multiple_of(first * LANES, LANES), quarter - LANES)
        return [pltpu.make_async_copy(b_refs[plan[p][0]].at[:, cols], bv.at[p, :, cols], b_sems.at[p, 0])]

    def b_end(p):
        copies = []
        for k, (operand, first, count, at, to) in enumerate(plan[p][1]):
            to = meta_ref[1] if to is None else to
            source = b_refs[operand].at[:, first * LANES : (first + count) * LANES]
            copies.append(pltpu.make_async_copy(source, bv.at[to, :, at * LANES : (at + count) * LANES], b_sems.at[p, k]))
        return copies

    def on_each(p, do):
        @pl.when(is_end == 0)
        def _():
            for copy in b_middle(p):
                do(copy)

        @pl.when(is_end != 0)
        def _():
            for copy in b_end(p):
                do(copy)

    copies = x_copies(x_refs, xv, x_sems, offset_of)
    for p in range(n_b):
        on_each(p, lambda copy: copy.start())
        for r in range(PARTS):
            copies[p, r].start()
    outs = [
        pltpu.make_async_copy(acc.at[g, :, low : low + quarter], out_ref.at[g], out_sems.at[g]) for g in range(2)
    ]

    def wait_for(p):
        for k in [p] if p < n_b - 2 else range(n_b - 2, n_b) if p == n_b - 2 else []:
            on_each(k, lambda copy: copy.wait())
        for r in range(PARTS):
            copies[p, r].wait()

    middle = quarter // LANES // 2

    def own(g, carry):
        acc[g, :, low : low + quarter] = jnp.dot(xv[g, g], bv[g], preferred_element_type=jnp.float32)
        return carry

    def step(i, carry):
        p = jnp.where(i < 4, i % 2, i // 2)
        g = jnp.where(i < 4, 1 - i % 2, i % 2)
        for k in range(2, n_b):
            pl.when(i == 2 * k)(functools.partial(wait_for, k))
        pl.when(i == 2 * n_b - 1)(outs[0].start)
        offset = offset_of(p, g)
        for k in range(2 * middle):
            if k == middle:
                continue
            first, last = max(0, middle - k), min(2 * middle, 3 * middle - k)

            @pl.when(offset == k)
            def _():
                strips = bv[p, :, first * LANES : last * LANES]
                acc[g, :, (k + first) * LANES : (k + last) * LANES] += jnp.dot(
                    xv[p, g], strips, preferred_element_type=jnp.float32
                )

        return carry

    for p in range(2):
        wait_for(p)
    lax.fori_loop(0, 2, own, 0)
    lax.fori_loop(2, 2 * n_b, step, 0)
    outs[1].start()
    for out in outs:
        out.wait()


def whole_products(meta, xs, operands, plan):
    rows = PARTS // 4 * xs[0].shape[0]
    panel, quarter = operands[plan[0][0]].shape
    n_b = len(plan)
    any_spec = pl.BlockSpec(memory_space=pl.ANY)
    x_spec = pl.BlockSpec(memory_space=pltpu.HBM)
    return pl.pallas_call(
        functools.partial(whole_kernel, plan),
        out_shape=jax.ShapeDtypeStruct((2, 2 * rows, quarter), jnp.float32),
        in_specs=[pl.BlockSpec(memory_space=pltpu.SMEM)] + [x_spec] * PARTS + [any_spec] * len(operands),
        out_specs=any_spec,
        scratch_shapes=[
            pltpu.VMEM((n_b, 2, 2 * rows, panel), jnp.bfloat16),
            pltpu.VMEM((n_b, panel, quarter), jnp.bfloat16),
            pltpu.VMEM((2, 2 * rows, 2 * quarter), jnp.float32),
            pltpu.SemaphoreType.DMA((n_b, PARTS)),
            pltpu.SemaphoreType.DMA((n_b, 3)),
            pltpu.SemaphoreType.DMA((2,)),
        ],
        compiler_params=pltpu.CompilerParams(vmem_limit_bytes=59 * MIB),
        cost_estimate=pl.CostEstimate(flops=6 * 10**9, bytes_accessed=36 * MIB, transcendentals=0),
        name="whole_products",
    )(meta, *xs, *operands)


def finish(acc, wait_for, add, at, out_refs, pieces, sems):
    half, width = out_refs[0].shape
    cols = pl.ds(pl.multiple_of(at * LANES, LANES), width)
    outs = [pltpu.make_async_copy(pieces.at[r], out_refs[r], sems.at[r]) for r in range(4)]

    def step(g, carry):
        for k in range(2):
            pl.when(g == k)(functools.partial(wait_for, k))
        add(g)
        for k in range(2):

            @pl.when(g == k)
            def _():
                for r in range(2 * k, 2 * k + 2):
                    rows = slice((r % 2) * half, (r % 2 + 1) * half)
                    pieces[r] = acc[k, rows, cols].astype(jnp.bfloat16)
                    outs[r].start()

        return carry

    lax.fori_loop(0, 2, step, 0)
    for copy in outs:
        copy.wait()


def last_kernel(has_b, meta_ref, *refs):
    x_refs, (prev_ref, middle_ref, end_ref, second_ref), refs = refs[:PARTS], refs[PARTS : PARTS + 4], refs[PARTS + 4 :]
    b_ref, refs = (refs[0], refs[1:]) if has_b else (None, refs)
    out_refs, xv, bv, acc, pieces, x_sems, b_sems, prev_sems, out_sems = refs[:4], *refs[4:]
    quarter = bv.shape[2]
    half = quarter // 2
    band = quarter // LANES
    width = out_refs[0].shape[1]
    is_end = meta_ref[0]

    def offset_of(p, g):
        return meta_ref[4 + 2 * p + g]

    def strips(first):
        return pl.ds(pl.multiple_of(first * LANES, LANES), width)

    x_loads = x_copies(x_refs, xv, x_sems, offset_of)
    middle = [
        pltpu.make_async_copy(middle_ref, bv.at[0], b_sems.at[0]),
        pltpu.make_async_copy(second_ref, bv.at[1], b_sems.at[1]),
    ]
    end = [pltpu.make_async_copy(end_ref, bv.at[0], b_sems.at[0])]
    if has_b:
        n_b = b_ref.shape[1]
        few = (n_b - LANES) // 2
        end.append(pltpu.make_async_copy(b_ref, bv.at[1, :, :n_b], b_sems.at[1]))
    prev = [
        pltpu.make_async_copy(
            prev_ref.at[g, :, strips(meta_ref[3])], acc.at[g, :, strips(meta_ref[3] + band // 2)], prev_sems.at[g]
        )
        for g in range(2)
    ]

    def on_b(do):
        @pl.when(is_end == 0)
        def _():
            for copy in middle:
                do(copy)

        @pl.when(is_end != 0)
        def _():
            for copy in end:
                do(copy)

    def rows_loads(g):
        return [prev[g]] + [copy for (_, r), copy in x_loads.items() if r // (PARTS // 2) == g]

    on_b(lambda copy: copy.start())
    for g in range(2):
        for copy in rows_loads(g):
            copy.start()

    def wait_for(g):
        for copy in rows_loads(g):
            copy.wait()
        if g == 0:
            on_b(lambda copy: copy.wait())

    def add(g):
        for p in range(2):
            add_product(acc, xv[p, g], bv[0, :, p * half : (p + 1) * half], g, offset_of(p, g) + meta_ref[1])

        @pl.when(is_end == 0)
        def _():
            for p in range(2):
                add_product(acc, xv[p, g], bv[1, :, p * half : (p + 1) * half], g, offset_of(p, g) + meta_ref[2])

        if has_b:

            @pl.when(is_end != 0)
            def _():
                for p in range(2):
                    add_product(acc, xv[p, g], bv[1, :, p * few : (p + 1) * few], g, offset_of(p, g) + meta_ref[8])
                p = meta_ref[10]
                add_product(acc, xv[p, g], bv[1, :, 2 * few : n_b], g, offset_of(p, g) + meta_ref[9])

    finish(acc, wait_for, add, meta_ref[3] + band // 2, out_refs, pieces, out_sems)


def last_products(meta, xs, prev, middle, end, second, b, count, name):
    rows = PARTS // 4 * xs[0].shape[0]
    panel, quarter = second.shape
    any_spec = pl.BlockSpec(memory_space=pl.ANY)
    x_spec = pl.BlockSpec(memory_space=pltpu.HBM)
    operands = [prev, middle, end, second] + ([] if b is None else [b])
    width = count * LANES
    return pl.pallas_call(
        functools.partial(last_kernel, b is not None),
        out_shape=[jax.ShapeDtypeStruct((rows, width), jnp.bfloat16)] * 4,
        in_specs=[pl.BlockSpec(memory_space=pltpu.SMEM)] + [x_spec] * PARTS + [any_spec] * len(operands),
        out_specs=[any_spec] * 4,
        scratch_shapes=[
            pltpu.VMEM((2, 2, 2 * rows, panel), jnp.bfloat16),
            pltpu.VMEM((2, panel, quarter), jnp.bfloat16),
            pltpu.VMEM((2, 2 * rows, 2 * quarter), jnp.float32),
            pltpu.VMEM((4, rows, width), jnp.bfloat16),
            pltpu.SemaphoreType.DMA((2, PARTS)),
            pltpu.SemaphoreType.DMA((2,)),
            pltpu.SemaphoreType.DMA((2,)),
            pltpu.SemaphoreType.DMA((4,)),
        ],
        compiler_params=pltpu.CompilerParams(vmem_limit_bytes=59 * MIB),
        cost_estimate=SMALL,
        name=name,
    )(meta, *xs, *operands)


def assemble_kernel(place_ref, mask_ref, *refs):
    n = 4
    pieces, (out_ref, made, sem) = refs[:n], refs[-3:]
    steps = mask_ref.shape[0]
    rows = made.shape[0] // steps
    panel = n * LANES
    first = pl.multiple_of(place_ref[1] * panel, panel)
    for r in range(n):
        t = jnp.bitwise_xor(place_ref[0], r)
        for j in range(made.shape[1] // panel):
            to = pl.multiple_of(j * panel + t * LANES, LANES)
            for i in range(steps):
                keep = mask_ref[i, :, pl.ds(pl.multiple_of(first + to, LANES), LANES)]
                value = pieces[r][i * rows : (i + 1) * rows, j * LANES : (j + 1) * LANES].astype(jnp.float32)
                made[i * rows : (i + 1) * rows, pl.ds(to, LANES)] = (value * keep).astype(jnp.bfloat16)
    copy = pltpu.make_async_copy(made, out_ref.at[:, pl.ds(first, made.shape[1])], sem)
    copy.start()
    copy.wait()


def assembled(place, keep_wide, pieces, out=None):
    rows, width = pieces[0].shape
    cols = keep_wide.shape[2]
    vmem_spec = pl.BlockSpec(memory_space=pltpu.VMEM)
    any_spec = pl.BlockSpec(memory_space=pltpu.HBM)
    operands = [place, keep_wide, *pieces] + ([] if out is None else [out])
    return pl.pallas_call(
        assemble_kernel,
        out_shape=jax.ShapeDtypeStruct((rows, cols), jnp.bfloat16),
        in_specs=[pl.BlockSpec(memory_space=pltpu.SMEM)] + [vmem_spec] * 5 + [any_spec] * (len(operands) - 6),
        out_specs=any_spec,
        scratch_shapes=[pltpu.VMEM((rows, width * len(pieces)), jnp.bfloat16), pltpu.SemaphoreType.DMA],
        input_output_aliases={} if out is None else {6: 0},
        compiler_params=pltpu.CompilerParams(vmem_limit_bytes=16 * MIB),
        cost_estimate=SMALL,
        name="assembled",
    )(*operands)


def widen(mask, block):
    rows, cols = mask.shape
    wide = jnp.broadcast_to(mask.astype(jnp.float32)[:, :, None], (rows, cols, block))
    return wide.reshape(rows, 1, cols * block)


def together(*values):
    return lax.optimization_barrier(values)


def pairs_in_line(x_band, w_band, a_mask, keep_mask):
    panel = x_band.shape[0]
    block = panel // a_mask.shape[0]
    g, c = lax.axis_index("grid"), lax.axis_index("depth")
    z, y = g // 2, g % 2
    left = z < 2
    is_end = ((z == 0) | (z == 3)).astype(jnp.int32)
    toward = jnp.where(left, 1, -1)
    q = 2 * y + c

    swap = [(0, 2), (1, 3), (2, 0), (3, 1), (4, 6), (5, 7), (6, 4), (7, 5)]
    outward = [(2, 0), (3, 1), (4, 6), (5, 7)]
    cross = [(2, 4), (3, 5), (4, 2), (5, 3)]
    across = [(i, i ^ 1) for i in range(8)]
    layers = [(0, 1), (1, 0)]
    opposite = [(i, i ^ 3) for i in range(16)]

    def line(value, pairs):
        return lax.ppermute(value, "grid", pairs)

    first_out, second_out = jnp.where(left, 0, 4), jnp.where(left, 4, 0)
    first_in, second_in = second_out, first_out
    last_in = jnp.where(left, 2, 4)

    sent_b = b_strips(w_band, q ^ 2, 58)
    own_b = line(sent_b, across)
    sent_b, w_band = together(sent_b, w_band)
    own_a = b_strips(w_band, q, 58)
    swap_a = line(own_a, swap)
    cross_a = line(own_a, cross)
    mask_wide = widen(a_mask, block)
    rows = a_mask.shape[0]
    x_mine = [masked_rows(x_band, mask_wide, c * rows // 2 + k * rows // 4, rows // 4) for k in range(2)]
    own_b, *x_mine = together(own_b, *x_mine)
    own_b, swap_a = together(own_b, swap_a)
    swap_b = line(own_b, swap)
    cross_b = line(own_b, cross)
    x_across = [line(part, across) for part in x_mine]
    x_rest = [masked_rows(x_band, mask_wide, (1 - c) * rows // 2 + k * rows // 4, rows // 4) for k in range(2)]

    mid_a = line(cross_a[:, 5 * LANES :], outward)
    mid_b, fwd_first = packed(
        [y, first_out],
        [cross_a, cross_b, swap_a, swap_b],
        [10, 8],
        [
            (0, 0, 3, 0, 0, (0, 0)),
            (1, 0, 3, 0, 0, (0, 1)),
            (0, 3, 2, 0, 3, None),
            (1, 3, 5, 0, 5, None),
            (2, (1,), 4, 1, 0, None),
            (3, (1,), 4, 1, 4, None),
        ],
    )
    (fwd_second,) = packed([second_out], [swap_a, swap_b], [8], [(0, (0,), 4, 0, 0, None), (1, (0,), 4, 0, 4, None)])
    mid_a, mid_b, fwd_first, *x_rest = together(mid_a, mid_b, fwd_first, *x_rest)
    mid_b = line(mid_b, outward)
    fwd_first = line(fwd_first, cross)
    fwd_second, *x_across = together(fwd_second, *x_across)
    far_first = line(fwd_first, outward)
    fwd_second = line(fwd_second, cross)
    x_opposite = [lax.ppermute(part, "depth", layers) for part in x_across]
    xs = x_mine + x_rest + x_across + x_opposite

    def offsets(delta):
        tilt = 2 * y - 1
        return [(2 * delta + 4) % 8, (2 * delta + tilt + 4) % 8, (2 * delta - tilt + 4) % 8, (2 * delta + 4) % 8]

    zero = jnp.zeros_like(z)
    third = offsets(jnp.where(is_end == 1, 2, -toward))
    fourth = offsets(jnp.where(is_end == 1, -toward, 2))
    meta = jnp.stack([is_end, 4 + y, jnp.where(left, 0, 1), *offsets(zero), *offsets(toward), *third]).astype(jnp.int32)
    plan = [
        (0, [(0, 0, 8, 0, 0)]),
        (1, [(1, 0, 8, 0, 1)]),
        (2, [(4, 0, 8, 0, 2)]),
        (3, [(5, 0, 8, 0, 3)]),
        (4, [(6, 0, 3, 0, None), (6, 3, 2, 3, 4), (7, 0, 3, 5, 4)]),
        (5, [(6, 5, 5, 3, 5)]),
    ]
    total = whole_products(meta, xs, [own_a, own_b, cross_a, cross_b, swap_a, swap_b, mid_b, mid_a], plan)
    last_at = jnp.where(left, 2, 0)
    total, last_at = together(total, last_at)
    extra_in, extra_panel = jnp.where(left, 1, 6), jnp.where(left, 1 - y, y)
    extra_at = jnp.where(left, 1, 2) + 4 * extra_panel
    (last,) = packed(
        [last_at, last_at + 4, extra_at],
        [fwd_second],
        [5],
        [(0, (0,), 2, 0, 0, None), (0, (1,), 2, 0, 2, None), (0, (2,), 1, 0, 4, None)],
    )
    far_second = line(last, outward)

    def exchanged(pieces):
        return [
            pieces[0],
            lax.ppermute(pieces[1], "depth", layers),
            line(pieces[2], across),
            lax.ppermute(pieces[3], ("grid", "depth"), opposite),
        ]

    done_at, rest_at = jnp.where(left, 3, 0), jnp.where(left, 0, 5)
    halves = [total, fwd_first, far_first, fwd_second]
    meta = jnp.stack([is_end, first_in, second_in, done_at, *fourth]).astype(jnp.int32)
    done = exchanged(last_products(meta, xs, *halves, None, 5, "half_products"))
    far_second, done[1] = together(far_second, done[1])
    keep_wide = widen(keep_mask, block)
    out = assembled(jnp.stack([q, done_at]).astype(jnp.int32), keep_wide, done)
    meta = [is_end, first_in, second_in, rest_at, *fourth, last_in, extra_in, extra_panel]
    meta = jnp.stack(meta).astype(jnp.int32)
    rest = exchanged(last_products(meta, xs, *halves, far_second, 3, "rest_products"))
    return assembled(jnp.stack([q, rest_at]).astype(jnp.int32), keep_wide, rest, out)


def solution(mesh):
    placed = (
        P(("groups", "grid"), None),
        P(("groups", "grid"), None),
        P(("groups", "grid"), None),
        P(("groups", "grid", "depth"), None),
    )

    def local(x_band, w_band, a_mask, keep_mask):
        panel, cols = x_band.shape
        pairs = mesh.shape["grid"] == 8 and mesh.shape["depth"] == 2
        pairs = pairs and cols == 8 * panel and panel == 4 * LANES
        return (pairs_in_line if pairs else ring)(x_band, w_band, a_mask, keep_mask)

    return jax.shard_map(
        local,
        mesh=mesh,
        in_specs=placed,
        out_specs=P(("groups", "grid", "depth"), None),
        check_vma=False,
    )
```
